32 devices in a mesh: section: 2 (over x), tensor: 4 (over y, core), dp: 4 (over z).
Axes of the slice: x: 2, y: 2, z: 4, core: 2. Of those that a mesh axis runs over, the one named last changes fastest.
Arguments:
- inputs: bfloat16 [8, 1024, 1280], P('dp', 'tensor'), may hold values from -6 to 6
- cotangent: bfloat16 [8, 1024, 1280], P('dp', 'tensor'), may hold values from -6 to 6
- gain_attn: float32 [2, 1280], P('section'), may hold values from 0.25 to 1.75
- w_query: bfloat16 [2, 1280, 1280], P('section', None, 'tensor'), may hold values from -0.15625 to 0.15625
- w_key: bfloat16 [2, 1280, 1280], P('section', None, 'tensor'), may hold values from -0.15625 to 0.15625
- w_value: bfloat16 [2, 1280, 1280], P('section', None, 'tensor'), may hold values from -0.15625 to 0.15625
- w_out: bfloat16 [2, 1280, 1280], P('section', 'tensor'), may hold values from -0.625 to 0.625
- dim_scale: float32 [2, 80], P('section'), may hold values from -1 to 1.5
- gain_mlp: float32 [2, 1280], P('section'), may hold values from 0.25 to 1.75
- w_up: bfloat16 [2, 1280, 1280], P('section', None, 'tensor'), may hold values from -0.15625 to 0.15625
- w_down: bfloat16 [2, 1280, 1280], P('section', 'tensor'), may hold values from -0.15625 to 0.15625
Outputs:
- layer_out: bfloat16 [2, 8, 1024, 1280], P('section', 'dp', 'tensor')
- input_grads: bfloat16 [2, 8, 1024, 1280], P('section', 'dp', 'tensor')
- grad_gain_attn: float32 [2, 1280], P('section')
- grad_query: float32 [2, 1280, 1280], P('section', 'dp', 'tensor')
- grad_key: float32 [2, 1280, 1280], P('section', 'dp', 'tensor')
- grad_value: float32 [2, 1280, 1280], P('section', 'dp', 'tensor')
- grad_out: float32 [2, 1280, 1280], P('section', 'tensor', 'dp')
- grad_scale: float32 [2, 80], P('section')
- gradient_feedforward_gain: float32 [2, 1280], P('section')
- grad_up: float32 [2, 1280, 1280], P('section', 'dp', 'tensor')
- grad_down: float32 [2, 1280, 1280], P('section', 'tensor', 'dp')
The draws below stay inside these ranges and needn't reach their ends.
All inputs are finite; a program needn't handle non-finite values.
Results may differ from the reference program's by a relative error of at most 0.025.
The reference program's roundings to bfloat16 on the way count: a program that leaves them out, or rounds other values in their place, can miss the bound.
Values may be sent and summed in bfloat16 or wider, within the bound.
A program may use at most 192 MiB of HBM per device.

```python
import math
import jax
import jax.numpy as jnp
from jax import lax

D = 1280
HEADS = 16
HD = 80
FF = 1280
LEN = 1024
SECTIONS = 2
SEQUENCES = 8


def raised(array, rng, source, target, blocks, factor):
    owner, partner = [(jnp.arange(array.shape[axis_at]) // (array.shape[axis_at] // blocks)).reshape([-1 if axis == axis_at else 1 for axis in range(array.ndim)]) for axis_at in (source, target)]
    chosen = jax.random.permutation(rng, blocks)[partner]
    strong = (owner == chosen) | (owner == (partner + blocks // 2) % blocks)
    return jnp.where(strong, factor * array, array)


def steps_of(stream_key, shape, cuts, least, largest):
    level, own = 1.0, jax.random.fold_in(stream_key, 6)
    for dim, blocks in cuts:
        draws = jnp.exp(jax.random.uniform(jax.random.fold_in(own, dim), (blocks,), jnp.float32, least / len(cuts), largest / len(cuts)))
        level = level * jnp.repeat(draws, shape[dim] // blocks).reshape([-1 if axis == dim else 1 for axis in range(len(shape))])
    return level


def normal_values(own_key, dims, width, most, split=(), dtype=jnp.bfloat16):
    drawn = width * jax.random.normal(own_key, dims, jnp.float32)
    if split:
        drawn = drawn * steps_of(own_key, dims, split, -0.22, 0.18)
    return jnp.clip(drawn, -most, most).astype(dtype)


def heavy_noise(rng, dims, spread, most, split, heavy, kind=jnp.bfloat16):
    drawn = spread * jax.random.normal(rng, dims, jnp.float32)
    if split:
        drawn = drawn * steps_of(rng, dims, split, -0.22, 0.18)
    return jnp.clip(raised(drawn, jax.random.fold_in(rng, 3), *heavy), -most, most).astype(kind)


def setup_inputs(seed: int = 0) -> dict:
    keys = jax.random.split(jax.random.key(seed), 12)
    inputs = heavy_noise(keys[0], (SEQUENCES, LEN, D), 1.0, 6.0, ((0, 4), (1, 4)), (0, 2, 4, 2.0))
    cotangent = normal_values(keys[1], (SEQUENCES, LEN, D), 1.0, 6.0, ((0, 4), (1, 4)))
    gain_attn = jnp.clip(1.0 + 0.15 * jax.random.normal(keys[2], (SECTIONS, D), jnp.float32), 0.25, 1.75)
    w_query = normal_values(keys[3], (SECTIONS, D, D), D ** -0.5, 0.15625, ((0, 2), (2, 4)))
    w_key = normal_values(keys[4], (SECTIONS, D, D), D ** -0.5, 0.15625, ((0, 2), (2, 4)))
    w_value = normal_values(keys[5], (SECTIONS, D, D), D ** -0.5, 0.15625, ((0, 2), (2, 4)))
    w_out = normal_values(keys[6], (SECTIONS, D, D), (D // 16) ** -0.5, 0.625, ((0, 2), (1, 4)))
    dim_scale = jnp.clip(-1.0 + 2.5 * jax.random.uniform(keys[7], (SECTIONS, HD), jnp.float32) ** steps_of(keys[7], (SECTIONS, HD), ((0, 2),), -0.2, 0.2), -1.0, 1.5)
    gain_mlp = jnp.clip(1.0 + 0.15 * jax.random.normal(keys[8], (SECTIONS, D), jnp.float32), 0.25, 1.75)
    w_up = normal_values(keys[9], (SECTIONS, D, FF), D ** -0.5, 0.15625, ((0, 2), (2, 4)))
    w_down = normal_values(keys[10], (SECTIONS, FF, D), FF ** -0.5, 0.15625, ((0, 2), (1, 4)))
    return dict(inputs=inputs, cotangent=cotangent, gain_attn=gain_attn, w_query=w_query, w_key=w_key, w_value=w_value, w_out=w_out, dim_scale=dim_scale, gain_mlp=gain_mlp, w_up=w_up, w_down=w_down)


@jax.custom_vjp
def low(v):
    return lax.optimization_barrier(v.astype(jnp.bfloat16)).astype(jnp.float32)

@jax.custom_vjp
def low_back(v):
    return v

def low_keep(v):
    return (low(v), None)

def low_pass(kept, grad):
    return (grad,)

def back_keep(v):
    return (v, None)

def back_low(kept, grad):
    return (low(grad),)
low.defvjp(low_keep, low_pass)
low_back.defvjp(back_keep, back_low)
EPS = 1e-06
LOG2E = 1.442695041

def matmul(left_operand, right_operand):
    return jnp.einsum('pjw,wi->pji', left_operand, right_operand, precision=lax.Precision.HIGHEST)

def rms_norm(hidden, gain):
    return hidden * lax.rsqrt(lax.optimization_barrier(jnp.mean(hidden * hidden, axis=-1, keepdims=True)) + EPS) * gain

def attention(triple):
    query, key, value = triple
    length = query.shape[0]
    q_heads = query.reshape(length, HEADS, HD)
    k_heads = key.reshape(length, HEADS, HD)
    v_heads = value.reshape(length, HEADS, HD)
    scores = low_back(jnp.einsum('qhd,khd->hqk', q_heads, k_heads, precision=lax.Precision.HIGHEST))
    keep = jnp.arange(length)[:, None] >= jnp.arange(length)[None, :]
    scores = jnp.where(keep[None], scores, -1e+30)
    probs = low(jax.nn.softmax(scores, axis=-1))
    mixed = jnp.einsum('hqk,khd->qhd', probs, v_heads, precision=lax.Precision.HIGHEST)
    return mixed.reshape(length, HEADS * HD)

def layer(hidden, gain_attn, w_query, w_key, w_value, w_out, dim_scale, gain_mlp, w_up, w_down):
    normed = low(rms_norm(hidden, gain_attn))
    multiplier = LOG2E / math.sqrt(HD) * jax.nn.softplus(dim_scale)
    scale = jnp.tile(multiplier, HEADS)
    query = low(low_back(matmul(normed, w_query)) * scale)
    key = low(low_back(matmul(normed, w_key)))
    value = low(low_back(matmul(normed, w_value)))
    mixed = lax.map(jax.checkpoint(attention), (query, key, value))
    mixed = low(low_back(mixed))
    middle = hidden + low_back(matmul(mixed, w_out))
    normed_two = low(rms_norm(middle, gain_mlp))
    activated = low(jax.nn.silu(low_back(matmul(normed_two, w_up))))
    return middle + low_back(matmul(activated, w_down))

def reference(inputs, cotangent, gain_attn, w_query, w_key, w_value, w_out, dim_scale, gain_mlp, w_up, w_down):
    params = tuple((p.astype(jnp.float32) for p in (gain_attn, w_query, w_key, w_value, w_out, dim_scale, gain_mlp, w_up, w_down)))
    start = inputs.astype(jnp.float32)
    probe = jnp.zeros_like(start)

    def forward(start, probe, params):
        first = layer(start, *[p[0] for p in params])
        passed = low(low_back(first + probe))
        second = layer(passed, *[p[1] for p in params])
        return (second, first)
    second, pull, first = jax.vjp(forward, start, probe, params, has_aux=True)
    grad_start, grad_probe, grads = pull(cotangent.astype(jnp.float32))
    layer_out = jnp.stack([first, second]).astype(jnp.bfloat16)
    input_grads = jnp.stack([grad_start, grad_probe]).astype(jnp.bfloat16)
    return (layer_out, input_grads, grads[0], grads[1], grads[2], grads[3], grads[4], grads[5], grads[6], grads[7], grads[8])
```

```python
import functools
import math

import jax
import jax.numpy as jnp
from jax import lax
from jax.experimental import pallas as pl
from jax.experimental.pallas import tpu as pltpu
from jax.sharding import PartitionSpec as P

EPS = 1e-06
LOG2E = 1.442695041
NEGATIVE = -1e30
BF16 = jnp.bfloat16
F32 = jnp.float32
MESH = pl.DeviceIdType.MESH
ANY = pl.BlockSpec(memory_space=pl.ANY)
VMEM = pl.BlockSpec(memory_space=pltpu.VMEM)
DMA = pltpu.SemaphoreType.DMA
MIB = 1 << 20
PIECES = 4


def plain(a, b):
    return jnp.dot(a, b, preferred_element_type=F32)


def by_last(a, b):
    return lax.dot_general(a, b, (((1,), (1,)), ((), ())), preferred_element_type=F32)


def by_first(a, b):
    return lax.dot_general(a, b, (((0,), (0,)), ((), ())), preferred_element_type=F32)


def other(index):
    return index + 1 - 2 * lax.rem(index, 2)


def remote(src, dst, send, receive, device):
    return pltpu.make_async_remote_copy(
        src_ref=src,
        dst_ref=dst,
        send_sem=send,
        recv_sem=receive,
        device_id=device,
        device_id_type=MESH,
    )


def greet(devices):
    barrier = pltpu.get_barrier_semaphore()
    for device in devices:
        pl.semaphore_signal(barrier, inc=1, device_id=device, device_id_type=MESH)
    pl.semaphore_wait(barrier, len(devices))


def inverse_rms(rows):
    return lax.rsqrt(jnp.mean(rows * rows, axis=1, keepdims=True) + EPS)


def forward_kernel(
    inputs, cotangent, w_in, w_o, w_u, w_d, gain_one, gain_two, scale,
    out_rows, h_out, n1_out, q_out, k_out, v_out, o_out, lse_out, m_out, n2_out, u_out, a_out,
    g_out, win_out, wo_out, wu_out, wd_out,
    land, win, wo, wu, wd, n1, q, k, v, o_heads, o, lse_cols, lse, ysend, yrecv, m, n2, u, a,
    zpart, zrecv, xout,
    own_sem, xs_sem, xr_sem, xfs_sem, xfr_sem, wys_sem, wyr_sem, wzs_sem, wzr_sem,
    ns_sem, nr_sem, nfs_sem, nfr_sem, ys_sem, yr_sem, zs_sem, zr_sem, os_sem, or_sem, save_sem,
):
    s, t, d = lax.axis_index("section"), lax.axis_index("tensor"), lax.axis_index("dp")
    blocks, rows, width = land.shape[1:]
    half = rows // 2
    local = w_o.shape[0]
    heads, _, head = q.shape
    per = heads // 2
    c, y = lax.rem(t, 2), t // 2
    core = (s, other(t), d)
    across = (s, lax.rem(t + 2, 4), d)
    diagonal = (s, other(lax.rem(t + 2, 4)), d)
    beside = (s, t, other(d))
    section = (1 - s, t, d)
    greet([core, across, diagonal, beside, section])

    mine = pl.ds(pl.multiple_of(c * half, half), half)
    theirs = pl.ds(pl.multiple_of((1 - c) * half, half), half)

    own = [
        pltpu.make_async_copy(w_in, win.at[0], own_sem.at[0]),
        pltpu.make_async_copy(w_o, wo.at[pl.ds(0, local)], own_sem.at[1]),
        pltpu.make_async_copy(w_u, wu.at[0], own_sem.at[2]),
        pltpu.make_async_copy(w_d, wd.at[pl.ds(0, local)], own_sem.at[3]),
    ]
    for copy in own:
        copy.start()

    def spread(source):
        for sequence in range(2):
            for part in range(2):
                target = 2 * sequence + part
                piece = pl.ds(part * half, half)
                src = source.at[sequence, piece]
                dst = land.at[0, t, piece]

                @pl.when(target == t)
                def _():
                    pltpu.make_async_copy(src, dst, xr_sem.at[t]).start()

                @pl.when(target != t)
                def _():
                    remote(src, dst, xs_sem.at[target], xr_sem.at[t], (s, target, d)).start()

    def gather_rows():
        for b in range(blocks):
            piece = land.at[0, b, mine]
            remote(piece, piece, xs_sem.at[b], xr_sem.at[b], core).wait_recv()
            remote(piece, piece, xfs_sem.at[b], xfr_sem.at[b], core).start()
        for b in range(blocks):
            piece = land.at[0, b, theirs]
            remote(piece, piece, xfs_sem.at[b], xfr_sem.at[b], core).wait_recv()

    parity = lax.rem(d, 2)
    step = width // 2 // PIECES
    in_pieces = [
        [pl.ds(pl.multiple_of(which * (width // 2) + i * step, step), step) for i in range(PIECES)]
        for which in (parity, 1 - parity)
    ]
    wide = [pl.ds(pl.multiple_of(w * (width // 2), width // 2), width // 2) for w in (parity, 1 - parity)]
    short = local // 2
    tall = [pl.ds(pl.multiple_of(w * short, short), short) for w in (parity, 1 - parity)]
    low = [pl.ds(pl.multiple_of(local + w * short, short), short) for w in (parity, 1 - parity)]

    def pieces(which):
        found = [(w_in.at[p], win.at[1, p]) for p in in_pieces[which]]
        found.append((w_o.at[tall[which]], wo.at[low[which]]))
        found.append((w_u.at[wide[which]], wu.at[1, wide[which]]))
        found.append((w_d.at[tall[which]], wd.at[low[which]]))
        return found

    sent, relayed = pieces(0), pieces(1)

    @pl.when(s == 0)
    def _():
        spread(inputs)

    for i, (src, dst) in enumerate(sent):
        remote(src, dst, wys_sem.at[i], wyr_sem.at[i], across).start()

    @pl.when(s == 1)
    def _():
        spread(cotangent)

    def relay(i):
        dst = sent[i][1]
        remote(dst, dst, wys_sem.at[i], wyr_sem.at[i], across).wait_recv()
        remote(dst, dst, wzs_sem.at[i], wzr_sem.at[i], beside).start()

    def arrived(i):
        dst = relayed[i][1]
        remote(dst, dst, wzs_sem.at[i], wzr_sem.at[i], beside).wait_recv()

    @pl.when(s == 0)
    def _():
        gather_rows()

    for i in range(PIECES):
        relay(i)
    own[0].wait()
    for i in range(PIECES):
        arrived(i)

    def save(kind, b, src, dst):
        pltpu.make_async_copy(src, dst, save_sem.at[kind, b]).start()

    causal = lax.broadcasted_iota(jnp.int32, (rows, rows), 0) >= lax.broadcasted_iota(
        jnp.int32, (rows, rows), 1
    )
    lane = lax.broadcasted_iota(jnp.int32, (rows, 128), 1)

    def attention(b, _):
        at = pl.ds(pl.multiple_of(b * rows, rows), rows)

        @pl.when(s == 1)
        def _():
            piece = land.at[1, b, mine]
            remote(piece, piece, ns_sem.at[b], nr_sem.at[b], core).wait_recv()
            remote(piece, piece, nfs_sem.at[b], nfr_sem.at[b], core).start()
            rest = land.at[1, b, theirs]
            remote(rest, rest, nfs_sem.at[b], nfr_sem.at[b], core).wait_recv()

        hidden = land[s, b].astype(F32)
        normed = (hidden * inverse_rms(hidden) * gain_one[...]).astype(BF16)
        n1[at] = normed
        for j in range(2):
            projected = plain(normed, win[j])
            for i in range(per):
                cut = slice(i * head, (i + 1) * head)
                q[j * per + i, at] = (projected[:, cut] * scale[...]).astype(BF16)
                k[j * per + i, at] = projected[:, local + i * head : local + (i + 1) * head].astype(
                    BF16
                )
                v[j * per + i, at] = projected[
                    :, 2 * local + i * head : 2 * local + (i + 1) * head
                ].astype(BF16)
        lse_cols[...] = jnp.zeros_like(lse_cols)
        for bb in range(blocks):

            @pl.when(b == bb)
            def _():
                def one(i, _):
                    qh = q[i, bb * rows : (bb + 1) * rows]
                    near = by_last(qh, k[i, bb * rows : (bb + 1) * rows])
                    near = jnp.where(causal, near, NEGATIVE)
                    top = jnp.max(near, axis=1, keepdims=True)
                    if bb:
                        far = by_last(qh, k[i, : bb * rows])
                        top = jnp.maximum(top, jnp.max(far, axis=1, keepdims=True))
                    near = jnp.exp(near - top)
                    total = jnp.sum(near, axis=1, keepdims=True)
                    mixed = plain(near.astype(BF16), v[i, bb * rows : (bb + 1) * rows])
                    if bb:
                        far = jnp.exp(far - top)
                        total = total + jnp.sum(far, axis=1, keepdims=True)
                        mixed = mixed + plain(far.astype(BF16), v[i, : bb * rows])
                    o_heads[i] = (mixed / total).astype(BF16)
                    lse_cols[...] = jnp.where(lane == i, top + jnp.log(total), lse_cols[...])
                    return 0

                lax.fori_loop(0, heads, one, 0, unroll=2)

        o[at] = jnp.concatenate([o_heads[i] for i in range(heads)], axis=1)
        lse[b] = jnp.transpose(lse_cols[...])[:heads]

        save(0, b, land.at[s, b], h_out.at[b])
        save(1, b, n1.at[at], n1_out.at[at])
        save(2, b, q.at[:, at], q_out.at[:, at])
        save(3, b, k.at[:, at], k_out.at[:, at])
        save(4, b, v.at[:, at], v_out.at[:, at])
        save(5, b, o.at[at], o_out.at[at])
        save(6, b, lse.at[b], lse_out.at[b])
        for i in range(3):

            @pl.when(b == blocks - 3 + i)
            def _():
                relay(PIECES + i)

        return 0

    lax.fori_loop(0, blocks, attention, 0)

    own[1].wait()
    arrived(PIECES)

    def project(b, _):
        at = pl.ds(pl.multiple_of(b * rows, rows), rows)
        ysend[b] = plain(o[at], wo[...]).astype(BF16)
        remote(ysend.at[b], yrecv.at[b], ys_sem.at[b], yr_sem.at[b], core).start()
        return 0

    lax.fori_loop(0, blocks, project, 0)

    own[2].wait()
    arrived(PIECES + 1)
    own[3].wait()
    arrived(PIECES + 2)
    weights = [(win, win_out), (wo, wo_out), (wu, wu_out), (wd, wd_out)]
    for i, (src, dst) in enumerate(weights):
        save(11, i, src, dst)

    def feed(b, _):
        at = pl.ds(pl.multiple_of(b * rows, rows), rows)
        remote(ysend.at[b], yrecv.at[b], ys_sem.at[b], yr_sem.at[b], core).wait_recv()
        middle = land[s, b].astype(F32) + (ysend[b].astype(F32) + yrecv[b].astype(F32))
        m[b] = middle
        normed = (middle * inverse_rms(middle) * gain_two[...]).astype(BF16)
        n2[at] = normed
        up = jnp.concatenate([plain(normed, wu[0]), plain(normed, wu[1])], axis=1)
        u[b] = up
        active = (up / (1.0 + jnp.exp(-up))).astype(BF16)
        a[at] = active
        zpart[b] = plain(active, wd[...])
        copy = remote(zpart.at[b, theirs], zrecv.at[b], zs_sem.at[b], zr_sem.at[b], core)
        copy.start()
        save(7, b, m.at[b], m_out.at[b])
        save(8, b, n2.at[at], n2_out.at[at])
        save(9, b, u.at[b], u_out.at[b])
        save(10, b, a.at[at], a_out.at[at])
        copy.wait_recv()
        xout[b] = (m[b, mine] + (zpart[b, mine] + zrecv[b])).astype(BF16)

        @pl.when(s == 0)
        def _():
            remote(xout.at[b], land.at[1, b, mine], ns_sem.at[b], nr_sem.at[b], section).start()

        place = out_rows.at[y, mine]

        @pl.when(b == t)
        def _():
            pltpu.make_async_copy(xout.at[b], place, or_sem.at[t]).start()

        @pl.when(b != t)
        def _():
            remote(xout.at[b], place, os_sem.at[b], or_sem.at[t], (s, b, d)).start()

        return 0

    lax.fori_loop(0, blocks, feed, 0)

    @pl.when(s == 1)
    def _():
        gather_rows()

    for b in range(blocks):
        pltpu.make_async_copy(land.at[0, b], g_out.at[b], save_sem.at[12, b]).start()

    for b in range(blocks):
        piece = land.at[0, b, mine]
        remote(piece, piece, xfs_sem.at[b], xfr_sem.at[b], core).wait_send()
        remote(ysend.at[b], yrecv.at[b], ys_sem.at[b], yr_sem.at[b], core).wait_send()
        remote(zpart.at[b, theirs], zrecv.at[b], zs_sem.at[b], zr_sem.at[b], core).wait_send()
        here = out_rows.at[b // 2, pl.ds((b % 2) * half, half)]
        remote(here, here, os_sem.at[b], or_sem.at[b], core).wait_recv()

        @pl.when(b != t)
        def _():
            remote(xout.at[b], here, os_sem.at[b], or_sem.at[b], core).wait_send()
            remote(piece, piece, xs_sem.at[b], xr_sem.at[b], core).wait_send()

        @pl.when(s == 0)
        def _():
            remote(xout.at[b], piece, ns_sem.at[b], nr_sem.at[b], section).wait_send()

        @pl.when(s == 1)
        def _():
            remote(piece, piece, nfs_sem.at[b], nfr_sem.at[b], core).wait_send()

    for i, (src, dst) in enumerate(sent):
        remote(src, dst, wys_sem.at[i], wyr_sem.at[i], across).wait_send()
        remote(dst, dst, wzs_sem.at[i], wzr_sem.at[i], beside).wait_send()
    for i, (src, dst) in enumerate(weights):
        pltpu.make_async_copy(src, dst, save_sem.at[11, i]).wait()
    for b in range(blocks):
        at = pl.ds(b * rows, rows)
        saved = [
            (land.at[s, b], h_out.at[b]),
            (n1.at[at], n1_out.at[at]),
            (q.at[:, at], q_out.at[:, at]),
            (k.at[:, at], k_out.at[:, at]),
            (v.at[:, at], v_out.at[:, at]),
            (o.at[at], o_out.at[at]),
            (lse.at[b], lse_out.at[b]),
            (m.at[b], m_out.at[b]),
            (n2.at[at], n2_out.at[at]),
            (u.at[b], u_out.at[b]),
            (a.at[at], a_out.at[at]),
        ]
        for kind, (src, dst) in enumerate(saved):
            pltpu.make_async_copy(src, dst, save_sem.at[kind, b]).wait()
        pltpu.make_async_copy(land.at[0, b], g_out.at[b], save_sem.at[12, b]).wait()


def forward(inputs, cotangent, w_in, w_o, w_u, w_d, gain_one, gain_two, scale, head):
    _, rows, width = inputs.shape
    local = w_o.shape[0]
    heads = 2 * local // head
    blocks = lax.axis_size("tensor")
    length = blocks * rows
    half = rows // 2
    shape = jax.ShapeDtypeStruct
    outs = [
        shape(inputs.shape, BF16),
        shape((blocks, rows, width), BF16),
        shape((length, width), BF16),
        shape((heads, length, head), BF16),
        shape((heads, length, head), BF16),
        shape((heads, length, head), BF16),
        shape((length, 2 * local), BF16),
        shape((blocks, heads, rows), F32),
        shape((blocks, rows, width), F32),
        shape((length, width), BF16),
        shape((blocks, rows, 2 * local), F32),
        shape((length, 2 * local), BF16),
        shape((blocks, rows, width), BF16),
        shape((2, width, 3 * local), BF16),
        shape((2 * local, width), BF16),
        shape((2, width, local), BF16),
        shape((2 * local, width), BF16),
    ]
    scratch = [
        pltpu.VMEM((2, blocks, rows, width), BF16),
        pltpu.VMEM((2, width, 3 * local), BF16),
        pltpu.VMEM((2 * local, width), BF16),
        pltpu.VMEM((2, width, local), BF16),
        pltpu.VMEM((2 * local, width), BF16),
        pltpu.VMEM((length, width), BF16),
        pltpu.VMEM((heads, length, head), BF16),
        pltpu.VMEM((heads, length, head), BF16),
        pltpu.VMEM((heads, length, head), BF16),
        pltpu.VMEM((heads, rows, head), BF16),
        pltpu.VMEM((length, 2 * local), BF16),
        pltpu.VMEM((rows, 128), F32),
        pltpu.VMEM((blocks, heads, rows), F32),
        pltpu.VMEM((blocks, rows, width), BF16),
        pltpu.VMEM((blocks, rows, width), BF16),
        pltpu.VMEM((blocks, rows, width), F32),
        pltpu.VMEM((length, width), BF16),
        pltpu.VMEM((blocks, rows, 2 * local), F32),
        pltpu.VMEM((length, 2 * local), BF16),
        pltpu.VMEM((blocks, rows, width), F32),
        pltpu.VMEM((blocks, half, width), F32),
        pltpu.VMEM((blocks, half, width), BF16),
        DMA((4,)),
        DMA((blocks,)),
        DMA((blocks,)),
        DMA((blocks,)),
        DMA((blocks,)),
        DMA((PIECES + 3,)),
        DMA((PIECES + 3,)),
        DMA((PIECES + 3,)),
        DMA((PIECES + 3,)),
        DMA((blocks,)),
        DMA((blocks,)),
        DMA((blocks,)),
        DMA((blocks,)),
        DMA((blocks,)),
        DMA((blocks,)),
        DMA((blocks,)),
        DMA((blocks,)),
        DMA((blocks,)),
        DMA((blocks,)),
        DMA((13, blocks)),
    ]
    return pl.pallas_call(
        forward_kernel,
        out_shape=outs,
        in_specs=[ANY] * 6 + [VMEM] * 3,
        out_specs=[ANY] * len(outs),
        scratch_shapes=scratch,
        compiler_params=pltpu.CompilerParams(
            collective_id=1, has_side_effects=True, vmem_limit_bytes=60 * MIB
        ),
        name="forward",
    )(inputs, cotangent, w_in, w_o, w_u, w_d, gain_one, gain_two, scale)


def backward_kernel(
    g_in, h_in, q_in, k_in, v_in, o_in, lse_in, m_in, u_in, win_in, wo_in, wu_in, wd_in,
    gain_one, gain_two, scale,
    out_rows, g_out, gu_out, gy_out, gp_out, dg1, dg2, ds,
    g, win, wo, wu, wd, h, q, k, v, o, lse, m, u, gu, gy, gp, ysend, yrecv, gm, go_heads, gq_heads,
    cols, delta, dk, dv, n1part, n1recv, xout,
    load_sem, w_sem, ns_sem, nr_sem, nfs_sem, nfr_sem, ys_sem, yr_sem, zs_sem, zr_sem, os_sem, or_sem,
    save_sem,
):
    s, t, d = lax.axis_index("section"), lax.axis_index("tensor"), lax.axis_index("dp")
    blocks, rows, width = g.shape
    half = rows // 2
    local = wu.shape[2]
    heads, _, head = q.shape
    per = heads // 2
    c, y = lax.rem(t, 2), t // 2
    core = (s, other(t), d)
    across = (s, lax.rem(t + 2, 4), d)
    diagonal = (s, other(lax.rem(t + 2, 4)), d)
    section = (1 - s, t, d)
    mine = pl.ds(pl.multiple_of(c * half, half), half)
    theirs = pl.ds(pl.multiple_of((1 - c) * half, half), half)

    weights = [(wd_in, wd), (wu_in, wu), (wo_in, wo), (win_in, win)]

    def loads(b):
        at = pl.ds(b * rows, rows)
        return [
            (u_in.at[b], u.at[b]),
            (m_in.at[b], m.at[b]),
            (o_in.at[at], o.at[at]),
            (q_in.at[:, at], q.at[:, at]),
            (k_in.at[:, at], k.at[:, at]),
            (v_in.at[:, at], v.at[:, at]),
            (lse_in.at[b], lse.at[b]),
            (h_in.at[b, mine], h.at[b]),
        ]

    for i, (src, dst) in enumerate(weights[:2]):
        pltpu.make_async_copy(src, dst, w_sem.at[i]).start()
    for kind, (src, dst) in enumerate(loads(blocks - 1)[:2]):
        pltpu.make_async_copy(src, dst, load_sem.at[kind, blocks - 1]).start()

    @pl.when(s == 1)
    def _():
        for b in reversed(range(blocks)):
            pltpu.make_async_copy(g_in.at[b], g.at[b], nr_sem.at[b]).start()

    for i, (src, dst) in enumerate(weights[2:]):
        pltpu.make_async_copy(src, dst, w_sem.at[2 + i]).start()
    for b in reversed(range(blocks)):
        for kind, (src, dst) in enumerate(loads(b)):
            if kind >= 2 or b < blocks - 1:
                pltpu.make_async_copy(src, dst, load_sem.at[kind, b]).start()

    greet([core, across, diagonal, section])

    dk[...] = jnp.zeros_like(dk)
    dv[...] = jnp.zeros_like(dv)
    dg1[...] = jnp.zeros_like(dg1)
    dg2[...] = jnp.zeros_like(dg2)
    ds[...] = jnp.zeros_like(ds)
    for i, (src, dst) in enumerate(weights):
        pltpu.make_async_copy(src, dst, w_sem.at[i]).wait()
    for b in range(blocks):
        for kind, (src, dst) in enumerate(loads(b)):
            if b != blocks - 1 or kind < 2:
                pass
            pltpu.make_async_copy(src, dst, load_sem.at[kind, b]).wait()

    causal = lax.broadcasted_iota(jnp.int32, (rows, rows), 0) <= lax.broadcasted_iota(
        jnp.int32, (rows, rows), 1
    )

    def save(kind, b, src, dst):
        pltpu.make_async_copy(src, dst, save_sem.at[kind, b]).start()

    def one_block(turn, _):
        b = blocks - 1 - turn
        at = pl.ds(pl.multiple_of(b * rows, rows), rows)

        @pl.when(s == 1)
        def _():
            pltpu.make_async_copy(g_in.at[b], g.at[b], nr_sem.at[b]).wait()

        @pl.when(s == 0)
        def _():
            piece = g.at[b, mine]
            remote(piece, piece, ns_sem.at[b], nr_sem.at[b], core).wait_recv()
            remote(piece, piece, nfs_sem.at[b], nfr_sem.at[b], core).start()
            rest = g.at[b, theirs]
            remote(rest, rest, nfs_sem.at[b], nfr_sem.at[b], core).wait_recv()

        save(0, b, g.at[b], g_out.at[at])
        grad = g[b]
        grad_act = by_last(grad, wd[...])
        up = u[b]
        sigma = 1.0 / (1.0 + jnp.exp(-up))
        grad_up = (grad_act * sigma * (1.0 + up * (1.0 - sigma))).astype(BF16)
        gu[at] = grad_up
        save(1, b, gu.at[at], gu_out.at[at])
        ysend[b] = (by_last(grad_up[:, :local], wu[0]) + by_last(grad_up[:, local:], wu[1])).astype(
            BF16
        )
        copy = remote(ysend.at[b], yrecv.at[b], ys_sem.at[b], yr_sem.at[b], core)
        copy.start()
        copy.wait_recv()
        grad_normed = ysend[b].astype(F32) + yrecv[b].astype(F32)
        middle = m[b]
        inverse = inverse_rms(middle)
        unit = middle * inverse
        grad_unit = grad_normed * gain_two[...]
        dg2[...] += jnp.sum(grad_normed * unit, axis=0, keepdims=True)
        grad_middle = grad.astype(F32) + inverse * (
            grad_unit - unit * jnp.mean(grad_unit * unit, axis=1, keepdims=True)
        )
        gm[...] = grad_middle
        grad_mid = grad_middle.astype(BF16)
        gy[at] = grad_mid
        save(2, b, gy.at[at], gy_out.at[at])
        grad_mixed = by_last(grad_mid, wo[...]).astype(BF16)
        both = grad_mixed.astype(F32) * o[at].astype(F32)
        lane = lax.broadcasted_iota(jnp.int32, (rows, 128), 1)
        found = jnp.zeros((rows, 128), F32)
        for i in range(heads):
            cut = slice(i * head, (i + 1) * head)
            go_heads[i] = grad_mixed[:, cut]
            found = jnp.where(lane == i, jnp.sum(both[:, cut], axis=1, keepdims=True), found)
        delta[...] = jnp.transpose(found)[:heads]
        for bb in range(blocks):

            @pl.when(b == bb)
            def _():
                def one(i, _):
                    qh = q[i, bb * rows : (bb + 1) * rows]
                    gh = go_heads[i]
                    offset = lse[bb, pl.ds(i, 1)]
                    inner = delta[pl.ds(i, 1)]
                    total = jnp.zeros((head, rows), F32)
                    for j in range(bb + 1):
                        cut = slice(j * rows, (j + 1) * rows)
                        kj = k[i, cut]
                        weight = jnp.exp(by_last(kj, qh) - offset)
                        if j == bb:
                            weight = jnp.where(causal, weight, 0.0)
                        grad_score = weight * (by_last(v[i, cut], gh) - inner)
                        grad_score = grad_score.astype(BF16)
                        dv[i, cut] += plain(weight.astype(BF16), gh)
                        dk[i, cut] += plain(grad_score, qh)
                        total = total + by_first(kj, grad_score)
                    gq_heads[i] = jnp.transpose(total)
                    return 0

                lax.fori_loop(0, heads, one, 0)

        for j in range(2):
            mine_heads = range(j * per, (j + 1) * per)
            grad_scaled = jnp.concatenate([gq_heads[i] for i in mine_heads], axis=1)
            queries = jnp.concatenate([q[i, at] for i in mine_heads], axis=1).astype(F32)
            ds[pl.ds(j, 1)] += jnp.sum(grad_scaled * queries, axis=0, keepdims=True)
            grads = [
                (grad_scaled * scale[...]).astype(BF16),
                jnp.concatenate([dk[i, at] for i in mine_heads], axis=1).astype(BF16),
                jnp.concatenate([dv[i, at] for i in mine_heads], axis=1).astype(BF16),
            ]
            gp[j, at] = jnp.concatenate(grads, axis=1)
        save(3, b, gp.at[:, at], gp_out.at[:, at])
        n1part[...] = by_last(gp[0, at], win[0]) + by_last(gp[1, at], win[1])
        copy = remote(n1part.at[theirs], n1recv.at[b], zs_sem.at[b], zr_sem.at[b], core)
        copy.start()
        copy.wait_recv()
        grad_normed = n1part[mine] + n1recv[b]
        hidden = h[b].astype(F32)
        inverse = inverse_rms(hidden)
        unit = hidden * inverse
        grad_unit = grad_normed * gain_one[...]
        dg1[...] += jnp.sum(grad_normed * unit, axis=0, keepdims=True)
        xout[b] = (
            gm[mine]
            + inverse * (grad_unit - unit * jnp.mean(grad_unit * unit, axis=1, keepdims=True))
        ).astype(BF16)

        @pl.when(s == 1)
        def _():
            remote(xout.at[b], g.at[b, mine], ns_sem.at[b], nr_sem.at[b], section).start()

        place = out_rows.at[y, mine]

        @pl.when(b == t)
        def _():
            pltpu.make_async_copy(xout.at[b], place, or_sem.at[t]).start()

        @pl.when(b != t)
        def _():
            remote(xout.at[b], place, os_sem.at[b], or_sem.at[t], (s, b, d)).start()

        copy.wait_send()
        return 0

    lax.fori_loop(0, blocks, one_block, 0)

    for b in range(blocks):
        at = pl.ds(b * rows, rows)
        piece = g.at[b, mine]
        remote(ysend.at[b], yrecv.at[b], ys_sem.at[b], yr_sem.at[b], core).wait_send()
        here = out_rows.at[b // 2, pl.ds((b % 2) * half, half)]
        remote(here, here, os_sem.at[b], or_sem.at[b], core).wait_recv()

        @pl.when(b != t)
        def _():
            remote(xout.at[b], here, os_sem.at[b], or_sem.at[b], core).wait_send()

        @pl.when(s == 1)
        def _():
            remote(xout.at[b], piece, ns_sem.at[b], nr_sem.at[b], section).wait_send()

        @pl.when(s == 0)
        def _():
            remote(piece, piece, nfs_sem.at[b], nfr_sem.at[b], core).wait_send()

        saved = [
            (g.at[b], g_out.at[at]),
            (gu.at[at], gu_out.at[at]),
            (gy.at[at], gy_out.at[at]),
            (gp.at[:, at], gp_out.at[:, at]),
        ]
        for kind, (src, dst) in enumerate(saved):
            pltpu.make_async_copy(src, dst, save_sem.at[kind, b]).wait()


def backward(saved, gain_one, gain_two, scale):
    g_in, h_in, q_in = saved[:3]
    win_in, wo_in, wu_in, wd_in = saved[9:]
    blocks, rows, width = g_in.shape
    heads, length, head = q_in.shape
    local = wu_in.shape[2]
    half = rows // 2
    shape = jax.ShapeDtypeStruct
    outs = [
        shape((2, rows, width), BF16),
        shape((length, width), BF16),
        shape((length, 2 * local), BF16),
        shape((length, width), BF16),
        shape((2, length, 3 * local), BF16),
        shape((1, width), F32),
        shape((1, width), F32),
        shape((2, local), F32),
    ]
    scratch = [
        pltpu.VMEM((blocks, rows, width), BF16),
        pltpu.VMEM(win_in.shape, BF16),
        pltpu.VMEM(wo_in.shape, BF16),
        pltpu.VMEM(wu_in.shape, BF16),
        pltpu.VMEM(wd_in.shape, BF16),
        pltpu.VMEM((blocks, half, width), BF16),
        pltpu.VMEM((heads, length, head), BF16),
        pltpu.VMEM((heads, length, head), BF16),
        pltpu.VMEM((heads, length, head), BF16),
        pltpu.VMEM((length, 2 * local), BF16),
        pltpu.VMEM((blocks, heads, rows), F32),
        pltpu.VMEM((blocks, rows, width), F32),
        pltpu.VMEM((blocks, rows, 2 * local), F32),
        pltpu.VMEM((length, 2 * local), BF16),
        pltpu.VMEM((length, width), BF16),
        pltpu.VMEM((2, length, 3 * local), BF16),
        pltpu.VMEM((blocks, rows, width), BF16),
        pltpu.VMEM((blocks, rows, width), BF16),
        pltpu.VMEM((rows, width), F32),
        pltpu.VMEM((heads, rows, head), BF16),
        pltpu.VMEM((heads, rows, head), F32),
        pltpu.VMEM((8, 128), F32),
        pltpu.VMEM((heads, rows), F32),
        pltpu.VMEM((heads, length, head), F32),
        pltpu.VMEM((heads, length, head), F32),
        pltpu.VMEM((rows, width), F32),
        pltpu.VMEM((blocks, half, width), F32),
        pltpu.VMEM((blocks, half, width), BF16),
        DMA((8, blocks)),
        DMA((4,)),
        DMA((blocks,)),
        DMA((blocks,)),
        DMA((blocks,)),
        DMA((blocks,)),
        DMA((blocks,)),
        DMA((blocks,)),
        DMA((blocks,)),
        DMA((blocks,)),
        DMA((blocks,)),
        DMA((blocks,)),
        DMA((4, blocks)),
    ]
    return pl.pallas_call(
        backward_kernel,
        out_shape=outs,
        in_specs=[ANY] * 13 + [VMEM] * 3,
        out_specs=[ANY] * 5 + [VMEM] * 3,
        scratch_shapes=scratch,
        compiler_params=pltpu.CompilerParams(
            collective_id=2, has_side_effects=True, vmem_limit_bytes=62 * MIB
        ),
        name="backward",
    )(*saved, gain_one, gain_two, scale)


def reduce_kernel(
    keep_in, give_in, out, keep, yrecv, right, left, sbuf,
    k_sem, ys_sem, yr_sem, rs_sem, rr_sem, ls_sem, lr_sem,
):
    s, t, d = lax.axis_index("section"), lax.axis_index("tensor"), lax.axis_index("dp")
    n, chunk, width = keep.shape
    groups = ys_sem.shape[1]
    step = width // groups
    across = (s, lax.rem(t + 2, 4), d)
    up = (s, t, lax.rem(d + 1, n))
    down = (s, t, lax.rem(d + n - 1, n))
    greet([across, up, down])

    def cut(i):
        return pl.ds(i * step, step)

    order = []
    for i in range((n + 1) // 2):
        order += [n - 1 - i, i] if n - 1 - i != i else [i]
    for e in order:
        pltpu.make_async_copy(keep_in.at[e], keep.at[e], k_sem.at[e]).start()
        for i in range(groups):
            remote(
                give_in.at[e, :, cut(i)],
                yrecv.at[e, :, cut(i)],
                ys_sem.at[e, i],
                yr_sem.at[e, i],
                across,
            ).start()

    def exchange(e, i):
        piece = yrecv.at[e, :, cut(i)]
        return remote(piece, piece, ys_sem.at[e, i], yr_sem.at[e, i], across)

    def to_right(e, i):
        return remote(
            sbuf.at[e, :, cut(i)], right.at[e, :, cut(i)], rs_sem.at[e, i], rr_sem.at[e, i], up
        )

    def to_left(e, i):
        return remote(
            sbuf.at[e, :, cut(i)], left.at[e, :, cut(i)], ls_sem.at[e, i], lr_sem.at[e, i], down
        )

    def paired(e, i):
        if i == 0:
            pltpu.make_async_copy(keep_in.at[e], keep.at[e], k_sem.at[e]).wait()
        exchange(e, i).wait_recv()
        lanes = slice(i * step, (i + 1) * step)
        return keep[e, :, lanes].astype(F32) + yrecv[e, :, lanes].astype(F32)

    for e in order:
        for i in range(groups):
            lanes = slice(i * step, (i + 1) * step)

            @pl.when(e > d)
            def _():
                out[:, lanes] = paired(e, i)

                @pl.when(d > 0)
                def _():
                    to_right(e, i).wait_recv()
                    out[:, lanes] += right[e, :, lanes].astype(F32)

                sbuf[e, :, lanes] = out[:, lanes].astype(BF16)
                to_right(e, i).start()

            @pl.when(e < d)
            def _():
                out[:, lanes] = paired(e, i)

                @pl.when(d < n - 1)
                def _():
                    to_left(e, i).wait_recv()
                    out[:, lanes] += left[e, :, lanes].astype(F32)

                sbuf[e, :, lanes] = out[:, lanes].astype(BF16)
                to_left(e, i).start()

    for e in order:
        for i in range(groups):
            lanes = slice(i * step, (i + 1) * step)

            @pl.when(e == d)
            def _():
                out[:, lanes] = paired(e, i)

                @pl.when(d > 0)
                def _():
                    to_right(e, i).wait_recv()
                    out[:, lanes] += right[e, :, lanes].astype(F32)

                @pl.when(d < n - 1)
                def _():
                    to_left(e, i).wait_recv()
                    out[:, lanes] += left[e, :, lanes].astype(F32)

    for e in order:
        for i in range(groups):
            exchange(e, i).wait_send()

            @pl.when(e > d)
            def _():
                to_right(e, i).wait_send()

            @pl.when(e < d)
            def _():
                to_left(e, i).wait_send()


def reduce(keep, give):
    n, chunk, width = keep.shape
    groups = 3
    return pl.pallas_call(
        reduce_kernel,
        out_shape=jax.ShapeDtypeStruct((chunk, width), F32),
        in_specs=[ANY] * 2,
        out_specs=VMEM,
        scratch_shapes=[pltpu.VMEM(keep.shape, BF16)] * 5 + [DMA((n,))] + [DMA((n, groups))] * 6,
        compiler_params=pltpu.CompilerParams(
            collective_id=3, has_side_effects=True, vmem_limit_bytes=60 * MIB
        ),
        name="reduce",
    )(keep, give)


def body(
    inputs, cotangent, gain_attn, w_query, w_key, w_value, w_out, dim_scale, gain_mlp, w_up, w_down
):
    local = w_query.shape[2]
    head = dim_scale.shape[1]
    width = inputs.shape[2]
    n = lax.axis_size("dp")
    w_in = jnp.concatenate([w_query[0], w_key[0], w_value[0]], axis=1)
    multiplier = LOG2E / math.sqrt(head)
    per_dim = multiplier * jax.nn.softplus(dim_scale)
    done = forward(
        inputs, cotangent, w_in, w_out[0], w_up[0], w_down[0], gain_attn, gain_mlp, per_dim, head
    )
    layer_out, h, n1, q, k, v, o, lse, m, n2, u, a, g, win, wo, wu, wd = done
    input_grads, g_all, gu, gy, gp, dg1, dg2, ds = backward(
        (g, h, q, k, v, o, lse, m, u, win, wo, wu, wd),
        gain_attn,
        gain_mlp,
        jnp.tile(per_dim, (1, local // head)),
    )

    def over_rows(a, b):
        return lax.dot_general(a, b, (((0,), (0,)), ((), ())), preferred_element_type=F32)

    parts = []
    for j in range(2):
        cut = slice(j * local, (j + 1) * local)
        parts.append(
            jnp.concatenate(
                [
                    over_rows(n1, gp[j]).astype(BF16),
                    over_rows(n2, gu[:, cut]).astype(BF16),
                    over_rows(gy, o[:, cut]).astype(BF16),
                    over_rows(g_all, a[:, cut]).astype(BF16),
                ],
                axis=1,
            ).reshape(n, width // n, 6 * local)
        )
    grads = reduce(*parts)
    first_core = lax.rem(lax.axis_index("tensor"), 2) == 0
    dg2 = jnp.where(first_core, dg2, 0.0)
    ds = jnp.sum(ds.reshape(-1, head), axis=0, keepdims=True)
    dg1, dg2, ds = lax.psum((dg1, dg2, ds), ("tensor", "dp"))
    grad_scale = ds / per_dim * multiplier * jax.nn.sigmoid(dim_scale)
    pieces = [grads[:, i * local : (i + 1) * local] for i in range(6)]
    return (
        layer_out[None],
        input_grads[None],
        dg1,
        pieces[0][None],
        pieces[1][None],
        pieces[2][None],
        pieces[4].T[None],
        grad_scale,
        dg2,
        pieces[3][None],
        pieces[5].T[None],
    )


def solution(mesh):
    in_specs = (
        P("dp", "tensor", None),
        P("dp", "tensor", None),
        P("section", None),
        P("section", None, "tensor"),
        P("section", None, "tensor"),
        P("section", None, "tensor"),
        P("section", "tensor", None),
        P("section", None),
        P("section", None),
        P("section", None, "tensor"),
        P("section", "tensor", None),
    )
    out_specs = (
        P("section", "dp", "tensor", None),
        P("section", "dp", "tensor", None),
        P("section", None),
        P("section", "dp", "tensor"),
        P("section", "dp", "tensor"),
        P("section", "dp", "tensor"),
        P("section", "tensor", "dp"),
        P("section", None),
        P("section", None),
        P("section", "dp", "tensor"),
        P("section", "tensor", "dp"),
    )
    return jax.shard_map(body, mesh=mesh, in_specs=in_specs, out_specs=out_specs, check_vma=False)
```

```python
import functools
import math

import jax
import jax.numpy as jnp
from jax import lax
from jax.experimental import pallas as pl
from jax.experimental.pallas import tpu as pltpu
from jax.sharding import PartitionSpec as P

EPS = 1e-06
LOG2E = 1.442695041
NEGATIVE = -1e30
BF16 = jnp.bfloat16
F32 = jnp.float32
MESH = pl.DeviceIdType.MESH
ANY = pl.BlockSpec(memory_space=pl.ANY)
VMEM = pl.BlockSpec(memory_space=pltpu.VMEM)
DMA = pltpu.SemaphoreType.DMA
MIB = 1 << 20
PIECES = 4


def plain(a, b):
    return jnp.dot(a, b, preferred_element_type=F32)


def by_last(a, b):
    return lax.dot_general(a, b, (((1,), (1,)), ((), ())), preferred_element_type=F32)


def by_first(a, b):
    return lax.dot_general(a, b, (((0,), (0,)), ((), ())), preferred_element_type=F32)


def other(index):
    return index + 1 - 2 * lax.rem(index, 2)


def remote(src, dst, send, receive, device):
    return pltpu.make_async_remote_copy(
        src_ref=src,
        dst_ref=dst,
        send_sem=send,
        recv_sem=receive,
        device_id=device,
        device_id_type=MESH,
    )


def greet(devices):
    barrier = pltpu.get_barrier_semaphore()
    for device in devices:
        pl.semaphore_signal(barrier, inc=1, device_id=device, device_id_type=MESH)
    pl.semaphore_wait(barrier, len(devices))


def inverse_rms(rows):
    return lax.rsqrt(jnp.mean(rows * rows, axis=1, keepdims=True) + EPS)


def forward_kernel(
    inputs, cotangent, w_in, w_o, w_u, w_d, gain_one, gain_two, scale,
    out_rows, h_out, n1_out, q_out, k_out, v_out, o_out, lse_out, m_out, n2_out, u_out, a_out,
    g_out, win_out, wo_out, wu_out, wd_out,
    land, win, wo, wu, wd, n1, q, k, v, o_heads, o, lse_cols, lse, ysend, yrecv, m, n2, u, a,
    zpart, zrecv, xout,
    own_sem, xs_sem, xr_sem, xfs_sem, xfr_sem, wys_sem, wyr_sem, wzs_sem, wzr_sem,
    ns_sem, nr_sem, nfs_sem, nfr_sem, ys_sem, yr_sem, zs_sem, zr_sem, os_sem, or_sem, save_sem,
):
    s, t, d = lax.axis_index("section"), lax.axis_index("tensor"), lax.axis_index("dp")
    blocks, rows, width = land.shape[1:]
    half = rows // 2
    local = w_o.shape[0]
    heads, _, head = q.shape
    per = heads // 2
    c, y = lax.rem(t, 2), t // 2
    core = (s, other(t), d)
    across = (s, lax.rem(t + 2, 4), d)
    diagonal = (s, other(lax.rem(t + 2, 4)), d)
    beside = (s, t, other(d))
    section = (1 - s, t, d)
    greet([core, across, diagonal, beside, section])

    mine = pl.ds(pl.multiple_of(c * half, half), half)
    theirs = pl.ds(pl.multiple_of((1 - c) * half, half), half)

    own = [
        pltpu.make_async_copy(w_in, win.at[0], own_sem.at[0]),
        pltpu.make_async_copy(w_o, wo.at[pl.ds(0, local)], own_sem.at[1]),
        pltpu.make_async_copy(w_u, wu.at[0], own_sem.at[2]),
        pltpu.make_async_copy(w_d, wd.at[pl.ds(0, local)], own_sem.at[3]),
    ]
    for copy in own:
        copy.start()

    def spread(source):
        for sequence in range(2):
            for part in range(2):
                target = 2 * sequence + part
                piece = pl.ds(part * half, half)
                src = source.at[sequence, piece]
                dst = land.at[0, t, piece]

                @pl.when(target == t)
                def _():
                    pltpu.make_async_copy(src, dst, xr_sem.at[t]).start()

                @pl.when(target != t)
                def _():
                    remote(src, dst, xs_sem.at[target], xr_sem.at[t], (s, target, d)).start()

    def gather_rows():
        for b in range(blocks):
            piece = land.at[0, b, mine]
            remote(piece, piece, xs_sem.at[b], xr_sem.at[b], core).wait_recv()
            remote(piece, piece, xfs_sem.at[b], xfr_sem.at[b], core).start()
        for b in range(blocks):
            piece = land.at[0, b, theirs]
            remote(piece, piece, xfs_sem.at[b], xfr_sem.at[b], core).wait_recv()

    parity = lax.rem(d, 2)
    step = width // 2 // PIECES
    in_pieces = [
        [pl.ds(pl.multiple_of(which * (width // 2) + i * step, step), step) for i in range(PIECES)]
        for which in (parity, 1 - parity)
    ]
    wide = [pl.ds(pl.multiple_of(w * (width // 2), width // 2), width // 2) for w in (parity, 1 - parity)]
    short = local // 2
    tall = [pl.ds(pl.multiple_of(w * short, short), short) for w in (parity, 1 - parity)]
    low = [pl.ds(pl.multiple_of(local + w * short, short), short) for w in (parity, 1 - parity)]

    def pieces(which):
        found = [(w_in.at[p], win.at[1, p]) for p in in_pieces[which]]
        found.append((w_o.at[tall[which]], wo.at[low[which]]))
        found.append((w_u.at[wide[which]], wu.at[1, wide[which]]))
        found.append((w_d.at[tall[which]], wd.at[low[which]]))
        return found

    sent, relayed = pieces(0), pieces(1)

    @pl.when(s == 0)
    def _():
        spread(inputs)

    for i, (src, dst) in enumerate(sent):
        remote(src, dst, wys_sem.at[i], wyr_sem.at[i], across).start()

    @pl.when(s == 1)
    def _():
        spread(cotangent)

    def relay(i):
        dst = sent[i][1]
        remote(dst, dst, wys_sem.at[i], wyr_sem.at[i], across).wait_recv()
        remote(dst, dst, wzs_sem.at[i], wzr_sem.at[i], beside).start()

    def arrived(i):
        dst = relayed[i][1]
        remote(dst, dst, wzs_sem.at[i], wzr_sem.at[i], beside).wait_recv()

    @pl.when(s == 0)
    def _():
        gather_rows()

    for i in range(PIECES):
        relay(i)
    own[0].wait()
    for i in range(PIECES):
        arrived(i)

    def save(kind, b, src, dst):
        pltpu.make_async_copy(src, dst, save_sem.at[kind, b]).start()

    causal = lax.broadcasted_iota(jnp.int32, (rows, rows), 0) >= lax.broadcasted_iota(
        jnp.int32, (rows, rows), 1
    )
    lane = lax.broadcasted_iota(jnp.int32, (rows, 128), 1)

    def attention(b, _):
        at = pl.ds(pl.multiple_of(b * rows, rows), rows)

        @pl.when(s == 1)
        def _():
            piece = land.at[1, b, mine]
            remote(piece, piece, ns_sem.at[b], nr_sem.at[b], core).wait_recv()
            remote(piece, piece, nfs_sem.at[b], nfr_sem.at[b], core).start()
            rest = land.at[1, b, theirs]
            remote(rest, rest, nfs_sem.at[b], nfr_sem.at[b], core).wait_recv()

        hidden = land[s, b].astype(F32)
        normed = (hidden * inverse_rms(hidden) * gain_one[...]).astype(BF16)
        n1[at] = normed
        for j in range(2):
            projected = plain(normed, win[j])
            for i in range(per):
                cut = slice(i * head, (i + 1) * head)
                q[j * per + i, at] = (projected[:, cut] * scale[...]).astype(BF16)
                k[j * per + i, at] = projected[:, local + i * head : local + (i + 1) * head].astype(
                    BF16
                )
                v[j * per + i, at] = projected[
                    :, 2 * local + i * head : 2 * local + (i + 1) * head
                ].astype(BF16)
        lse_cols[...] = jnp.zeros_like(lse_cols)
        for bb in range(blocks):

            @pl.when(b == bb)
            def _():
                def one(i, _):
                    qh = q[i, bb * rows : (bb + 1) * rows]
                    near = by_last(qh, k[i, bb * rows : (bb + 1) * rows])
                    near = jnp.where(causal, near, NEGATIVE)
                    top = jnp.max(near, axis=1, keepdims=True)
                    if bb:
                        far = by_last(qh, k[i, : bb * rows])
                        top = jnp.maximum(top, jnp.max(far, axis=1, keepdims=True))
                    near = jnp.exp(near - top)
                    total = jnp.sum(near, axis=1, keepdims=True)
                    mixed = plain(near.astype(BF16), v[i, bb * rows : (bb + 1) * rows])
                    if bb:
                        far = jnp.exp(far - top)
                        total = total + jnp.sum(far, axis=1, keepdims=True)
                        mixed = mixed + plain(far.astype(BF16), v[i, : bb * rows])
                    o_heads[i] = (mixed / total).astype(BF16)
                    lse_cols[...] = jnp.where(lane == i, top + jnp.log(total), lse_cols[...])
                    return 0

                lax.fori_loop(0, heads, one, 0, unroll=2)

        o[at] = jnp.concatenate([o_heads[i] for i in range(heads)], axis=1)
        lse[b] = jnp.transpose(lse_cols[...])[:heads]

        save(0, b, land.at[s, b], h_out.at[b])
        save(1, b, n1.at[at], n1_out.at[at])
        save(2, b, q.at[:, at], q_out.at[:, at])
        save(3, b, k.at[:, at], k_out.at[:, at])
        save(4, b, v.at[:, at], v_out.at[:, at])
        save(5, b, o.at[at], o_out.at[at])
        save(6, b, lse.at[b], lse_out.at[b])
        for i in range(3):

            @pl.when(b == blocks - 3 + i)
            def _():
                relay(PIECES + i)

        return 0

    lax.fori_loop(0, blocks, attention, 0)

    own[1].wait()
    arrived(PIECES)

    def project(b, _):
        at = pl.ds(pl.multiple_of(b * rows, rows), rows)
        ysend[b] = plain(o[at], wo[...]).astype(BF16)
        remote(ysend.at[b], yrecv.at[b], ys_sem.at[b], yr_sem.at[b], core).start()
        return 0

    lax.fori_loop(0, blocks, project, 0)

    own[2].wait()
    arrived(PIECES + 1)
    own[3].wait()
    arrived(PIECES + 2)
    weights = [(win, win_out), (wo, wo_out), (wu, wu_out), (wd, wd_out)]
    for i, (src, dst) in enumerate(weights):
        save(11, i, src, dst)

    def feed(b, _):
        at = pl.ds(pl.multiple_of(b * rows, rows), rows)
        remote(ysend.at[b], yrecv.at[b], ys_sem.at[b], yr_sem.at[b], core).wait_recv()
        middle = land[s, b].astype(F32) + (ysend[b].astype(F32) + yrecv[b].astype(F32))
        m[b] = middle
        normed = (middle * inverse_rms(middle) * gain_two[...]).astype(BF16)
        n2[at] = normed
        up = jnp.concatenate([plain(normed, wu[0]), plain(normed, wu[1])], axis=1)
        u[b] = up
        active = (up / (1.0 + jnp.exp(-up))).astype(BF16)
        a[at] = active
        zpart[b] = plain(active, wd[...])
        copy = remote(zpart.at[b, theirs], zrecv.at[b], zs_sem.at[b], zr_sem.at[b], core)
        copy.start()
        save(7, b, m.at[b], m_out.at[b])
        save(8, b, n2.at[at], n2_out.at[at])
        save(9, b, u.at[b], u_out.at[b])
        save(10, b, a.at[at], a_out.at[at])
        copy.wait_recv()
        xout[b] = (m[b, mine] + (zpart[b, mine] + zrecv[b])).astype(BF16)

        @pl.when(s == 0)
        def _():
            remote(xout.at[b], land.at[1, b, mine], ns_sem.at[b], nr_sem.at[b], section).start()

        place = out_rows.at[y, mine]

        @pl.when(b == t)
        def _():
            pltpu.make_async_copy(xout.at[b], place, or_sem.at[t]).start()

        @pl.when(b != t)
        def _():
            remote(xout.at[b], place, os_sem.at[b], or_sem.at[t], (s, b, d)).start()

        return 0

    lax.fori_loop(0, blocks, feed, 0)

    @pl.when(s == 1)
    def _():
        gather_rows()

    for b in range(blocks):
        pltpu.make_async_copy(land.at[0, b], g_out.at[b], save_sem.at[12, b]).start()

    for b in range(blocks):
        piece = land.at[0, b, mine]
        remote(piece, piece, xfs_sem.at[b], xfr_sem.at[b], core).wait_send()
        remote(ysend.at[b], yrecv.at[b], ys_sem.at[b], yr_sem.at[b], core).wait_send()
        remote(zpart.at[b, theirs], zrecv.at[b], zs_sem.at[b], zr_sem.at[b], core).wait_send()
        here = out_rows.at[b // 2, pl.ds((b % 2) * half, half)]
        remote(here, here, os_sem.at[b], or_sem.at[b], core).wait_recv()

        @pl.when(b != t)
        def _():
            remote(xout.at[b], here, os_sem.at[b], or_sem.at[b], core).wait_send()
            remote(piece, piece, xs_sem.at[b], xr_sem.at[b], core).wait_send()

        @pl.when(s == 0)
        def _():
            remote(xout.at[b], piece, ns_sem.at[b], nr_sem.at[b], section).wait_send()

        @pl.when(s == 1)
        def _():
            remote(piece, piece, nfs_sem.at[b], nfr_sem.at[b], core).wait_send()

    for i, (src, dst) in enumerate(sent):
        remote(src, dst, wys_sem.at[i], wyr_sem.at[i], across).wait_send()
        remote(dst, dst, wzs_sem.at[i], wzr_sem.at[i], beside).wait_send()
    for i, (src, dst) in enumerate(weights):
        pltpu.make_async_copy(src, dst, save_sem.at[11, i]).wait()
    for b in range(blocks):
        at = pl.ds(b * rows, rows)
        saved = [
            (land.at[s, b], h_out.at[b]),
            (n1.at[at], n1_out.at[at]),
            (q.at[:, at], q_out.at[:, at]),
            (k.at[:, at], k_out.at[:, at]),
            (v.at[:, at], v_out.at[:, at]),
            (o.at[at], o_out.at[at]),
            (lse.at[b], lse_out.at[b]),
            (m.at[b], m_out.at[b]),
            (n2.at[at], n2_out.at[at]),
            (u.at[b], u_out.at[b]),
            (a.at[at], a_out.at[at]),
        ]
        for kind, (src, dst) in enumerate(saved):
            pltpu.make_async_copy(src, dst, save_sem.at[kind, b]).wait()
        pltpu.make_async_copy(land.at[0, b], g_out.at[b], save_sem.at[12, b]).wait()


def forward(inputs, cotangent, w_in, w_o, w_u, w_d, gain_one, gain_two, scale, head):
    _, rows, width = inputs.shape
    local = w_o.shape[0]
    heads = 2 * local // head
    blocks = lax.axis_size("tensor")
    length = blocks * rows
    half = rows // 2
    shape = jax.ShapeDtypeStruct
    outs = [
        shape(inputs.shape, BF16),
        shape((blocks, rows, width), BF16),
        shape((length, width), BF16),
        shape((heads, length, head), BF16),
        shape((heads, length, head), BF16),
        shape((heads, length, head), BF16),
        shape((length, 2 * local), BF16),
        shape((blocks, heads, rows), F32),
        shape((blocks, rows, width), F32),
        shape((length, width), BF16),
        shape((blocks, rows, 2 * local), F32),
        shape((length, 2 * local), BF16),
        shape((blocks, rows, width), BF16),
        shape((2, width, 3 * local), BF16),
        shape((2 * local, width), BF16),
        shape((2, width, local), BF16),
        shape((2 * local, width), BF16),
    ]
    scratch = [
        pltpu.VMEM((2, blocks, rows, width), BF16),
        pltpu.VMEM((2, width, 3 * local), BF16),
        pltpu.VMEM((2 * local, width), BF16),
        pltpu.VMEM((2, width, local), BF16),
        pltpu.VMEM((2 * local, width), BF16),
        pltpu.VMEM((length, width), BF16),
        pltpu.VMEM((heads, length, head), BF16),
        pltpu.VMEM((heads, length, head), BF16),
        pltpu.VMEM((heads, length, head), BF16),
        pltpu.VMEM((heads, rows, head), BF16),
        pltpu.VMEM((length, 2 * local), BF16),
        pltpu.VMEM((rows, 128), F32),
        pltpu.VMEM((blocks, heads, rows), F32),
        pltpu.VMEM((blocks, rows, width), BF16),
        pltpu.VMEM((blocks, rows, width), BF16),
        pltpu.VMEM((blocks, rows, width), F32),
        pltpu.VMEM((length, width), BF16),
        pltpu.VMEM((blocks, rows, 2 * local), F32),
        pltpu.VMEM((length, 2 * local), BF16),
        pltpu.VMEM((blocks, rows, width), F32),
        pltpu.VMEM((blocks, half, width), F32),
        pltpu.VMEM((blocks, half, width), BF16),
        DMA((4,)),
        DMA((blocks,)),
        DMA((blocks,)),
        DMA((blocks,)),
        DMA((blocks,)),
        DMA((PIECES + 3,)),
        DMA((PIECES + 3,)),
        DMA((PIECES + 3,)),
        DMA((PIECES + 3,)),
        DMA((blocks,)),
        DMA((blocks,)),
        DMA((blocks,)),
        DMA((blocks,)),
        DMA((blocks,)),
        DMA((blocks,)),
        DMA((blocks,)),
        DMA((blocks,)),
        DMA((blocks,)),
        DMA((blocks,)),
        DMA((13, blocks)),
    ]
    return pl.pallas_call(
        forward_kernel,
        out_shape=outs,
        in_specs=[ANY] * 6 + [VMEM] * 3,
        out_specs=[ANY] * len(outs),
        scratch_shapes=scratch,
        compiler_params=pltpu.CompilerParams(
            collective_id=1, has_side_effects=True, vmem_limit_bytes=60 * MIB
        ),
        name="forward",
    )(inputs, cotangent, w_in, w_o, w_u, w_d, gain_one, gain_two, scale)


def backward_kernel(
    g_in, h_in, q_in, k_in, v_in, o_in, lse_in, m_in, u_in, win_in, wo_in, wu_in, wd_in,
    gain_one, gain_two, scale,
    out_rows, g_out, gu_out, gy_out, gp_out, dg1, dg2, ds,
    g, win, wo, wu, wd, h, q, k, v, o, lse, m, u, gu, gy, gp, ysend, yrecv, gm, go_heads, gq_heads,
    cols, delta, dk, dv, n1part, n1recv, xout,
    load_sem, w_sem, ns_sem, nr_sem, nfs_sem, nfr_sem, ys_sem, yr_sem, zs_sem, zr_sem, os_sem, or_sem,
    save_sem,
):
    s, t, d = lax.axis_index("section"), lax.axis_index("tensor"), lax.axis_index("dp")
    blocks, rows, width = g.shape
    half = rows // 2
    local = wu.shape[2]
    heads, _, head = q.shape
    per = heads // 2
    c, y = lax.rem(t, 2), t // 2
    core = (s, other(t), d)
    across = (s, lax.rem(t + 2, 4), d)
    diagonal = (s, other(lax.rem(t + 2, 4)), d)
    section = (1 - s, t, d)
    mine = pl.ds(pl.multiple_of(c * half, half), half)
    theirs = pl.ds(pl.multiple_of((1 - c) * half, half), half)

    weights = [(wd_in, wd), (wu_in, wu), (wo_in, wo), (win_in, win)]

    def loads(b):
        at = pl.ds(b * rows, rows)
        return [
            (u_in.at[b], u.at[b]),
            (m_in.at[b], m.at[b]),
            (o_in.at[at], o.at[at]),
            (q_in.at[:, at], q.at[:, at]),
            (k_in.at[:, at], k.at[:, at]),
            (v_in.at[:, at], v.at[:, at]),
            (lse_in.at[b], lse.at[b]),
            (h_in.at[b, mine], h.at[b]),
        ]

    for i, (src, dst) in enumerate(weights[:2]):
        pltpu.make_async_copy(src, dst, w_sem.at[i]).start()
    for kind, (src, dst) in enumerate(loads(blocks - 1)[:2]):
        pltpu.make_async_copy(src, dst, load_sem.at[kind, blocks - 1]).start()

    @pl.when(s == 1)
    def _():
        for b in reversed(range(blocks)):
            pltpu.make_async_copy(g_in.at[b], g.at[b], nr_sem.at[b]).start()

    for i, (src, dst) in enumerate(weights[2:]):
        pltpu.make_async_copy(src, dst, w_sem.at[2 + i]).start()
    for b in reversed(range(blocks)):
        for kind, (src, dst) in enumerate(loads(b)):
            if kind >= 2 or b < blocks - 1:
                pltpu.make_async_copy(src, dst, load_sem.at[kind, b]).start()

    greet([core, across, diagonal, section])

    dk[...] = jnp.zeros_like(dk)
    dv[...] = jnp.zeros_like(dv)
    dg1[...] = jnp.zeros_like(dg1)
    dg2[...] = jnp.zeros_like(dg2)
    ds[...] = jnp.zeros_like(ds)
    for i, (src, dst) in enumerate(weights):
        pltpu.make_async_copy(src, dst, w_sem.at[i]).wait()
    for b in range(blocks):
        for kind, (src, dst) in enumerate(loads(b)):
            if b != blocks - 1 or kind < 2:
                pass
            pltpu.make_async_copy(src, dst, load_sem.at[kind, b]).wait()

    causal = lax.broadcasted_iota(jnp.int32, (rows, rows), 0) <= lax.broadcasted_iota(
        jnp.int32, (rows, rows), 1
    )

    def save(kind, b, src, dst):
        pltpu.make_async_copy(src, dst, save_sem.at[kind, b]).start()

    def one_block(turn, _):
        b = blocks - 1 - turn
        at = pl.ds(pl.multiple_of(b * rows, rows), rows)

        @pl.when(s == 1)
        def _():
            pltpu.make_async_copy(g_in.at[b], g.at[b], nr_sem.at[b]).wait()

        @pl.when(s == 0)
        def _():
            piece = g.at[b, mine]
            remote(piece, piece, ns_sem.at[b], nr_sem.at[b], core).wait_recv()
            remote(piece, piece, nfs_sem.at[b], nfr_sem.at[b], core).start()
            rest = g.at[b, theirs]
            remote(rest, rest, nfs_sem.at[b], nfr_sem.at[b], core).wait_recv()

        save(0, b, g.at[b], g_out.at[at])
        grad = g[b]
        grad_act = by_last(grad, wd[...])
        up = u[b]
        sigma = 1.0 / (1.0 + jnp.exp(-up))
        grad_up = (grad_act * sigma * (1.0 + up * (1.0 - sigma))).astype(BF16)
        gu[at] = grad_up
        save(1, b, gu.at[at], gu_out.at[at])
        ysend[b] = (by_last(grad_up[:, :local], wu[0]) + by_last(grad_up[:, local:], wu[1])).astype(
            BF16
        )
        copy = remote(ysend.at[b], yrecv.at[b], ys_sem.at[b], yr_sem.at[b], core)
        copy.start()
        copy.wait_recv()
        grad_normed = ysend[b].astype(F32) + yrecv[b].astype(F32)
        middle = m[b]
        inverse = inverse_rms(middle)
        unit = middle * inverse
        grad_unit = grad_normed * gain_two[...]
        dg2[...] += jnp.sum(grad_normed * unit, axis=0, keepdims=True)
        grad_middle = grad.astype(F32) + inverse * (
            grad_unit - unit * jnp.mean(grad_unit * unit, axis=1, keepdims=True)
        )
        gm[...] = grad_middle
        grad_mid = grad_middle.astype(BF16)
        gy[at] = grad_mid
        save(2, b, gy.at[at], gy_out.at[at])
        grad_mixed = by_last(grad_mid, wo[...]).astype(BF16)
        both = grad_mixed.astype(F32) * o[at].astype(F32)
        lane = lax.broadcasted_iota(jnp.int32, (rows, 128), 1)
        found = jnp.zeros((rows, 128), F32)
        for i in range(heads):
            cut = slice(i * head, (i + 1) * head)
            go_heads[i] = grad_mixed[:, cut]
            found = jnp.where(lane == i, jnp.sum(both[:, cut], axis=1, keepdims=True), found)
        delta[...] = jnp.transpose(found)[:heads]
        for bb in range(blocks):

            @pl.when(b == bb)
            def _():
                def one(i, _):
                    qh = q[i, bb * rows : (bb + 1) * rows]
                    gh = go_heads[i]
                    offset = lse[bb, pl.ds(i, 1)]
                    inner = delta[pl.ds(i, 1)]
                    total = jnp.zeros((head, rows), F32)
                    for j in range(bb + 1):
                        cut = slice(j * rows, (j + 1) * rows)
                        kj = k[i, cut]
                        weight = jnp.exp(by_last(kj, qh) - offset)
                        if j == bb:
                            weight = jnp.where(causal, weight, 0.0)
                        grad_score = weight * (by_last(v[i, cut], gh) - inner)
                        grad_score = grad_score.astype(BF16)
                        dv[i, cut] += plain(weight.astype(BF16), gh)
                        dk[i, cut] += plain(grad_score, qh)
                        total = total + by_first(kj, grad_score)
                    gq_heads[i] = jnp.transpose(total)
                    return 0

                lax.fori_loop(0, heads, one, 0)

        for j in range(2):
            mine_heads = range(j * per, (j + 1) * per)
            grad_scaled = jnp.concatenate([gq_heads[i] for i in mine_heads], axis=1)
            queries = jnp.concatenate([q[i, at] for i in mine_heads], axis=1).astype(F32)
            ds[pl.ds(j, 1)] += jnp.sum(grad_scaled * queries, axis=0, keepdims=True)
            grads = [
                (grad_scaled * scale[...]).astype(BF16),
                jnp.concatenate([dk[i, at] for i in mine_heads], axis=1).astype(BF16),
                jnp.concatenate([dv[i, at] for i in mine_heads], axis=1).astype(BF16),
            ]
            gp[j, at] = jnp.concatenate(grads, axis=1)
        save(3, b, gp.at[:, at], gp_out.at[:, at])
        n1part[...] = by_last(gp[0, at], win[0]) + by_last(gp[1, at], win[1])
        copy = remote(n1part.at[theirs], n1recv.at[b], zs_sem.at[b], zr_sem.at[b], core)
        copy.start()
        copy.wait_recv()
        grad_normed = n1part[mine] + n1recv[b]
        hidden = h[b].astype(F32)
        inverse = inverse_rms(hidden)
        unit = hidden * inverse
        grad_unit = grad_normed * gain_one[...]
        dg1[...] += jnp.sum(grad_normed * unit, axis=0, keepdims=True)
        xout[b] = (
            gm[mine]
            + inverse * (grad_unit - unit * jnp.mean(grad_unit * unit, axis=1, keepdims=True))
        ).astype(BF16)

        @pl.when(s == 1)
        def _():
            remote(xout.at[b], g.at[b, mine], ns_sem.at[b], nr_sem.at[b], section).start()

        place = out_rows.at[y, mine]

        @pl.when(b == t)
        def _():
            pltpu.make_async_copy(xout.at[b], place, or_sem.at[t]).start()

        @pl.when(b != t)
        def _():
            remote(xout.at[b], place, os_sem.at[b], or_sem.at[t], (s, b, d)).start()

        copy.wait_send()
        return 0

    lax.fori_loop(0, blocks, one_block, 0)

    for b in range(blocks):
        at = pl.ds(b * rows, rows)
        piece = g.at[b, mine]
        remote(ysend.at[b], yrecv.at[b], ys_sem.at[b], yr_sem.at[b], core).wait_send()
        here = out_rows.at[b // 2, pl.ds((b % 2) * half, half)]
        remote(here, here, os_sem.at[b], or_sem.at[b], core).wait_recv()

        @pl.when(b != t)
        def _():
            remote(xout.at[b], here, os_sem.at[b], or_sem.at[b], core).wait_send()

        @pl.when(s == 1)
        def _():
            remote(xout.at[b], piece, ns_sem.at[b], nr_sem.at[b], section).wait_send()

        @pl.when(s == 0)
        def _():
            remote(piece, piece, nfs_sem.at[b], nfr_sem.at[b], core).wait_send()

        saved = [
            (g.at[b], g_out.at[at]),
            (gu.at[at], gu_out.at[at]),
            (gy.at[at], gy_out.at[at]),
            (gp.at[:, at], gp_out.at[:, at]),
        ]
        for kind, (src, dst) in enumerate(saved):
            pltpu.make_async_copy(src, dst, save_sem.at[kind, b]).wait()


def backward(saved, gain_one, gain_two, scale):
    g_in, h_in, q_in = saved[:3]
    win_in, wo_in, wu_in, wd_in = saved[9:]
    blocks, rows, width = g_in.shape
    heads, length, head = q_in.shape
    local = wu_in.shape[2]
    half = rows // 2
    shape = jax.ShapeDtypeStruct
    outs = [
        shape((2, rows, width), BF16),
        shape((length, width), BF16),
        shape((length, 2 * local), BF16),
        shape((length, width), BF16),
        shape((2, length, 3 * local), BF16),
        shape((1, width), F32),
        shape((1, width), F32),
        shape((2, local), F32),
    ]
    scratch = [
        pltpu.VMEM((blocks, rows, width), BF16),
        pltpu.VMEM(win_in.shape, BF16),
        pltpu.VMEM(wo_in.shape, BF16),
        pltpu.VMEM(wu_in.shape, BF16),
        pltpu.VMEM(wd_in.shape, BF16),
        pltpu.VMEM((blocks, half, width), BF16),
        pltpu.VMEM((heads, length, head), BF16),
        pltpu.VMEM((heads, length, head), BF16),
        pltpu.VMEM((heads, length, head), BF16),
        pltpu.VMEM((length, 2 * local), BF16),
        pltpu.VMEM((blocks, heads, rows), F32),
        pltpu.VMEM((blocks, rows, width), F32),
        pltpu.VMEM((blocks, rows, 2 * local), F32),
        pltpu.VMEM((length, 2 * local), BF16),
        pltpu.VMEM((length, width), BF16),
        pltpu.VMEM((2, length, 3 * local), BF16),
        pltpu.VMEM((blocks, rows, width), BF16),
        pltpu.VMEM((blocks, rows, width), BF16),
        pltpu.VMEM((rows, width), F32),
        pltpu.VMEM((heads, rows, head), BF16),
        pltpu.VMEM((heads, rows, head), F32),
        pltpu.VMEM((8, 128), F32),
        pltpu.VMEM((heads, rows), F32),
        pltpu.VMEM((heads, length, head), F32),
        pltpu.VMEM((heads, length, head), F32),
        pltpu.VMEM((rows, width), F32),
        pltpu.VMEM((blocks, half, width), F32),
        pltpu.VMEM((blocks, half, width), BF16),
        DMA((8, blocks)),
        DMA((4,)),
        DMA((blocks,)),
        DMA((blocks,)),
        DMA((blocks,)),
        DMA((blocks,)),
        DMA((blocks,)),
        DMA((blocks,)),
        DMA((blocks,)),
        DMA((blocks,)),
        DMA((blocks,)),
        DMA((blocks,)),
        DMA((4, blocks)),
    ]
    return pl.pallas_call(
        backward_kernel,
        out_shape=outs,
        in_specs=[ANY] * 13 + [VMEM] * 3,
        out_specs=[ANY] * 5 + [VMEM] * 3,
        scratch_shapes=scratch,
        compiler_params=pltpu.CompilerParams(
            collective_id=2, has_side_effects=True, vmem_limit_bytes=62 * MIB
        ),
        name="backward",
    )(*saved, gain_one, gain_two, scale)


def farthest_first(d, k, n):
    found = 0
    for i in range(n):
        above = list(range(n - 1, i, -1))
        below = list(range(i))
        first, second = (above, below) if len(above) >= len(below) else (below, above)
        lead = len(first) - len(second) - 1
        order = first[: max(lead, 0)]
        rest = first[max(lead, 0) :]
        for j in range(max(len(rest), len(second))):
            order += rest[j : j + 1] + second[j : j + 1]
        order.append(i)
        picked = 0
        for j, e in enumerate(order):
            picked = picked + jnp.where(k == j, e, 0)
        found = found + jnp.where(d == i, picked, 0)
    return found


def gradient_kernel(
    n1_in, n2_in, gy_in, g_in, gp_in, gu_in, o_in, a_in, small,
    out, small_out,
    x, xt, gp, gu, o, a, keep, give, yrecv, flow, last, keep_d, give_d, flow_k, flow_g, last_k, last_g,
    yd, smalls, chain,
    x_sem, g_sem, ys_sem, yr_sem, fs_sem, fr_sem, last_sem, ks_sem, kr_sem, gs_sem, gr_sem, last_d_sem,
    yds_sem, ydr_sem, ss_sem, sr_sem, cs_sem, cr_sem,
):
    s, t, d = lax.axis_index("section"), lax.axis_index("tensor"), lax.axis_index("dp")
    n, chunk, wide = keep.shape
    local = keep_d.shape[2]
    pieces = ys_sem.shape[1]
    step = chunk // pieces
    core = (s, other(t), d)
    across = (s, lax.rem(t + 2, 4), d)
    diagonal = (s, other(lax.rem(t + 2, 4)), d)
    up = (s, t, lax.rem(d + 1, n))
    down = (s, t, lax.rem(d + n - 1, n))

    def load(i, source):
        return pltpu.make_async_copy(source, x.at[i % 2], x_sem.at[i])

    sources = [g_in, n1_in, n2_in, gy_in]
    load(0, g_in).start()
    operands = [(a_in, a), (gp_in, gp), (gu_in, gu), (o_in, o)]
    pltpu.make_async_copy(a_in, a, g_sem.at[0]).start()
    load(1, n1_in).start()
    for i in range(1, 4):
        pltpu.make_async_copy(operands[i][0], operands[i][1], g_sem.at[i]).start()

    greet([core, across, diagonal, up, down])

    partners = [core, across, diagonal]

    def share(i):
        return remote(small, smalls.at[i], ss_sem.at[i], sr_sem.at[i], partners[i])

    for i in range(3):
        share(i).start()

    def turn(i):
        load(i, sources[i]).wait()
        turned = jnp.transpose(x[i % 2])
        for e in range(n):
            xt[i, e] = turned[e * chunk : (e + 1) * chunk]
        if i + 2 < 4:
            load(i + 2, sources[i + 2]).start()

    def flow_piece(buffer, into, e, send, receive, device):
        return remote(buffer.at[e], into.at[e], send.at[e], receive.at[e], device)

    turn(0)
    pltpu.make_async_copy(a_in, a, g_sem.at[0]).wait()

    def down_product(e, _):
        both = plain(xt[0, e], a[...])
        keep_d[e] = both[:, :local].astype(BF16)
        give_d[e] = both[:, local:].astype(BF16)
        return 0

    lax.fori_loop(0, n, down_product, 0)

    line_d = [(keep_d, flow_k, last_k, ks_sem, kr_sem, 0), (give_d, flow_g, last_g, gs_sem, gr_sem, 1)]

    def upstream_d(e, buffer, into, send, receive):
        piece = into.at[e]
        remote(piece, piece, send.at[e], receive.at[e], up).wait_recv()
        buffer[e] = (buffer[e].astype(F32) + into[e].astype(F32)).astype(BF16)

    def send_d(e, buffer, into, spare, send, receive, i):
        @pl.when(e > d)
        def _():
            remote(buffer.at[e], into.at[e], send.at[e], receive.at[e], up).start()

        @pl.when(e < d - 1)
        def _():
            remote(buffer.at[e], into.at[e], send.at[e], receive.at[e], down).start()

        @pl.when(e == d - 1)
        def _():
            remote(buffer.at[e], spare, send.at[e], last_d_sem.at[i], down).start()

    def ends(k, _):
        e = farthest_first(d, k, n)
        for buffer, into, spare, send, receive, i in line_d:

            @pl.when(((d == 0) | (d == n - 1)) & (e != d))
            def _():
                send_d(e, buffer, into, spare, send, receive, i)

        return 0

    lax.fori_loop(0, n, ends, 0)

    turn(1)
    turn(2)
    turn(3)
    for i in range(1, 4):
        pltpu.make_async_copy(operands[i][0], operands[i][1], g_sem.at[i]).wait()

    def exchange(e, i):
        rows = pl.ds(i * step, step)
        return remote(
            give.at[e, rows], yrecv.at[e, rows], ys_sem.at[e, i], yr_sem.at[e, i], across
        )

    def products(k, _):
        e = farthest_first(d, k, n)
        ups = plain(xt[2, e], gu[...])
        outs = plain(xt[3, e], o[...])
        for j, target in ((1, give), (0, keep)):
            cut = slice(j * local, (j + 1) * local)
            target[e] = jnp.concatenate(
                [
                    plain(xt[1, e], gp[j]).astype(BF16),
                    ups[:, cut].astype(BF16),
                    outs[:, cut].astype(BF16),
                ],
                axis=1,
            )
            if j:
                for i in range(pieces):
                    exchange(e, i).start()
        return 0

    lax.fori_loop(0, n, products, 0)

    for i in range(3):
        share(i).wait_recv()
    mine = small[...] + smalls[0] + (smalls[1] + smalls[2])
    small_out[...] = mine

    def link(i, device):
        return remote(chain.at[i], chain.at[2 + i], cs_sem.at[i], cr_sem.at[i], device)

    for i, first, final, device in ((0, d == 0, d == n - 1, up), (1, d == n - 1, d == 0, down)):
        chain[i] = mine

        @pl.when(jnp.logical_not(first))
        def _():
            link(i, device).wait_recv()
            chain[i] = mine + chain[2 + i]
            small_out[...] += chain[2 + i]

        @pl.when(jnp.logical_not(final))
        def _():
            link(i, device).start()

    def middle(k, _):
        e = farthest_first(d, k, n)
        for buffer, into, spare, send, receive, i in line_d:

            @pl.when((d > 0) & (d < n - 1) & (e != d))
            def _():
                upstream_d(e, buffer, into, send, receive)
                send_d(e, buffer, into, spare, send, receive, i)

        return 0

    lax.fori_loop(0, n, middle, 0)

    def flows(k, _):
        e = farthest_first(d, k, n)
        for i in range(pieces):
            at = pl.ds(i * step, step)

            first = ((e > d) & (d == 0)) | ((e < d) & (d == n - 1))

            @pl.when(e != d)
            def _():
                exchange(e, i).wait_recv()

            @pl.when((e != d) & first)
            def _():
                keep[e, at] = (keep[e, at].astype(F32) + yrecv[e, at].astype(F32)).astype(BF16)

            @pl.when((e != d) & jnp.logical_not(first))
            def _():
                piece = flow.at[e, at]
                remote(piece, piece, fs_sem.at[e, i], fr_sem.at[e, i], up).wait_recv()
                total = keep[e, at].astype(F32) + yrecv[e, at].astype(F32)
                keep[e, at] = (total + flow[e, at].astype(F32)).astype(BF16)

            src = keep.at[e, at]

            @pl.when(e > d)
            def _():
                remote(src, flow.at[e, at], fs_sem.at[e, i], fr_sem.at[e, i], up).start()

            @pl.when(e < d - 1)
            def _():
                remote(src, flow.at[e, at], fs_sem.at[e, i], fr_sem.at[e, i], down).start()

            @pl.when(e == d - 1)
            def _():
                remote(src, last.at[at], fs_sem.at[e, i], last_sem.at[i], down).start()

        return 0

    lax.fori_loop(0, n, flows, 0)

    for buffer, into, spare, send, receive, i in line_d:

        @pl.when(d > 0)
        def _():
            upstream_d(d, buffer, into, send, receive)

        @pl.when(d < n - 1)
        def _():
            remote(spare, spare, send.at[0], last_d_sem.at[i], down).wait_recv()
            buffer[d] = (buffer[d].astype(F32) + spare[...].astype(F32)).astype(BF16)

    crossing = remote(give_d.at[d], yd, yds_sem, ydr_sem, across)
    crossing.start()
    for i in range(pieces):
        at = pl.ds(i * step, step)
        exchange(d, i).wait_recv()
        out[at, :wide] = keep[d, at].astype(F32) + yrecv[d, at].astype(F32)

        @pl.when(d > 0)
        def _():
            piece = flow.at[d, at]
            remote(piece, piece, fs_sem.at[d, i], fr_sem.at[d, i], up).wait_recv()
            out[at, :wide] += flow[d, at].astype(F32)

        @pl.when(d < n - 1)
        def _():
            piece = last.at[at]
            remote(piece, piece, fs_sem.at[d, i], last_sem.at[i], down).wait_recv()
            out[at, :wide] += last[at].astype(F32)

    crossing.wait_recv()
    out[:, wide:] = keep_d[d].astype(F32) + yd[...].astype(F32)

    crossing.wait_send()
    for i in range(3):
        share(i).wait_send()

    @pl.when(d < n - 1)
    def _():
        link(0, up).wait_send()

    @pl.when(d > 0)
    def _():
        link(1, down).wait_send()

    def drain(e, _):
        for i in range(pieces):
            exchange(e, i).wait_send()

        @pl.when(e != d)
        def _():
            for i in range(pieces):
                piece = keep.at[e, pl.ds(i * step, step)]
                remote(piece, piece, fs_sem.at[e, i], fr_sem.at[e, i], up).wait_send()
            for buffer, into, spare, send, receive, i in line_d:
                remote(buffer.at[e], buffer.at[e], send.at[e], receive.at[e], up).wait_send()

        return 0

    lax.fori_loop(0, n, drain, 0)


def gradients(n1, n2, gy, g, gp, gu, o, a, small):
    n = lax.axis_size("dp")
    length, width = n1.shape
    local = gp.shape[2] // 3
    chunk = width // n
    wide = 5 * local
    pieces = 4 if chunk % 64 == 0 else 1
    big = pltpu.VMEM((n, chunk, wide), BF16)
    line = pltpu.VMEM((n, chunk, local), BF16)
    return pl.pallas_call(
        gradient_kernel,
        out_shape=[
            jax.ShapeDtypeStruct((chunk, 6 * local), F32),
            jax.ShapeDtypeStruct(small.shape, F32),
        ],
        in_specs=[ANY] * 8 + [VMEM],
        out_specs=[VMEM, VMEM],
        scratch_shapes=[
            pltpu.VMEM((2, length, width), BF16),
            pltpu.VMEM((4, n, chunk, length), BF16),
            pltpu.VMEM(gp.shape, BF16),
            pltpu.VMEM(gu.shape, BF16),
            pltpu.VMEM(o.shape, BF16),
            pltpu.VMEM(a.shape, BF16),
            big,
            big,
            big,
            big,
            pltpu.VMEM((chunk, wide), BF16),
            line,
            line,
            line,
            line,
            pltpu.VMEM((chunk, local), BF16),
            pltpu.VMEM((chunk, local), BF16),
            pltpu.VMEM((chunk, local), BF16),
            pltpu.VMEM((3,) + small.shape, F32),
            pltpu.VMEM((4,) + small.shape, F32),
            DMA((4,)),
            DMA((4,)),
            DMA((n, pieces)),
            DMA((n, pieces)),
            DMA((n, pieces)),
            DMA((n, pieces)),
            DMA((pieces,)),
            DMA((n,)),
            DMA((n,)),
            DMA((n,)),
            DMA((n,)),
            DMA((2,)),
            DMA,
            DMA,
            DMA((3,)),
            DMA((3,)),
            DMA((2,)),
            DMA((2,)),
        ],
        compiler_params=pltpu.CompilerParams(
            collective_id=3, has_side_effects=True, vmem_limit_bytes=62 * MIB
        ),
        name="gradients",
    )(n1, n2, gy, g, gp, gu, o, a, small)


def body(
    inputs, cotangent, gain_attn, w_query, w_key, w_value, w_out, dim_scale, gain_mlp, w_up, w_down
):
    local = w_query.shape[2]
    head = dim_scale.shape[1]
    width = inputs.shape[2]
    w_in = jnp.concatenate([w_query[0], w_key[0], w_value[0]], axis=1)
    multiplier = LOG2E / math.sqrt(head)
    per_dim = multiplier * jax.nn.softplus(dim_scale)
    done = forward(
        inputs, cotangent, w_in, w_out[0], w_up[0], w_down[0], gain_attn, gain_mlp, per_dim, head
    )
    layer_out, h, n1, q, k, v, o, lse, m, n2, u, a, g, win, wo, wu, wd = done
    input_grads, g_all, gu, gy, gp, dg1, dg2, ds = backward(
        (g, h, q, k, v, o, lse, m, u, win, wo, wu, wd),
        gain_attn,
        gain_mlp,
        jnp.tile(per_dim, (1, local // head)),
    )

    first_core = lax.rem(lax.axis_index("tensor"), 2) == 0
    dg2 = jnp.where(first_core, dg2, 0.0)
    small = jnp.concatenate([dg1, dg2, ds.reshape(1, -1)], axis=1)
    grads, small = gradients(n1, n2, gy, g_all, gp, gu, o, a, small)
    dg1, dg2 = small[:, :width], small[:, width : 2 * width]
    ds = jnp.sum(small[:, 2 * width :].reshape(-1, head), axis=0, keepdims=True)
    grad_scale = ds / per_dim * multiplier * jax.nn.sigmoid(dim_scale)
    pieces = [grads[:, i * local : (i + 1) * local] for i in range(6)]
    return (
        layer_out[None],
        input_grads[None],
        dg1,
        pieces[0][None],
        pieces[1][None],
        pieces[2][None],
        pieces[4].T[None],
        grad_scale,
        dg2,
        pieces[3][None],
        pieces[5].T[None],
    )


def solution(mesh):
    in_specs = (
        P("dp", "tensor", None),
        P("dp", "tensor", None),
        P("section", None),
        P("section", None, "tensor"),
        P("section", None, "tensor"),
        P("section", None, "tensor"),
        P("section", "tensor", None),
        P("section", None),
        P("section", None),
        P("section", None, "tensor"),
        P("section", "tensor", None),
    )
    out_specs = (
        P("section", "dp", "tensor", None),
        P("section", "dp", "tensor", None),
        P("section", None),
        P("section", "dp", "tensor"),
        P("section", "dp", "tensor"),
        P("section", "dp", "tensor"),
        P("section", "tensor", "dp"),
        P("section", None),
        P("section", None),
        P("section", "dp", "tensor"),
        P("section", "tensor", "dp"),
    )
    return jax.shard_map(body, mesh=mesh, in_specs=in_specs, out_specs=out_specs, check_vma=False)
```

```python
import functools
import math

import jax
import jax.numpy as jnp
from jax import lax
from jax.experimental import pallas as pl
from jax.experimental.pallas import tpu as pltpu
from jax.sharding import PartitionSpec as P

EPS = 1e-06
LOG2E = 1.442695041
NEGATIVE = -1e30
BF16 = jnp.bfloat16
F32 = jnp.float32
MESH = pl.DeviceIdType.MESH
ANY = pl.BlockSpec(memory_space=pl.ANY)
VMEM = pl.BlockSpec(memory_space=pltpu.VMEM)
DMA = pltpu.SemaphoreType.DMA
MIB = 1 << 20
PIECES = 4


def plain(a, b):
    return jnp.dot(a, b, preferred_element_type=F32)


def by_last(a, b):
    return lax.dot_general(a, b, (((1,), (1,)), ((), ())), preferred_element_type=F32)


def by_first(a, b):
    return lax.dot_general(a, b, (((0,), (0,)), ((), ())), preferred_element_type=F32)


def other(index):
    return index + 1 - 2 * lax.rem(index, 2)


def remote(src, dst, send, receive, device):
    return pltpu.make_async_remote_copy(
        src_ref=src,
        dst_ref=dst,
        send_sem=send,
        recv_sem=receive,
        device_id=device,
        device_id_type=MESH,
    )


def greet(devices):
    barrier = pltpu.get_barrier_semaphore()
    for device in devices:
        pl.semaphore_signal(barrier, inc=1, device_id=device, device_id_type=MESH)
    pl.semaphore_wait(barrier, len(devices))


def inverse_rms(rows):
    return lax.rsqrt(jnp.mean(rows * rows, axis=1, keepdims=True) + EPS)


def forward_kernel(
    inputs, cotangent, w_q, w_k, w_v, w_o, w_u, w_d, gain_one, gain_two, scale,
    out_rows, h_out, n1_out, q_out, k_out, v_out, o_out, lse_out, m_out, n2_out, u_out, a_out,
    g_out, win_out, wo_out, wu_out, wd_out,
    land, win, wo, wu, wd, passing, n1, q, k, v, o_heads, o, lse_cols, lse, ysend, yrecv, m, n2, u, a,
    zpart, zrecv, xout,
    own_sem, ps_sem, pr_sem, xs_sem, xp_sem, xr_sem, xfs_sem, wys_sem, wyr_sem, wzs_sem, wzr_sem,
    ns_sem, nr_sem, nfs_sem, nfr_sem, ys_sem, yr_sem, zs_sem, zr_sem, os_sem, or_sem, save_sem,
):
    s, t, d = lax.axis_index("section"), lax.axis_index("tensor"), lax.axis_index("dp")
    blocks, rows, width = land.shape[1:]
    half = rows // 2
    local = w_o.shape[0]
    heads, _, head = q.shape
    per = heads // 2
    c, y = lax.rem(t, 2), t // 2
    t_core, t_across = other(t), lax.rem(t + 2, 4)
    t_diagonal = other(t_across)
    core = (s, t_core, d)
    across = (s, t_across, d)
    diagonal = (s, t_diagonal, d)
    beside = (s, t, other(d))
    section = (1 - s, t, d)
    greet([core, across, diagonal, beside, section])

    mine = pl.ds(pl.multiple_of(c * half, half), half)
    theirs = pl.ds(pl.multiple_of((1 - c) * half, half), half)

    shards = [w_q, w_k, w_v, w_o, w_u, w_d]

    def place(i, slot, start, size):
        if i < 3:
            return win.at[slot, pl.ds(pl.multiple_of(i * local + start, 16), size)]
        return (wo, wu, wd)[i - 3].at[pl.ds(pl.multiple_of(slot * local + start, 16), size)]

    short = local // 2
    parity = lax.rem(d, 2)

    def own(i):
        return pltpu.make_async_copy(shards[i], place(i, 0, 0, local), own_sem.at[i])

    def crossing(i):
        start = pl.multiple_of(parity * short, short)
        dst = place(i, 1, start, short)
        return remote(
            shards[i].at[pl.ds(start, short)], dst, wys_sem.at[i], wyr_sem.at[i], across
        )

    def beside_copy(i, which):
        piece = place(i, 1, pl.multiple_of(which * short, short), short)
        return remote(piece, piece, wzs_sem.at[i], wzr_sem.at[i], beside)

    def relay(i):
        crossing(i).wait_recv()
        beside_copy(i, parity).start()

    def arrived(i):
        beside_copy(i, 1 - parity).wait_recv()

    step = rows // PIECES

    def passing_copy(i):
        piece = pl.ds(i * step, step)
        return remote(
            inputs.at[1 - y, piece], passing.at[piece], ps_sem.at[i], pr_sem.at[i], across
        )

    def onward(i):
        piece = pl.ds(i * step, step)
        return remote(
            passing.at[piece], land.at[0, t_across, piece], ps_sem.at[PIECES + i], xp_sem.at[i], section
        )

    def over(i):
        piece = pl.ds(i * step, step)
        return remote(
            cotangent.at[1 - y, piece], land.at[0, t, piece], xs_sem.at[i], xp_sem.at[i], across
        )

    def local_rows(source):
        pltpu.make_async_copy(source.at[y], land.at[0, t], xr_sem.at[t]).start()
        remote(source.at[y], land.at[0, t], xs_sem.at[PIECES], xr_sem.at[t], core).start()

    def block_wait(b):
        piece = land.at[0, b]
        remote(piece, piece, xs_sem.at[PIECES], xr_sem.at[b], core).wait_recv()

    def far_rows():
        for i in range(PIECES):
            piece = land.at[0, t_across, pl.ds(i * step, step)]
            remote(piece, piece, xfs_sem, xp_sem.at[i], core).wait_recv()
        piece = land.at[0, t_across]
        remote(piece, piece, xfs_sem, xr_sem.at[t_across], core).start()
        block_wait(t_diagonal)

    def near_rows():
        block_wait(t)
        block_wait(t_core)

    for i in range(3):
        own(i).start()

    @pl.when(s == 0)
    def _():
        local_rows(inputs)

    @pl.when(s == 1)
    def _():
        for i in range(PIECES):
            passing_copy(i).start()

    for i in range(6):
        crossing(i).start()
    for i in range(3, 6):
        own(i).start()

    @pl.when(s == 1)
    def _():
        local_rows(cotangent)
        for i in range(PIECES):
            over(i).start()
        for i in range(PIECES):
            passing_copy(i).wait_recv()
            onward(i).start()
        for i in range(6):
            relay(i)

    for i in range(3):
        own(i).wait()

    def save(kind, b, src, dst):
        pltpu.make_async_copy(src, dst, save_sem.at[kind, b]).start()

    causal = lax.broadcasted_iota(jnp.int32, (rows, rows), 0) >= lax.broadcasted_iota(
        jnp.int32, (rows, rows), 1
    )
    lane = lax.broadcasted_iota(jnp.int32, (rows, 128), 1)

    def attention(turn, _):
        b = jnp.where(s == 0, lax.rem(turn, blocks), turn // 2)
        j = jnp.where(s == 0, turn // blocks, lax.rem(turn, 2))
        at = pl.ds(pl.multiple_of(b * rows, rows), rows)

        @pl.when((s == 0) & (turn == 0))
        def _():
            near_rows()

        @pl.when((s == 0) & (turn == 2 * (1 - y)))
        def _():
            relay(0)
            relay(1)
            far_rows()

        @pl.when((s == 0) & (turn == blocks))
        def _():
            for i in range(3):
                arrived(i)

        @pl.when((s == 1) & (turn == 0))
        def _():
            for i in range(3):
                arrived(i)

        @pl.when((s == 1) & (j == 0))
        def _():
            piece = land.at[1, b, mine]
            remote(piece, piece, ns_sem.at[b], nr_sem.at[b], core).wait_recv()
            remote(piece, piece, nfs_sem.at[b], nfr_sem.at[b], core).start()
            rest = land.at[1, b, theirs]
            remote(rest, rest, nfs_sem.at[b], nfr_sem.at[b], core).wait_recv()

        @pl.when(j == 0)
        def _():
            hidden = land[s, b].astype(F32)
            n1[at] = (hidden * inverse_rms(hidden) * gain_one[...]).astype(BF16)
            lse_cols[b] = jnp.zeros(lse_cols.shape[1:], F32)
            save(0, b, land.at[s, b], h_out.at[b])
            save(1, b, n1.at[at], n1_out.at[at])

        projected = by_last(n1[at], win[j])
        first = j * per
        for i in range(per):
            cut = i * head
            q[first + i, at] = (projected[:, cut : cut + head] * scale[...]).astype(BF16)
            cut += local
            k[first + i, at] = projected[:, cut : cut + head].astype(BF16)
            cut += local
            v[first + i, at] = projected[:, cut : cut + head].astype(BF16)
        for bb in range(blocks):

            @pl.when(b == bb)
            def _():
                for i in range(per):
                    hd = first + i
                    qh = q[hd, bb * rows : (bb + 1) * rows]
                    near = by_last(qh, k[hd, bb * rows : (bb + 1) * rows])
                    near = jnp.where(causal, near, NEGATIVE)
                    top = jnp.max(near, axis=1, keepdims=True)
                    if bb:
                        far = by_last(qh, k[hd, : bb * rows])
                        top = jnp.maximum(top, jnp.max(far, axis=1, keepdims=True))
                    near = jnp.exp(near - top)
                    total = jnp.sum(near, axis=1, keepdims=True)
                    mixed = plain(near.astype(BF16), v[hd, bb * rows : (bb + 1) * rows])
                    if bb:
                        far = jnp.exp(far - top)
                        total = total + jnp.sum(far, axis=1, keepdims=True)
                        mixed = mixed + plain(far.astype(BF16), v[hd, : bb * rows])
                    o_heads[hd, bb * rows : (bb + 1) * rows] = (mixed / total).astype(BF16)
                    lse_cols[bb] = jnp.where(lane == hd, top + jnp.log(total), lse_cols[bb])

        @pl.when(j == 1)
        def _():
            o[at] = jnp.concatenate([o_heads[i, at] for i in range(heads)], axis=1)
            lse[b] = jnp.transpose(lse_cols[b])[:heads]
            save(2, b, q.at[:, at], q_out.at[:, at])
            save(3, b, k.at[:, at], k_out.at[:, at])
            save(4, b, v.at[:, at], v_out.at[:, at])
            save(5, b, o.at[at], o_out.at[at])
            save(6, b, lse.at[b], lse_out.at[b])

        for i, when in ((2, 2), (3, 4), (4, 5), (5, 7)):

            @pl.when((s == 0) & (turn == when))
            def _():
                relay(i)

        return 0

    lax.fori_loop(0, 2 * blocks, attention, 0)

    own(3).wait()
    arrived(3)

    def project(b, _):
        at = pl.ds(pl.multiple_of(b * rows, rows), rows)
        ysend[b] = plain(o[at], wo[...]).astype(BF16)
        remote(ysend.at[b], yrecv.at[b], ys_sem.at[b], yr_sem.at[b], core).start()
        return 0

    lax.fori_loop(0, blocks, project, 0)

    for i in range(4, 6):
        own(i).wait()
        arrived(i)
    weights = [(win, win_out), (wo, wo_out), (wu, wu_out), (wd, wd_out)]
    for i, (src, dst) in enumerate(weights):
        save(11, i, src, dst)

    def feed(b, _):
        at = pl.ds(pl.multiple_of(b * rows, rows), rows)
        remote(ysend.at[b], yrecv.at[b], ys_sem.at[b], yr_sem.at[b], core).wait_recv()
        middle = land[s, b].astype(F32) + (ysend[b].astype(F32) + yrecv[b].astype(F32))
        m[b] = middle
        normed = (middle * inverse_rms(middle) * gain_two[...]).astype(BF16)
        n2[at] = normed
        up = by_last(normed, wu[...])
        u[b] = up
        active = (up / (1.0 + jnp.exp(-up))).astype(BF16)
        a[at] = active
        zpart[b] = plain(active, wd[...])
        copy = remote(zpart.at[b, theirs], zrecv.at[b], zs_sem.at[b], zr_sem.at[b], core)
        copy.start()
        save(7, b, m.at[b], m_out.at[b])
        save(8, b, n2.at[at], n2_out.at[at])
        save(9, b, u.at[b], u_out.at[b])
        save(10, b, a.at[at], a_out.at[at])
        copy.wait_recv()
        xout[b] = (m[b, mine] + (zpart[b, mine] + zrecv[b])).astype(BF16)

        @pl.when(s == 0)
        def _():
            remote(xout.at[b], land.at[1, b, mine], ns_sem.at[b], nr_sem.at[b], section).start()

        spot = out_rows.at[y, mine]

        @pl.when(b == t)
        def _():
            pltpu.make_async_copy(xout.at[b], spot, or_sem.at[t]).start()

        @pl.when(b != t)
        def _():
            remote(xout.at[b], spot, os_sem.at[b], or_sem.at[t], (s, b, d)).start()

        return 0

    lax.fori_loop(0, blocks, feed, 0)

    @pl.when(s == 1)
    def _():
        near_rows()
        far_rows()

    for b in range(blocks):
        pltpu.make_async_copy(land.at[0, b], g_out.at[b], save_sem.at[12, b]).start()

    block = land.at[0, t]
    remote(block, block, xs_sem.at[PIECES], xr_sem.at[t], core).wait_send()
    remote(block, block, xfs_sem, xr_sem.at[t], core).wait_send()

    @pl.when(s == 1)
    def _():
        for i in range(PIECES):
            passing_copy(i).wait_send()
            onward(i).wait_send()
            over(i).wait_send()

    for b in range(blocks):
        piece = land.at[0, b, mine]
        remote(ysend.at[b], yrecv.at[b], ys_sem.at[b], yr_sem.at[b], core).wait_send()
        remote(zpart.at[b, theirs], zrecv.at[b], zs_sem.at[b], zr_sem.at[b], core).wait_send()
        here = out_rows.at[b // 2, pl.ds((b % 2) * half, half)]
        remote(here, here, os_sem.at[b], or_sem.at[b], core).wait_recv()

        @pl.when(b != t)
        def _():
            remote(xout.at[b], here, os_sem.at[b], or_sem.at[b], core).wait_send()

        @pl.when(s == 0)
        def _():
            remote(xout.at[b], piece, ns_sem.at[b], nr_sem.at[b], section).wait_send()

        @pl.when(s == 1)
        def _():
            remote(piece, piece, nfs_sem.at[b], nfr_sem.at[b], core).wait_send()

    for i in range(6):
        crossing(i).wait_send()
        beside_copy(i, parity).wait_send()
    for i, (src, dst) in enumerate(weights):
        pltpu.make_async_copy(src, dst, save_sem.at[11, i]).wait()
    for b in range(blocks):
        at = pl.ds(b * rows, rows)
        saved = [
            (land.at[s, b], h_out.at[b]),
            (n1.at[at], n1_out.at[at]),
            (q.at[:, at], q_out.at[:, at]),
            (k.at[:, at], k_out.at[:, at]),
            (v.at[:, at], v_out.at[:, at]),
            (o.at[at], o_out.at[at]),
            (lse.at[b], lse_out.at[b]),
            (m.at[b], m_out.at[b]),
            (n2.at[at], n2_out.at[at]),
            (u.at[b], u_out.at[b]),
            (a.at[at], a_out.at[at]),
        ]
        for kind, (src, dst) in enumerate(saved):
            pltpu.make_async_copy(src, dst, save_sem.at[kind, b]).wait()
        pltpu.make_async_copy(land.at[0, b], g_out.at[b], save_sem.at[12, b]).wait()


def forward(inputs, cotangent, shards, gain_one, gain_two, scale, head):
    _, rows, width = inputs.shape
    local = shards[0].shape[0]
    heads = 2 * local // head
    blocks = lax.axis_size("tensor")
    length = blocks * rows
    half = rows // 2
    shape = jax.ShapeDtypeStruct
    weights = [(2, 3 * local, width), (2 * local, width), (2 * local, width), (2 * local, width)]
    outs = [
        shape(inputs.shape, BF16),
        shape((blocks, rows, width), BF16),
        shape((length, width), BF16),
        shape((heads, length, head), BF16),
        shape((heads, length, head), BF16),
        shape((heads, length, head), BF16),
        shape((length, 2 * local), BF16),
        shape((blocks, heads, rows), F32),
        shape((blocks, rows, width), F32),
        shape((length, width), BF16),
        shape((blocks, rows, 2 * local), F32),
        shape((length, 2 * local), BF16),
        shape((blocks, rows, width), BF16),
    ] + [shape(w, BF16) for w in weights]
    scratch = [pltpu.VMEM((2, blocks, rows, width), BF16)]
    scratch += [pltpu.VMEM(w, BF16) for w in weights]
    scratch += [
        pltpu.VMEM((rows, width), BF16),
        pltpu.VMEM((length, width), BF16),
        pltpu.VMEM((heads, length, head), BF16),
        pltpu.VMEM((heads, length, head), BF16),
        pltpu.VMEM((heads, length, head), BF16),
        pltpu.VMEM((heads, length, head), BF16),
        pltpu.VMEM((length, 2 * local), BF16),
        pltpu.VMEM((blocks, rows, 128), F32),
        pltpu.VMEM((blocks, heads, rows), F32),
        pltpu.VMEM((blocks, rows, width), BF16),
        pltpu.VMEM((blocks, rows, width), BF16),
        pltpu.VMEM((blocks, rows, width), F32),
        pltpu.VMEM((length, width), BF16),
        pltpu.VMEM((blocks, rows, 2 * local), F32),
        pltpu.VMEM((length, 2 * local), BF16),
        pltpu.VMEM((blocks, rows, width), F32),
        pltpu.VMEM((blocks, half, width), F32),
        pltpu.VMEM((blocks, half, width), BF16),
        DMA((6,)),
        DMA((2 * PIECES,)),
        DMA((PIECES,)),
        DMA((PIECES + 1,)),
        DMA((PIECES,)),
        DMA((blocks,)),
        DMA,
        DMA((6,)),
        DMA((6,)),
        DMA((6,)),
        DMA((6,)),
    ]
    scratch += [DMA((blocks,))] * 10 + [DMA((13, blocks))]
    return pl.pallas_call(
        forward_kernel,
        out_shape=outs,
        in_specs=[ANY] * 8 + [VMEM] * 3,
        out_specs=[ANY] * len(outs),
        scratch_shapes=scratch,
        compiler_params=pltpu.CompilerParams(
            collective_id=1, has_side_effects=True, vmem_limit_bytes=62 * MIB
        ),
        name="forward",
    )(inputs, cotangent, *shards, gain_one, gain_two, scale)


def backward_kernel(
    g_in, h_in, q_in, k_in, v_in, o_in, lse_in, m_in, u_in, win_in, wo_in, wu_in, wd_in,
    gain_one, gain_two, scale,
    out_rows, g_out, gu_out, gy_out, gp_out, dg1, dg2, ds,
    g, win, wo, wu, wd, h, q, k, v, o, lse, m, u, gu, gy, gp, ysend, yrecv, gm, go_heads, gq_heads,
    delta, dk, dv, n1part, n1recv, xout,
    load_sem, w_sem, ns_sem, nr_sem, nfs_sem, nfr_sem, ys_sem, yr_sem, zs_sem, zr_sem, os_sem, or_sem,
    save_sem,
):
    s, t, d = lax.axis_index("section"), lax.axis_index("tensor"), lax.axis_index("dp")
    blocks, rows, width = g.shape
    half = rows // 2
    local = wu.shape[0] // 2
    heads, _, head = q.shape
    per = heads // 2
    c, y = lax.rem(t, 2), t // 2
    core = (s, other(t), d)
    across = (s, lax.rem(t + 2, 4), d)
    diagonal = (s, other(lax.rem(t + 2, 4)), d)
    section = (1 - s, t, d)
    mine = pl.ds(pl.multiple_of(c * half, half), half)
    theirs = pl.ds(pl.multiple_of((1 - c) * half, half), half)

    weights = [(wd_in, wd), (wu_in, wu), (wo_in, wo), (win_in, win)]

    def weight(i):
        return pltpu.make_async_copy(*weights[i], w_sem.at[i])

    def load(kind, b):
        at = pl.ds(pl.multiple_of(b * rows, rows), rows)
        src, dst = [
            (u_in.at[b], u.at[b]),
            (m_in.at[b], m.at[b]),
            (o_in.at[at], o.at[at]),
            (q_in.at[:, at], q.at[:, at]),
            (k_in.at[:, at], k.at[:, at]),
            (v_in.at[:, at], v.at[:, at]),
            (lse_in.at[b], lse.at[b]),
            (h_in.at[b, mine], h.at[b]),
        ][kind]
        return pltpu.make_async_copy(src, dst, load_sem.at[kind, b])

    def incoming(b):
        return pltpu.make_async_copy(g_in.at[b], g.at[b], nr_sem.at[b])

    last = blocks - 1

    @pl.when(s == 1)
    def _():
        incoming(last).start()

    weight(0).start()
    load(0, last).start()
    weight(1).start()
    load(1, last).start()
    weight(2).start()
    for kind in range(2, 7):
        load(kind, last).start()
    for b in reversed(range(last)):
        load(4, b).start()
        load(5, b).start()
    weight(3).start()
    load(7, last).start()
    for b in reversed(range(last)):
        for kind in (0, 1, 2, 3, 6, 7):
            load(kind, b).start()

    @pl.when(s == 1)
    def _():
        for b in reversed(range(last)):
            incoming(b).start()

    greet([core, across, diagonal, section])

    dk[...] = jnp.zeros_like(dk)
    dv[...] = jnp.zeros_like(dv)
    dg1[...] = jnp.zeros_like(dg1)
    dg2[...] = jnp.zeros_like(dg2)
    ds[...] = jnp.zeros_like(ds)

    causal = lax.broadcasted_iota(jnp.int32, (rows, rows), 0) <= lax.broadcasted_iota(
        jnp.int32, (rows, rows), 1
    )
    lane = lax.broadcasted_iota(jnp.int32, (rows, 128), 1)

    def save(kind, b, src, dst):
        pltpu.make_async_copy(src, dst, save_sem.at[kind, b]).start()

    def one_block(turn, _):
        b = last - turn
        at = pl.ds(pl.multiple_of(b * rows, rows), rows)

        @pl.when(s == 1)
        def _():
            incoming(b).wait()

        @pl.when(s == 0)
        def _():
            piece = g.at[b, mine]
            remote(piece, piece, ns_sem.at[b], nr_sem.at[b], core).wait_recv()
            remote(piece, piece, nfs_sem.at[b], nfr_sem.at[b], core).start()
            rest = g.at[b, theirs]
            remote(rest, rest, nfs_sem.at[b], nfr_sem.at[b], core).wait_recv()

        @pl.when(turn == 0)
        def _():
            weight(0).wait()
            weight(1).wait()

        load(0, b).wait()
        save(0, b, g.at[b], g_out.at[at])
        grad = g[b]
        grad_act = by_last(grad, wd[...])
        up = u[b]
        sigma = 1.0 / (1.0 + jnp.exp(-up))
        grad_up = (grad_act * sigma * (1.0 + up * (1.0 - sigma))).astype(BF16)
        gu[at] = grad_up
        save(1, b, gu.at[at], gu_out.at[at])
        ysend[b] = plain(grad_up, wu[...]).astype(BF16)
        copy = remote(ysend.at[b], yrecv.at[b], ys_sem.at[b], yr_sem.at[b], core)
        copy.start()
        load(1, b).wait()

        @pl.when(turn == 0)
        def _():
            weight(2).wait()
            weight(3).wait()
            for bb in range(blocks):
                load(4, bb).wait()
                load(5, bb).wait()

        for kind in (2, 3, 6, 7):
            load(kind, b).wait()
        copy.wait_recv()
        grad_normed = ysend[b].astype(F32) + yrecv[b].astype(F32)
        middle = m[b]
        inverse = inverse_rms(middle)
        unit = middle * inverse
        grad_unit = grad_normed * gain_two[...]
        dg2[...] += jnp.sum(grad_normed * unit, axis=0, keepdims=True)
        grad_middle = grad.astype(F32) + inverse * (
            grad_unit - unit * jnp.mean(grad_unit * unit, axis=1, keepdims=True)
        )
        gm[...] = grad_middle
        grad_mid = grad_middle.astype(BF16)
        gy[at] = grad_mid
        save(2, b, gy.at[at], gy_out.at[at])
        grad_mixed = by_last(grad_mid, wo[...]).astype(BF16)
        both = grad_mixed.astype(F32) * o[at].astype(F32)
        found = jnp.zeros((rows, 128), F32)
        for i in range(heads):
            cut = slice(i * head, (i + 1) * head)
            go_heads[i] = grad_mixed[:, cut]
            found = jnp.where(lane == i, jnp.sum(both[:, cut], axis=1, keepdims=True), found)
        delta[...] = jnp.transpose(found)[:heads]
        for bb in range(blocks):

            @pl.when(b == bb)
            def _():
                def group(first, _):
                    for j in range(per):
                        i = first * per + j
                        qh = q[i, bb * rows : (bb + 1) * rows]
                        gh = go_heads[i]
                        offset = lse[bb, pl.ds(i, 1)]
                        inner = delta[pl.ds(i, 1)]
                        total = None
                        for lo, hi in ((bb * rows, (bb + 1) * rows), (0, bb * rows)):
                            if lo == hi:
                                continue
                            kj = k[i, lo:hi]
                            weight = jnp.exp(by_last(kj, qh) - offset)
                            if lo == bb * rows and hi > lo and hi == (bb + 1) * rows:
                                weight = jnp.where(causal, weight, 0.0)
                            grad_score = weight * (by_last(v[i, lo:hi], gh) - inner)
                            grad_score = grad_score.astype(BF16)
                            dv[i, lo:hi] += plain(weight.astype(BF16), gh)
                            dk[i, lo:hi] += plain(grad_score, qh)
                            part = by_first(kj, grad_score)
                            total = part if total is None else total + part
                        gq_heads[i] = jnp.transpose(total)
                    return 0

                lax.fori_loop(0, 2, group, 0)

        for j in range(2):
            mine_heads = range(j * per, (j + 1) * per)
            grad_scaled = jnp.concatenate([gq_heads[i] for i in mine_heads], axis=1)
            queries = jnp.concatenate([q[i, at] for i in mine_heads], axis=1).astype(F32)
            ds[pl.ds(j, 1)] += jnp.sum(grad_scaled * queries, axis=0, keepdims=True)
            grads = [
                (grad_scaled * scale[...]).astype(BF16),
                jnp.concatenate([dk[i, at] for i in mine_heads], axis=1).astype(BF16),
                jnp.concatenate([dv[i, at] for i in mine_heads], axis=1).astype(BF16),
            ]
            gp[j, at] = jnp.concatenate(grads, axis=1)
        save(3, b, gp.at[:, at], gp_out.at[:, at])
        n1part[...] = plain(gp[0, at], win[0]) + plain(gp[1, at], win[1])
        copy = remote(n1part.at[theirs], n1recv.at[b], zs_sem.at[b], zr_sem.at[b], core)
        copy.start()
        hidden = h[b].astype(F32)
        inverse = inverse_rms(hidden)
        unit = hidden * inverse
        copy.wait_recv()
        grad_normed = n1part[mine] + n1recv[b]
        grad_unit = grad_normed * gain_one[...]
        dg1[...] += jnp.sum(grad_normed * unit, axis=0, keepdims=True)
        xout[b] = (
            gm[mine]
            + inverse * (grad_unit - unit * jnp.mean(grad_unit * unit, axis=1, keepdims=True))
        ).astype(BF16)

        @pl.when(s == 1)
        def _():
            remote(xout.at[b], g.at[b, mine], ns_sem.at[b], nr_sem.at[b], section).start()

        spot = out_rows.at[y, mine]

        @pl.when(b == t)
        def _():
            pltpu.make_async_copy(xout.at[b], spot, or_sem.at[t]).start()

        @pl.when(b != t)
        def _():
            remote(xout.at[b], spot, os_sem.at[b], or_sem.at[t], (s, b, d)).start()

        copy.wait_send()
        return 0

    lax.fori_loop(0, blocks, one_block, 0)

    for b in range(blocks):
        at = pl.ds(b * rows, rows)
        piece = g.at[b, mine]
        remote(ysend.at[b], yrecv.at[b], ys_sem.at[b], yr_sem.at[b], core).wait_send()
        here = out_rows.at[b // 2, pl.ds((b % 2) * half, half)]
        remote(here, here, os_sem.at[b], or_sem.at[b], core).wait_recv()

        @pl.when(b != t)
        def _():
            remote(xout.at[b], here, os_sem.at[b], or_sem.at[b], core).wait_send()

        @pl.when(s == 1)
        def _():
            remote(xout.at[b], piece, ns_sem.at[b], nr_sem.at[b], section).wait_send()

        @pl.when(s == 0)
        def _():
            remote(piece, piece, nfs_sem.at[b], nfr_sem.at[b], core).wait_send()

        saved = [
            (g.at[b], g_out.at[at]),
            (gu.at[at], gu_out.at[at]),
            (gy.at[at], gy_out.at[at]),
            (gp.at[:, at], gp_out.at[:, at]),
        ]
        for kind, (src, dst) in enumerate(saved):
            pltpu.make_async_copy(src, dst, save_sem.at[kind, b]).wait()


def backward(saved, gain_one, gain_two, scale):
    g_in, h_in, q_in = saved[:3]
    win_in, wo_in, wu_in, wd_in = saved[9:]
    blocks, rows, width = g_in.shape
    heads, length, head = q_in.shape
    local = wu_in.shape[0] // 2
    half = rows // 2
    shape = jax.ShapeDtypeStruct
    outs = [
        shape((2, rows, width), BF16),
        shape((length, width), BF16),
        shape((length, 2 * local), BF16),
        shape((length, width), BF16),
        shape((2, length, 3 * local), BF16),
        shape((1, width), F32),
        shape((1, width), F32),
        shape((2, local), F32),
    ]
    scratch = [
        pltpu.VMEM((blocks, rows, width), BF16),
        pltpu.VMEM(win_in.shape, BF16),
        pltpu.VMEM(wo_in.shape, BF16),
        pltpu.VMEM(wu_in.shape, BF16),
        pltpu.VMEM(wd_in.shape, BF16),
        pltpu.VMEM((blocks, half, width), BF16),
        pltpu.VMEM((heads, length, head), BF16),
        pltpu.VMEM((heads, length, head), BF16),
        pltpu.VMEM((heads, length, head), BF16),
        pltpu.VMEM((length, 2 * local), BF16),
        pltpu.VMEM((blocks, heads, rows), F32),
        pltpu.VMEM((blocks, rows, width), F32),
        pltpu.VMEM((blocks, rows, 2 * local), F32),
        pltpu.VMEM((length, 2 * local), BF16),
        pltpu.VMEM((length, width), BF16),
        pltpu.VMEM((2, length, 3 * local), BF16),
        pltpu.VMEM((blocks, rows, width), BF16),
        pltpu.VMEM((blocks, rows, width), BF16),
        pltpu.VMEM((rows, width), F32),
        pltpu.VMEM((heads, rows, head), BF16),
        pltpu.VMEM((heads, rows, head), F32),
        pltpu.VMEM((heads, rows), F32),
        pltpu.VMEM((heads, length, head), F32),
        pltpu.VMEM((heads, length, head), F32),
        pltpu.VMEM((rows, width), F32),
        pltpu.VMEM((blocks, half, width), F32),
        pltpu.VMEM((blocks, half, width), BF16),
        DMA((8, blocks)),
        DMA((4,)),
    ]
    scratch += [DMA((blocks,))] * 10 + [DMA((4, blocks))]
    return pl.pallas_call(
        backward_kernel,
        out_shape=outs,
        in_specs=[ANY] * 13 + [VMEM] * 3,
        out_specs=[ANY] * 5 + [VMEM] * 3,
        scratch_shapes=scratch,
        compiler_params=pltpu.CompilerParams(
            collective_id=2, has_side_effects=True, vmem_limit_bytes=62 * MIB
        ),
        name="backward",
    )(*saved, gain_one, gain_two, scale)


def farthest_first(d, k, n):
    found = 0
    for i in range(n):
        above = list(range(n - 1, i, -1))
        below = list(range(i))
        first, second = (above, below) if len(above) >= len(below) else (below, above)
        lead = len(first) - len(second) - 1
        order = first[: max(lead, 0)]
        rest = first[max(lead, 0) :]
        for j in range(max(len(rest), len(second))):
            order += rest[j : j + 1] + second[j : j + 1]
        order.append(i)
        picked = 0
        for j, e in enumerate(order):
            picked = picked + jnp.where(k == j, e, 0)
        found = found + jnp.where(d == i, picked, 0)
    return found


def gradient_kernel(
    n1_in, n2_in, gy_in, g_in, gp_in, gu_in, o_in, a_in, small,
    out, small_out,
    x, xt, gp, gu, o, a, keep, give, yrecv, flow, last, keep_d, give_d, flow_k, flow_g, last_k, last_g,
    yd, smalls, chain,
    x_sem, g_sem, ys_sem, yr_sem, fs_sem, fr_sem, last_sem, ks_sem, kr_sem, gs_sem, gr_sem, last_d_sem,
    yds_sem, ydr_sem, ss_sem, sr_sem, cs_sem, cr_sem,
):
    s, t, d = lax.axis_index("section"), lax.axis_index("tensor"), lax.axis_index("dp")
    n, chunk, wide = keep.shape
    local = keep_d.shape[2]
    pieces = ys_sem.shape[1]
    step = chunk // pieces
    core = (s, other(t), d)
    across = (s, lax.rem(t + 2, 4), d)
    diagonal = (s, other(lax.rem(t + 2, 4)), d)
    up = (s, t, lax.rem(d + 1, n))
    down = (s, t, lax.rem(d + n - 1, n))

    def load(i, source):
        return pltpu.make_async_copy(source, x.at[i % 2], x_sem.at[i])

    sources = [g_in, n1_in, n2_in, gy_in]
    load(0, g_in).start()
    operands = [(a_in, a), (gp_in, gp), (gu_in, gu), (o_in, o)]
    pltpu.make_async_copy(a_in, a, g_sem.at[0]).start()
    load(1, n1_in).start()
    for i in range(1, 4):
        pltpu.make_async_copy(operands[i][0], operands[i][1], g_sem.at[i]).start()

    greet([core, across, diagonal, up, down])

    partners = [core, across, diagonal]

    def share(i):
        return remote(small, smalls.at[i], ss_sem.at[i], sr_sem.at[i], partners[i])

    for i in range(3):
        share(i).start()

    def turn(i):
        load(i, sources[i]).wait()
        turned = jnp.transpose(x[i % 2])
        for e in range(n):
            xt[i, e] = turned[e * chunk : (e + 1) * chunk]
        if i + 2 < 4:
            load(i + 2, sources[i + 2]).start()

    def flow_piece(buffer, into, e, send, receive, device):
        return remote(buffer.at[e], into.at[e], send.at[e], receive.at[e], device)

    turn(0)
    pltpu.make_async_copy(a_in, a, g_sem.at[0]).wait()

    def down_product(e, _):
        both = plain(xt[0, e], a[...])
        keep_d[e] = both[:, :local].astype(BF16)
        give_d[e] = both[:, local:].astype(BF16)
        return 0

    lax.fori_loop(0, n, down_product, 0)

    line_d = [(keep_d, flow_k, last_k, ks_sem, kr_sem, 0), (give_d, flow_g, last_g, gs_sem, gr_sem, 1)]

    def upstream_d(e, buffer, into, send, receive):
        piece = into.at[e]
        remote(piece, piece, send.at[e], receive.at[e], up).wait_recv()
        buffer[e] = (buffer[e].astype(F32) + into[e].astype(F32)).astype(BF16)

    def send_d(e, buffer, into, spare, send, receive, i):
        @pl.when(e > d)
        def _():
            remote(buffer.at[e], into.at[e], send.at[e], receive.at[e], up).start()

        @pl.when(e < d - 1)
        def _():
            remote(buffer.at[e], into.at[e], send.at[e], receive.at[e], down).start()

        @pl.when(e == d - 1)
        def _():
            remote(buffer.at[e], spare, send.at[e], last_d_sem.at[i], down).start()

    def ends(k, _):
        e = farthest_first(d, k, n)
        for buffer, into, spare, send, receive, i in line_d:

            @pl.when(((d == 0) | (d == n - 1)) & (e != d))
            def _():
                send_d(e, buffer, into, spare, send, receive, i)

        return 0

    lax.fori_loop(0, n, ends, 0)

    turn(1)
    turn(2)
    turn(3)
    for i in range(1, 4):
        pltpu.make_async_copy(operands[i][0], operands[i][1], g_sem.at[i]).wait()

    def exchange(e, i):
        rows = pl.ds(i * step, step)
        return remote(
            give.at[e, rows], yrecv.at[e, rows], ys_sem.at[e, i], yr_sem.at[e, i], across
        )

    def products(k, _):
        e = farthest_first(d, k, n)
        ups = plain(xt[2, e], gu[...])
        outs = plain(xt[3, e], o[...])
        for j, target in ((1, give), (0, keep)):
            cut = slice(j * local, (j + 1) * local)
            target[e] = jnp.concatenate(
                [
                    plain(xt[1, e], gp[j]).astype(BF16),
                    ups[:, cut].astype(BF16),
                    outs[:, cut].astype(BF16),
                ],
                axis=1,
            )
            if j:
                for i in range(pieces):
                    exchange(e, i).start()
        return 0

    lax.fori_loop(0, n, products, 0)

    for i in range(3):
        share(i).wait_recv()
    mine = small[...] + smalls[0] + (smalls[1] + smalls[2])
    small_out[...] = mine

    def link(i, device):
        return remote(chain.at[i], chain.at[2 + i], cs_sem.at[i], cr_sem.at[i], device)

    for i, first, final, device in ((0, d == 0, d == n - 1, up), (1, d == n - 1, d == 0, down)):
        chain[i] = mine

        @pl.when(jnp.logical_not(first))
        def _():
            link(i, device).wait_recv()
            chain[i] = mine + chain[2 + i]
            small_out[...] += chain[2 + i]

        @pl.when(jnp.logical_not(final))
        def _():
            link(i, device).start()

    def middle(k, _):
        e = farthest_first(d, k, n)
        for buffer, into, spare, send, receive, i in line_d:

            @pl.when((d > 0) & (d < n - 1) & (e != d))
            def _():
                upstream_d(e, buffer, into, send, receive)
                send_d(e, buffer, into, spare, send, receive, i)

        return 0

    lax.fori_loop(0, n, middle, 0)

    def flows(k, _):
        e = farthest_first(d, k, n)
        for i in range(pieces):
            at = pl.ds(i * step, step)

            first = ((e > d) & (d == 0)) | ((e < d) & (d == n - 1))

            @pl.when(e != d)
            def _():
                exchange(e, i).wait_recv()

            @pl.when((e != d) & first)
            def _():
                keep[e, at] = (keep[e, at].astype(F32) + yrecv[e, at].astype(F32)).astype(BF16)

            @pl.when((e != d) & jnp.logical_not(first))
            def _():
                piece = flow.at[e, at]
                remote(piece, piece, fs_sem.at[e, i], fr_sem.at[e, i], up).wait_recv()
                total = keep[e, at].astype(F32) + yrecv[e, at].astype(F32)
                keep[e, at] = (total + flow[e, at].astype(F32)).astype(BF16)

            src = keep.at[e, at]

            @pl.when(e > d)
            def _():
                remote(src, flow.at[e, at], fs_sem.at[e, i], fr_sem.at[e, i], up).start()

            @pl.when(e < d - 1)
            def _():
                remote(src, flow.at[e, at], fs_sem.at[e, i], fr_sem.at[e, i], down).start()

            @pl.when(e == d - 1)
            def _():
                remote(src, last.at[at], fs_sem.at[e, i], last_sem.at[i], down).start()

        return 0

    lax.fori_loop(0, n, flows, 0)

    for buffer, into, spare, send, receive, i in line_d:

        @pl.when(d > 0)
        def _():
            upstream_d(d, buffer, into, send, receive)

        @pl.when(d < n - 1)
        def _():
            remote(spare, spare, send.at[0], last_d_sem.at[i], down).wait_recv()
            buffer[d] = (buffer[d].astype(F32) + spare[...].astype(F32)).astype(BF16)

    crossing = remote(give_d.at[d], yd, yds_sem, ydr_sem, across)
    crossing.start()
    for i in range(pieces):
        at = pl.ds(i * step, step)
        exchange(d, i).wait_recv()
        out[at, :wide] = keep[d, at].astype(F32) + yrecv[d, at].astype(F32)

        @pl.when(d > 0)
        def _():
            piece = flow.at[d, at]
            remote(piece, piece, fs_sem.at[d, i], fr_sem.at[d, i], up).wait_recv()
            out[at, :wide] += flow[d, at].astype(F32)

        @pl.when(d < n - 1)
        def _():
            piece = last.at[at]
            remote(piece, piece, fs_sem.at[d, i], last_sem.at[i], down).wait_recv()
            out[at, :wide] += last[at].astype(F32)

    crossing.wait_recv()
    out[:, wide:] = keep_d[d].astype(F32) + yd[...].astype(F32)

    crossing.wait_send()
    for i in range(3):
        share(i).wait_send()

    @pl.when(d < n - 1)
    def _():
        link(0, up).wait_send()

    @pl.when(d > 0)
    def _():
        link(1, down).wait_send()

    def drain(e, _):
        for i in range(pieces):
            exchange(e, i).wait_send()

        @pl.when(e != d)
        def _():
            for i in range(pieces):
                piece = keep.at[e, pl.ds(i * step, step)]
                remote(piece, piece, fs_sem.at[e, i], fr_sem.at[e, i], up).wait_send()
            for buffer, into, spare, send, receive, i in line_d:
                remote(buffer.at[e], buffer.at[e], send.at[e], receive.at[e], up).wait_send()

        return 0

    lax.fori_loop(0, n, drain, 0)


def gradients(n1, n2, gy, g, gp, gu, o, a, small):
    n = lax.axis_size("dp")
    length, width = n1.shape
    local = gp.shape[2] // 3
    chunk = width // n
    wide = 5 * local
    pieces = 4 if chunk % 64 == 0 else 1
    big = pltpu.VMEM((n, chunk, wide), BF16)
    line = pltpu.VMEM((n, chunk, local), BF16)
    return pl.pallas_call(
        gradient_kernel,
        out_shape=[
            jax.ShapeDtypeStruct((chunk, 6 * local), F32),
            jax.ShapeDtypeStruct(small.shape, F32),
        ],
        in_specs=[ANY] * 8 + [VMEM],
        out_specs=[VMEM, VMEM],
        scratch_shapes=[
            pltpu.VMEM((2, length, width), BF16),
            pltpu.VMEM((4, n, chunk, length), BF16),
            pltpu.VMEM(gp.shape, BF16),
            pltpu.VMEM(gu.shape, BF16),
            pltpu.VMEM(o.shape, BF16),
            pltpu.VMEM(a.shape, BF16),
            big,
            big,
            big,
            big,
            pltpu.VMEM((chunk, wide), BF16),
            line,
            line,
            line,
            line,
            pltpu.VMEM((chunk, local), BF16),
            pltpu.VMEM((chunk, local), BF16),
            pltpu.VMEM((chunk, local), BF16),
            pltpu.VMEM((3,) + small.shape, F32),
            pltpu.VMEM((4,) + small.shape, F32),
            DMA((4,)),
            DMA((4,)),
            DMA((n, pieces)),
            DMA((n, pieces)),
            DMA((n, pieces)),
            DMA((n, pieces)),
            DMA((pieces,)),
            DMA((n,)),
            DMA((n,)),
            DMA((n,)),
            DMA((n,)),
            DMA((2,)),
            DMA,
            DMA,
            DMA((3,)),
            DMA((3,)),
            DMA((2,)),
            DMA((2,)),
        ],
        compiler_params=pltpu.CompilerParams(
            collective_id=3, has_side_effects=True, vmem_limit_bytes=62 * MIB
        ),
        name="gradients",
    )(n1, n2, gy, g, gp, gu, o, a, small)


def body(
    inputs, cotangent, gain_attn, w_query, w_key, w_value, w_out, dim_scale, gain_mlp, w_up, w_down
):
    local = w_query.shape[2]
    head = dim_scale.shape[1]
    width = inputs.shape[2]
    shards = (w_query[0].T, w_key[0].T, w_value[0].T, w_out[0], w_up[0].T, w_down[0])
    multiplier = LOG2E / math.sqrt(head)
    per_dim = multiplier * jax.nn.softplus(dim_scale)
    done = forward(
        inputs, cotangent, shards, gain_attn, gain_mlp, per_dim, head
    )
    layer_out, h, n1, q, k, v, o, lse, m, n2, u, a, g, win, wo, wu, wd = done
    input_grads, g_all, gu, gy, gp, dg1, dg2, ds = backward(
        (g, h, q, k, v, o, lse, m, u, win, wo, wu, wd),
        gain_attn,
        gain_mlp,
        jnp.tile(per_dim, (1, local // head)),
    )

    first_core = lax.rem(lax.axis_index("tensor"), 2) == 0
    dg2 = jnp.where(first_core, dg2, 0.0)
    small = jnp.concatenate([dg1, dg2, ds.reshape(1, -1)], axis=1)
    grads, small = gradients(n1, n2, gy, g_all, gp, gu, o, a, small)
    dg1, dg2 = small[:, :width], small[:, width : 2 * width]
    ds = jnp.sum(small[:, 2 * width :].reshape(-1, head), axis=0, keepdims=True)
    grad_scale = ds / per_dim * multiplier * jax.nn.sigmoid(dim_scale)
    pieces = [grads[:, i * local : (i + 1) * local] for i in range(6)]
    return (
        layer_out[None],
        input_grads[None],
        dg1,
        pieces[0][None],
        pieces[1][None],
        pieces[2][None],
        pieces[4].T[None],
        grad_scale,
        dg2,
        pieces[3][None],
        pieces[5].T[None],
    )


def solution(mesh):
    in_specs = (
        P("dp", "tensor", None),
        P("dp", "tensor", None),
        P("section", None),
        P("section", None, "tensor"),
        P("section", None, "tensor"),
        P("section", None, "tensor"),
        P("section", "tensor", None),
        P("section", None),
        P("section", None),
        P("section", None, "tensor"),
        P("section", "tensor", None),
    )
    out_specs = (
        P("section", "dp", "tensor", None),
        P("section", "dp", "tensor", None),
        P("section", None),
        P("section", "dp", "tensor"),
        P("section", "dp", "tensor"),
        P("section", "dp", "tensor"),
        P("section", "tensor", "dp"),
        P("section", None),
        P("section", None),
        P("section", "dp", "tensor"),
        P("section", "tensor", "dp"),
    )
    return jax.shard_map(body, mesh=mesh, in_specs=in_specs, out_specs=out_specs, check_vma=False)
```

```python
import functools
import math

import jax
import jax.numpy as jnp
from jax import lax
from jax.experimental import pallas as pl
from jax.experimental.pallas import tpu as pltpu
from jax.sharding import PartitionSpec as P

EPS = 1e-06
LOG2E = 1.442695041
NEGATIVE = -1e30
BF16 = jnp.bfloat16
F32 = jnp.float32
MESH = pl.DeviceIdType.MESH
ANY = pl.BlockSpec(memory_space=pl.ANY)
VMEM = pl.BlockSpec(memory_space=pltpu.VMEM)
DMA = pltpu.SemaphoreType.DMA
MIB = 1 << 20
PIECES = 4


def plain(a, b):
    return jnp.dot(a, b, preferred_element_type=F32)


def by_last(a, b):
    return lax.dot_general(a, b, (((1,), (1,)), ((), ())), preferred_element_type=F32)


def by_first(a, b):
    return lax.dot_general(a, b, (((0,), (0,)), ((), ())), preferred_element_type=F32)


def other(index):
    return index + 1 - 2 * lax.rem(index, 2)


def remote(src, dst, send, receive, device):
    return pltpu.make_async_remote_copy(
        src_ref=src,
        dst_ref=dst,
        send_sem=send,
        recv_sem=receive,
        device_id=device,
        device_id_type=MESH,
    )


def greet(devices):
    barrier = pltpu.get_barrier_semaphore()
    for device in devices:
        pl.semaphore_signal(barrier, inc=1, device_id=device, device_id_type=MESH)
    pl.semaphore_wait(barrier, len(devices))


def per_dim(raw):
    grown = jnp.maximum(raw, 0.0) + jnp.log(1.0 + jnp.exp(-jnp.abs(raw)))
    return (LOG2E / math.sqrt(raw.shape[1])) * grown


def inverse_rms(rows):
    return lax.rsqrt(jnp.mean(rows * rows, axis=1, keepdims=True) + EPS)


def forward_kernel(
    inputs, cotangent, w_q, w_k, w_v, w_o, w_u, w_d, gain_one, gain_two, scale,
    x_out, h_out, n1_out, q_out, k_out, v_out, o_out, lse_out, m_out, n2_out, u_out, a_out,
    g_out, win_out, wo_out, wu_out, wd_out,
    land, win, wo, wu, wd, passing, down_a, down_b, n1, q, k, v, o_heads, o, lse_cols, lse, ysend, yrecv,
    m, n2, u, a, zpart, zrecv, xout,
    own_sem, ps_sem, pr_sem, xs_sem, xp_sem, xr_sem, xfs_sem, wys_sem, wyr_sem, wzs_sem, wzr_sem,
    das_sem, dar_sem, dbs_sem, dbr_sem, dcs_sem, dcr_sem,
    ns_sem, nr_sem, nfs_sem, nfr_sem, ys_sem, yr_sem, zs_sem, zr_sem, save_sem,
):
    s, t, d = lax.axis_index("section"), lax.axis_index("tensor"), lax.axis_index("dp")
    blocks, rows, width = land.shape[1:]
    half = rows // 2
    local = w_o.shape[0]
    heads, _, head = q.shape
    per = heads // 2
    c, y = lax.rem(t, 2), t // 2
    t_core, t_across = other(t), lax.rem(t + 2, 4)
    t_diagonal = other(t_across)
    core = (s, t_core, d)
    across = (s, t_across, d)
    diagonal = (s, t_diagonal, d)
    beside = (s, t, other(d))
    section = (1 - s, t, d)
    greet([core, across, diagonal, beside, section])

    mine = pl.ds(pl.multiple_of(c * half, half), half)
    theirs = pl.ds(pl.multiple_of((1 - c) * half, half), half)

    shards = [w_q, w_k, w_v, w_o, w_u, w_d]

    def place(i, slot, start, size):
        if i < 3:
            return win.at[slot, pl.ds(pl.multiple_of(i * local + start, 16), size)]
        return (wo, wu, wd)[i - 3].at[pl.ds(pl.multiple_of(slot * local + start, 16), size)]

    short = local // 4
    parity = lax.rem(d, 2)

    def own(i):
        return pltpu.make_async_copy(shards[i], place(i, 0, 0, local), own_sem.at[i])

    def strip(i, which):
        return pl.multiple_of(which * 2 * short + i % 2 * short, 16)

    def crossing(i):
        start = strip(i, parity)
        dst = place(i // 2, 1, start, short)
        return remote(
            shards[i // 2].at[pl.ds(start, short)], dst, wys_sem.at[i], wyr_sem.at[i], across
        )

    def beside_copy(i, which):
        piece = place(i // 2, 1, strip(i, which), short)
        return remote(piece, piece, wzs_sem.at[i], wzr_sem.at[i], beside)

    def relay(i):
        crossing(i).wait_recv()
        beside_copy(i, parity).start()

    def arrived(i):
        beside_copy(i, 1 - parity).wait_recv()

    quarter = local // PIECES

    def down_piece(buffer, i):
        return buffer.at[pl.ds(i * quarter, quarter)]

    def down_first(i):
        return remote(
            down_piece(w_d, i), down_piece(down_a, i), das_sem.at[i], dar_sem.at[i], section
        )

    def down_second(i):
        return remote(
            down_piece(down_a, i), down_piece(down_b, i), dbs_sem.at[i], dbr_sem.at[i], across
        )

    def down_third(i):
        return remote(
            down_piece(down_b, i), wd.at[pl.ds(local + i * quarter, quarter)],
            dcs_sem.at[i], dcr_sem.at[i], section,
        )

    step = rows // PIECES

    def passing_copy(i):
        piece = pl.ds(i * step, step)
        return remote(
            inputs.at[1 - y, piece], passing.at[piece], ps_sem.at[i], pr_sem.at[i], across
        )

    def onward(i):
        piece = pl.ds(i * step, step)
        return remote(
            passing.at[piece], land.at[0, t_across, piece], ps_sem.at[PIECES + i], xp_sem.at[i], section
        )

    def over(i):
        piece = pl.ds(i * step, step)
        return remote(
            cotangent.at[1 - y, piece], land.at[0, t, piece], xs_sem.at[i], xp_sem.at[i], across
        )

    def local_rows(source):
        pltpu.make_async_copy(source.at[y], land.at[0, t], xr_sem.at[t]).start()
        remote(source.at[y], land.at[0, t], xs_sem.at[PIECES], xr_sem.at[t], core).start()

    def block_wait(b):
        piece = land.at[0, b]
        remote(piece, piece, xs_sem.at[PIECES], xr_sem.at[b], core).wait_recv()

    def far_rows():
        for i in range(PIECES):
            piece = land.at[0, t_across, pl.ds(i * step, step)]
            remote(piece, piece, xfs_sem, xp_sem.at[i], core).wait_recv()
        piece = land.at[0, t_across]
        remote(piece, piece, xfs_sem, xr_sem.at[t_across], core).start()
        block_wait(t_diagonal)

    def near_rows():
        block_wait(t)
        block_wait(t_core)

    for i in range(3):
        own(i).start()

    @pl.when(s == 0)
    def _():
        for i in range(10):
            crossing(i).start()
        local_rows(inputs)
        for i in range(PIECES):
            down_first(i).start()

    @pl.when(s == 1)
    def _():
        for i in range(PIECES):
            passing_copy(i).start()
        local_rows(cotangent)

    for i in range(3, 6):
        own(i).start()

    @pl.when(s == 1)
    def _():
        for i in range(PIECES):
            passing_copy(i).wait_recv()
            onward(i).start()
            down_first(i).wait_recv()
            down_second(i).start()
        for i in range(12):
            crossing(i).start()
        for i in range(PIECES):
            over(i).start()
        for i in range(PIECES):
            down_second(i).wait_recv()
            down_third(i).start()
        for i in range(6):
            relay(i)

    for i in range(3):
        own(i).wait()

    def save(kind, b, src, dst):
        pltpu.make_async_copy(src, dst, save_sem.at[kind, b]).start()

    causal = lax.broadcasted_iota(jnp.int32, (rows, rows), 0) >= lax.broadcasted_iota(
        jnp.int32, (rows, rows), 1
    )
    lane = lax.broadcasted_iota(jnp.int32, (rows, 128), 1)

    factor = per_dim(scale[...])

    def attention(turn, _):
        b = jnp.where(s == 0, lax.rem(turn, blocks), turn // 2)
        j = jnp.where(s == 0, turn // blocks, lax.rem(turn, 2))
        at = pl.ds(pl.multiple_of(b * rows, rows), rows)

        @pl.when((s == 0) & (turn == 0))
        def _():
            near_rows()

        @pl.when((s == 0) & (turn == 2 * (1 - y)))
        def _():
            for i in range(4):
                relay(i)
            far_rows()

        @pl.when((s == 0) & (turn == blocks))
        def _():
            relay(6)
            relay(7)
            for i in range(6):
                arrived(i)

        @pl.when((s == 1) & (turn == 0))
        def _():
            for i in range(6):
                arrived(i)

        @pl.when((s == 1) & (j == 0))
        def _():
            piece = land.at[1, b, mine]
            remote(piece, piece, ns_sem.at[b], nr_sem.at[b], core).wait_recv()
            remote(piece, piece, nfs_sem.at[b], nfr_sem.at[b], core).start()
            rest = land.at[1, b, theirs]
            remote(rest, rest, nfs_sem.at[b], nfr_sem.at[b], core).wait_recv()

        @pl.when(j == 0)
        def _():
            hidden = land[s, b].astype(F32)
            n1[at] = (hidden * inverse_rms(hidden) * gain_one[...]).astype(BF16)
            lse_cols[b] = jnp.zeros(lse_cols.shape[1:], F32)
            save(0, b, land.at[s, b], h_out.at[b])
            save(1, b, n1.at[at], n1_out.at[at])

        projected = by_last(n1[at], win[j])
        first = j * per
        for i in range(per):
            cut = i * head
            q[first + i, at] = (projected[:, cut : cut + head] * factor).astype(BF16)
            cut += local
            k[first + i, at] = projected[:, cut : cut + head].astype(BF16)
            cut += local
            v[first + i, at] = projected[:, cut : cut + head].astype(BF16)
        for bb in range(blocks):

            @pl.when(b == bb)
            def _():
                for i in range(per):
                    hd = first + i
                    qh = q[hd, bb * rows : (bb + 1) * rows]
                    near = by_last(qh, k[hd, bb * rows : (bb + 1) * rows])
                    near = jnp.where(causal, near, NEGATIVE)
                    top = jnp.max(near, axis=1, keepdims=True)
                    if bb:
                        far = by_last(qh, k[hd, : bb * rows])
                        top = jnp.maximum(top, jnp.max(far, axis=1, keepdims=True))
                    near = jnp.exp(near - top)
                    total = jnp.sum(near, axis=1, keepdims=True)
                    mixed = plain(near.astype(BF16), v[hd, bb * rows : (bb + 1) * rows])
                    if bb:
                        far = jnp.exp(far - top)
                        total = total + jnp.sum(far, axis=1, keepdims=True)
                        mixed = mixed + plain(far.astype(BF16), v[hd, : bb * rows])
                    o_heads[hd, bb * rows : (bb + 1) * rows] = (mixed / total).astype(BF16)
                    lse_cols[bb] = jnp.where(lane == hd, top + jnp.log(total), lse_cols[bb])

        @pl.when(j == 1)
        def _():
            o[at] = jnp.concatenate([o_heads[i, at] for i in range(heads)], axis=1)
            lse[b] = jnp.transpose(lse_cols[b])[:heads]
            save(2, b, q.at[:, at], q_out.at[:, at])
            save(3, b, k.at[:, at], k_out.at[:, at])
            save(4, b, v.at[:, at], v_out.at[:, at])
            save(5, b, o.at[at], o_out.at[at])
            save(6, b, lse.at[b], lse_out.at[b])

        for i, when in ((4, 2), (5, 3), (8, 4), (9, 5)):

            @pl.when((s == 0) & (turn == when))
            def _():
                relay(i)

        for i in range(6):

            @pl.when((s == 1) & (turn == i))
            def _():
                relay(6 + i)

        return 0

    lax.fori_loop(0, 2 * blocks, attention, 0)

    own(3).wait()
    arrived(6)
    arrived(7)

    def project(b, _):
        at = pl.ds(pl.multiple_of(b * rows, rows), rows)
        ysend[b] = plain(o[at], wo[...]).astype(BF16)
        remote(ysend.at[b], yrecv.at[b], ys_sem.at[b], yr_sem.at[b], core).start()
        return 0

    lax.fori_loop(0, blocks, project, 0)

    own(4).wait()
    own(5).wait()
    arrived(8)
    arrived(9)

    @pl.when(s == 0)
    def _():
        for i in range(PIECES):
            down_third(i).wait_recv()

    @pl.when(s == 1)
    def _():
        arrived(10)
        arrived(11)

    weights = [(win, win_out), (wo, wo_out), (wu, wu_out), (wd, wd_out)]
    for i, (src, dst) in enumerate(weights):
        save(11, i, src, dst)

    def feed(b, _):
        at = pl.ds(pl.multiple_of(b * rows, rows), rows)
        remote(ysend.at[b], yrecv.at[b], ys_sem.at[b], yr_sem.at[b], core).wait_recv()
        middle = land[s, b].astype(F32) + (ysend[b].astype(F32) + yrecv[b].astype(F32))
        m[b] = middle
        normed = (middle * inverse_rms(middle) * gain_two[...]).astype(BF16)
        n2[at] = normed
        up = by_last(normed, wu[...])
        u[b] = up
        active = (up / (1.0 + jnp.exp(-up))).astype(BF16)
        a[at] = active
        zpart[b] = plain(active, wd[...])
        copy = remote(zpart.at[b, theirs], zrecv.at[b], zs_sem.at[b], zr_sem.at[b], core)
        copy.start()
        save(7, b, m.at[b], m_out.at[b])
        save(8, b, n2.at[at], n2_out.at[at])
        save(9, b, u.at[b], u_out.at[b])
        save(10, b, a.at[at], a_out.at[at])
        copy.wait_recv()
        xout[b] = (m[b, mine] + (zpart[b, mine] + zrecv[b])).astype(BF16)

        @pl.when(s == 0)
        def _():
            remote(xout.at[b], land.at[1, b, mine], ns_sem.at[b], nr_sem.at[b], section).start()

        save(13, b, xout.at[b], x_out.at[b])
        return 0

    lax.fori_loop(0, blocks, feed, 0)

    @pl.when(s == 1)
    def _():
        near_rows()
        far_rows()

    for b in range(blocks):
        pltpu.make_async_copy(land.at[0, b], g_out.at[b], save_sem.at[12, b]).start()

    block = land.at[0, t]
    remote(block, block, xs_sem.at[PIECES], xr_sem.at[t], core).wait_send()
    remote(block, block, xfs_sem, xr_sem.at[t], core).wait_send()

    @pl.when(s == 1)
    def _():
        for i in range(PIECES):
            passing_copy(i).wait_send()
            onward(i).wait_send()
            over(i).wait_send()
            down_second(i).wait_send()
            down_third(i).wait_send()
        for i in range(10, 12):
            crossing(i).wait_send()
            beside_copy(i, parity).wait_send()

    @pl.when(s == 0)
    def _():
        for i in range(PIECES):
            down_first(i).wait_send()

    for b in range(blocks):
        piece = land.at[0, b, mine]
        remote(ysend.at[b], yrecv.at[b], ys_sem.at[b], yr_sem.at[b], core).wait_send()
        remote(zpart.at[b, theirs], zrecv.at[b], zs_sem.at[b], zr_sem.at[b], core).wait_send()

        @pl.when(s == 0)
        def _():
            remote(xout.at[b], piece, ns_sem.at[b], nr_sem.at[b], section).wait_send()

        @pl.when(s == 1)
        def _():
            remote(piece, piece, nfs_sem.at[b], nfr_sem.at[b], core).wait_send()

    for i in range(10):
        crossing(i).wait_send()
        beside_copy(i, parity).wait_send()
    for i, (src, dst) in enumerate(weights):
        pltpu.make_async_copy(src, dst, save_sem.at[11, i]).wait()
    for b in range(blocks):
        at = pl.ds(b * rows, rows)
        saved = [
            (land.at[s, b], h_out.at[b]),
            (n1.at[at], n1_out.at[at]),
            (q.at[:, at], q_out.at[:, at]),
            (k.at[:, at], k_out.at[:, at]),
            (v.at[:, at], v_out.at[:, at]),
            (o.at[at], o_out.at[at]),
            (lse.at[b], lse_out.at[b]),
            (m.at[b], m_out.at[b]),
            (n2.at[at], n2_out.at[at]),
            (u.at[b], u_out.at[b]),
            (a.at[at], a_out.at[at]),
        ]
        for kind, (src, dst) in enumerate(saved):
            pltpu.make_async_copy(src, dst, save_sem.at[kind, b]).wait()
        pltpu.make_async_copy(land.at[0, b], g_out.at[b], save_sem.at[12, b]).wait()
        pltpu.make_async_copy(xout.at[b], x_out.at[b], save_sem.at[13, b]).wait()


def forward(inputs, cotangent, shards, gain_one, gain_two, scale, head):
    _, rows, width = inputs.shape
    local = shards[0].shape[0]
    heads = 2 * local // head
    blocks = lax.axis_size("tensor")
    length = blocks * rows
    half = rows // 2
    shape = jax.ShapeDtypeStruct
    weights = [(2, 3 * local, width), (2 * local, width), (2 * local, width), (2 * local, width)]
    outs = [
        shape((blocks, half, width), BF16),
        shape((blocks, rows, width), BF16),
        shape((length, width), BF16),
        shape((heads, length, head), BF16),
        shape((heads, length, head), BF16),
        shape((heads, length, head), BF16),
        shape((length, 2 * local), BF16),
        shape((blocks, heads, rows), F32),
        shape((blocks, rows, width), F32),
        shape((length, width), BF16),
        shape((blocks, rows, 2 * local), F32),
        shape((length, 2 * local), BF16),
        shape((blocks, rows, width), BF16),
    ] + [shape(w, BF16) for w in weights]
    scratch = [pltpu.VMEM((2, blocks, rows, width), BF16)]
    scratch += [pltpu.VMEM(w, BF16) for w in weights]
    scratch += [
        pltpu.VMEM((rows, width), BF16),
        pltpu.VMEM((local, width), BF16),
        pltpu.VMEM((local, width), BF16),
        pltpu.VMEM((length, width), BF16),
        pltpu.VMEM((heads, length, head), BF16),
        pltpu.VMEM((heads, length, head), BF16),
        pltpu.VMEM((heads, length, head), BF16),
        pltpu.VMEM((heads, length, head), BF16),
        pltpu.VMEM((length, 2 * local), BF16),
        pltpu.VMEM((blocks, rows, 128), F32),
        pltpu.VMEM((blocks, heads, rows), F32),
        pltpu.VMEM((blocks, rows, width), BF16),
        pltpu.VMEM((blocks, rows, width), BF16),
        pltpu.VMEM((blocks, rows, width), F32),
        pltpu.VMEM((length, width), BF16),
        pltpu.VMEM((blocks, rows, 2 * local), F32),
        pltpu.VMEM((length, 2 * local), BF16),
        pltpu.VMEM((blocks, rows, width), F32),
        pltpu.VMEM((blocks, half, width), F32),
        pltpu.VMEM((blocks, half, width), BF16),
        DMA((6,)),
        DMA((2 * PIECES,)),
        DMA((PIECES,)),
        DMA((PIECES + 1,)),
        DMA((PIECES,)),
        DMA((blocks,)),
        DMA,
    ]
    scratch += [DMA((12,))] * 4 + [DMA((PIECES,))] * 6 + [DMA((blocks,))] * 8 + [DMA((14, blocks))]
    return pl.pallas_call(
        forward_kernel,
        out_shape=outs,
        in_specs=[ANY] * 8 + [VMEM] * 3,
        out_specs=[ANY] * len(outs),
        scratch_shapes=scratch,
        compiler_params=pltpu.CompilerParams(
            collective_id=1, has_side_effects=True, vmem_limit_bytes=62 * MIB
        ),
        name="forward",
    )(inputs, cotangent, *shards, gain_one, gain_two, scale)


def backward_kernel(
    g_in, h_in, q_in, k_in, v_in, o_in, lse_in, m_in, u_in, win_in, wo_in, wu_in, wd_in, x_in,
    gain_one, gain_two, scale,
    x_rows, out_rows, final, g_out, gu_out, gy_out, gp_out, dg1, dg2, ds,
    g, win, wo, wu, wd, h, q, k, v, o, lse, m, u, gu, gy, gp, ysend, yrecv, gm, go_heads, gq_heads,
    delta, dk, dv, n1part, n1recv, xout,
    load_sem, w_sem, ns_sem, nr_sem, nfs_sem, nfr_sem, ys_sem, yr_sem, zs_sem, zr_sem, os_sem, or_sem,
    xs_sem, xr_sem, save_sem,
):
    s, t, d = lax.axis_index("section"), lax.axis_index("tensor"), lax.axis_index("dp")
    blocks, rows, width = g.shape
    half = rows // 2
    local = wu.shape[0] // 2
    heads, _, head = q.shape
    per = heads // 2
    c, y = lax.rem(t, 2), t // 2
    core = (s, other(t), d)
    across = (s, lax.rem(t + 2, 4), d)
    diagonal = (s, other(lax.rem(t + 2, 4)), d)
    section = (1 - s, t, d)
    mine = pl.ds(pl.multiple_of(c * half, half), half)
    theirs = pl.ds(pl.multiple_of((1 - c) * half, half), half)

    weights = [(wd_in, wd), (wu_in, wu), (wo_in, wo), (win_in, win)]

    def weight(i):
        return pltpu.make_async_copy(*weights[i], w_sem.at[i])

    def load(kind, b):
        at = pl.ds(pl.multiple_of(b * rows, rows), rows)
        src, dst = [
            (u_in.at[b], u.at[b]),
            (m_in.at[b], m.at[b]),
            (o_in.at[at], o.at[at]),
            (q_in.at[:, at], q.at[:, at]),
            (k_in.at[:, at], k.at[:, at]),
            (v_in.at[:, at], v.at[:, at]),
            (lse_in.at[b], lse.at[b]),
            (h_in.at[b, mine], h.at[b]),
        ][kind]
        return pltpu.make_async_copy(src, dst, load_sem.at[kind, b])

    def incoming(b):
        return pltpu.make_async_copy(g_in.at[b], g.at[b], nr_sem.at[b])

    last = blocks - 1

    @pl.when(s == 1)
    def _():
        incoming(last).start()

    weight(0).start()
    load(0, last).start()
    weight(1).start()
    load(1, last).start()

    greet([core, across, diagonal, section])

    spot = out_rows.at[y, mine]

    def owner_copy(b, src, dst, send, receive, act):
        @pl.when(b == t)
        def _():
            act(pltpu.make_async_copy(src, dst, receive.at[t]))

        @pl.when(b != t)
        def _():
            act(remote(src, dst, send.at[b], receive.at[t], (s, b, d)))

    for b in range(blocks):
        owner_copy(b, x_in.at[b], x_rows.at[y, mine], xs_sem, xr_sem, lambda copy: copy.start())

    dk[...] = jnp.zeros_like(dk)
    dv[...] = jnp.zeros_like(dv)
    dg1[...] = jnp.zeros_like(dg1)
    dg2[...] = jnp.zeros_like(dg2)
    ds[...] = jnp.zeros_like(ds)

    causal = lax.broadcasted_iota(jnp.int32, (rows, rows), 0) <= lax.broadcasted_iota(
        jnp.int32, (rows, rows), 1
    )
    factor = jnp.concatenate([per_dim(scale[...])] * per, axis=1)
    width_two = heads * head
    row_head = lax.broadcasted_iota(jnp.int32, (heads, width_two), 0)
    start = row_head * head
    place = lax.broadcasted_iota(jnp.int32, (heads, width_two), 1)
    member = jnp.where((place >= start) & (place < start + head), 1.0, 0.0)

    def save(kind, b, src, dst):
        pltpu.make_async_copy(src, dst, save_sem.at[kind, b]).start()

    def neighbours_sum(b):
        return remote(ysend.at[b], yrecv.at[b], ys_sem.at[b], yr_sem.at[b], core)

    def up_part(turn):
        b = last - turn
        at = pl.ds(pl.multiple_of(b * rows, rows), rows)

        @pl.when(s == 1)
        def _():
            incoming(b).wait()

        @pl.when(s == 0)
        def _():
            piece = g.at[b, mine]
            remote(piece, piece, ns_sem.at[b], nr_sem.at[b], core).wait_recv()
            remote(piece, piece, nfs_sem.at[b], nfr_sem.at[b], core).start()
            rest = g.at[b, theirs]
            remote(rest, rest, nfs_sem.at[b], nfr_sem.at[b], core).wait_recv()

        @pl.when(turn == 0)
        def _():
            weight(0).wait()

        load(0, b).wait()
        save(0, b, g.at[b], g_out.at[at])
        grad = g[b]
        grad_act = by_last(grad, wd[...])
        up = u[b]
        sigma = 1.0 / (1.0 + jnp.exp(-up))
        grad_up = (grad_act * sigma * (1.0 + up * (1.0 - sigma))).astype(BF16)
        gu[at] = grad_up

        @pl.when(turn == 0)
        def _():
            weight(1).wait()
            weight(2).start()
            for kind in (2, 3, 6):
                load(kind, last).start()
            for bb in reversed(range(blocks)):
                load(4, bb).start()
                load(5, bb).start()

        save(1, b, gu.at[at], gu_out.at[at])
        ysend[b] = plain(grad_up, wu[...]).astype(BF16)
        neighbours_sum(b).start()

    def one_block(turn, _):
        b = last - turn
        at = pl.ds(pl.multiple_of(b * rows, rows), rows)
        load(1, b).wait()
        neighbours_sum(b).wait_recv()
        grad = g[b]
        grad_normed = ysend[b].astype(F32) + yrecv[b].astype(F32)
        middle = m[b]
        inverse = inverse_rms(middle)
        unit = middle * inverse
        grad_unit = grad_normed * gain_two[...]
        dg2[...] += jnp.sum(grad_normed * unit, axis=0, keepdims=True)
        grad_middle = grad.astype(F32) + inverse * (
            grad_unit - unit * jnp.mean(grad_unit * unit, axis=1, keepdims=True)
        )
        gm[...] = grad_middle
        grad_mid = grad_middle.astype(BF16)
        gy[at] = grad_mid
        save(2, b, gy.at[at], gy_out.at[at])

        @pl.when(turn == 0)
        def _():
            weight(2).wait()
            weight(3).start()
            load(7, last).start()

        load(2, b).wait()
        grad_mixed = by_last(grad_mid, wo[...]).astype(BF16)
        both = grad_mixed.astype(F32) * o[at].astype(F32)
        delta[...] = lax.dot_general(
            member,
            both,
            (((1,), (1,)), ((), ())),
            precision=lax.Precision.HIGHEST,
            preferred_element_type=F32,
        )
        for i in range(heads):
            go_heads[i] = grad_mixed[:, i * head : (i + 1) * head]

        @pl.when(turn == 0)
        def _():
            for bb in range(blocks):
                load(4, bb).wait()
                load(5, bb).wait()

        load(3, b).wait()
        load(6, b).wait()

        @pl.when(turn < last)
        def _():
            for kind in (0, 1, 2, 3, 6, 7):
                load(kind, b - 1).start()

        @pl.when((turn < last) & (s == 1))
        def _():
            incoming(b - 1).start()

        for bb in range(blocks):

            @pl.when(b == bb)
            def _():
                def group(first, _):
                    for j in range(per):
                        i = first * per + j
                        qh = q[i, bb * rows : (bb + 1) * rows]
                        gh = go_heads[i]
                        offset = lse[bb, pl.ds(i, 1)]
                        inner = delta[pl.ds(i, 1)]
                        total = None
                        for lo, hi in ((bb * rows, (bb + 1) * rows), (0, bb * rows)):
                            if lo == hi:
                                continue
                            kj = k[i, lo:hi]
                            weight = jnp.exp(by_last(kj, qh) - offset)
                            if lo == bb * rows and hi > lo and hi == (bb + 1) * rows:
                                weight = jnp.where(causal, weight, 0.0)
                            grad_score = weight * (by_last(v[i, lo:hi], gh) - inner)
                            grad_score = grad_score.astype(BF16)
                            dv[i, lo:hi] += plain(weight.astype(BF16), gh)
                            dk[i, lo:hi] += plain(grad_score, qh)
                            part = by_first(kj, grad_score)
                            total = part if total is None else total + part
                        gq_heads[i] = jnp.transpose(total)
                    return 0

                lax.fori_loop(0, 2, group, 0)

        for j in range(2):
            mine_heads = range(j * per, (j + 1) * per)
            grad_scaled = jnp.concatenate([gq_heads[i] for i in mine_heads], axis=1)
            queries = jnp.concatenate([q[i, at] for i in mine_heads], axis=1).astype(F32)
            ds[pl.ds(j, 1)] += jnp.sum(grad_scaled * queries, axis=0, keepdims=True)
            grads = [
                (grad_scaled * factor).astype(BF16),
                jnp.concatenate([dk[i, at] for i in mine_heads], axis=1).astype(BF16),
                jnp.concatenate([dv[i, at] for i in mine_heads], axis=1).astype(BF16),
            ]
            gp[j, at] = jnp.concatenate(grads, axis=1)
        save(3, b, gp.at[:, at], gp_out.at[:, at])

        @pl.when(turn == 0)
        def _():
            weight(3).wait()

        n1part[...] = plain(gp[0, at], win[0]) + plain(gp[1, at], win[1])
        copy = remote(n1part.at[theirs], n1recv.at[b], zs_sem.at[b], zr_sem.at[b], core)
        copy.start()

        @pl.when(turn < last)
        def _():
            up_part(turn + 1)

        load(7, b).wait()
        hidden = h[b].astype(F32)
        inverse = inverse_rms(hidden)
        unit = hidden * inverse
        copy.wait_recv()
        grad_normed = n1part[mine] + n1recv[b]
        grad_unit = grad_normed * gain_one[...]
        dg1[...] += jnp.sum(grad_normed * unit, axis=0, keepdims=True)
        xout[b] = (
            gm[mine]
            + inverse * (grad_unit - unit * jnp.mean(grad_unit * unit, axis=1, keepdims=True))
        ).astype(BF16)

        @pl.when(s == 1)
        def _():
            remote(xout.at[b], g.at[b, mine], ns_sem.at[b], nr_sem.at[b], section).start()

        @pl.when(b > 0)
        def _():
            owner_copy(b, xout.at[b], spot, os_sem, or_sem, lambda copy: copy.start())

        @pl.when(b == 0)
        def _():
            save(4, 0, xout.at[0], final)

        copy.wait_send()
        return 0

    up_part(jnp.int32(0))
    lax.fori_loop(0, blocks, one_block, 0)

    for b in range(blocks):
        at = pl.ds(b * rows, rows)
        piece = g.at[b, mine]
        remote(ysend.at[b], yrecv.at[b], ys_sem.at[b], yr_sem.at[b], core).wait_send()
        here = x_rows.at[b // 2, pl.ds((b % 2) * half, half)]
        remote(here, here, xs_sem.at[b], xr_sem.at[b], core).wait_recv()

        @pl.when(b != t)
        def _():
            remote(x_in.at[b], here, xs_sem.at[b], xr_sem.at[b], core).wait_send()

        @pl.when(t > 0)
        def _():
            here = out_rows.at[b // 2, pl.ds((b % 2) * half, half)]
            remote(here, here, os_sem.at[b], or_sem.at[b], core).wait_recv()

        @pl.when((b != t) & (b > 0))
        def _():
            remote(xout.at[b], here, os_sem.at[b], or_sem.at[b], core).wait_send()

        @pl.when(s == 1)
        def _():
            remote(xout.at[b], piece, ns_sem.at[b], nr_sem.at[b], section).wait_send()

        @pl.when(s == 0)
        def _():
            remote(piece, piece, nfs_sem.at[b], nfr_sem.at[b], core).wait_send()

        saved = [
            (g.at[b], g_out.at[at]),
            (gu.at[at], gu_out.at[at]),
            (gy.at[at], gy_out.at[at]),
            (gp.at[:, at], gp_out.at[:, at]),
        ]
        for kind, (src, dst) in enumerate(saved):
            pltpu.make_async_copy(src, dst, save_sem.at[kind, b]).wait()
    pltpu.make_async_copy(xout.at[0], final, save_sem.at[4, 0]).wait()


def backward(saved, gain_one, gain_two, scale):
    g_in, h_in, q_in = saved[:3]
    win_in, wo_in, wu_in, wd_in = saved[9:13]
    blocks, rows, width = g_in.shape
    heads, length, head = q_in.shape
    local = wu_in.shape[0] // 2
    half = rows // 2
    shape = jax.ShapeDtypeStruct
    outs = [
        shape((2, rows, width), BF16),
        shape((2, rows, width), BF16),
        shape((half, width), BF16),
        shape((length, width), BF16),
        shape((length, 2 * local), BF16),
        shape((length, width), BF16),
        shape((2, length, 3 * local), BF16),
        shape((1, width), F32),
        shape((1, width), F32),
        shape((2, local), F32),
    ]
    scratch = [
        pltpu.VMEM((blocks, rows, width), BF16),
        pltpu.VMEM(win_in.shape, BF16),
        pltpu.VMEM(wo_in.shape, BF16),
        pltpu.VMEM(wu_in.shape, BF16),
        pltpu.VMEM(wd_in.shape, BF16),
        pltpu.VMEM((blocks, half, width), BF16),
        pltpu.VMEM((heads, length, head), BF16),
        pltpu.VMEM((heads, length, head), BF16),
        pltpu.VMEM((heads, length, head), BF16),
        pltpu.VMEM((length, 2 * local), BF16),
        pltpu.VMEM((blocks, heads, rows), F32),
        pltpu.VMEM((blocks, rows, width), F32),
        pltpu.VMEM((blocks, rows, 2 * local), F32),
        pltpu.VMEM((length, 2 * local), BF16),
        pltpu.VMEM((length, width), BF16),
        pltpu.VMEM((2, length, 3 * local), BF16),
        pltpu.VMEM((blocks, rows, width), BF16),
        pltpu.VMEM((blocks, rows, width), BF16),
        pltpu.VMEM((rows, width), F32),
        pltpu.VMEM((heads, rows, head), BF16),
        pltpu.VMEM((heads, rows, head), F32),
        pltpu.VMEM((heads, rows), F32),
        pltpu.VMEM((heads, length, head), F32),
        pltpu.VMEM((heads, length, head), F32),
        pltpu.VMEM((rows, width), F32),
        pltpu.VMEM((blocks, half, width), F32),
        pltpu.VMEM((blocks, half, width), BF16),
        DMA((8, blocks)),
        DMA((4,)),
    ]
    scratch += [DMA((blocks,))] * 12 + [DMA((5, blocks))]
    return pl.pallas_call(
        backward_kernel,
        out_shape=outs,
        in_specs=[ANY] * 14 + [VMEM] * 3,
        out_specs=[ANY] * 7 + [VMEM] * 3,
        scratch_shapes=scratch,
        compiler_params=pltpu.CompilerParams(
            collective_id=2, has_side_effects=True, vmem_limit_bytes=62 * MIB
        ),
        name="backward",
    )(*saved, gain_one, gain_two, scale)


def farthest_first(d, k, n):
    found = 0
    for i in range(n):
        above = list(range(n - 1, i, -1))
        below = list(range(i))
        first, second = (above, below) if len(above) >= len(below) else (below, above)
        lead = len(first) - len(second) - 1
        order = first[: max(lead, 0)]
        rest = first[max(lead, 0) :]
        for j in range(max(len(rest), len(second))):
            order += rest[j : j + 1] + second[j : j + 1]
        order.append(i)
        picked = 0
        for j, e in enumerate(order):
            picked = picked + jnp.where(k == j, e, 0)
        found = found + jnp.where(d == i, picked, 0)
    return found


def gradient_kernel(
    n1_in, n2_in, gy_in, g_in, gp_in, gu_in, o_in, a_in, final, rows_in, dg1, dg2, ds, dim_scale,
    out_q, out_k, out_v, out_u, out_o, out_d, rows_out, out_g1, out_g2, out_s,
    x, xt, gp, gu, o, a,
    keep_a, give_a, yrecv_a, flow_a, last_a, keep_b, give_b, yrecv_b, flow_b, last_b,
    line, flow_d, last_d, rest, yd, small, smalls, chain,
    x_sem, g_sem, ys_sem, yr_sem, fs_sem, fr_sem, last_sem, ds_sem, dr_sem, last_d_sem,
    yds_sem, ydr_sem, ss_sem, sr_sem, cs_sem, cr_sem, es_sem, er_sem,
):
    s, t, d = lax.axis_index("section"), lax.axis_index("tensor"), lax.axis_index("dp")
    n, chunk, _ = keep_a.shape
    local = a.shape[1] // 2
    split = yd.shape[1]
    width = dg1.shape[1]
    pieces = ys_sem.shape[2]
    step = chunk // pieces
    core = (s, other(t), d)
    across = (s, lax.rem(t + 2, 4), d)
    diagonal = (s, other(lax.rem(t + 2, 4)), d)
    up = (s, t, lax.rem(d + 1, n))
    down = (s, t, lax.rem(d + n - 1, n))
    c, y = lax.rem(t, 2), t // 2

    sources = [g_in, n1_in, n2_in, gy_in]
    operands = [(a_in, a), (gp_in, gp), (gu_in, gu), (o_in, o)]

    def load(i):
        return pltpu.make_async_copy(sources[i], x.at[i % 2], x_sem.at[i])

    def operand(i):
        return pltpu.make_async_copy(*operands[i], g_sem.at[i])

    load(0).start()
    operand(0).start()
    load(1).start()
    for i in range(1, 4):
        operand(i).start()

    small[0:1, :width] = dg1[...]
    small[0:1, width : 2 * width] = jnp.where(c == 0, dg2[...], 0.0)
    small[0:1, 2 * width : 2 * width + local] = ds[0:1]
    small[0:1, 2 * width + 384 : 2 * width + 384 + local] = ds[1:2]

    greet([core, across, diagonal, up, down])

    partners = [core, across, diagonal]

    def share(i):
        return remote(small, smalls.at[i], ss_sem.at[i], sr_sem.at[i], partners[i])

    for i in range(3):
        share(i).start()

    def turn(i):
        load(i).wait()
        turned = jnp.transpose(x[i % 2])
        for e in range(n):
            xt[i, e] = turned[e * chunk : (e + 1) * chunk]
        if i + 2 < 4:
            load(i + 2).start()

    groups = [(keep_a, give_a, yrecv_a, flow_a, last_a), (keep_b, give_b, yrecv_b, flow_b, last_b)]

    def exchange(which, e, i):
        _, give, yrecv, _, _ = groups[which]
        rows = pl.ds(i * step, step)
        return remote(
            give.at[e, rows], yrecv.at[e, rows], ys_sem.at[which, e, i], yr_sem.at[which, e, i], across
        )

    def send_all(which, e):
        for i in range(pieces):
            exchange(which, e, i).start()

    def send_d(e):
        src = line.at[e]

        @pl.when(e > d)
        def _():
            remote(src, flow_d.at[e], ds_sem.at[e], dr_sem.at[e], up).start()

        @pl.when(e < d - 1)
        def _():
            remote(src, flow_d.at[e], ds_sem.at[e], dr_sem.at[e], down).start()

        @pl.when(e == d - 1)
        def _():
            remote(src, last_d, ds_sem.at[e], last_d_sem, down).start()

    def upstream_d(e):
        piece = flow_d.at[e]
        remote(piece, piece, ds_sem.at[e], dr_sem.at[e], up).wait_recv()
        line[e] = (line[e].astype(F32) + flow_d[e].astype(F32)).astype(BF16)

    turn(0)
    operand(0).wait()

    def down_product(k, _):
        e = farthest_first(d, k, n)
        both = plain(xt[0, e], a[...]).astype(BF16)
        line[e] = jnp.concatenate([both[:, :split], both[:, local : local + split]], axis=1)
        for j in range(2):
            rest[j, e] = both[:, j * local + split : (j + 1) * local]

        @pl.when(((d == 0) | (d == n - 1)) & (e != d))
        def _():
            send_d(e)

        return 0

    lax.fori_loop(0, n, down_product, 0)

    turn(1)
    operand(1).wait()

    def in_product(k, _):
        e = farthest_first(d, k, n)
        for j, target in ((1, give_a), (0, keep_a)):
            target[e] = jnp.concatenate(
                [plain(xt[1, e], gp[j]).astype(BF16), rest[j, e]], axis=1
            )
            if j:
                send_all(0, e)
        return 0

    lax.fori_loop(0, n, in_product, 0)

    turn(2)
    turn(3)
    operand(2).wait()
    operand(3).wait()

    def other_product(k, _):
        e = farthest_first(d, k, n)
        ups = plain(xt[2, e], gu[...])
        outs = plain(xt[3, e], o[...])
        for j, target in ((1, give_b), (0, keep_b)):
            cut = slice(j * local, (j + 1) * local)
            target[e] = jnp.concatenate([ups[:, cut], outs[:, cut]], axis=1).astype(BF16)
            if j:
                send_all(1, e)
        return 0

    lax.fori_loop(0, n, other_product, 0)

    half = final.shape[0]
    owner = (s, 0, d)
    spot = rows_out.at[y, pl.ds(pl.multiple_of(c * half, half), half)]

    @pl.when(t == 0)
    def _():
        pltpu.make_async_copy(final, spot, er_sem.at[0]).start()

    @pl.when(t != 0)
    def _():
        remote(final, spot, es_sem, er_sem.at[t], owner).start()

    for i in range(3):
        share(i).wait_recv()
    mine = small[...] + smalls[0] + (smalls[1] + smalls[2])

    def link(i, device):
        return remote(chain.at[i], chain.at[2 + i], cs_sem.at[i], cr_sem.at[i], device)

    smalls[0] = mine
    for i, opens, closes, device in ((0, d == 0, d == n - 1, up), (1, d == n - 1, d == 0, down)):
        chain[i] = mine

        @pl.when(jnp.logical_not(opens))
        def _():
            link(i, device).wait_recv()
            chain[i] = mine + chain[2 + i]
            smalls[0] += chain[2 + i]

        @pl.when(jnp.logical_not(closes))
        def _():
            link(i, device).start()

    def middle(k):
        e = farthest_first(d, k, n)

        @pl.when((d > 0) & (d < n - 1) & (e != d))
        def _():
            upstream_d(e)
            send_d(e)

    def flows(which, k):
        e = farthest_first(d, k, n)
        keep, give, yrecv, flow, last = groups[which]
        send, receive = fs_sem.at[which], fr_sem.at[which]
        for i in range(pieces):
            at = pl.ds(i * step, step)
            exchange(which, e, i).wait_recv()
            first = ((e > d) & (d == 0)) | ((e < d) & (d == n - 1))

            @pl.when((e != d) & first)
            def _():
                keep[e, at] = (keep[e, at].astype(F32) + yrecv[e, at].astype(F32)).astype(BF16)

            @pl.when((e != d) & jnp.logical_not(first))
            def _():
                piece = flow.at[e, at]
                remote(piece, piece, send.at[e, i], receive.at[e, i], up).wait_recv()
                total = keep[e, at].astype(F32) + yrecv[e, at].astype(F32)
                keep[e, at] = (total + flow[e, at].astype(F32)).astype(BF16)

            src = keep.at[e, at]

            @pl.when(e > d)
            def _():
                remote(src, flow.at[e, at], send.at[e, i], receive.at[e, i], up).start()

            @pl.when(e < d - 1)
            def _():
                remote(src, flow.at[e, at], send.at[e, i], receive.at[e, i], down).start()

            @pl.when(e == d - 1)
            def _():
                remote(src, last.at[at], send.at[e, i], last_sem.at[which, i], down).start()

    def flows_in(k, _):
        middle(k)
        flows(0, k)
        return 0

    def flows_other(k, _):
        flows(1, k)
        return 0

    lax.fori_loop(0, n, flows_in, 0)

    @pl.when(d > 0)
    def _():
        upstream_d(d)

    @pl.when(d < n - 1)
    def _():
        remote(last_d, last_d, ds_sem.at[0], last_d_sem, down).wait_recv()
        line[d] = (line[d].astype(F32) + last_d[...].astype(F32)).astype(BF16)

    crossing = remote(line.at[d, :, pl.ds(split, split)], yd, yds_sem, ydr_sem, across)
    crossing.start()

    lax.fori_loop(0, n, flows_other, 0)

    def landed(which, i):
        keep, _, yrecv, flow, last = groups[which]
        at = pl.ds(i * step, step)

        @pl.when(d > 0)
        def _():
            piece = flow.at[d, at]
            remote(
                piece, piece, fs_sem.at[which, d, i], fr_sem.at[which, d, i], up
            ).wait_recv()

        @pl.when(d < n - 1)
        def _():
            piece = last.at[at]
            remote(
                piece, piece, fs_sem.at[which, d, i], last_sem.at[which, i], down
            ).wait_recv()

        above = jnp.where(d > 0, flow[d, at].astype(F32), 0.0)
        below = jnp.where(d < n - 1, last[at].astype(F32), 0.0)
        return (keep[d, at].astype(F32) + yrecv[d, at].astype(F32)) + (above + below)

    rests = []
    for i in range(pieces):
        at = pl.ds(i * step, step)
        total = landed(0, i)
        for j, ref in enumerate((out_q, out_k, out_v)):
            ref[at] = total[:, j * local : (j + 1) * local]
        rests.append(total[:, 3 * local :])
    crossing.wait_recv()
    most = line[d, :, :split].astype(F32) + yd[...].astype(F32)
    out_d[...] = jnp.transpose(jnp.concatenate([most, jnp.concatenate(rests, axis=0)], axis=1))
    found = smalls[0]
    out_g1[...] = found[0:1, :width]
    out_g2[...] = found[0:1, width : 2 * width]
    head = dim_scale.shape[1]
    scale = jnp.zeros((1, head), F32)
    for j in range(2):
        for i in range(local // head):
            start = 2 * width + j * 384 + i * head
            scale = scale + found[0:1, start : start + head]
    raw = dim_scale[...]
    grown = jnp.maximum(raw, 0.0) + jnp.log(1.0 + jnp.exp(-jnp.abs(raw)))
    out_s[...] = scale / grown * (1.0 / (1.0 + jnp.exp(-raw)))
    totals = []
    for i in range(pieces):
        total = landed(1, i)
        out_u[pl.ds(i * step, step)] = total[:, :local]
        totals.append(total[:, local:])
    out_o[...] = jnp.transpose(jnp.concatenate(totals, axis=0))

    @pl.when(t == 0)
    def _():
        for i in range(4):
            piece = rows_out.at[i // 2, pl.ds(i % 2 * half, half)]
            remote(piece, piece, es_sem, er_sem.at[i], owner).wait_recv()

    @pl.when(t != 0)
    def _():
        remote(final, spot, es_sem, er_sem.at[t], owner).wait_send()

    crossing.wait_send()
    for i in range(3):
        share(i).wait_send()

    @pl.when(d < n - 1)
    def _():
        link(0, up).wait_send()

    @pl.when(d > 0)
    def _():
        link(1, down).wait_send()

    def drain(e, _):
        for which in range(2):
            for i in range(pieces):
                exchange(which, e, i).wait_send()

        @pl.when(e != d)
        def _():
            for which in range(2):
                for i in range(pieces):
                    piece = groups[which][0].at[e, pl.ds(i * step, step)]
                    remote(
                        piece, piece, fs_sem.at[which, e, i], fr_sem.at[which, e, i], up
                    ).wait_send()
            remote(line.at[e], line.at[e], ds_sem.at[e], dr_sem.at[e], up).wait_send()

        return 0

    lax.fori_loop(0, n, drain, 0)


def gradients(n1, n2, gy, g, gp, gu, o, a, final, rows, dg1, dg2, ds, dim_scale):
    n = lax.axis_size("dp")
    length, width = n1.shape
    local = gp.shape[2] // 3
    chunk = width // n
    pieces = 4 if chunk % 64 == 0 else 1
    small = (1, 2 * width + 768)

    def lines(columns):
        return [pltpu.VMEM((n, chunk, columns), BF16)] * 4 + [pltpu.VMEM((chunk, columns), BF16)]

    split = local // 128 * 128
    line = pltpu.VMEM((n, chunk, 2 * split), BF16)
    return pl.pallas_call(
        gradient_kernel,
        out_shape=[jax.ShapeDtypeStruct((chunk, local), F32)] * 4
        + [jax.ShapeDtypeStruct((local, chunk), F32)] * 2
        + [
            jax.ShapeDtypeStruct(rows.shape, BF16),
            jax.ShapeDtypeStruct(dg1.shape, F32),
            jax.ShapeDtypeStruct(dg2.shape, F32),
            jax.ShapeDtypeStruct(dim_scale.shape, F32),
        ],
        in_specs=[ANY] * 10 + [VMEM] * 4,
        out_specs=[VMEM] * 6 + [ANY] + [VMEM] * 3,
        input_output_aliases={9: 6},
        scratch_shapes=[
            pltpu.VMEM((2, length, width), BF16),
            pltpu.VMEM((4, n, chunk, length), BF16),
            pltpu.VMEM(gp.shape, BF16),
            pltpu.VMEM(gu.shape, BF16),
            pltpu.VMEM(o.shape, BF16),
            pltpu.VMEM(a.shape, BF16),
        ]
        + lines(4 * local - split)
        + lines(2 * local)
        + [line] * 2
        + [
            pltpu.VMEM((chunk, 2 * split), BF16),
            pltpu.VMEM((2, n, chunk, local - split), BF16),
            pltpu.VMEM((chunk, split), BF16),
            pltpu.VMEM(small, F32),
            pltpu.VMEM((3,) + small, F32),
            pltpu.VMEM((4,) + small, F32),
            DMA((4,)),
            DMA((4,)),
        ]
        + [DMA((2, n, pieces))] * 4
        + [
            DMA((2, pieces)),
            DMA((n,)),
            DMA((n,)),
            DMA,
            DMA,
            DMA,
            DMA((3,)),
            DMA((3,)),
            DMA((2,)),
            DMA((2,)),
            DMA,
            DMA((4,)),
        ],
        compiler_params=pltpu.CompilerParams(
            collective_id=3, has_side_effects=True, vmem_limit_bytes=62 * MIB
        ),
        name="gradients",
    )(n1, n2, gy, g, gp, gu, o, a, final, rows, dg1, dg2, ds, dim_scale)


def body(
    inputs, cotangent, gain_attn, w_query, w_key, w_value, w_out, dim_scale, gain_mlp, w_up, w_down
):
    head = dim_scale.shape[1]
    shards = (w_query[0].T, w_key[0].T, w_value[0].T, w_out[0], w_up[0].T, w_down[0])
    done = forward(
        inputs, cotangent, shards, gain_attn, gain_mlp, dim_scale, head
    )
    x_halves, h, n1, q, k, v, o, lse, m, n2, u, a, g, win, wo, wu, wd = done
    layer_out, input_grads, final, g_all, gu, gy, gp, dg1, dg2, ds = backward(
        (g, h, q, k, v, o, lse, m, u, win, wo, wu, wd, x_halves),
        gain_attn,
        gain_mlp,
        dim_scale,
    )

    *pieces, input_grads, dg1, dg2, grad_scale = gradients(
        n1, n2, gy, g_all, gp, gu, o, a, final, input_grads, dg1, dg2, ds, dim_scale
    )
    return (
        layer_out[None],
        input_grads[None],
        dg1,
        pieces[0][None],
        pieces[1][None],
        pieces[2][None],
        pieces[4][None],
        grad_scale,
        dg2,
        pieces[3][None],
        pieces[5][None],
    )


def solution(mesh):
    in_specs = (
        P("dp", "tensor", None),
        P("dp", "tensor", None),
        P("section", None),
        P("section", None, "tensor"),
        P("section", None, "tensor"),
        P("section", None, "tensor"),
        P("section", "tensor", None),
        P("section", None),
        P("section", None),
        P("section", None, "tensor"),
        P("section", "tensor", None),
    )
    out_specs = (
        P("section", "dp", "tensor", None),
        P("section", "dp", "tensor", None),
        P("section", None),
        P("section", "dp", "tensor"),
        P("section", "dp", "tensor"),
        P("section", "dp", "tensor"),
        P("section", "tensor", "dp"),
        P("section", None),
        P("section", None),
        P("section", "dp", "tensor"),
        P("section", "tensor", "dp"),
    )
    return jax.shard_map(body, mesh=mesh, in_specs=in_specs, out_specs=out_specs, check_vma=False)
```

```python
import functools
import math

import jax
import jax.numpy as jnp
from jax import lax
from jax.experimental import pallas as pl
from jax.experimental.pallas import tpu as pltpu
from jax.sharding import PartitionSpec as P

EPS = 1e-06
LOG2E = 1.442695041
NEGATIVE = -1e30
BF16 = jnp.bfloat16
F32 = jnp.float32
MESH = pl.DeviceIdType.MESH
ANY = pl.BlockSpec(memory_space=pl.ANY)
VMEM = pl.BlockSpec(memory_space=pltpu.VMEM)
DMA = pltpu.SemaphoreType.DMA
MIB = 1 << 20
PIECES = 4


def plain(a, b):
    return jnp.dot(a, b, preferred_element_type=F32)


def by_last(a, b):
    return lax.dot_general(a, b, (((1,), (1,)), ((), ())), preferred_element_type=F32)


def by_first(a, b):
    return lax.dot_general(a, b, (((0,), (0,)), ((), ())), preferred_element_type=F32)


def other(index):
    return index + 1 - 2 * lax.rem(index, 2)


def remote(src, dst, send, receive, device):
    return pltpu.make_async_remote_copy(
        src_ref=src,
        dst_ref=dst,
        send_sem=send,
        recv_sem=receive,
        device_id=device,
        device_id_type=MESH,
    )


def greet(devices):
    barrier = pltpu.get_barrier_semaphore()
    for device in devices:
        pl.semaphore_signal(barrier, inc=1, device_id=device, device_id_type=MESH)
    pl.semaphore_wait(barrier, len(devices))


def per_dim(raw):
    grown = jnp.maximum(raw, 0.0) + jnp.log(1.0 + jnp.exp(-jnp.abs(raw)))
    return (LOG2E / math.sqrt(raw.shape[1])) * grown


def inverse_rms(rows):
    return lax.rsqrt(jnp.mean(rows * rows, axis=1, keepdims=True) + EPS)


def forward_kernel(
    inputs, cotangent, w_q, w_k, w_v, w_o, w_u, w_d, gain_one, gain_two, scale,
    x_out, h_out, n1_out, q_out, k_out, v_out, o_out, lse_out, m_out, n2_out, u_out, a_out,
    g_out, win_out, wo_out, wu_out, wd_out,
    land, win, wo, wu, wd, passing, down_a, down_b, n1, q, k, v, o_heads, o, lse_cols, lse, ysend, yrecv,
    m, n2, u, a, zpart, zrecv, xout,
    own_sem, ps_sem, pr_sem, xs_sem, xp_sem, xr_sem, xfs_sem, wys_sem, wyr_sem, wzs_sem, wzr_sem,
    das_sem, dar_sem, dbs_sem, dbr_sem, dcs_sem, dcr_sem,
    ns_sem, nr_sem, nfs_sem, nfr_sem, ys_sem, yr_sem, zs_sem, zr_sem, save_sem,
):
    s, t, d = lax.axis_index("section"), lax.axis_index("tensor"), lax.axis_index("dp")
    blocks, rows, width = land.shape[1:]
    half = rows // 2
    local = w_o.shape[0]
    heads, _, head = q.shape
    per = heads // 2
    c, y = lax.rem(t, 2), t // 2
    t_core, t_across = other(t), lax.rem(t + 2, 4)
    t_diagonal = other(t_across)
    core = (s, t_core, d)
    across = (s, t_across, d)
    diagonal = (s, t_diagonal, d)
    beside = (s, t, other(d))
    section = (1 - s, t, d)
    greet([core, across, diagonal, beside, section])

    mine = pl.ds(pl.multiple_of(c * half, half), half)
    theirs = pl.ds(pl.multiple_of((1 - c) * half, half), half)

    shards = [w_q, w_k, w_v, w_o, w_u, w_d]

    def place(i, slot, start, size):
        if i < 3:
            return win.at[slot, pl.ds(pl.multiple_of(i * local + start, 16), size)]
        return (wo, wu, wd)[i - 3].at[pl.ds(pl.multiple_of(slot * local + start, 16), size)]

    short = local // 4
    parity = lax.rem(d, 2)

    def own(i):
        return pltpu.make_async_copy(shards[i], place(i, 0, 0, local), own_sem.at[i])

    def strip(i, which):
        return pl.multiple_of(which * 2 * short + i % 2 * short, 16)

    def crossing(i):
        start = strip(i, parity)
        dst = place(i // 2, 1, start, short)
        return remote(
            shards[i // 2].at[pl.ds(start, short)], dst, wys_sem.at[i], wyr_sem.at[i], across
        )

    def beside_copy(i, which):
        piece = place(i // 2, 1, strip(i, which), short)
        return remote(piece, piece, wzs_sem.at[i], wzr_sem.at[i], beside)

    def relay(i):
        crossing(i).wait_recv()
        beside_copy(i, parity).start()

    def arrived(i):
        beside_copy(i, 1 - parity).wait_recv()

    quarter = local // PIECES

    def down_piece(buffer, i):
        return buffer.at[pl.ds(i * quarter, quarter)]

    def down_first(i):
        return remote(
            down_piece(w_d, i), down_piece(down_a, i), das_sem.at[i], dar_sem.at[i], section
        )

    def down_second(i):
        return remote(
            down_piece(down_a, i), down_piece(down_b, i), dbs_sem.at[i], dbr_sem.at[i], across
        )

    def down_third(i):
        return remote(
            down_piece(down_b, i), wd.at[pl.ds(local + i * quarter, quarter)],
            dcs_sem.at[i], dcr_sem.at[i], section,
        )

    step = rows // PIECES

    def passing_copy(i):
        piece = pl.ds(i * step, step)
        return remote(
            inputs.at[1 - y, piece], passing.at[piece], ps_sem.at[i], pr_sem.at[i], across
        )

    def onward(i):
        piece = pl.ds(i * step, step)
        return remote(
            passing.at[piece], land.at[0, t_across, piece], ps_sem.at[PIECES + i], xp_sem.at[i], section
        )

    def over(i):
        piece = pl.ds(i * step, step)
        return remote(
            cotangent.at[1 - y, piece], land.at[0, t, piece], xs_sem.at[i], xp_sem.at[i], across
        )

    def local_rows(source):
        pltpu.make_async_copy(source.at[y], land.at[0, t], xr_sem.at[t]).start()
        remote(source.at[y], land.at[0, t], xs_sem.at[PIECES], xr_sem.at[t], core).start()

    def block_wait(b):
        piece = land.at[0, b]
        remote(piece, piece, xs_sem.at[PIECES], xr_sem.at[b], core).wait_recv()

    def far_rows():
        for i in range(PIECES):
            piece = land.at[0, t_across, pl.ds(i * step, step)]
            remote(piece, piece, xfs_sem, xp_sem.at[i], core).wait_recv()
        piece = land.at[0, t_across]
        remote(piece, piece, xfs_sem, xr_sem.at[t_across], core).start()
        block_wait(t_diagonal)

    def near_rows():
        block_wait(t)
        block_wait(t_core)

    for i in range(3):
        own(i).start()

    @pl.when(s == 0)
    def _():
        for i in range(10):
            crossing(i).start()
        local_rows(inputs)
        for i in range(PIECES):
            down_first(i).start()

    @pl.when(s == 1)
    def _():
        for i in range(PIECES):
            passing_copy(i).start()
        local_rows(cotangent)

    for i in range(3, 6):
        own(i).start()

    @pl.when(s == 1)
    def _():
        for i in range(PIECES):
            passing_copy(i).wait_recv()
            onward(i).start()
            down_first(i).wait_recv()
            down_second(i).start()
        for i in range(12):
            crossing(i).start()
        for i in range(PIECES):
            over(i).start()
        for i in range(PIECES):
            down_second(i).wait_recv()
            down_third(i).start()
        for i in range(6):
            relay(i)

    for i in range(3):
        own(i).wait()

    def save(kind, b, src, dst):
        pltpu.make_async_copy(src, dst, save_sem.at[kind, b]).start()

    causal = lax.broadcasted_iota(jnp.int32, (rows, rows), 0) >= lax.broadcasted_iota(
        jnp.int32, (rows, rows), 1
    )
    lane = lax.broadcasted_iota(jnp.int32, (rows, 128), 1)

    factor = per_dim(scale[...])

    def attention(turn, _):
        b = jnp.where(s == 0, lax.rem(turn, blocks), turn // 2)
        j = jnp.where(s == 0, turn // blocks, lax.rem(turn, 2))
        at = pl.ds(pl.multiple_of(b * rows, rows), rows)

        @pl.when((s == 0) & (turn == 0))
        def _():
            near_rows()

        @pl.when((s == 0) & (turn == 2 * (1 - y)))
        def _():
            for i in range(4):
                relay(i)
            far_rows()

        @pl.when((s == 0) & (turn == blocks))
        def _():
            relay(6)
            relay(7)
            for i in range(6):
                arrived(i)

        @pl.when((s == 1) & (turn == 0))
        def _():
            for i in range(6):
                arrived(i)

        @pl.when((s == 1) & (j == 0))
        def _():
            piece = land.at[1, b, mine]
            remote(piece, piece, ns_sem.at[b], nr_sem.at[b], core).wait_recv()
            remote(piece, piece, nfs_sem.at[b], nfr_sem.at[b], core).start()
            rest = land.at[1, b, theirs]
            remote(rest, rest, nfs_sem.at[b], nfr_sem.at[b], core).wait_recv()

        @pl.when(j == 0)
        def _():
            hidden = land[s, b].astype(F32)
            n1[at] = (hidden * inverse_rms(hidden) * gain_one[...]).astype(BF16)
            lse_cols[b] = jnp.zeros(lse_cols.shape[1:], F32)
            save(0, b, land.at[s, b], h_out.at[b])
            save(1, b, n1.at[at], n1_out.at[at])

        projected = by_last(n1[at], win[j])
        first = j * per
        for i in range(per):
            cut = i * head
            q[first + i, at] = (projected[:, cut : cut + head] * factor).astype(BF16)
            cut += local
            k[first + i, at] = projected[:, cut : cut + head].astype(BF16)
            cut += local
            v[first + i, at] = projected[:, cut : cut + head].astype(BF16)
        for bb in range(blocks):

            @pl.when(b == bb)
            def _():
                for i in range(per):
                    hd = first + i
                    qh = q[hd, bb * rows : (bb + 1) * rows]
                    near = by_last(qh, k[hd, bb * rows : (bb + 1) * rows])
                    near = jnp.where(causal, near, NEGATIVE)
                    top = jnp.max(near, axis=1, keepdims=True)
                    if bb:
                        far = by_last(qh, k[hd, : bb * rows])
                        top = jnp.maximum(top, jnp.max(far, axis=1, keepdims=True))
                    near = jnp.exp(near - top)
                    total = jnp.sum(near, axis=1, keepdims=True)
                    mixed = plain(near.astype(BF16), v[hd, bb * rows : (bb + 1) * rows])
                    if bb:
                        far = jnp.exp(far - top)
                        total = total + jnp.sum(far, axis=1, keepdims=True)
                        mixed = mixed + plain(far.astype(BF16), v[hd, : bb * rows])
                    o_heads[hd, bb * rows : (bb + 1) * rows] = (mixed / total).astype(BF16)
                    lse_cols[bb] = jnp.where(lane == hd, top + jnp.log(total), lse_cols[bb])

        @pl.when(j == 1)
        def _():
            o[at] = jnp.concatenate([o_heads[i, at] for i in range(heads)], axis=1)
            lse[b] = jnp.transpose(lse_cols[b])[:heads]
            save(2, b, q.at[:, at], q_out.at[:, at])
            save(3, b, k.at[:, at], k_out.at[:, at])
            save(4, b, v.at[:, at], v_out.at[:, at])
            save(5, b, o.at[at], o_out.at[at])
            save(6, b, lse.at[b], lse_out.at[b])

        for i, when in ((4, 2), (5, 3), (8, 4), (9, 5)):

            @pl.when((s == 0) & (turn == when))
            def _():
                relay(i)

        for i in range(6):

            @pl.when((s == 1) & (turn == i))
            def _():
                relay(6 + i)

        return 0

    lax.fori_loop(0, 2 * blocks, attention, 0)

    own(3).wait()
    arrived(6)
    arrived(7)

    def project(b, _):
        at = pl.ds(pl.multiple_of(b * rows, rows), rows)
        ysend[b] = plain(o[at], wo[...]).astype(BF16)
        remote(ysend.at[b], yrecv.at[b], ys_sem.at[b], yr_sem.at[b], core).start()
        return 0

    lax.fori_loop(0, blocks, project, 0)

    own(4).wait()
    own(5).wait()
    arrived(8)
    arrived(9)

    @pl.when(s == 0)
    def _():
        for i in range(PIECES):
            down_third(i).wait_recv()

    @pl.when(s == 1)
    def _():
        arrived(10)
        arrived(11)

    weights = [(win, win_out), (wo, wo_out), (wu, wu_out), (wd, wd_out)]
    for i, (src, dst) in enumerate(weights):
        save(11, i, src, dst)

    def feed(b, _):
        at = pl.ds(pl.multiple_of(b * rows, rows), rows)
        remote(ysend.at[b], yrecv.at[b], ys_sem.at[b], yr_sem.at[b], core).wait_recv()
        middle = land[s, b].astype(F32) + (ysend[b].astype(F32) + yrecv[b].astype(F32))
        m[b] = middle
        normed = (middle * inverse_rms(middle) * gain_two[...]).astype(BF16)
        n2[at] = normed
        up = by_last(normed, wu[...])
        u[b] = up
        active = (up / (1.0 + jnp.exp(-up))).astype(BF16)
        a[at] = active
        zpart[b] = plain(active, wd[...])
        copy = remote(zpart.at[b, theirs], zrecv.at[b], zs_sem.at[b], zr_sem.at[b], core)
        copy.start()
        save(7, b, m.at[b], m_out.at[b])
        save(8, b, n2.at[at], n2_out.at[at])
        save(9, b, u.at[b], u_out.at[b])
        save(10, b, a.at[at], a_out.at[at])

        @pl.when(s == 0)
        def _():
            finish(b)

        @pl.when((s == 1) & (b > 0))
        def _():
            finish(b - 1)

        return 0

    def finish(b):
        copy = remote(zpart.at[b, theirs], zrecv.at[b], zs_sem.at[b], zr_sem.at[b], core)
        copy.wait_recv()
        xout[b] = (m[b, mine] + (zpart[b, mine] + zrecv[b])).astype(BF16)

        @pl.when(s == 0)
        def _():
            remote(xout.at[b], land.at[1, b, mine], ns_sem.at[b], nr_sem.at[b], section).start()

        save(13, b, xout.at[b], x_out.at[b])

    lax.fori_loop(0, blocks, feed, 0)

    @pl.when(s == 1)
    def _():
        finish(blocks - 1)


    @pl.when(s == 1)
    def _():
        near_rows()
        far_rows()

    for b in range(blocks):
        pltpu.make_async_copy(land.at[0, b], g_out.at[b], save_sem.at[12, b]).start()

    block = land.at[0, t]
    remote(block, block, xs_sem.at[PIECES], xr_sem.at[t], core).wait_send()
    remote(block, block, xfs_sem, xr_sem.at[t], core).wait_send()

    @pl.when(s == 1)
    def _():
        for i in range(PIECES):
            passing_copy(i).wait_send()
            onward(i).wait_send()
            over(i).wait_send()
            down_second(i).wait_send()
            down_third(i).wait_send()
        for i in range(10, 12):
            crossing(i).wait_send()
            beside_copy(i, parity).wait_send()

    @pl.when(s == 0)
    def _():
        for i in range(PIECES):
            down_first(i).wait_send()

    for b in range(blocks):
        piece = land.at[0, b, mine]
        remote(ysend.at[b], yrecv.at[b], ys_sem.at[b], yr_sem.at[b], core).wait_send()
        remote(zpart.at[b, theirs], zrecv.at[b], zs_sem.at[b], zr_sem.at[b], core).wait_send()

        @pl.when(s == 0)
        def _():
            remote(xout.at[b], piece, ns_sem.at[b], nr_sem.at[b], section).wait_send()

        @pl.when(s == 1)
        def _():
            remote(piece, piece, nfs_sem.at[b], nfr_sem.at[b], core).wait_send()

    for i in range(10):
        crossing(i).wait_send()
        beside_copy(i, parity).wait_send()
    for i, (src, dst) in enumerate(weights):
        pltpu.make_async_copy(src, dst, save_sem.at[11, i]).wait()
    for b in range(blocks):
        at = pl.ds(b * rows, rows)
        saved = [
            (land.at[s, b], h_out.at[b]),
            (n1.at[at], n1_out.at[at]),
            (q.at[:, at], q_out.at[:, at]),
            (k.at[:, at], k_out.at[:, at]),
            (v.at[:, at], v_out.at[:, at]),
            (o.at[at], o_out.at[at]),
            (lse.at[b], lse_out.at[b]),
            (m.at[b], m_out.at[b]),
            (n2.at[at], n2_out.at[at]),
            (u.at[b], u_out.at[b]),
            (a.at[at], a_out.at[at]),
        ]
        for kind, (src, dst) in enumerate(saved):
            pltpu.make_async_copy(src, dst, save_sem.at[kind, b]).wait()
        pltpu.make_async_copy(land.at[0, b], g_out.at[b], save_sem.at[12, b]).wait()
        pltpu.make_async_copy(xout.at[b], x_out.at[b], save_sem.at[13, b]).wait()


def forward(inputs, cotangent, shards, gain_one, gain_two, scale, head):
    _, rows, width = inputs.shape
    local = shards[0].shape[0]
    heads = 2 * local // head
    blocks = lax.axis_size("tensor")
    length = blocks * rows
    half = rows // 2
    shape = jax.ShapeDtypeStruct
    weights = [(2, 3 * local, width), (2 * local, width), (2 * local, width), (2 * local, width)]
    outs = [
        shape((blocks, half, width), BF16),
        shape((blocks, rows, width), BF16),
        shape((length, width), BF16),
        shape((heads, length, head), BF16),
        shape((heads, length, head), BF16),
        shape((heads, length, head), BF16),
        shape((length, 2 * local), BF16),
        shape((blocks, heads, rows), F32),
        shape((blocks, rows, width), F32),
        shape((length, width), BF16),
        shape((blocks, rows, 2 * local), F32),
        shape((length, 2 * local), BF16),
        shape((blocks, rows, width), BF16),
    ] + [shape(w, BF16) for w in weights]
    scratch = [pltpu.VMEM((2, blocks, rows, width), BF16)]
    scratch += [pltpu.VMEM(w, BF16) for w in weights]
    scratch += [
        pltpu.VMEM((rows, width), BF16),
        pltpu.VMEM((local, width), BF16),
        pltpu.VMEM((local, width), BF16),
        pltpu.VMEM((length, width), BF16),
        pltpu.VMEM((heads, length, head), BF16),
        pltpu.VMEM((heads, length, head), BF16),
        pltpu.VMEM((heads, length, head), BF16),
        pltpu.VMEM((heads, length, head), BF16),
        pltpu.VMEM((length, 2 * local), BF16),
        pltpu.VMEM((blocks, rows, 128), F32),
        pltpu.VMEM((blocks, heads, rows), F32),
        pltpu.VMEM((blocks, rows, width), BF16),
        pltpu.VMEM((blocks, rows, width), BF16),
        pltpu.VMEM((blocks, rows, width), F32),
        pltpu.VMEM((length, width), BF16),
        pltpu.VMEM((blocks, rows, 2 * local), F32),
        pltpu.VMEM((length, 2 * local), BF16),
        pltpu.VMEM((blocks, rows, width), F32),
        pltpu.VMEM((blocks, half, width), F32),
        pltpu.VMEM((blocks, half, width), BF16),
        DMA((6,)),
        DMA((2 * PIECES,)),
        DMA((PIECES,)),
        DMA((PIECES + 1,)),
        DMA((PIECES,)),
        DMA((blocks,)),
        DMA,
    ]
    scratch += [DMA((12,))] * 4 + [DMA((PIECES,))] * 6 + [DMA((blocks,))] * 8 + [DMA((14, blocks))]
    return pl.pallas_call(
        forward_kernel,
        out_shape=outs,
        in_specs=[ANY] * 8 + [VMEM] * 3,
        out_specs=[ANY] * len(outs),
        scratch_shapes=scratch,
        compiler_params=pltpu.CompilerParams(
            collective_id=1, has_side_effects=True, vmem_limit_bytes=62 * MIB
        ),
        name="forward",
    )(inputs, cotangent, *shards, gain_one, gain_two, scale)


def backward_kernel(
    g_in, h_in, q_in, k_in, v_in, o_in, lse_in, m_in, u_in, win_in, wo_in, wu_in, wd_in, x_in,
    gain_one, gain_two, scale,
    x_rows, out_rows, final, g_out, gu_out, gy_out, gp_out, dg1, dg2, ds,
    g, win, wo, wu, wd, h, q, k, v, o, lse, m, u, gu, gy, gp, ysend, yrecv, gm, go_heads, gq_heads,
    delta, dk, dv, n1part, n1recv, xout,
    load_sem, w_sem, ns_sem, nr_sem, nfs_sem, nfr_sem, ys_sem, yr_sem, zs_sem, zr_sem, os_sem, or_sem,
    xs_sem, xr_sem, save_sem,
):
    s, t, d = lax.axis_index("section"), lax.axis_index("tensor"), lax.axis_index("dp")
    blocks, rows, width = g.shape
    half = rows // 2
    local = wu.shape[0] // 2
    heads, _, head = q.shape
    per = heads // 2
    c, y = lax.rem(t, 2), t // 2
    core = (s, other(t), d)
    across = (s, lax.rem(t + 2, 4), d)
    diagonal = (s, other(lax.rem(t + 2, 4)), d)
    section = (1 - s, t, d)
    mine = pl.ds(pl.multiple_of(c * half, half), half)
    theirs = pl.ds(pl.multiple_of((1 - c) * half, half), half)

    weights = [(wd_in, wd), (wu_in, wu), (wo_in, wo), (win_in, win)]

    def weight(i):
        return pltpu.make_async_copy(*weights[i], w_sem.at[i])

    def load(kind, b):
        at = pl.ds(pl.multiple_of(b * rows, rows), rows)
        src, dst = [
            (u_in.at[b], u.at[b]),
            (m_in.at[b], m.at[b]),
            (o_in.at[at], o.at[at]),
            (q_in.at[:, at], q.at[:, at]),
            (k_in.at[:, at], k.at[:, at]),
            (v_in.at[:, at], v.at[:, at]),
            (lse_in.at[b], lse.at[b]),
            (h_in.at[b, mine], h.at[b]),
        ][kind]
        return pltpu.make_async_copy(src, dst, load_sem.at[kind, b])

    def incoming(b):
        return pltpu.make_async_copy(g_in.at[b], g.at[b], nr_sem.at[b])

    last = blocks - 1

    @pl.when(s == 1)
    def _():
        incoming(last).start()

    weight(0).start()
    load(0, last).start()
    weight(1).start()
    load(1, last).start()

    barrier = pltpu.get_barrier_semaphore()
    for device in (core, across, diagonal, section):
        pl.semaphore_signal(barrier, inc=1, device_id=device, device_id_type=MESH)

    spot = out_rows.at[y, mine]

    def owner_copy(b, src, dst, send, receive, act):
        @pl.when(b == t)
        def _():
            act(pltpu.make_async_copy(src, dst, receive.at[t]))

        @pl.when(b != t)
        def _():
            act(remote(src, dst, send.at[b], receive.at[t], (s, b, d)))

    dg1[...] = jnp.zeros_like(dg1)
    dg2[...] = jnp.zeros_like(dg2)
    ds[...] = jnp.zeros_like(ds)

    causal = lax.broadcasted_iota(jnp.int32, (rows, rows), 0) <= lax.broadcasted_iota(
        jnp.int32, (rows, rows), 1
    )
    factor = jnp.concatenate([per_dim(scale[...])] * per, axis=1)
    width_two = heads * head
    row_head = lax.broadcasted_iota(jnp.int32, (heads, width_two), 0)
    start = row_head * head
    place = lax.broadcasted_iota(jnp.int32, (heads, width_two), 1)
    member = jnp.where((place >= start) & (place < start + head), 1.0, 0.0)

    def save(kind, b, src, dst):
        pltpu.make_async_copy(src, dst, save_sem.at[kind, b]).start()

    def neighbours_sum(b):
        return remote(ysend.at[b], yrecv.at[b], ys_sem.at[b], yr_sem.at[b], core)

    def up_part(turn):
        b = last - turn
        at = pl.ds(pl.multiple_of(b * rows, rows), rows)

        @pl.when(s == 1)
        def _():
            incoming(b).wait()

        @pl.when(turn == 0)
        def _():
            pl.semaphore_wait(barrier, 4)

        @pl.when(s == 0)
        def _():
            piece = g.at[b, mine]
            remote(piece, piece, ns_sem.at[b], nr_sem.at[b], core).wait_recv()
            remote(piece, piece, nfs_sem.at[b], nfr_sem.at[b], core).start()
            rest = g.at[b, theirs]
            remote(rest, rest, nfs_sem.at[b], nfr_sem.at[b], core).wait_recv()

        @pl.when(turn == 0)
        def _():
            weight(0).wait()

        load(0, b).wait()
        save(0, b, g.at[b], g_out.at[at])
        grad = g[b]
        grad_act = by_last(grad, wd[...])
        up = u[b]
        sigma = 1.0 / (1.0 + jnp.exp(-up))
        grad_up = (grad_act * sigma * (1.0 + up * (1.0 - sigma))).astype(BF16)
        gu[at] = grad_up

        @pl.when(turn == 0)
        def _():
            weight(1).wait()
            weight(2).start()
            for kind in (2, 3, 6):
                load(kind, last).start()
            for bb in reversed(range(blocks)):
                load(4, bb).start()
                load(5, bb).start()

        save(1, b, gu.at[at], gu_out.at[at])
        ysend[b] = plain(grad_up, wu[...]).astype(BF16)
        neighbours_sum(b).start()

        @pl.when(turn == 0)
        def _():
            for bb in range(blocks):
                owner_copy(
                    bb, x_in.at[bb], x_rows.at[y, mine], xs_sem, xr_sem, lambda copy: copy.start()
                )

    def one_block(turn, _):
        b = last - turn
        at = pl.ds(pl.multiple_of(b * rows, rows), rows)
        load(1, b).wait()
        neighbours_sum(b).wait_recv()
        grad = g[b]
        grad_normed = ysend[b].astype(F32) + yrecv[b].astype(F32)
        middle = m[b]
        inverse = inverse_rms(middle)
        unit = middle * inverse
        grad_unit = grad_normed * gain_two[...]
        dg2[...] += jnp.sum(grad_normed * unit, axis=0, keepdims=True)
        grad_middle = grad.astype(F32) + inverse * (
            grad_unit - unit * jnp.mean(grad_unit * unit, axis=1, keepdims=True)
        )
        gm[...] = grad_middle
        grad_mid = grad_middle.astype(BF16)
        gy[at] = grad_mid
        save(2, b, gy.at[at], gy_out.at[at])

        @pl.when(turn == 0)
        def _():
            weight(2).wait()
            weight(3).start()
            load(7, last).start()

        load(2, b).wait()
        grad_mixed = by_last(grad_mid, wo[...]).astype(BF16)
        both = grad_mixed.astype(F32) * o[at].astype(F32)
        delta[...] = lax.dot_general(
            member,
            both,
            (((1,), (1,)), ((), ())),
            precision=lax.Precision.HIGHEST,
            preferred_element_type=F32,
        )
        for i in range(heads):
            go_heads[i] = grad_mixed[:, i * head : (i + 1) * head]

        @pl.when(turn == 0)
        def _():
            for bb in range(blocks):
                load(4, bb).wait()
                load(5, bb).wait()

        load(3, b).wait()
        load(6, b).wait()

        @pl.when(turn < last)
        def _():
            for kind in (0, 1, 2, 3, 6, 7):
                load(kind, b - 1).start()

        @pl.when((turn < last) & (s == 1))
        def _():
            incoming(b - 1).start()

        for bb in range(blocks):

            @pl.when(b == bb)
            def _():
                def group(first, _):
                    for j in range(per):
                        i = first * per + j
                        qh = q[i, bb * rows : (bb + 1) * rows]
                        gh = go_heads[i]
                        offset = lse[bb, pl.ds(i, 1)]
                        inner = delta[pl.ds(i, 1)]
                        total = None
                        for lo, hi in ((bb * rows, (bb + 1) * rows), (0, bb * rows)):
                            if lo == hi:
                                continue
                            kj = k[i, lo:hi]
                            weight = jnp.exp(by_last(kj, qh) - offset)
                            if lo == bb * rows and hi > lo and hi == (bb + 1) * rows:
                                weight = jnp.where(causal, weight, 0.0)
                            grad_score = weight * (by_last(v[i, lo:hi], gh) - inner)
                            grad_score = grad_score.astype(BF16)
                            more_v = plain(weight.astype(BF16), gh)
                            more_k = plain(grad_score, qh)
                            if bb == last:
                                dv[i, lo:hi] = more_v
                                dk[i, lo:hi] = more_k
                            else:
                                dv[i, lo:hi] += more_v
                                dk[i, lo:hi] += more_k
                            part = by_first(kj, grad_score)
                            total = part if total is None else total + part
                        gq_heads[i] = jnp.transpose(total)
                    return 0

                lax.fori_loop(0, 2, group, 0)

        for j in range(2):
            mine_heads = range(j * per, (j + 1) * per)
            grad_scaled = jnp.concatenate([gq_heads[i] for i in mine_heads], axis=1)
            queries = jnp.concatenate([q[i, at] for i in mine_heads], axis=1).astype(F32)
            ds[pl.ds(j, 1)] += jnp.sum(grad_scaled * queries, axis=0, keepdims=True)
            grads = [
                (grad_scaled * factor).astype(BF16),
                jnp.concatenate([dk[i, at] for i in mine_heads], axis=1).astype(BF16),
                jnp.concatenate([dv[i, at] for i in mine_heads], axis=1).astype(BF16),
            ]
            gp[j, at] = jnp.concatenate(grads, axis=1)
        save(3, b, gp.at[:, at], gp_out.at[:, at])

        @pl.when(turn == 0)
        def _():
            weight(3).wait()

        n1part[...] = plain(gp[0, at], win[0]) + plain(gp[1, at], win[1])
        copy = remote(n1part.at[theirs], n1recv.at[b], zs_sem.at[b], zr_sem.at[b], core)
        copy.start()

        @pl.when(turn < last)
        def _():
            up_part(turn + 1)

        load(7, b).wait()
        hidden = h[b].astype(F32)
        inverse = inverse_rms(hidden)
        unit = hidden * inverse
        copy.wait_recv()
        grad_normed = n1part[mine] + n1recv[b]
        grad_unit = grad_normed * gain_one[...]
        dg1[...] += jnp.sum(grad_normed * unit, axis=0, keepdims=True)
        xout[b] = (
            gm[mine]
            + inverse * (grad_unit - unit * jnp.mean(grad_unit * unit, axis=1, keepdims=True))
        ).astype(BF16)

        @pl.when(s == 1)
        def _():
            remote(xout.at[b], g.at[b, mine], ns_sem.at[b], nr_sem.at[b], section).start()

        @pl.when(b > 0)
        def _():
            owner_copy(b, xout.at[b], spot, os_sem, or_sem, lambda copy: copy.start())

        @pl.when(b == 0)
        def _():
            save(4, 0, xout.at[0], final)

        copy.wait_send()
        return 0

    up_part(jnp.int32(0))
    lax.fori_loop(0, blocks, one_block, 0)

    for b in range(blocks):
        at = pl.ds(b * rows, rows)
        piece = g.at[b, mine]
        remote(ysend.at[b], yrecv.at[b], ys_sem.at[b], yr_sem.at[b], core).wait_send()
        here = x_rows.at[b // 2, pl.ds((b % 2) * half, half)]
        remote(here, here, xs_sem.at[b], xr_sem.at[b], core).wait_recv()

        @pl.when(b != t)
        def _():
            remote(x_in.at[b], here, xs_sem.at[b], xr_sem.at[b], core).wait_send()

        @pl.when(t > 0)
        def _():
            here = out_rows.at[b // 2, pl.ds((b % 2) * half, half)]
            remote(here, here, os_sem.at[b], or_sem.at[b], core).wait_recv()

        @pl.when((b != t) & (b > 0))
        def _():
            remote(xout.at[b], here, os_sem.at[b], or_sem.at[b], core).wait_send()

        @pl.when(s == 1)
        def _():
            remote(xout.at[b], piece, ns_sem.at[b], nr_sem.at[b], section).wait_send()

        @pl.when(s == 0)
        def _():
            remote(piece, piece, nfs_sem.at[b], nfr_sem.at[b], core).wait_send()

        saved = [
            (g.at[b], g_out.at[at]),
            (gu.at[at], gu_out.at[at]),
            (gy.at[at], gy_out.at[at]),
            (gp.at[:, at], gp_out.at[:, at]),
        ]
        for kind, (src, dst) in enumerate(saved):
            pltpu.make_async_copy(src, dst, save_sem.at[kind, b]).wait()
    pltpu.make_async_copy(xout.at[0], final, save_sem.at[4, 0]).wait()


def backward(saved, gain_one, gain_two, scale):
    g_in, h_in, q_in = saved[:3]
    win_in, wo_in, wu_in, wd_in = saved[9:13]
    blocks, rows, width = g_in.shape
    heads, length, head = q_in.shape
    local = wu_in.shape[0] // 2
    half = rows // 2
    shape = jax.ShapeDtypeStruct
    outs = [
        shape((2, rows, width), BF16),
        shape((2, rows, width), BF16),
        shape((half, width), BF16),
        shape((length, width), BF16),
        shape((length, 2 * local), BF16),
        shape((length, width), BF16),
        shape((2, length, 3 * local), BF16),
        shape((1, width), F32),
        shape((1, width), F32),
        shape((2, local), F32),
    ]
    scratch = [
        pltpu.VMEM((blocks, rows, width), BF16),
        pltpu.VMEM(win_in.shape, BF16),
        pltpu.VMEM(wo_in.shape, BF16),
        pltpu.VMEM(wu_in.shape, BF16),
        pltpu.VMEM(wd_in.shape, BF16),
        pltpu.VMEM((blocks, half, width), BF16),
        pltpu.VMEM((heads, length, head), BF16),
        pltpu.VMEM((heads, length, head), BF16),
        pltpu.VMEM((heads, length, head), BF16),
        pltpu.VMEM((length, 2 * local), BF16),
        pltpu.VMEM((blocks, heads, rows), F32),
        pltpu.VMEM((blocks, rows, width), F32),
        pltpu.VMEM((blocks, rows, 2 * local), F32),
        pltpu.VMEM((length, 2 * local), BF16),
        pltpu.VMEM((length, width), BF16),
        pltpu.VMEM((2, length, 3 * local), BF16),
        pltpu.VMEM((blocks, rows, width), BF16),
        pltpu.VMEM((blocks, rows, width), BF16),
        pltpu.VMEM((rows, width), F32),
        pltpu.VMEM((heads, rows, head), BF16),
        pltpu.VMEM((heads, rows, head), F32),
        pltpu.VMEM((heads, rows), F32),
        pltpu.VMEM((heads, length, head), F32),
        pltpu.VMEM((heads, length, head), F32),
        pltpu.VMEM((rows, width), F32),
        pltpu.VMEM((blocks, half, width), F32),
        pltpu.VMEM((blocks, half, width), BF16),
        DMA((8, blocks)),
        DMA((4,)),
    ]
    scratch += [DMA((blocks,))] * 12 + [DMA((5, blocks))]
    return pl.pallas_call(
        backward_kernel,
        out_shape=outs,
        in_specs=[ANY] * 14 + [VMEM] * 3,
        out_specs=[ANY] * 7 + [VMEM] * 3,
        scratch_shapes=scratch,
        compiler_params=pltpu.CompilerParams(
            collective_id=2, has_side_effects=True, vmem_limit_bytes=62 * MIB
        ),
        name="backward",
    )(*saved, gain_one, gain_two, scale)


def farthest_first(d, k, n):
    found = 0
    for i in range(n):
        above = list(range(n - 1, i, -1))
        below = list(range(i))
        first, second = (above, below) if len(above) >= len(below) else (below, above)
        lead = len(first) - len(second) - 1
        order = first[: max(lead, 0)]
        rest = first[max(lead, 0) :]
        for j in range(max(len(rest), len(second))):
            order += rest[j : j + 1] + second[j : j + 1]
        order.append(i)
        picked = 0
        for j, e in enumerate(order):
            picked = picked + jnp.where(k == j, e, 0)
        found = found + jnp.where(d == i, picked, 0)
    return found


def gradient_kernel(
    n1_in, n2_in, gy_in, g_in, gp_in, gu_in, o_in, a_in, final, rows_in, dg1, dg2, ds, dim_scale,
    q_out, k_out, v_out, u_out, o_out, d_out, rows_out, out_g1, out_g2, out_s,
    out_q, out_k, out_v, out_u, out_o, out_d, x, xt, gp, gu, o, a,
    keep_a, give_a, yrecv_a, flow_a, last_a, keep_b, give_b, yrecv_b, flow_b, last_b,
    line, flow_d, last_d, rest, yd, small, smalls, chain, out_rows_a, out_rows_b,
    x_sem, g_sem, ys_sem, yr_sem, fs_sem, fr_sem, last_sem, ds_sem, dr_sem, last_d_sem,
    yds_sem, ydr_sem, ss_sem, sr_sem, cs_sem, cr_sem, es_sem, er_sem, out_sem, rs_sem, hop_sem, here_sem,
):
    s, t, d = lax.axis_index("section"), lax.axis_index("tensor"), lax.axis_index("dp")
    n, chunk, _ = keep_a.shape
    local = a.shape[1] // 2
    split = yd.shape[1]
    width = dg1.shape[1]
    pieces = ys_sem.shape[2]
    step = chunk // pieces
    core = (s, other(t), d)
    across = (s, lax.rem(t + 2, 4), d)
    diagonal = (s, other(lax.rem(t + 2, 4)), d)
    up = (s, t, lax.rem(d + 1, n))
    down = (s, t, lax.rem(d + n - 1, n))
    c, y = lax.rem(t, 2), t // 2

    sources = [g_in, n1_in, n2_in, gy_in]
    operands = [(a_in, a), (gp_in, gp), (gu_in, gu), (o_in, o)]

    def load(i):
        return pltpu.make_async_copy(sources[i], x.at[i % 2], x_sem.at[i])

    def operand(i):
        return pltpu.make_async_copy(*operands[i], g_sem.at[i])

    section = (1 - s, t, d)
    slanted = (1 - s, 1 - t, d)
    barrier = pltpu.get_barrier_semaphore()
    for device in (core, across, diagonal, up, down):
        pl.semaphore_signal(barrier, inc=1, device_id=device, device_id_type=MESH)

    @pl.when((s == 1) & (t != 1))
    def _():
        pl.semaphore_signal(barrier, inc=1, device_id=section, device_id_type=MESH)

    @pl.when((s == 1) & (t == 1))
    def _():
        pl.semaphore_signal(barrier, inc=1, device_id=slanted, device_id_type=MESH)

    load(0).start()
    operand(0).start()
    load(1).start()
    for i in range(1, 4):
        operand(i).start()

    small[0:1, :width] = dg1[...]
    small[0:1, width : 2 * width] = jnp.where(c == 0, dg2[...], 0.0)
    small[0:1, 2 * width : 2 * width + local] = ds[0:1]
    small[0:1, 2 * width + 384 : 2 * width + 384 + local] = ds[1:2]

    partners = [core, across, diagonal]

    def share(i):
        return remote(small, smalls.at[i], ss_sem.at[i], sr_sem.at[i], partners[i])

    def turn(i):
        load(i).wait()
        turned = jnp.transpose(x[i % 2])
        for e in range(n):
            xt[i, e] = turned[e * chunk : (e + 1) * chunk]
        if i + 2 < 4:
            load(i + 2).start()

    groups = [(keep_a, give_a, yrecv_a, flow_a, last_a), (keep_b, give_b, yrecv_b, flow_b, last_b)]

    def exchange(which, e, i):
        _, give, yrecv, _, _ = groups[which]
        rows = pl.ds(i * step, step)
        return remote(
            give.at[e, rows], yrecv.at[e, rows], ys_sem.at[which, e, i], yr_sem.at[which, e, i], across
        )

    def send_all(which, e):
        for i in range(pieces):
            exchange(which, e, i).start()

    def send_d(e):
        src = line.at[e]

        @pl.when(e > d)
        def _():
            remote(src, flow_d.at[e], ds_sem.at[e], dr_sem.at[e], up).start()

        @pl.when(e < d - 1)
        def _():
            remote(src, flow_d.at[e], ds_sem.at[e], dr_sem.at[e], down).start()

        @pl.when(e == d - 1)
        def _():
            remote(src, last_d, ds_sem.at[e], last_d_sem, down).start()

    def upstream_d(e):
        piece = flow_d.at[e]
        remote(piece, piece, ds_sem.at[e], dr_sem.at[e], up).wait_recv()
        line[e] = (line[e].astype(F32) + flow_d[e].astype(F32)).astype(BF16)

    def down_product(k):
        e = farthest_first(d, k, n)
        both = plain(xt[0, e], a[...]).astype(BF16)
        line[e] = jnp.concatenate([both[:, :split], both[:, local : local + split]], axis=1)
        for j in range(2):
            rest[j, e] = both[:, j * local + split : (j + 1) * local]

    def first_d(k):
        e = farthest_first(d, k, n)

        @pl.when(((d == 0) | (d == n - 1)) & (e != d))
        def _():
            send_d(e)

    def in_product(k, j):
        e = farthest_first(d, k, n)
        (keep_a, give_a)[j][e] = jnp.concatenate(
            [plain(xt[1, e], gp[j]).astype(BF16), rest[j, e]], axis=1
        )

    turn(0)
    operand(0).wait()
    down_product(0)
    turn(1)
    operand(1).wait()
    in_product(0, 1)

    heard = jnp.where(s == 0, jnp.where(t == 0, 2, jnp.where(t == 1, 0, 1)), 0)
    pl.semaphore_wait(barrier, 5 + heard)

    @pl.when((s == 0) & (t == 0))
    def _():
        pl.semaphore_signal(here_sem, inc=1, device_id=section, device_id_type=MESH)
        pl.semaphore_signal(here_sem, inc=1, device_id=slanted, device_id_type=MESH)

    send_all(0, farthest_first(d, 0, n))
    first_d(0)
    for i in range(3):
        share(i).start()

    half = final.shape[0]
    owner = (s, 0, d)
    spot = rows_out.at[y, pl.ds(pl.multiple_of(c * half, half), half)]

    @pl.when(t == 0)
    def _():
        pltpu.make_async_copy(final, spot, er_sem.at[0]).start()

    direct = (t == 1) | ((t > 1) & (s == 1))
    aside = (t > 1) & (s == 0)

    @pl.when(t == 1)
    def _():
        remote(final, spot, es_sem, er_sem.at[t], owner).start()

    @pl.when(aside)
    def _():
        remote(final, out_rows_a, es_sem, rs_sem.at[0], section).start()

    def more_down(k, _):
        down_product(k)
        first_d(k)
        return 0

    lax.fori_loop(1, n, more_down, 0)

    def more_in(k, _):
        in_product(k, 1)
        send_all(0, farthest_first(d, k, n))
        in_product(k, 0)
        return 0

    lax.fori_loop(1, n, more_in, 0)
    in_product(0, 0)

    turn(2)
    turn(3)
    operand(2).wait()
    operand(3).wait()

    def other_product(k, _):
        e = farthest_first(d, k, n)
        ups = plain(xt[2, e], gu[...])
        outs = plain(xt[3, e], o[...])
        for j, target in ((1, give_b), (0, keep_b)):
            cut = slice(j * local, (j + 1) * local)
            target[e] = jnp.concatenate([ups[:, cut], outs[:, cut]], axis=1).astype(BF16)
            if j:
                send_all(1, e)
        return 0

    lax.fori_loop(0, n, other_product, 0)

    @pl.when((t > 1) & (s == 1))
    def _():
        remote(final, spot, es_sem, er_sem.at[t], owner).start()

    for i in range(3):
        share(i).wait_recv()
    mine = small[...] + smalls[0] + (smalls[1] + smalls[2])

    def link(i, device):
        return remote(chain.at[i], chain.at[2 + i], cs_sem.at[i], cr_sem.at[i], device)

    smalls[0] = mine
    for i, opens, closes, device in ((0, d == 0, d == n - 1, up), (1, d == n - 1, d == 0, down)):
        chain[i] = mine

        @pl.when(jnp.logical_not(opens))
        def _():
            link(i, device).wait_recv()
            chain[i] = mine + chain[2 + i]
            smalls[0] += chain[2 + i]

        @pl.when(jnp.logical_not(closes))
        def _():
            link(i, device).start()

    def middle(k):
        e = farthest_first(d, k, n)

        @pl.when((d > 0) & (d < n - 1) & (e != d))
        def _():
            upstream_d(e)
            send_d(e)

    def flows(which, k):
        e = farthest_first(d, k, n)
        keep, give, yrecv, flow, last = groups[which]
        send, receive = fs_sem.at[which], fr_sem.at[which]
        for i in range(pieces):
            at = pl.ds(i * step, step)
            exchange(which, e, i).wait_recv()
            first = ((e > d) & (d == 0)) | ((e < d) & (d == n - 1))

            @pl.when((e != d) & first)
            def _():
                keep[e, at] = (keep[e, at].astype(F32) + yrecv[e, at].astype(F32)).astype(BF16)

            @pl.when((e != d) & jnp.logical_not(first))
            def _():
                piece = flow.at[e, at]
                remote(piece, piece, send.at[e, i], receive.at[e, i], up).wait_recv()
                total = keep[e, at].astype(F32) + yrecv[e, at].astype(F32)
                keep[e, at] = (total + flow[e, at].astype(F32)).astype(BF16)

            src = keep.at[e, at]

            @pl.when(e > d)
            def _():
                remote(src, flow.at[e, at], send.at[e, i], receive.at[e, i], up).start()

            @pl.when(e < d - 1)
            def _():
                remote(src, flow.at[e, at], send.at[e, i], receive.at[e, i], down).start()

            @pl.when(e == d - 1)
            def _():
                remote(src, last.at[at], send.at[e, i], last_sem.at[which, i], down).start()

    def flows_in(k, _):
        middle(k)
        flows(0, k)
        return 0

    def flows_other(k, _):
        flows(1, k)
        return 0

    lax.fori_loop(0, n, flows_in, 0)

    @pl.when(d > 0)
    def _():
        upstream_d(d)

    @pl.when(d < n - 1)
    def _():
        remote(last_d, last_d, ds_sem.at[0], last_d_sem, down).wait_recv()
        line[d] = (line[d].astype(F32) + last_d[...].astype(F32)).astype(BF16)

    crossing = remote(line.at[d, :, pl.ds(split, split)], yd, yds_sem, ydr_sem, across)
    crossing.start()

    lax.fori_loop(0, n, flows_other, 0)

    second = remote(out_rows_a, out_rows_b, hop_sem.at[0], rs_sem.at[1], across)
    mine_half = pl.ds(pl.multiple_of(c * half, half), half)
    third_dst = rows_out.at[1, mine_half]

    def third(device):
        return remote(out_rows_b, third_dst, hop_sem.at[1], er_sem.at[2 + c], device)

    @pl.when((s == 1) & (t > 1))
    def _():
        remote(out_rows_a, out_rows_a, hop_sem.at[0], rs_sem.at[0], section).wait_recv()
        second.start()

    @pl.when((s == 1) & (t < 2))
    def _():
        second.wait_recv()
        pl.semaphore_wait(here_sem, 1)

    @pl.when((s == 1) & (t == 0))
    def _():
        third(section).start()

    @pl.when((s == 1) & (t == 1))
    def _():
        third(slanted).start()

    def landed(which, i):
        keep, _, yrecv, flow, last = groups[which]
        at = pl.ds(i * step, step)

        @pl.when(d > 0)
        def _():
            piece = flow.at[d, at]
            remote(
                piece, piece, fs_sem.at[which, d, i], fr_sem.at[which, d, i], up
            ).wait_recv()

        @pl.when(d < n - 1)
        def _():
            piece = last.at[at]
            remote(
                piece, piece, fs_sem.at[which, d, i], last_sem.at[which, i], down
            ).wait_recv()

        above = jnp.where(d > 0, flow[d, at].astype(F32), 0.0)
        below = jnp.where(d < n - 1, last[at].astype(F32), 0.0)
        return (keep[d, at].astype(F32) + yrecv[d, at].astype(F32)) + (above + below)

    results = [
        pltpu.make_async_copy(src, dst, out_sem.at[i])
        for i, (src, dst) in enumerate(
            ((out_q, q_out), (out_k, k_out), (out_v, v_out), (out_u, u_out), (out_o, o_out), (out_d, d_out))
        )
    ]
    rests = []
    for i in range(pieces):
        at = pl.ds(i * step, step)
        total = landed(0, i)
        for j, ref in enumerate((out_q, out_k, out_v)):
            ref[at] = total[:, j * local : (j + 1) * local]
        rests.append(total[:, 3 * local :])
    for i in range(3):
        results[i].start()
    crossing.wait_recv()
    most = line[d, :, :split].astype(F32) + yd[...].astype(F32)
    out_d[...] = jnp.transpose(jnp.concatenate([most, jnp.concatenate(rests, axis=0)], axis=1))
    results[5].start()
    found = smalls[0]
    out_g1[...] = found[0:1, :width]
    out_g2[...] = found[0:1, width : 2 * width]
    head = dim_scale.shape[1]
    scale = jnp.zeros((1, head), F32)
    for j in range(2):
        for i in range(local // head):
            start = 2 * width + j * 384 + i * head
            scale = scale + found[0:1, start : start + head]
    raw = dim_scale[...]
    grown = jnp.maximum(raw, 0.0) + jnp.log(1.0 + jnp.exp(-jnp.abs(raw)))
    out_s[...] = scale / grown * (1.0 / (1.0 + jnp.exp(-raw)))
    totals = []
    for i in range(pieces):
        total = landed(1, i)
        out_u[pl.ds(i * step, step)] = total[:, :local]
        totals.append(total[:, local:])
    results[3].start()
    out_o[...] = jnp.transpose(jnp.concatenate(totals, axis=0))
    results[4].start()

    @pl.when(t == 0)
    def _():
        for i in range(4):
            piece = rows_out.at[i // 2, pl.ds(i % 2 * half, half)]
            remote(piece, piece, es_sem, er_sem.at[i], owner).wait_recv()

    @pl.when(direct)
    def _():
        remote(final, spot, es_sem, er_sem.at[t], owner).wait_send()

    @pl.when(aside)
    def _():
        remote(final, out_rows_a, es_sem, rs_sem.at[0], section).wait_send()

    @pl.when((s == 1) & (t > 1))
    def _():
        second.wait_send()

    @pl.when((s == 1) & (t < 2))
    def _():
        third(section).wait_send()

    for copy in results:
        copy.wait()
    crossing.wait_send()
    for i in range(3):
        share(i).wait_send()

    @pl.when(d < n - 1)
    def _():
        link(0, up).wait_send()

    @pl.when(d > 0)
    def _():
        link(1, down).wait_send()

    def drain(e, _):
        for which in range(2):
            for i in range(pieces):
                exchange(which, e, i).wait_send()

        @pl.when(e != d)
        def _():
            for which in range(2):
                for i in range(pieces):
                    piece = groups[which][0].at[e, pl.ds(i * step, step)]
                    remote(
                        piece, piece, fs_sem.at[which, e, i], fr_sem.at[which, e, i], up
                    ).wait_send()
            remote(line.at[e], line.at[e], ds_sem.at[e], dr_sem.at[e], up).wait_send()

        return 0

    lax.fori_loop(0, n, drain, 0)


def gradients(n1, n2, gy, g, gp, gu, o, a, final, rows, dg1, dg2, ds, dim_scale):
    n = lax.axis_size("dp")
    length, width = n1.shape
    local = gp.shape[2] // 3
    chunk = width // n
    pieces = 4 if chunk % 64 == 0 else 1
    small = (1, 2 * width + 768)

    def lines(columns):
        return [pltpu.VMEM((n, chunk, columns), BF16)] * 4 + [pltpu.VMEM((chunk, columns), BF16)]

    split = local // 128 * 128
    line = pltpu.VMEM((n, chunk, 2 * split), BF16)
    return pl.pallas_call(
        gradient_kernel,
        out_shape=[jax.ShapeDtypeStruct((chunk, local), F32)] * 4
        + [jax.ShapeDtypeStruct((local, chunk), F32)] * 2
        + [
            jax.ShapeDtypeStruct(rows.shape, BF16),
            jax.ShapeDtypeStruct(dg1.shape, F32),
            jax.ShapeDtypeStruct(dg2.shape, F32),
            jax.ShapeDtypeStruct(dim_scale.shape, F32),
        ],
        in_specs=[ANY] * 10 + [VMEM] * 4,
        out_specs=[ANY] * 7 + [VMEM] * 3,
        input_output_aliases={9: 6},
        scratch_shapes=[pltpu.VMEM((chunk, local), F32)] * 4
        + [pltpu.VMEM((local, chunk), F32)] * 2
        + [
            pltpu.VMEM((2, length, width), BF16),
            pltpu.VMEM((4, n, chunk, length), BF16),
            pltpu.VMEM(gp.shape, BF16),
            pltpu.VMEM(gu.shape, BF16),
            pltpu.VMEM(o.shape, BF16),
            pltpu.VMEM(a.shape, BF16),
        ]
        + lines(4 * local - split)
        + lines(2 * local)
        + [line] * 2
        + [
            pltpu.VMEM((chunk, 2 * split), BF16),
            pltpu.VMEM((2, n, chunk, local - split), BF16),
            pltpu.VMEM((chunk, split), BF16),
            pltpu.VMEM(small, F32),
            pltpu.VMEM((3,) + small, F32),
            pltpu.VMEM((4,) + small, F32),
            pltpu.VMEM(final.shape, BF16),
            pltpu.VMEM(final.shape, BF16),
            DMA((4,)),
            DMA((4,)),
        ]
        + [DMA((2, n, pieces))] * 4
        + [
            DMA((2, pieces)),
            DMA((n,)),
            DMA((n,)),
            DMA,
            DMA,
            DMA,
            DMA((3,)),
            DMA((3,)),
            DMA((2,)),
            DMA((2,)),
            DMA,
            DMA((4,)),
            DMA((6,)),
            DMA((2,)),
            DMA((2,)),
            pltpu.SemaphoreType.REGULAR,
        ],
        compiler_params=pltpu.CompilerParams(
            collective_id=3, has_side_effects=True, vmem_limit_bytes=62 * MIB
        ),
        name="gradients",
    )(n1, n2, gy, g, gp, gu, o, a, final, rows, dg1, dg2, ds, dim_scale)


def hand_over_kernel(*refs):
    count = (len(refs) - 2) // 3
    sources, results, kept = refs[:count], refs[count : 2 * count], refs[2 * count : 3 * count]
    in_sem, out_sem = refs[3 * count :]
    come = [pltpu.make_async_copy(sources[i], kept[i], in_sem.at[i]) for i in range(count)]
    go = [pltpu.make_async_copy(kept[i], results[i], out_sem.at[i]) for i in range(count)]
    for copy in come:
        copy.start()
    for i in range(count):
        come[i].wait()
        go[i].start()
    for copy in go:
        copy.wait()


def hand_over(arrays):
    count = len(arrays)
    return pl.pallas_call(
        hand_over_kernel,
        out_shape=[jax.ShapeDtypeStruct(x.shape, x.dtype) for x in arrays],
        in_specs=[ANY] * count,
        out_specs=[ANY] * count,
        scratch_shapes=[pltpu.VMEM(x.shape, x.dtype) for x in arrays] + [DMA((count,)), DMA((count,))],
        compiler_params=pltpu.CompilerParams(vmem_limit_bytes=62 * MIB),
        name="hand_over",
    )(*arrays)


def body(
    inputs, cotangent, gain_attn, w_query, w_key, w_value, w_out, dim_scale, gain_mlp, w_up, w_down
):
    head = dim_scale.shape[1]
    shards = (w_query[0].T, w_key[0].T, w_value[0].T, w_out[0], w_up[0].T, w_down[0])
    done = forward(
        inputs, cotangent, shards, gain_attn, gain_mlp, dim_scale, head
    )
    x_halves, h, n1, q, k, v, o, lse, m, n2, u, a, g, win, wo, wu, wd = done
    layer_out, input_grads, final, g_all, gu, gy, gp, dg1, dg2, ds = backward(
        (g, h, q, k, v, o, lse, m, u, win, wo, wu, wd, x_halves),
        gain_attn,
        gain_mlp,
        dim_scale,
    )

    *pieces, input_grads, dg1, dg2, grad_scale = gradients(
        n1, n2, gy, g_all, gp, gu, o, a, final, input_grads, dg1, dg2, ds, dim_scale
    )
    results = hand_over([layer_out, input_grads, dg1, *pieces, grad_scale, dg2])
    layer_out, input_grads, dg1, *pieces, grad_scale, dg2 = results
    return (
        layer_out[None],
        input_grads[None],
        dg1,
        pieces[0][None],
        pieces[1][None],
        pieces[2][None],
        pieces[4][None],
        grad_scale,
        dg2,
        pieces[3][None],
        pieces[5][None],
    )


def solution(mesh):
    in_specs = (
        P("dp", "tensor", None),
        P("dp", "tensor", None),
        P("section", None),
        P("section", None, "tensor"),
        P("section", None, "tensor"),
        P("section", None, "tensor"),
        P("section", "tensor", None),
        P("section", None),
        P("section", None),
        P("section", None, "tensor"),
        P("section", "tensor", None),
    )
    out_specs = (
        P("section", "dp", "tensor", None),
        P("section", "dp", "tensor", None),
        P("section", None),
        P("section", "dp", "tensor"),
        P("section", "dp", "tensor"),
        P("section", "dp", "tensor"),
        P("section", "tensor", "dp"),
        P("section", None),
        P("section", None),
        P("section", "dp", "tensor"),
        P("section", "tensor", "dp"),
    )
    return jax.shard_map(body, mesh=mesh, in_specs=in_specs, out_specs=out_specs, check_vma=False)
```

```python
import functools
import math

import jax
import jax.numpy as jnp
from jax import lax
from jax.experimental import pallas as pl
from jax.experimental.pallas import tpu as pltpu
from jax.sharding import PartitionSpec as P

EPS = 1e-06
LOG2E = 1.442695041
NEGATIVE = -1e30
BF16 = jnp.bfloat16
F32 = jnp.float32
MESH = pl.DeviceIdType.MESH
ANY = pl.BlockSpec(memory_space=pl.ANY)
VMEM = pl.BlockSpec(memory_space=pltpu.VMEM)
DMA = pltpu.SemaphoreType.DMA
MIB = 1 << 20
PIECES = 4


def plain(a, b):
    return jnp.dot(a, b, preferred_element_type=F32)


def by_last(a, b):
    return lax.dot_general(a, b, (((1,), (1,)), ((), ())), preferred_element_type=F32)


def by_first(a, b):
    return lax.dot_general(a, b, (((0,), (0,)), ((), ())), preferred_element_type=F32)


def other(index):
    return index + 1 - 2 * lax.rem(index, 2)


def remote(src, dst, send, receive, device):
    return pltpu.make_async_remote_copy(
        src_ref=src,
        dst_ref=dst,
        send_sem=send,
        recv_sem=receive,
        device_id=device,
        device_id_type=MESH,
    )


def greet(devices):
    barrier = pltpu.get_barrier_semaphore()
    for device in devices:
        pl.semaphore_signal(barrier, inc=1, device_id=device, device_id_type=MESH)
    pl.semaphore_wait(barrier, len(devices))


def per_dim(raw):
    grown = jnp.maximum(raw, 0.0) + jnp.log(1.0 + jnp.exp(-jnp.abs(raw)))
    return (LOG2E / math.sqrt(raw.shape[1])) * grown


def inverse_rms(rows):
    return lax.rsqrt(jnp.mean(rows * rows, axis=1, keepdims=True) + EPS)


def forward_kernel(
    inputs, cotangent, w_q, w_k, w_v, w_o, w_u, w_d, gain_one, gain_two, scale,
    x_out, h_out, n1_out, q_out, k_out, v_out, o_out, lse_out, m_out, n2_out, u_out, a_out,
    g_out, win_out, wo_out, wu_out, wd_out,
    land, win, wo, wu, wd, passing, down_a, down_b, n1, q, k, v, o_heads, o, lse_cols, lse, ysend, yrecv,
    m, n2, u, a, zpart, zrecv, xout,
    own_sem, ps_sem, pr_sem, xs_sem, xp_sem, xr_sem, xfs_sem, wys_sem, wyr_sem, wzs_sem, wzr_sem,
    das_sem, dar_sem, dbs_sem, dbr_sem, dcs_sem, dcr_sem,
    ns_sem, nr_sem, nfs_sem, nfr_sem, ys_sem, yr_sem, zs_sem, zr_sem, save_sem,
):
    s, t, d = lax.axis_index("section"), lax.axis_index("tensor"), lax.axis_index("dp")
    blocks, rows, width = land.shape[1:]
    half = rows // 2
    local = w_o.shape[0]
    heads, _, head = q.shape
    per = heads // 2
    c, y = lax.rem(t, 2), t // 2
    t_core, t_across = other(t), lax.rem(t + 2, 4)
    t_diagonal = other(t_across)
    core = (s, t_core, d)
    across = (s, t_across, d)
    diagonal = (s, t_diagonal, d)
    beside = (s, t, other(d))
    section = (1 - s, t, d)
    greet([core, across, diagonal, beside, section])

    mine = pl.ds(pl.multiple_of(c * half, half), half)
    theirs = pl.ds(pl.multiple_of((1 - c) * half, half), half)

    shards = [w_q, w_k, w_v, w_o, w_u, w_d]

    def place(i, slot, start, size):
        if i < 3:
            return win.at[slot, pl.ds(pl.multiple_of(i * local + start, 16), size)]
        return (wo, wu, wd)[i - 3].at[pl.ds(pl.multiple_of(slot * local + start, 16), size)]

    short = local // 4
    parity = lax.rem(d, 2)

    def own(i):
        return pltpu.make_async_copy(shards[i], place(i, 0, 0, local), own_sem.at[i])

    def strip(i, which):
        return pl.multiple_of(which * 2 * short + i % 2 * short, 16)

    def crossing(i):
        start = strip(i, parity)
        dst = place(i // 2, 1, start, short)
        return remote(
            shards[i // 2].at[pl.ds(start, short)], dst, wys_sem.at[i], wyr_sem.at[i], across
        )

    def beside_copy(i, which):
        piece = place(i // 2, 1, strip(i, which), short)
        return remote(piece, piece, wzs_sem.at[i], wzr_sem.at[i], beside)

    def relay(i):
        crossing(i).wait_recv()
        beside_copy(i, parity).start()

    def arrived(i):
        beside_copy(i, 1 - parity).wait_recv()

    quarter = local // PIECES

    def down_piece(buffer, i):
        return buffer.at[pl.ds(i * quarter, quarter)]

    def down_first(i):
        return remote(
            down_piece(w_d, i), down_piece(down_a, i), das_sem.at[i], dar_sem.at[i], section
        )

    def down_second(i):
        return remote(
            down_piece(down_a, i), down_piece(down_b, i), dbs_sem.at[i], dbr_sem.at[i], across
        )

    def down_third(i):
        return remote(
            down_piece(down_b, i), wd.at[pl.ds(local + i * quarter, quarter)],
            dcs_sem.at[i], dcr_sem.at[i], section,
        )

    step = rows // PIECES

    def passing_copy(i):
        piece = pl.ds(i * step, step)
        return remote(
            inputs.at[1 - y, piece], passing.at[piece], ps_sem.at[i], pr_sem.at[i], across
        )

    def onward(i):
        piece = pl.ds(i * step, step)
        return remote(
            passing.at[piece], land.at[0, t_across, piece], ps_sem.at[PIECES + i], xp_sem.at[i], section
        )

    def over(i):
        piece = pl.ds(i * step, step)
        return remote(
            cotangent.at[1 - y, piece], land.at[0, t, piece], xs_sem.at[i], xp_sem.at[i], across
        )

    def local_rows(source):
        pltpu.make_async_copy(source.at[y], land.at[0, t], xr_sem.at[t]).start()
        remote(source.at[y], land.at[0, t], xs_sem.at[PIECES], xr_sem.at[t], core).start()

    def block_wait(b):
        piece = land.at[0, b]
        remote(piece, piece, xs_sem.at[PIECES], xr_sem.at[b], core).wait_recv()

    def far_rows():
        for i in range(PIECES):
            piece = land.at[0, t_across, pl.ds(i * step, step)]
            remote(piece, piece, xfs_sem, xp_sem.at[i], core).wait_recv()
        piece = land.at[0, t_across]
        remote(piece, piece, xfs_sem, xr_sem.at[t_across], core).start()
        block_wait(t_diagonal)

    def near_rows():
        block_wait(t)
        block_wait(t_core)

    for i in range(3):
        own(i).start()

    @pl.when(s == 0)
    def _():
        for i in range(10):
            crossing(i).start()
        local_rows(inputs)
        for i in range(PIECES):
            down_first(i).start()

    @pl.when(s == 1)
    def _():
        for i in range(PIECES):
            passing_copy(i).start()
        local_rows(cotangent)

    for i in range(3, 6):
        own(i).start()

    @pl.when(s == 1)
    def _():
        for i in range(PIECES):
            passing_copy(i).wait_recv()
            onward(i).start()
            down_first(i).wait_recv()
            down_second(i).start()
        for i in range(12):
            crossing(i).start()
        for i in range(PIECES):
            over(i).start()
        for i in range(PIECES):
            down_second(i).wait_recv()
            down_third(i).start()
        for i in range(6):
            relay(i)

    for i in range(3):
        own(i).wait()

    def save(kind, b, src, dst):
        pltpu.make_async_copy(src, dst, save_sem.at[kind, b]).start()

    causal = lax.broadcasted_iota(jnp.int32, (rows, rows), 0) >= lax.broadcasted_iota(
        jnp.int32, (rows, rows), 1
    )
    lane = lax.broadcasted_iota(jnp.int32, (rows, 128), 1)

    factor = per_dim(scale[...])

    def attention(turn, _):
        b = jnp.where(s == 0, lax.rem(turn, blocks), turn // 2)
        j = jnp.where(s == 0, turn // blocks, lax.rem(turn, 2))
        at = pl.ds(pl.multiple_of(b * rows, rows), rows)

        @pl.when((s == 0) & (turn == 0))
        def _():
            near_rows()

        @pl.when((s == 0) & (turn == 2 * (1 - y)))
        def _():
            for i in range(4):
                relay(i)
            far_rows()

        @pl.when((s == 0) & (turn == blocks))
        def _():
            relay(6)
            relay(7)
            for i in range(6):
                arrived(i)

        @pl.when((s == 1) & (turn == 0))
        def _():
            for i in range(6):
                arrived(i)

        @pl.when((s == 1) & (j == 0))
        def _():
            piece = land.at[1, b, mine]
            remote(piece, piece, ns_sem.at[b], nr_sem.at[b], core).wait_recv()
            remote(piece, piece, nfs_sem.at[b], nfr_sem.at[b], core).start()
            rest = land.at[1, b, theirs]
            remote(rest, rest, nfs_sem.at[b], nfr_sem.at[b], core).wait_recv()

        @pl.when(j == 0)
        def _():
            hidden = land[s, b].astype(F32)
            n1[at] = (hidden * inverse_rms(hidden) * gain_one[...]).astype(BF16)
            lse_cols[b] = jnp.zeros(lse_cols.shape[1:], F32)
            save(0, b, land.at[s, b], h_out.at[b])
            save(1, b, n1.at[at], n1_out.at[at])

        projected = by_last(n1[at], win[j])
        first = j * per
        for i in range(per):
            cut = i * head
            q[first + i, at] = (projected[:, cut : cut + head] * factor).astype(BF16)
            cut += local
            k[first + i, at] = projected[:, cut : cut + head].astype(BF16)
            cut += local
            v[first + i, at] = projected[:, cut : cut + head].astype(BF16)
        for bb in range(blocks):

            @pl.when(b == bb)
            def _():
                for i in range(per):
                    hd = first + i
                    qh = q[hd, bb * rows : (bb + 1) * rows]
                    near = by_last(qh, k[hd, bb * rows : (bb + 1) * rows])
                    near = jnp.where(causal, near, NEGATIVE)
                    top = jnp.max(near, axis=1, keepdims=True)
                    if bb:
                        far = by_last(qh, k[hd, : bb * rows])
                        top = jnp.maximum(top, jnp.max(far, axis=1, keepdims=True))
                    near = jnp.exp(near - top)
                    total = jnp.sum(near, axis=1, keepdims=True)
                    mixed = plain(near.astype(BF16), v[hd, bb * rows : (bb + 1) * rows])
                    if bb:
                        far = jnp.exp(far - top)
                        total = total + jnp.sum(far, axis=1, keepdims=True)
                        mixed = mixed + plain(far.astype(BF16), v[hd, : bb * rows])
                    o_heads[hd, bb * rows : (bb + 1) * rows] = (mixed / total).astype(BF16)
                    lse_cols[bb] = jnp.where(lane == hd, top + jnp.log(total), lse_cols[bb])

        @pl.when(j == 1)
        def _():
            o[at] = jnp.concatenate([o_heads[i, at] for i in range(heads)], axis=1)
            lse[b] = jnp.transpose(lse_cols[b])[:heads]
            save(2, b, q.at[:, at], q_out.at[:, at])
            save(3, b, k.at[:, at], k_out.at[:, at])
            save(4, b, v.at[:, at], v_out.at[:, at])
            save(5, b, o.at[at], o_out.at[at])
            save(6, b, lse.at[b], lse_out.at[b])

        for i, when in ((4, 2), (5, 3), (8, 4), (9, 5)):

            @pl.when((s == 0) & (turn == when))
            def _():
                relay(i)

        for i in range(6):

            @pl.when((s == 1) & (turn == i))
            def _():
                relay(6 + i)

        return 0

    def project(b, _):
        @pl.when(b == 0)
        def _():
            own(3).wait()
            arrived(6)
            arrived(7)

        at = pl.ds(pl.multiple_of(b * rows, rows), rows)
        ysend[b] = plain(o[at], wo[...]).astype(BF16)
        remote(ysend.at[b], yrecv.at[b], ys_sem.at[b], yr_sem.at[b], core).start()
        return 0

    lax.fori_loop(0, 2 * blocks, attention, 0)

    lax.fori_loop(0, blocks, project, 0)

    own(4).wait()
    own(5).wait()
    arrived(8)
    arrived(9)

    @pl.when(s == 0)
    def _():
        for i in range(PIECES):
            down_third(i).wait_recv()

    @pl.when(s == 1)
    def _():
        arrived(10)
        arrived(11)

    weights = [(win, win_out), (wo, wo_out), (wu, wu_out), (wd, wd_out)]
    for i, (src, dst) in enumerate(weights):
        save(11, i, src, dst)

    def feed(b, _):
        at = pl.ds(pl.multiple_of(b * rows, rows), rows)
        remote(ysend.at[b], yrecv.at[b], ys_sem.at[b], yr_sem.at[b], core).wait_recv()
        middle = land[s, b].astype(F32) + (ysend[b].astype(F32) + yrecv[b].astype(F32))
        m[b] = middle
        normed = (middle * inverse_rms(middle) * gain_two[...]).astype(BF16)
        n2[at] = normed
        up = by_last(normed, wu[...])
        u[b] = up
        active = (up / (1.0 + jnp.exp(-up))).astype(BF16)
        a[at] = active
        zpart[b] = plain(active, wd[...])
        copy = remote(zpart.at[b, theirs], zrecv.at[b], zs_sem.at[b], zr_sem.at[b], core)
        copy.start()
        save(7, b, m.at[b], m_out.at[b])
        save(8, b, n2.at[at], n2_out.at[at])
        save(9, b, u.at[b], u_out.at[b])
        save(10, b, a.at[at], a_out.at[at])

        @pl.when(s == 0)
        def _():
            finish(b)

        @pl.when((s == 1) & (b > 0))
        def _():
            finish(b - 1)

        return 0

    def finish(b):
        copy = remote(zpart.at[b, theirs], zrecv.at[b], zs_sem.at[b], zr_sem.at[b], core)
        copy.wait_recv()
        xout[b] = (m[b, mine] + (zpart[b, mine] + zrecv[b])).astype(BF16)

        @pl.when(s == 0)
        def _():
            remote(xout.at[b], land.at[1, b, mine], ns_sem.at[b], nr_sem.at[b], section).start()

        save(13, b, xout.at[b], x_out.at[b])

    lax.fori_loop(0, blocks, feed, 0)

    @pl.when(s == 1)
    def _():
        finish(blocks - 1)


    @pl.when(s == 1)
    def _():
        near_rows()
        far_rows()

    for b in range(blocks):
        pltpu.make_async_copy(land.at[0, b], g_out.at[b], save_sem.at[12, b]).start()

    block = land.at[0, t]
    remote(block, block, xs_sem.at[PIECES], xr_sem.at[t], core).wait_send()
    remote(block, block, xfs_sem, xr_sem.at[t], core).wait_send()

    @pl.when(s == 1)
    def _():
        for i in range(PIECES):
            passing_copy(i).wait_send()
            onward(i).wait_send()
            over(i).wait_send()
            down_second(i).wait_send()
            down_third(i).wait_send()
        for i in range(10, 12):
            crossing(i).wait_send()
            beside_copy(i, parity).wait_send()

    @pl.when(s == 0)
    def _():
        for i in range(PIECES):
            down_first(i).wait_send()

    for b in range(blocks):
        piece = land.at[0, b, mine]
        remote(ysend.at[b], yrecv.at[b], ys_sem.at[b], yr_sem.at[b], core).wait_send()
        remote(zpart.at[b, theirs], zrecv.at[b], zs_sem.at[b], zr_sem.at[b], core).wait_send()

        @pl.when(s == 0)
        def _():
            remote(xout.at[b], piece, ns_sem.at[b], nr_sem.at[b], section).wait_send()

        @pl.when(s == 1)
        def _():
            remote(piece, piece, nfs_sem.at[b], nfr_sem.at[b], core).wait_send()

    for i in range(10):
        crossing(i).wait_send()
        beside_copy(i, parity).wait_send()
    for i, (src, dst) in enumerate(weights):
        pltpu.make_async_copy(src, dst, save_sem.at[11, i]).wait()
    for b in range(blocks):
        at = pl.ds(b * rows, rows)
        saved = [
            (land.at[s, b], h_out.at[b]),
            (n1.at[at], n1_out.at[at]),
            (q.at[:, at], q_out.at[:, at]),
            (k.at[:, at], k_out.at[:, at]),
            (v.at[:, at], v_out.at[:, at]),
            (o.at[at], o_out.at[at]),
            (lse.at[b], lse_out.at[b]),
            (m.at[b], m_out.at[b]),
            (n2.at[at], n2_out.at[at]),
            (u.at[b], u_out.at[b]),
            (a.at[at], a_out.at[at]),
        ]
        for kind, (src, dst) in enumerate(saved):
            pltpu.make_async_copy(src, dst, save_sem.at[kind, b]).wait()
        pltpu.make_async_copy(land.at[0, b], g_out.at[b], save_sem.at[12, b]).wait()
        pltpu.make_async_copy(xout.at[b], x_out.at[b], save_sem.at[13, b]).wait()


def forward(inputs, cotangent, shards, gain_one, gain_two, scale, head):
    _, rows, width = inputs.shape
    local = shards[0].shape[0]
    heads = 2 * local // head
    blocks = lax.axis_size("tensor")
    length = blocks * rows
    half = rows // 2
    shape = jax.ShapeDtypeStruct
    weights = [(2, 3 * local, width), (2 * local, width), (2 * local, width), (2 * local, width)]
    outs = [
        shape((blocks, half, width), BF16),
        shape((blocks, rows, width), BF16),
        shape((length, width), BF16),
        shape((heads, length, head), BF16),
        shape((heads, length, head), BF16),
        shape((heads, length, head), BF16),
        shape((length, 2 * local), BF16),
        shape((blocks, heads, rows), F32),
        shape((blocks, rows, width), F32),
        shape((length, width), BF16),
        shape((blocks, rows, 2 * local), F32),
        shape((length, 2 * local), BF16),
        shape((blocks, rows, width), BF16),
    ] + [shape(w, BF16) for w in weights]
    scratch = [pltpu.VMEM((2, blocks, rows, width), BF16)]
    scratch += [pltpu.VMEM(w, BF16) for w in weights]
    scratch += [
        pltpu.VMEM((rows, width), BF16),
        pltpu.VMEM((local, width), BF16),
        pltpu.VMEM((local, width), BF16),
        pltpu.VMEM((length, width), BF16),
        pltpu.VMEM((heads, length, head), BF16),
        pltpu.VMEM((heads, length, head), BF16),
        pltpu.VMEM((heads, length, head), BF16),
        pltpu.VMEM((heads, length, head), BF16),
        pltpu.VMEM((length, 2 * local), BF16),
        pltpu.VMEM((blocks, rows, 128), F32),
        pltpu.VMEM((blocks, heads, rows), F32),
        pltpu.VMEM((blocks, rows, width), BF16),
        pltpu.VMEM((blocks, rows, width), BF16),
        pltpu.VMEM((blocks, rows, width), F32),
        pltpu.VMEM((length, width), BF16),
        pltpu.VMEM((blocks, rows, 2 * local), F32),
        pltpu.VMEM((length, 2 * local), BF16),
        pltpu.VMEM((blocks, rows, width), F32),
        pltpu.VMEM((blocks, half, width), F32),
        pltpu.VMEM((blocks, half, width), BF16),
        DMA((6,)),
        DMA((2 * PIECES,)),
        DMA((PIECES,)),
        DMA((PIECES + 1,)),
        DMA((PIECES,)),
        DMA((blocks,)),
        DMA,
    ]
    scratch += [DMA((12,))] * 4 + [DMA((PIECES,))] * 6 + [DMA((blocks,))] * 8 + [DMA((14, blocks))]
    return pl.pallas_call(
        forward_kernel,
        out_shape=outs,
        in_specs=[ANY] * 8 + [VMEM] * 3,
        out_specs=[ANY] * len(outs),
        scratch_shapes=scratch,
        compiler_params=pltpu.CompilerParams(
            collective_id=1, has_side_effects=True, vmem_limit_bytes=62 * MIB
        ),
        name="forward",
    )(inputs, cotangent, *shards, gain_one, gain_two, scale)


def backward_kernel(
    g_in, h_in, q_in, k_in, v_in, o_in, lse_in, m_in, u_in, win_in, wo_in, wu_in, wd_in, x_in,
    gain_one, gain_two, scale,
    x_rows, out_rows, final, g_out, gu_out, gy_out, gp_out, dg1, dg2, ds,
    g, win, wo, wu, wd, h, q, k, v, o, lse, m, u, gu, gy, gp, ysend, yrecv, gm, go_heads, gq_heads,
    delta, dk, dv, n1part, n1recv, xout,
    load_sem, w_sem, ns_sem, nr_sem, nfs_sem, nfr_sem, ys_sem, yr_sem, zs_sem, zr_sem, os_sem, or_sem,
    xs_sem, xr_sem, save_sem,
):
    s, t, d = lax.axis_index("section"), lax.axis_index("tensor"), lax.axis_index("dp")
    blocks, rows, width = g.shape
    half = rows // 2
    local = wu.shape[0] // 2
    heads, _, head = q.shape
    per = heads // 2
    c, y = lax.rem(t, 2), t // 2
    core = (s, other(t), d)
    across = (s, lax.rem(t + 2, 4), d)
    diagonal = (s, other(lax.rem(t + 2, 4)), d)
    section = (1 - s, t, d)
    mine = pl.ds(pl.multiple_of(c * half, half), half)
    theirs = pl.ds(pl.multiple_of((1 - c) * half, half), half)

    weights = [(wd_in, wd), (wu_in, wu), (wo_in, wo), (win_in, win)]

    def weight(i):
        return pltpu.make_async_copy(*weights[i], w_sem.at[i])

    def load(kind, b):
        at = pl.ds(pl.multiple_of(b * rows, rows), rows)
        src, dst = [
            (u_in.at[b], u.at[b]),
            (m_in.at[b], m.at[b]),
            (o_in.at[at], o.at[at]),
            (q_in.at[:, at], q.at[:, at]),
            (k_in.at[:, at], k.at[:, at]),
            (v_in.at[:, at], v.at[:, at]),
            (lse_in.at[b], lse.at[b]),
            (h_in.at[b, mine], h.at[b]),
        ][kind]
        return pltpu.make_async_copy(src, dst, load_sem.at[kind, b])

    def incoming(b):
        return pltpu.make_async_copy(g_in.at[b], g.at[b], nr_sem.at[b])

    last = blocks - 1

    @pl.when(s == 1)
    def _():
        incoming(last).start()

    weight(0).start()
    load(0, last).start()
    weight(1).start()
    load(1, last).start()

    barrier = pltpu.get_barrier_semaphore()
    for device in (core, across, diagonal, section):
        pl.semaphore_signal(barrier, inc=1, device_id=device, device_id_type=MESH)

    weight(2).start()
    for kind in (2, 3, 6):
        load(kind, last).start()
    for bb in reversed(range(blocks)):
        load(4, bb).start()
        load(5, bb).start()
    weight(3).start()
    load(7, last).start()

    spot = out_rows.at[y, mine]

    def owner_copy(b, src, dst, send, receive, act):
        @pl.when(b == t)
        def _():
            act(pltpu.make_async_copy(src, dst, receive.at[t]))

        @pl.when(b != t)
        def _():
            act(remote(src, dst, send.at[b], receive.at[t], (s, b, d)))

    dg1[...] = jnp.zeros_like(dg1)
    dg2[...] = jnp.zeros_like(dg2)
    ds[...] = jnp.zeros_like(ds)

    causal = lax.broadcasted_iota(jnp.int32, (rows, rows), 0) <= lax.broadcasted_iota(
        jnp.int32, (rows, rows), 1
    )
    factor = jnp.concatenate([per_dim(scale[...])] * per, axis=1)
    width_two = heads * head
    row_head = lax.broadcasted_iota(jnp.int32, (heads, width_two), 0)
    start = row_head * head
    place = lax.broadcasted_iota(jnp.int32, (heads, width_two), 1)
    member = jnp.where((place >= start) & (place < start + head), 1.0, 0.0).astype(BF16)

    def save(kind, b, src, dst):
        pltpu.make_async_copy(src, dst, save_sem.at[kind, b]).start()

    def neighbours_sum(b, i):
        lanes = pl.ds(i * (width // 2), width // 2)
        return remote(
            ysend.at[b, :, lanes], yrecv.at[b, :, lanes], ys_sem.at[i, b], yr_sem.at[i, b], core
        )

    def up_part(turn):
        b = last - turn
        at = pl.ds(pl.multiple_of(b * rows, rows), rows)

        @pl.when(s == 1)
        def _():
            incoming(b).wait()

        @pl.when(turn == 0)
        def _():
            pl.semaphore_wait(barrier, 4)

        @pl.when(s == 0)
        def _():
            piece = g.at[b, mine]
            remote(piece, piece, ns_sem.at[b], nr_sem.at[b], core).wait_recv()
            remote(piece, piece, nfs_sem.at[b], nfr_sem.at[b], core).start()
            rest = g.at[b, theirs]
            remote(rest, rest, nfs_sem.at[b], nfr_sem.at[b], core).wait_recv()

        @pl.when(turn == 0)
        def _():
            weight(0).wait()

        load(0, b).wait()
        save(0, b, g.at[b], g_out.at[at])
        grad = g[b]
        grad_act = by_last(grad, wd[...])
        up = u[b]
        sigma = 1.0 / (1.0 + jnp.exp(-up))
        grad_up = (grad_act * sigma * (1.0 + up * (1.0 - sigma))).astype(BF16)
        gu[at] = grad_up

        @pl.when(turn == 0)
        def _():
            weight(1).wait()

        save(1, b, gu.at[at], gu_out.at[at])
        for i in range(2):
            lanes = slice(i * (width // 2), (i + 1) * (width // 2))
            ysend[b, :, lanes] = plain(grad_up, wu[:, lanes]).astype(BF16)
            neighbours_sum(b, i).start()

        @pl.when(turn == 0)
        def _():
            for bb in range(blocks):
                owner_copy(
                    bb, x_in.at[bb], x_rows.at[y, mine], xs_sem, xr_sem, lambda copy: copy.start()
                )

    def one_block(turn, _):
        b = last - turn
        at = pl.ds(pl.multiple_of(b * rows, rows), rows)
        load(1, b).wait()
        for i in range(2):
            neighbours_sum(b, i).wait_recv()
        grad = g[b]
        grad_normed = ysend[b].astype(F32) + yrecv[b].astype(F32)
        middle = m[b]
        inverse = inverse_rms(middle)
        unit = middle * inverse
        grad_unit = grad_normed * gain_two[...]
        dg2[...] += jnp.sum(grad_normed * unit, axis=0, keepdims=True)
        grad_middle = grad.astype(F32) + inverse * (
            grad_unit - unit * jnp.mean(grad_unit * unit, axis=1, keepdims=True)
        )
        gm[...] = grad_middle
        grad_mid = grad_middle.astype(BF16)
        gy[at] = grad_mid
        save(2, b, gy.at[at], gy_out.at[at])

        @pl.when(turn == 0)
        def _():
            weight(2).wait()

        load(2, b).wait()
        grad_mixed = by_last(grad_mid, wo[...]).astype(BF16)
        both = grad_mixed.astype(F32) * o[at].astype(F32)
        high = both.astype(BF16)
        low = (both - high.astype(F32)).astype(BF16)
        delta[...] = by_last(member, high) + by_last(member, low)
        for i in range(heads):
            go_heads[i] = grad_mixed[:, i * head : (i + 1) * head]

        @pl.when(turn == 0)
        def _():
            for bb in range(blocks):
                load(4, bb).wait()
                load(5, bb).wait()

        load(3, b).wait()
        load(6, b).wait()

        @pl.when(turn < last)
        def _():
            for kind in (0, 1, 2, 3, 6, 7):
                load(kind, b - 1).start()

        @pl.when((turn < last) & (s == 1))
        def _():
            incoming(b - 1).start()

        for bb in range(blocks):

            @pl.when(b == bb)
            def _():
                def group(first, _):
                    for j in range(per):
                        i = first * per + j
                        qh = q[i, bb * rows : (bb + 1) * rows]
                        gh = go_heads[i]
                        offset = lse[bb, pl.ds(i, 1)]
                        inner = delta[pl.ds(i, 1)]
                        total = None
                        for lo, hi in ((bb * rows, (bb + 1) * rows), (0, bb * rows)):
                            if lo == hi:
                                continue
                            kj = k[i, lo:hi]
                            weight = jnp.exp(by_last(kj, qh) - offset)
                            if lo == bb * rows and hi > lo and hi == (bb + 1) * rows:
                                weight = jnp.where(causal, weight, 0.0)
                            grad_score = weight * (by_last(v[i, lo:hi], gh) - inner)
                            grad_score = grad_score.astype(BF16)
                            more_v = plain(weight.astype(BF16), gh)
                            more_k = plain(grad_score, qh)
                            if bb == last:
                                dv[i, lo:hi] = more_v
                                dk[i, lo:hi] = more_k
                            else:
                                dv[i, lo:hi] += more_v
                                dk[i, lo:hi] += more_k
                            part = by_first(kj, grad_score)
                            total = part if total is None else total + part
                        gq_heads[i] = jnp.transpose(total)
                    return 0

                lax.fori_loop(0, 2, group, 0)

        for j in range(2):
            mine_heads = range(j * per, (j + 1) * per)
            grad_scaled = jnp.concatenate([gq_heads[i] for i in mine_heads], axis=1)
            queries = jnp.concatenate([q[i, at] for i in mine_heads], axis=1).astype(F32)
            ds[pl.ds(j, 1)] += jnp.sum(grad_scaled * queries, axis=0, keepdims=True)
            grads = [
                (grad_scaled * factor).astype(BF16),
                jnp.concatenate([dk[i, at] for i in mine_heads], axis=1).astype(BF16),
                jnp.concatenate([dv[i, at] for i in mine_heads], axis=1).astype(BF16),
            ]
            gp[j, at] = jnp.concatenate(grads, axis=1)
        save(3, b, gp.at[:, at], gp_out.at[:, at])

        @pl.when(turn == 0)
        def _():
            weight(3).wait()

        n1part[...] = plain(gp[0, at], win[0]) + plain(gp[1, at], win[1])
        copy = remote(n1part.at[theirs], n1recv.at[b], zs_sem.at[b], zr_sem.at[b], core)
        copy.start()

        @pl.when(turn < last)
        def _():
            up_part(turn + 1)

        load(7, b).wait()
        hidden = h[b].astype(F32)
        inverse = inverse_rms(hidden)
        unit = hidden * inverse
        copy.wait_recv()
        grad_normed = n1part[mine] + n1recv[b]
        grad_unit = grad_normed * gain_one[...]
        dg1[...] += jnp.sum(grad_normed * unit, axis=0, keepdims=True)
        xout[b] = (
            gm[mine]
            + inverse * (grad_unit - unit * jnp.mean(grad_unit * unit, axis=1, keepdims=True))
        ).astype(BF16)

        @pl.when(s == 1)
        def _():
            remote(xout.at[b], g.at[b, mine], ns_sem.at[b], nr_sem.at[b], section).start()

        @pl.when(b > 0)
        def _():
            owner_copy(b, xout.at[b], spot, os_sem, or_sem, lambda copy: copy.start())

        @pl.when(b == 0)
        def _():
            save(4, 0, xout.at[0], final)

        copy.wait_send()
        return 0

    up_part(jnp.int32(0))
    lax.fori_loop(0, blocks, one_block, 0)

    for b in range(blocks):
        at = pl.ds(b * rows, rows)
        piece = g.at[b, mine]
        for i in range(2):
            neighbours_sum(b, i).wait_send()
        here = x_rows.at[b // 2, pl.ds((b % 2) * half, half)]
        remote(here, here, xs_sem.at[b], xr_sem.at[b], core).wait_recv()

        @pl.when(b != t)
        def _():
            remote(x_in.at[b], here, xs_sem.at[b], xr_sem.at[b], core).wait_send()

        @pl.when(t > 0)
        def _():
            here = out_rows.at[b // 2, pl.ds((b % 2) * half, half)]
            remote(here, here, os_sem.at[b], or_sem.at[b], core).wait_recv()

        @pl.when((b != t) & (b > 0))
        def _():
            remote(xout.at[b], here, os_sem.at[b], or_sem.at[b], core).wait_send()

        @pl.when(s == 1)
        def _():
            remote(xout.at[b], piece, ns_sem.at[b], nr_sem.at[b], section).wait_send()

        @pl.when(s == 0)
        def _():
            remote(piece, piece, nfs_sem.at[b], nfr_sem.at[b], core).wait_send()

        saved = [
            (g.at[b], g_out.at[at]),
            (gu.at[at], gu_out.at[at]),
            (gy.at[at], gy_out.at[at]),
            (gp.at[:, at], gp_out.at[:, at]),
        ]
        for kind, (src, dst) in enumerate(saved):
            pltpu.make_async_copy(src, dst, save_sem.at[kind, b]).wait()
    pltpu.make_async_copy(xout.at[0], final, save_sem.at[4, 0]).wait()


def backward(saved, gain_one, gain_two, scale):
    g_in, h_in, q_in = saved[:3]
    win_in, wo_in, wu_in, wd_in = saved[9:13]
    blocks, rows, width = g_in.shape
    heads, length, head = q_in.shape
    local = wu_in.shape[0] // 2
    half = rows // 2
    shape = jax.ShapeDtypeStruct
    outs = [
        shape((2, rows, width), BF16),
        shape((2, rows, width), BF16),
        shape((half, width), BF16),
        shape((length, width), BF16),
        shape((length, 2 * local), BF16),
        shape((length, width), BF16),
        shape((2, length, 3 * local), BF16),
        shape((1, width), F32),
        shape((1, width), F32),
        shape((2, local), F32),
    ]
    scratch = [
        pltpu.VMEM((blocks, rows, width), BF16),
        pltpu.VMEM(win_in.shape, BF16),
        pltpu.VMEM(wo_in.shape, BF16),
        pltpu.VMEM(wu_in.shape, BF16),
        pltpu.VMEM(wd_in.shape, BF16),
        pltpu.VMEM((blocks, half, width), BF16),
        pltpu.VMEM((heads, length, head), BF16),
        pltpu.VMEM((heads, length, head), BF16),
        pltpu.VMEM((heads, length, head), BF16),
        pltpu.VMEM((length, 2 * local), BF16),
        pltpu.VMEM((blocks, heads, rows), F32),
        pltpu.VMEM((blocks, rows, width), F32),
        pltpu.VMEM((blocks, rows, 2 * local), F32),
        pltpu.VMEM((length, 2 * local), BF16),
        pltpu.VMEM((length, width), BF16),
        pltpu.VMEM((2, length, 3 * local), BF16),
        pltpu.VMEM((blocks, rows, width), BF16),
        pltpu.VMEM((blocks, rows, width), BF16),
        pltpu.VMEM((rows, width), F32),
        pltpu.VMEM((heads, rows, head), BF16),
        pltpu.VMEM((heads, rows, head), F32),
        pltpu.VMEM((heads, rows), F32),
        pltpu.VMEM((heads, length, head), F32),
        pltpu.VMEM((heads, length, head), F32),
        pltpu.VMEM((rows, width), F32),
        pltpu.VMEM((blocks, half, width), F32),
        pltpu.VMEM((blocks, half, width), BF16),
        DMA((8, blocks)),
        DMA((4,)),
    ]
    scratch += [DMA((blocks,))] * 4 + [DMA((2, blocks))] * 2 + [DMA((blocks,))] * 6 + [DMA((5, blocks))]
    return pl.pallas_call(
        backward_kernel,
        out_shape=outs,
        in_specs=[ANY] * 14 + [VMEM] * 3,
        out_specs=[ANY] * 7 + [VMEM] * 3,
        scratch_shapes=scratch,
        compiler_params=pltpu.CompilerParams(
            collective_id=2, has_side_effects=True, vmem_limit_bytes=62 * MIB
        ),
        name="backward",
    )(*saved, gain_one, gain_two, scale)


def farthest_first(d, k, n):
    found = 0
    for i in range(n):
        above = list(range(n - 1, i, -1))
        below = list(range(i))
        first, second = (above, below) if len(above) >= len(below) else (below, above)
        lead = len(first) - len(second) - 1
        order = first[: max(lead, 0)]
        rest = first[max(lead, 0) :]
        for j in range(max(len(rest), len(second))):
            order += rest[j : j + 1] + second[j : j + 1]
        order.append(i)
        picked = 0
        for j, e in enumerate(order):
            picked = picked + jnp.where(k == j, e, 0)
        found = found + jnp.where(d == i, picked, 0)
    return found


def gradient_kernel(
    n1_in, n2_in, gy_in, g_in, gp_in, gu_in, o_in, a_in, final, rows_in, dg1, dg2, ds, dim_scale,
    q_out, k_out, v_out, u_out, o_out, d_out, rows_out, out_g1, out_g2, out_s,
    out_q, out_k, out_v, out_u, out_o, out_d, x, xt, gp, gu, o, a,
    keep_a, give_a, yrecv_a, flow_a, last_a, keep_b, give_b, yrecv_b, flow_b, last_b,
    line, flow_d, last_d, rest, yd, small, smalls, chain, out_rows_a, out_rows_b,
    x_sem, g_sem, ys_sem, yr_sem, fs_sem, fr_sem, last_sem, ds_sem, dr_sem, last_d_sem,
    yds_sem, ydr_sem, ss_sem, sr_sem, cs_sem, cr_sem, es_sem, er_sem, out_sem, rs_sem, hop_sem, here_sem,
):
    s, t, d = lax.axis_index("section"), lax.axis_index("tensor"), lax.axis_index("dp")
    n, chunk, _ = keep_a.shape
    local = a.shape[1] // 2
    split = yd.shape[1]
    width = dg1.shape[1]
    pieces = ys_sem.shape[2]
    step = chunk // pieces
    core = (s, other(t), d)
    across = (s, lax.rem(t + 2, 4), d)
    diagonal = (s, other(lax.rem(t + 2, 4)), d)
    up = (s, t, lax.rem(d + 1, n))
    down = (s, t, lax.rem(d + n - 1, n))
    c, y = lax.rem(t, 2), t // 2

    sources = [g_in, n1_in, n2_in, gy_in]
    operands = [(a_in, a), (gp_in, gp), (gu_in, gu), (o_in, o)]

    def load(i):
        return pltpu.make_async_copy(sources[i], x.at[i % 2], x_sem.at[i])

    def operand(i):
        return pltpu.make_async_copy(*operands[i], g_sem.at[i])

    section = (1 - s, t, d)
    slanted = (1 - s, 1 - t, d)
    barrier = pltpu.get_barrier_semaphore()
    for device in (core, across, diagonal, up, down):
        pl.semaphore_signal(barrier, inc=1, device_id=device, device_id_type=MESH)

    @pl.when((s == 1) & (t != 1))
    def _():
        pl.semaphore_signal(barrier, inc=1, device_id=section, device_id_type=MESH)

    @pl.when((s == 1) & (t == 1))
    def _():
        pl.semaphore_signal(barrier, inc=1, device_id=slanted, device_id_type=MESH)

    load(0).start()
    operand(0).start()
    load(1).start()
    for i in range(1, 4):
        operand(i).start()

    small[0:1, :width] = dg1[...]
    small[0:1, width : 2 * width] = jnp.where(c == 0, dg2[...], 0.0)
    small[0:1, 2 * width : 2 * width + local] = ds[0:1]
    small[0:1, 2 * width + 384 : 2 * width + 384 + local] = ds[1:2]

    partners = [core, across, diagonal]

    def share(i):
        return remote(small, smalls.at[i], ss_sem.at[i], sr_sem.at[i], partners[i])

    def turn(i):
        load(i).wait()
        turned = jnp.transpose(x[i % 2])
        for e in range(n):
            xt[i, e] = turned[e * chunk : (e + 1) * chunk]
        if i + 2 < 4:
            load(i + 2).start()

    groups = [(keep_a, give_a, yrecv_a, flow_a, last_a), (keep_b, give_b, yrecv_b, flow_b, last_b)]

    def exchange(which, e, i):
        _, give, yrecv, _, _ = groups[which]
        rows = pl.ds(i * step, step)
        return remote(
            give.at[e, rows], yrecv.at[e, rows], ys_sem.at[which, e, i], yr_sem.at[which, e, i], across
        )

    def send_all(which, e):
        for i in range(pieces):
            exchange(which, e, i).start()

    def send_d(e):
        src = line.at[e]

        @pl.when(e > d)
        def _():
            remote(src, flow_d.at[e], ds_sem.at[e], dr_sem.at[e], up).start()

        @pl.when(e < d - 1)
        def _():
            remote(src, flow_d.at[e], ds_sem.at[e], dr_sem.at[e], down).start()

        @pl.when(e == d - 1)
        def _():
            remote(src, last_d, ds_sem.at[e], last_d_sem, down).start()

    def upstream_d(e):
        piece = flow_d.at[e]
        remote(piece, piece, ds_sem.at[e], dr_sem.at[e], up).wait_recv()
        line[e] = (line[e].astype(F32) + flow_d[e].astype(F32)).astype(BF16)

    def down_product(k):
        e = farthest_first(d, k, n)
        both = plain(xt[0, e], a[...]).astype(BF16)
        line[e] = jnp.concatenate([both[:, :split], both[:, local : local + split]], axis=1)
        for j in range(2):
            rest[j, e] = both[:, j * local + split : (j + 1) * local]

    def first_d(k):
        e = farthest_first(d, k, n)

        @pl.when(((d == 0) | (d == n - 1)) & (e != d))
        def _():
            send_d(e)

    def in_product(k, j):
        e = farthest_first(d, k, n)
        (keep_a, give_a)[j][e] = jnp.concatenate(
            [plain(xt[1, e], gp[j]).astype(BF16), rest[j, e]], axis=1
        )

    turn(0)
    operand(0).wait()
    down_product(0)
    turn(1)
    operand(1).wait()
    in_product(0, 1)

    heard = jnp.where(s == 0, jnp.where(t == 0, 2, jnp.where(t == 1, 0, 1)), 0)
    pl.semaphore_wait(barrier, 5 + heard)

    @pl.when((s == 0) & (t == 0))
    def _():
        pl.semaphore_signal(here_sem, inc=1, device_id=section, device_id_type=MESH)
        pl.semaphore_signal(here_sem, inc=1, device_id=slanted, device_id_type=MESH)

    send_all(0, farthest_first(d, 0, n))
    first_d(0)
    for i in range(3):
        share(i).start()

    half = final.shape[0]
    owner = (s, 0, d)
    spot = rows_out.at[y, pl.ds(pl.multiple_of(c * half, half), half)]

    @pl.when(t == 0)
    def _():
        pltpu.make_async_copy(final, spot, er_sem.at[0]).start()

    direct = (t == 1) | ((t > 1) & (s == 1))
    aside = (t > 1) & (s == 0)

    @pl.when(t == 1)
    def _():
        remote(final, spot, es_sem, er_sem.at[t], owner).start()

    @pl.when(aside)
    def _():
        remote(final, out_rows_a, es_sem, rs_sem.at[0], section).start()

    def more_down(k, _):
        down_product(k)
        first_d(k)
        return 0

    lax.fori_loop(1, n, more_down, 0)

    def more_in(k, _):
        in_product(k, 1)

        @pl.when(k < n - 1)
        def _():
            send_all(0, farthest_first(d, k, n))

        in_product(k, 0)
        return 0

    lax.fori_loop(1, n, more_in, 0)
    in_product(0, 0)

    turn(2)
    turn(3)
    operand(2).wait()
    operand(3).wait()

    def other_product(k, _):
        e = farthest_first(d, k, n)
        ups = plain(xt[2, e], gu[...])
        outs = plain(xt[3, e], o[...])
        for j, target in ((1, give_b), (0, keep_b)):
            cut = slice(j * local, (j + 1) * local)
            target[e] = jnp.concatenate([ups[:, cut], outs[:, cut]], axis=1).astype(BF16)
            if j:

                @pl.when(k < n - 1)
                def _():
                    send_all(1, e)

        return 0

    lax.fori_loop(0, n, other_product, 0)
    send_all(0, d)
    send_all(1, d)

    @pl.when((t > 1) & (s == 1))
    def _():
        remote(final, spot, es_sem, er_sem.at[t], owner).start()

    for i in range(3):
        share(i).wait_recv()
    mine = small[...] + smalls[0] + (smalls[1] + smalls[2])

    def link(i, device):
        return remote(chain.at[i], chain.at[2 + i], cs_sem.at[i], cr_sem.at[i], device)

    smalls[0] = mine
    for i, opens, closes, device in ((0, d == 0, d == n - 1, up), (1, d == n - 1, d == 0, down)):
        chain[i] = mine

        @pl.when(jnp.logical_not(opens))
        def _():
            link(i, device).wait_recv()
            chain[i] = mine + chain[2 + i]
            smalls[0] += chain[2 + i]

        @pl.when(jnp.logical_not(closes))
        def _():
            link(i, device).start()

    def middle(k):
        e = farthest_first(d, k, n)

        @pl.when((d > 0) & (d < n - 1) & (e != d))
        def _():
            upstream_d(e)
            send_d(e)

    def flows(which, k):
        e = farthest_first(d, k, n)
        keep, give, yrecv, flow, last = groups[which]
        send, receive = fs_sem.at[which], fr_sem.at[which]
        for i in range(pieces):
            at = pl.ds(i * step, step)
            exchange(which, e, i).wait_recv()
            first = ((e > d) & (d == 0)) | ((e < d) & (d == n - 1))

            @pl.when((e != d) & first)
            def _():
                keep[e, at] = (keep[e, at].astype(F32) + yrecv[e, at].astype(F32)).astype(BF16)

            @pl.when((e != d) & jnp.logical_not(first))
            def _():
                piece = flow.at[e, at]
                remote(piece, piece, send.at[e, i], receive.at[e, i], up).wait_recv()
                total = keep[e, at].astype(F32) + yrecv[e, at].astype(F32)
                keep[e, at] = (total + flow[e, at].astype(F32)).astype(BF16)

            src = keep.at[e, at]

            @pl.when(e > d)
            def _():
                remote(src, flow.at[e, at], send.at[e, i], receive.at[e, i], up).start()

            @pl.when(e < d - 1)
            def _():
                remote(src, flow.at[e, at], send.at[e, i], receive.at[e, i], down).start()

            @pl.when(e == d - 1)
            def _():
                remote(src, last.at[at], send.at[e, i], last_sem.at[which, i], down).start()

    def flows_in(k, _):
        middle(k)
        flows(0, k)
        return 0

    def flows_other(k, _):
        flows(1, k)
        return 0

    lax.fori_loop(0, n - 1, flows_in, 0)

    @pl.when(d > 0)
    def _():
        upstream_d(d)

    @pl.when(d < n - 1)
    def _():
        remote(last_d, last_d, ds_sem.at[0], last_d_sem, down).wait_recv()
        line[d] = (line[d].astype(F32) + last_d[...].astype(F32)).astype(BF16)

    crossing = remote(line.at[d, :, pl.ds(split, split)], yd, yds_sem, ydr_sem, across)
    crossing.start()

    lax.fori_loop(0, n - 1, flows_other, 0)

    second = remote(out_rows_a, out_rows_b, hop_sem.at[0], rs_sem.at[1], across)
    mine_half = pl.ds(pl.multiple_of(c * half, half), half)
    third_dst = rows_out.at[1, mine_half]

    def third(device):
        return remote(out_rows_b, third_dst, hop_sem.at[1], er_sem.at[2 + c], device)

    @pl.when((s == 1) & (t > 1))
    def _():
        remote(out_rows_a, out_rows_a, hop_sem.at[0], rs_sem.at[0], section).wait_recv()
        second.start()

    @pl.when((s == 1) & (t < 2))
    def _():
        second.wait_recv()
        pl.semaphore_wait(here_sem, 1)

    @pl.when((s == 1) & (t == 0))
    def _():
        third(section).start()

    @pl.when((s == 1) & (t == 1))
    def _():
        third(slanted).start()

    def landed(which, i):
        keep, _, yrecv, flow, last = groups[which]
        at = pl.ds(i * step, step)
        exchange(which, d, i).wait_recv()

        @pl.when(d > 0)
        def _():
            piece = flow.at[d, at]
            remote(
                piece, piece, fs_sem.at[which, d, i], fr_sem.at[which, d, i], up
            ).wait_recv()

        @pl.when(d < n - 1)
        def _():
            piece = last.at[at]
            remote(
                piece, piece, fs_sem.at[which, d, i], last_sem.at[which, i], down
            ).wait_recv()

        above = jnp.where(d > 0, flow[d, at].astype(F32), 0.0)
        below = jnp.where(d < n - 1, last[at].astype(F32), 0.0)
        return (keep[d, at].astype(F32) + yrecv[d, at].astype(F32)) + (above + below)

    results = [
        pltpu.make_async_copy(src, dst, out_sem.at[i])
        for i, (src, dst) in enumerate(
            ((out_q, q_out), (out_k, k_out), (out_v, v_out), (out_u, u_out), (out_o, o_out), (out_d, d_out))
        )
    ]
    rests = []
    for i in range(pieces):
        at = pl.ds(i * step, step)
        total = landed(0, i)
        for j, ref in enumerate((out_q, out_k, out_v)):
            ref[at] = total[:, j * local : (j + 1) * local]
        rests.append(total[:, 3 * local :])
    for i in range(3):
        results[i].start()
    found = smalls[0]
    out_g1[...] = found[0:1, :width]
    out_g2[...] = found[0:1, width : 2 * width]
    head = dim_scale.shape[1]
    scale = jnp.zeros((1, head), F32)
    for j in range(2):
        for i in range(local // head):
            start = 2 * width + j * 384 + i * head
            scale = scale + found[0:1, start : start + head]
    raw = dim_scale[...]
    grown = jnp.maximum(raw, 0.0) + jnp.log(1.0 + jnp.exp(-jnp.abs(raw)))
    out_s[...] = scale / grown * (1.0 / (1.0 + jnp.exp(-raw)))
    totals = []
    for i in range(pieces):
        total = landed(1, i)
        out_u[pl.ds(i * step, step)] = total[:, :local]
        totals.append(total[:, local:])
    results[3].start()
    out_o[...] = jnp.transpose(jnp.concatenate(totals, axis=0))
    results[4].start()
    crossing.wait_recv()
    most = line[d, :, :split].astype(F32) + yd[...].astype(F32)
    out_d[...] = jnp.transpose(jnp.concatenate([most, jnp.concatenate(rests, axis=0)], axis=1))
    results[5].start()

    @pl.when(t == 0)
    def _():
        for i in range(4):
            piece = rows_out.at[i // 2, pl.ds(i % 2 * half, half)]
            remote(piece, piece, es_sem, er_sem.at[i], owner).wait_recv()

    @pl.when(direct)
    def _():
        remote(final, spot, es_sem, er_sem.at[t], owner).wait_send()

    @pl.when(aside)
    def _():
        remote(final, out_rows_a, es_sem, rs_sem.at[0], section).wait_send()

    @pl.when((s == 1) & (t > 1))
    def _():
        second.wait_send()

    @pl.when((s == 1) & (t < 2))
    def _():
        third(section).wait_send()

    for copy in results:
        copy.wait()
    crossing.wait_send()
    for i in range(3):
        share(i).wait_send()

    @pl.when(d < n - 1)
    def _():
        link(0, up).wait_send()

    @pl.when(d > 0)
    def _():
        link(1, down).wait_send()

    def drain(e, _):
        for which in range(2):
            for i in range(pieces):
                exchange(which, e, i).wait_send()

        @pl.when(e != d)
        def _():
            for which in range(2):
                for i in range(pieces):
                    piece = groups[which][0].at[e, pl.ds(i * step, step)]
                    remote(
                        piece, piece, fs_sem.at[which, e, i], fr_sem.at[which, e, i], up
                    ).wait_send()
            remote(line.at[e], line.at[e], ds_sem.at[e], dr_sem.at[e], up).wait_send()

        return 0

    lax.fori_loop(0, n, drain, 0)


def gradients(n1, n2, gy, g, gp, gu, o, a, final, rows, dg1, dg2, ds, dim_scale):
    n = lax.axis_size("dp")
    length, width = n1.shape
    local = gp.shape[2] // 3
    chunk = width // n
    pieces = 4 if chunk % 64 == 0 else 1
    small = (1, 2 * width + 768)

    def lines(columns):
        return [pltpu.VMEM((n, chunk, columns), BF16)] * 4 + [pltpu.VMEM((chunk, columns), BF16)]

    split = local // 128 * 128
    line = pltpu.VMEM((n, chunk, 2 * split), BF16)
    return pl.pallas_call(
        gradient_kernel,
        out_shape=[jax.ShapeDtypeStruct((chunk, local), F32)] * 4
        + [jax.ShapeDtypeStruct((local, chunk), F32)] * 2
        + [
            jax.ShapeDtypeStruct(rows.shape, BF16),
            jax.ShapeDtypeStruct(dg1.shape, F32),
            jax.ShapeDtypeStruct(dg2.shape, F32),
            jax.ShapeDtypeStruct(dim_scale.shape, F32),
        ],
        in_specs=[ANY] * 10 + [VMEM] * 4,
        out_specs=[ANY] * 7 + [VMEM] * 3,
        input_output_aliases={9: 6},
        scratch_shapes=[pltpu.VMEM((chunk, local), F32)] * 4
        + [pltpu.VMEM((local, chunk), F32)] * 2
        + [
            pltpu.VMEM((2, length, width), BF16),
            pltpu.VMEM((4, n, chunk, length), BF16),
            pltpu.VMEM(gp.shape, BF16),
            pltpu.VMEM(gu.shape, BF16),
            pltpu.VMEM(o.shape, BF16),
            pltpu.VMEM(a.shape, BF16),
        ]
        + lines(4 * local - split)
        + lines(2 * local)
        + [line] * 2
        + [
            pltpu.VMEM((chunk, 2 * split), BF16),
            pltpu.VMEM((2, n, chunk, local - split), BF16),
            pltpu.VMEM((chunk, split), BF16),
            pltpu.VMEM(small, F32),
            pltpu.VMEM((3,) + small, F32),
            pltpu.VMEM((4,) + small, F32),
            pltpu.VMEM(final.shape, BF16),
            pltpu.VMEM(final.shape, BF16),
            DMA((4,)),
            DMA((4,)),
        ]
        + [DMA((2, n, pieces))] * 4
        + [
            DMA((2, pieces)),
            DMA((n,)),
            DMA((n,)),
            DMA,
            DMA,
            DMA,
            DMA((3,)),
            DMA((3,)),
            DMA((2,)),
            DMA((2,)),
            DMA,
            DMA((4,)),
            DMA((6,)),
            DMA((2,)),
            DMA((2,)),
            pltpu.SemaphoreType.REGULAR,
        ],
        compiler_params=pltpu.CompilerParams(
            collective_id=3, has_side_effects=True, vmem_limit_bytes=62 * MIB
        ),
        name="gradients",
    )(n1, n2, gy, g, gp, gu, o, a, final, rows, dg1, dg2, ds, dim_scale)


def hand_over_kernel(*refs):
    count = (len(refs) - 2) // 3
    sources, results, kept = refs[:count], refs[count : 2 * count], refs[2 * count : 3 * count]
    in_sem, out_sem = refs[3 * count :]
    come = [pltpu.make_async_copy(sources[i], kept[i], in_sem.at[i]) for i in range(count)]
    go = [pltpu.make_async_copy(kept[i], results[i], out_sem.at[i]) for i in range(count)]
    for copy in come:
        copy.start()
    for i in range(count):
        come[i].wait()
        go[i].start()
    for copy in go:
        copy.wait()


def hand_over(arrays):
    count = len(arrays)
    return pl.pallas_call(
        hand_over_kernel,
        out_shape=[jax.ShapeDtypeStruct(x.shape, x.dtype) for x in arrays],
        in_specs=[ANY] * count,
        out_specs=[ANY] * count,
        scratch_shapes=[pltpu.VMEM(x.shape, x.dtype) for x in arrays] + [DMA((count,)), DMA((count,))],
        compiler_params=pltpu.CompilerParams(vmem_limit_bytes=62 * MIB),
        name="hand_over",
    )(*arrays)


def body(
    inputs, cotangent, gain_attn, w_query, w_key, w_value, w_out, dim_scale, gain_mlp, w_up, w_down
):
    head = dim_scale.shape[1]
    shards = (w_query[0].T, w_key[0].T, w_value[0].T, w_out[0], w_up[0].T, w_down[0])
    done = forward(
        inputs, cotangent, shards, gain_attn, gain_mlp, dim_scale, head
    )
    x_halves, h, n1, q, k, v, o, lse, m, n2, u, a, g, win, wo, wu, wd = done
    layer_out, input_grads, final, g_all, gu, gy, gp, dg1, dg2, ds = backward(
        (g, h, q, k, v, o, lse, m, u, win, wo, wu, wd, x_halves),
        gain_attn,
        gain_mlp,
        dim_scale,
    )

    *pieces, input_grads, dg1, dg2, grad_scale = gradients(
        n1, n2, gy, g_all, gp, gu, o, a, final, input_grads, dg1, dg2, ds, dim_scale
    )
    results = hand_over([layer_out, input_grads, dg1, *pieces, grad_scale, dg2])
    layer_out, input_grads, dg1, *pieces, grad_scale, dg2 = results
    return (
        layer_out[None],
        input_grads[None],
        dg1,
        pieces[0][None],
        pieces[1][None],
        pieces[2][None],
        pieces[4][None],
        grad_scale,
        dg2,
        pieces[3][None],
        pieces[5][None],
    )


def solution(mesh):
    in_specs = (
        P("dp", "tensor", None),
        P("dp", "tensor", None),
        P("section", None),
        P("section", None, "tensor"),
        P("section", None, "tensor"),
        P("section", None, "tensor"),
        P("section", "tensor", None),
        P("section", None),
        P("section", None),
        P("section", None, "tensor"),
        P("section", "tensor", None),
    )
    out_specs = (
        P("section", "dp", "tensor", None),
        P("section", "dp", "tensor", None),
        P("section", None),
        P("section", "dp", "tensor"),
        P("section", "dp", "tensor"),
        P("section", "dp", "tensor"),
        P("section", "tensor", "dp"),
        P("section", None),
        P("section", None),
        P("section", "dp", "tensor"),
        P("section", "tensor", "dp"),
    )
    return jax.shard_map(body, mesh=mesh, in_specs=in_specs, out_specs=out_specs, check_vma=False)
```

```python
import functools
import math

import jax
import jax.numpy as jnp
from jax import lax
from jax.experimental import pallas as pl
from jax.experimental.pallas import tpu as pltpu
from jax.sharding import PartitionSpec as P

EPS = 1e-06
LOG2E = 1.442695041
NEGATIVE = -1e30
BF16 = jnp.bfloat16
F32 = jnp.float32
MESH = pl.DeviceIdType.MESH
ANY = pl.BlockSpec(memory_space=pl.ANY)
VMEM = pl.BlockSpec(memory_space=pltpu.VMEM)
DMA = pltpu.SemaphoreType.DMA
MIB = 1 << 20
PIECES = 4


def plain(a, b):
    return jnp.dot(a, b, preferred_element_type=F32)


def by_last(a, b):
    return lax.dot_general(a, b, (((1,), (1,)), ((), ())), preferred_element_type=F32)


def by_first(a, b):
    return lax.dot_general(a, b, (((0,), (0,)), ((), ())), preferred_element_type=F32)


def other(index):
    return index + 1 - 2 * lax.rem(index, 2)


def remote(src, dst, send, receive, device):
    return pltpu.make_async_remote_copy(
        src_ref=src,
        dst_ref=dst,
        send_sem=send,
        recv_sem=receive,
        device_id=device,
        device_id_type=MESH,
    )


def greet(devices):
    barrier = pltpu.get_barrier_semaphore()
    for device in devices:
        pl.semaphore_signal(barrier, inc=1, device_id=device, device_id_type=MESH)
    pl.semaphore_wait(barrier, len(devices))


def per_dim(raw):
    grown = jnp.maximum(raw, 0.0) + jnp.log(1.0 + jnp.exp(-jnp.abs(raw)))
    return (LOG2E / math.sqrt(raw.shape[1])) * grown


def inverse_rms(rows):
    return lax.rsqrt(jnp.mean(rows * rows, axis=1, keepdims=True) + EPS)


def forward_kernel(
    inputs, cotangent, w_q, w_k, w_v, w_o, w_u, w_d, gain_one, gain_two, scale,
    x_out, h_out, n1_out, q_out, k_out, v_out, o_out, lse_out, m_out, n2_out, u_out, a_out,
    g_out, win_out, wo_out, wu_out, wd_out,
    land, win, wo, wu, wd, passing, down_a, down_b, n1, q, k, v, o_heads, o, lse_cols, lse, ysend, yrecv,
    m, n2, u, a, zpart, zrecv, xout,
    own_sem, ps_sem, pr_sem, xs_sem, xp_sem, xr_sem, xfs_sem, wys_sem, wyr_sem, wzs_sem, wzr_sem,
    das_sem, dar_sem, dbs_sem, dbr_sem, dcs_sem, dcr_sem,
    ns_sem, nr_sem, nfs_sem, nfr_sem, ys_sem, yr_sem, zs_sem, zr_sem, save_sem,
):
    s, t, d = lax.axis_index("section"), lax.axis_index("tensor"), lax.axis_index("dp")
    blocks, rows, width = land.shape[1:]
    half = rows // 2
    local = w_o.shape[0]
    heads, _, head = q.shape
    per = heads // 2
    c, y = lax.rem(t, 2), t // 2
    t_core, t_across = other(t), lax.rem(t + 2, 4)
    t_diagonal = other(t_across)
    core = (s, t_core, d)
    across = (s, t_across, d)
    diagonal = (s, t_diagonal, d)
    beside = (s, t, other(d))
    section = (1 - s, t, d)
    greet([core, across, diagonal, beside, section])

    mine = pl.ds(pl.multiple_of(c * half, half), half)
    theirs = pl.ds(pl.multiple_of((1 - c) * half, half), half)

    shards = [w_q, w_k, w_v, w_o, w_u, w_d]

    def place(i, slot, start, size):
        if i < 3:
            return win.at[slot, pl.ds(pl.multiple_of(i * local + start, 16), size)]
        return (wo, wu, wd)[i - 3].at[pl.ds(pl.multiple_of(slot * local + start, 16), size)]

    short = local // 4
    parity = lax.rem(d, 2)

    def own(i):
        return pltpu.make_async_copy(shards[i], place(i, 0, 0, local), own_sem.at[i])

    def strip(i, which):
        return pl.multiple_of(which * 2 * short + i % 2 * short, 16)

    def crossing(i):
        start = strip(i, parity)
        dst = place(i // 2, 1, start, short)
        return remote(
            shards[i // 2].at[pl.ds(start, short)], dst, wys_sem.at[i], wyr_sem.at[i], across
        )

    def beside_copy(i, which):
        piece = place(i // 2, 1, strip(i, which), short)
        return remote(piece, piece, wzs_sem.at[i], wzr_sem.at[i], beside)

    def relay(i):
        crossing(i).wait_recv()
        beside_copy(i, parity).start()

    def arrived(i):
        beside_copy(i, 1 - parity).wait_recv()

    quarter = local // PIECES

    def down_piece(buffer, i):
        return buffer.at[pl.ds(i * quarter, quarter)]

    def down_first(i):
        return remote(
            down_piece(w_d, i), down_piece(down_a, i), das_sem.at[i], dar_sem.at[i], section
        )

    def down_second(i):
        return remote(
            down_piece(down_a, i), down_piece(down_b, i), dbs_sem.at[i], dbr_sem.at[i], across
        )

    def down_third(i):
        return remote(
            down_piece(down_b, i), wd.at[pl.ds(local + i * quarter, quarter)],
            dcs_sem.at[i], dcr_sem.at[i], section,
        )

    step = rows // PIECES

    def passing_copy(i):
        piece = pl.ds(i * step, step)
        return remote(
            inputs.at[1 - y, piece], passing.at[piece], ps_sem.at[i], pr_sem.at[i], across
        )

    def onward(i):
        piece = pl.ds(i * step, step)
        return remote(
            passing.at[piece], land.at[0, t_across, piece], ps_sem.at[PIECES + i], xp_sem.at[i], section
        )

    def over(i):
        piece = pl.ds(i * step, step)
        return remote(
            cotangent.at[1 - y, piece], land.at[0, t, piece], xs_sem.at[i], xp_sem.at[i], across
        )

    def local_rows(source):
        pltpu.make_async_copy(source.at[y], land.at[0, t], xr_sem.at[t]).start()
        remote(source.at[y], land.at[0, t], xs_sem.at[PIECES], xr_sem.at[t], core).start()

    def block_wait(b):
        piece = land.at[0, b]
        remote(piece, piece, xs_sem.at[PIECES], xr_sem.at[b], core).wait_recv()

    def far_rows():
        for i in range(PIECES):
            piece = land.at[0, t_across, pl.ds(i * step, step)]
            remote(piece, piece, xfs_sem, xp_sem.at[i], core).wait_recv()
        piece = land.at[0, t_across]
        remote(piece, piece, xfs_sem, xr_sem.at[t_across], core).start()

    def near_rows():
        block_wait(t)
        block_wait(t_core)

    for i in range(3):
        own(i).start()

    @pl.when(s == 0)
    def _():
        for i in range(10):
            crossing(i).start()
        local_rows(inputs)
        for i in range(PIECES):
            down_first(i).start()

    @pl.when(s == 1)
    def _():
        for i in range(PIECES):
            passing_copy(i).start()
        local_rows(cotangent)

    for i in range(3, 6):
        own(i).start()

    @pl.when(s == 1)
    def _():
        for i in range(PIECES):
            passing_copy(i).wait_recv()
            onward(i).start()
            down_first(i).wait_recv()
            down_second(i).start()
        for i in range(12):
            crossing(i).start()
        for i in range(PIECES):
            over(i).start()
        for i in range(PIECES):
            down_second(i).wait_recv()
            down_third(i).start()
        for i in range(6):
            relay(i)

    for i in range(3):
        own(i).wait()

    def save(kind, b, src, dst):
        pltpu.make_async_copy(src, dst, save_sem.at[kind, b]).start()

    causal = lax.broadcasted_iota(jnp.int32, (rows, rows), 0) >= lax.broadcasted_iota(
        jnp.int32, (rows, rows), 1
    )
    lane = lax.broadcasted_iota(jnp.int32, (rows, 128), 1)

    factor = per_dim(scale[...])

    def attention(turn, _):
        b = jnp.where(s == 0, lax.rem(turn, blocks), turn // 2)
        j = jnp.where(s == 0, turn // blocks, lax.rem(turn, 2))
        at = pl.ds(pl.multiple_of(b * rows, rows), rows)

        @pl.when((s == 0) & (turn == 0))
        def _():
            near_rows()

        @pl.when((s == 0) & (turn == 2 * (1 - y)))
        def _():
            for i in range(4):
                relay(i)
            far_rows()
            block_wait(t_diagonal)

        @pl.when((s == 0) & (turn == blocks))
        def _():
            relay(6)
            relay(7)
            for i in range(6):
                arrived(i)

        @pl.when((s == 1) & (turn == 0))
        def _():
            for i in range(6):
                arrived(i)

        @pl.when((s == 1) & (j == 0))
        def _():
            piece = land.at[1, b, mine]
            remote(piece, piece, ns_sem.at[b], nr_sem.at[b], core).wait_recv()
            remote(piece, piece, nfs_sem.at[b], nfr_sem.at[b], core).start()
            rest = land.at[1, b, theirs]
            remote(rest, rest, nfs_sem.at[b], nfr_sem.at[b], core).wait_recv()

        @pl.when(j == 0)
        def _():
            hidden = land[s, b].astype(F32)
            n1[at] = (hidden * inverse_rms(hidden) * gain_one[...]).astype(BF16)
            lse_cols[b] = jnp.zeros(lse_cols.shape[1:], F32)
            save(0, b, land.at[s, b], h_out.at[b])
            save(1, b, n1.at[at], n1_out.at[at])

        projected = by_last(n1[at], win[j])
        first = j * per
        for i in range(per):
            cut = i * head
            q[first + i, at] = (projected[:, cut : cut + head] * factor).astype(BF16)
            cut += local
            k[first + i, at] = projected[:, cut : cut + head].astype(BF16)
            cut += local
            v[first + i, at] = projected[:, cut : cut + head].astype(BF16)
        for bb in range(blocks):

            @pl.when(b == bb)
            def _():
                for i in range(per):
                    hd = first + i
                    qh = q[hd, bb * rows : (bb + 1) * rows]
                    near = by_last(qh, k[hd, bb * rows : (bb + 1) * rows])
                    near = jnp.where(causal, near, NEGATIVE)
                    top = jnp.max(near, axis=1, keepdims=True)
                    if bb:
                        far = by_last(qh, k[hd, : bb * rows])
                        top = jnp.maximum(top, jnp.max(far, axis=1, keepdims=True))
                    near = jnp.exp(near - top)
                    total = jnp.sum(near, axis=1, keepdims=True)
                    mixed = plain(near.astype(BF16), v[hd, bb * rows : (bb + 1) * rows])
                    if bb:
                        far = jnp.exp(far - top)
                        total = total + jnp.sum(far, axis=1, keepdims=True)
                        mixed = mixed + plain(far.astype(BF16), v[hd, : bb * rows])
                    o_heads[hd, bb * rows : (bb + 1) * rows] = (mixed / total).astype(BF16)
                    lse_cols[bb] = jnp.where(lane == hd, top + jnp.log(total), lse_cols[bb])

        @pl.when(j == 1)
        def _():
            o[at] = jnp.concatenate([o_heads[i, at] for i in range(heads)], axis=1)
            lse[b] = jnp.transpose(lse_cols[b])[:heads]
            save(2, b, q.at[:, at], q_out.at[:, at])
            save(3, b, k.at[:, at], k_out.at[:, at])
            save(4, b, v.at[:, at], v_out.at[:, at])
            save(5, b, o.at[at], o_out.at[at])
            save(6, b, lse.at[b], lse_out.at[b])

        for i, when in ((4, 2), (5, 3), (8, 4), (9, 5)):

            @pl.when((s == 0) & (turn == when))
            def _():
                relay(i)

        for i in range(6):

            @pl.when((s == 1) & (turn == i))
            def _():
                relay(6 + i)

        return 0

    def project(b, _):
        @pl.when(b == 0)
        def _():
            own(3).wait()
            arrived(6)
            arrived(7)

        at = pl.ds(pl.multiple_of(b * rows, rows), rows)
        ysend[b] = plain(o[at], wo[...]).astype(BF16)
        remote(ysend.at[b], yrecv.at[b], ys_sem.at[b], yr_sem.at[b], core).start()
        return 0

    lax.fori_loop(0, 2 * blocks, attention, 0)

    lax.fori_loop(0, blocks, project, 0)

    own(4).wait()
    own(5).wait()
    arrived(8)
    arrived(9)

    @pl.when(s == 0)
    def _():
        for i in range(PIECES):
            down_third(i).wait_recv()

    @pl.when(s == 1)
    def _():
        arrived(10)
        arrived(11)

    weights = [(win, win_out), (wo, wo_out), (wu, wu_out), (wd, wd_out)]
    for i, (src, dst) in enumerate(weights):
        save(11, i, src, dst)

    def feed(b, _):
        at = pl.ds(pl.multiple_of(b * rows, rows), rows)
        remote(ysend.at[b], yrecv.at[b], ys_sem.at[b], yr_sem.at[b], core).wait_recv()
        middle = land[s, b].astype(F32) + (ysend[b].astype(F32) + yrecv[b].astype(F32))
        m[b] = middle
        normed = (middle * inverse_rms(middle) * gain_two[...]).astype(BF16)
        n2[at] = normed
        up = by_last(normed, wu[...])
        u[b] = up
        active = (up / (1.0 + jnp.exp(-up))).astype(BF16)
        a[at] = active
        zpart[b] = plain(active, wd[...])
        copy = remote(zpart.at[b, theirs], zrecv.at[b], zs_sem.at[b], zr_sem.at[b], core)
        copy.start()
        save(7, b, m.at[b], m_out.at[b])
        save(8, b, n2.at[at], n2_out.at[at])
        save(9, b, u.at[b], u_out.at[b])
        save(10, b, a.at[at], a_out.at[at])

        @pl.when(s == 0)
        def _():
            finish(b)

        @pl.when((s == 1) & (b > 0))
        def _():
            finish(b - 1)

        @pl.when((s == 1) & (b == blocks - 2))
        def _():
            near_rows()
            far_rows()

        return 0

    def finish(b):
        copy = remote(zpart.at[b, theirs], zrecv.at[b], zs_sem.at[b], zr_sem.at[b], core)
        copy.wait_recv()
        xout[b] = (m[b, mine] + (zpart[b, mine] + zrecv[b])).astype(BF16)

        @pl.when(s == 0)
        def _():
            remote(xout.at[b], land.at[1, b, mine], ns_sem.at[b], nr_sem.at[b], section).start()

        save(13, b, xout.at[b], x_out.at[b])

    lax.fori_loop(0, blocks, feed, 0)

    @pl.when(s == 1)
    def _():
        finish(blocks - 1)


    @pl.when(s == 1)
    def _():
        block_wait(t_diagonal)

    for b in range(blocks):
        pltpu.make_async_copy(land.at[0, b], g_out.at[b], save_sem.at[12, b]).start()

    block = land.at[0, t]
    remote(block, block, xs_sem.at[PIECES], xr_sem.at[t], core).wait_send()
    remote(block, block, xfs_sem, xr_sem.at[t], core).wait_send()

    @pl.when(s == 1)
    def _():
        for i in range(PIECES):
            passing_copy(i).wait_send()
            onward(i).wait_send()
            over(i).wait_send()
            down_second(i).wait_send()
            down_third(i).wait_send()
        for i in range(10, 12):
            crossing(i).wait_send()
            beside_copy(i, parity).wait_send()

    @pl.when(s == 0)
    def _():
        for i in range(PIECES):
            down_first(i).wait_send()

    for b in range(blocks):
        piece = land.at[0, b, mine]
        remote(ysend.at[b], yrecv.at[b], ys_sem.at[b], yr_sem.at[b], core).wait_send()
        remote(zpart.at[b, theirs], zrecv.at[b], zs_sem.at[b], zr_sem.at[b], core).wait_send()

        @pl.when(s == 0)
        def _():
            remote(xout.at[b], piece, ns_sem.at[b], nr_sem.at[b], section).wait_send()

        @pl.when(s == 1)
        def _():
            remote(piece, piece, nfs_sem.at[b], nfr_sem.at[b], core).wait_send()

    for i in range(10):
        crossing(i).wait_send()
        beside_copy(i, parity).wait_send()
    for i, (src, dst) in enumerate(weights):
        pltpu.make_async_copy(src, dst, save_sem.at[11, i]).wait()
    for b in range(blocks):
        at = pl.ds(b * rows, rows)
        saved = [
            (land.at[s, b], h_out.at[b]),
            (n1.at[at], n1_out.at[at]),
            (q.at[:, at], q_out.at[:, at]),
            (k.at[:, at], k_out.at[:, at]),
            (v.at[:, at], v_out.at[:, at]),
            (o.at[at], o_out.at[at]),
            (lse.at[b], lse_out.at[b]),
            (m.at[b], m_out.at[b]),
            (n2.at[at], n2_out.at[at]),
            (u.at[b], u_out.at[b]),
            (a.at[at], a_out.at[at]),
        ]
        for kind, (src, dst) in enumerate(saved):
            pltpu.make_async_copy(src, dst, save_sem.at[kind, b]).wait()
        pltpu.make_async_copy(land.at[0, b], g_out.at[b], save_sem.at[12, b]).wait()
        pltpu.make_async_copy(xout.at[b], x_out.at[b], save_sem.at[13, b]).wait()


def forward(inputs, cotangent, shards, gain_one, gain_two, scale, head):
    _, rows, width = inputs.shape
    local = shards[0].shape[0]
    heads = 2 * local // head
    blocks = lax.axis_size("tensor")
    length = blocks * rows
    half = rows // 2
    shape = jax.ShapeDtypeStruct
    weights = [(2, 3 * local, width), (2 * local, width), (2 * local, width), (2 * local, width)]
    outs = [
        shape((blocks, half, width), BF16),
        shape((blocks, rows, width), BF16),
        shape((length, width), BF16),
        shape((heads, length, head), BF16),
        shape((heads, length, head), BF16),
        shape((heads, length, head), BF16),
        shape((length, 2 * local), BF16),
        shape((blocks, heads, rows), F32),
        shape((blocks, rows, width), F32),
        shape((length, width), BF16),
        shape((blocks, rows, 2 * local), F32),
        shape((length, 2 * local), BF16),
        shape((blocks, rows, width), BF16),
    ] + [shape(w, BF16) for w in weights]
    scratch = [pltpu.VMEM((2, blocks, rows, width), BF16)]
    scratch += [pltpu.VMEM(w, BF16) for w in weights]
    scratch += [
        pltpu.VMEM((rows, width), BF16),
        pltpu.VMEM((local, width), BF16),
        pltpu.VMEM((local, width), BF16),
        pltpu.VMEM((length, width), BF16),
        pltpu.VMEM((heads, length, head), BF16),
        pltpu.VMEM((heads, length, head), BF16),
        pltpu.VMEM((heads, length, head), BF16),
        pltpu.VMEM((heads, length, head), BF16),
        pltpu.VMEM((length, 2 * local), BF16),
        pltpu.VMEM((blocks, rows, 128), F32),
        pltpu.VMEM((blocks, heads, rows), F32),
        pltpu.VMEM((blocks, rows, width), BF16),
        pltpu.VMEM((blocks, rows, width), BF16),
        pltpu.VMEM((blocks, rows, width), F32),
        pltpu.VMEM((length, width), BF16),
        pltpu.VMEM((blocks, rows, 2 * local), F32),
        pltpu.VMEM((length, 2 * local), BF16),
        pltpu.VMEM((blocks, rows, width), F32),
        pltpu.VMEM((blocks, half, width), F32),
        pltpu.VMEM((blocks, half, width), BF16),
        DMA((6,)),
        DMA((2 * PIECES,)),
        DMA((PIECES,)),
        DMA((PIECES + 1,)),
        DMA((PIECES,)),
        DMA((blocks,)),
        DMA,
    ]
    scratch += [DMA((12,))] * 4 + [DMA((PIECES,))] * 6 + [DMA((blocks,))] * 8 + [DMA((14, blocks))]
    return pl.pallas_call(
        forward_kernel,
        out_shape=outs,
        in_specs=[ANY] * 8 + [VMEM] * 3,
        out_specs=[ANY] * len(outs),
        scratch_shapes=scratch,
        compiler_params=pltpu.CompilerParams(
            collective_id=1, has_side_effects=True, vmem_limit_bytes=62 * MIB
        ),
        name="forward",
    )(inputs, cotangent, *shards, gain_one, gain_two, scale)


def backward_kernel(
    g_in, h_in, q_in, k_in, v_in, o_in, lse_in, m_in, u_in, win_in, wo_in, wu_in, wd_in, x_in,
    gain_one, gain_two, scale,
    x_rows, out_rows, final, g_out, gu_out, gy_out, gp_out, dg1, dg2, ds,
    g, win, wo, wu, wd, h, q, k, v, o, lse, m, u, gu, gy, gp, ysend, yrecv, gm, go_heads, gq_heads,
    delta, dk, dv, n1part, n1recv, xout,
    load_sem, w_sem, ns_sem, nr_sem, nfs_sem, nfr_sem, ys_sem, yr_sem, zs_sem, zr_sem, os_sem, or_sem,
    xs_sem, xr_sem, save_sem,
):
    s, t, d = lax.axis_index("section"), lax.axis_index("tensor"), lax.axis_index("dp")
    blocks, rows, width = g.shape
    half = rows // 2
    local = wu.shape[0] // 2
    heads, _, head = q.shape
    per = heads // 2
    c, y = lax.rem(t, 2), t // 2
    core = (s, other(t), d)
    across = (s, lax.rem(t + 2, 4), d)
    diagonal = (s, other(lax.rem(t + 2, 4)), d)
    section = (1 - s, t, d)
    mine = pl.ds(pl.multiple_of(c * half, half), half)
    theirs = pl.ds(pl.multiple_of((1 - c) * half, half), half)

    weights = [(wd_in, wd), (wu_in, wu), (wo_in, wo), (win_in, win)]

    def weight(i):
        return pltpu.make_async_copy(*weights[i], w_sem.at[i])

    def load(kind, b):
        at = pl.ds(pl.multiple_of(b * rows, rows), rows)
        src, dst = [
            (u_in.at[b], u.at[b]),
            (m_in.at[b], m.at[b]),
            (o_in.at[at], o.at[at]),
            (q_in.at[:, at], q.at[:, at]),
            (k_in.at[:, at], k.at[:, at]),
            (v_in.at[:, at], v.at[:, at]),
            (lse_in.at[b], lse.at[b]),
            (h_in.at[b, mine], h.at[b]),
        ][kind]
        return pltpu.make_async_copy(src, dst, load_sem.at[kind, b])

    def incoming(b):
        return pltpu.make_async_copy(g_in.at[b], g.at[b], nr_sem.at[b])

    last = blocks - 1

    @pl.when(s == 1)
    def _():
        incoming(last).start()

    weight(0).start()
    load(0, last).start()
    weight(1).start()
    load(1, last).start()

    barrier = pltpu.get_barrier_semaphore()
    for device in (core, across, diagonal, section):
        pl.semaphore_signal(barrier, inc=1, device_id=device, device_id_type=MESH)

    weight(2).start()
    for kind in (2, 3, 6):
        load(kind, last).start()
    for bb in reversed(range(blocks)):
        load(4, bb).start()
        load(5, bb).start()
    weight(3).start()
    load(7, last).start()

    spot = out_rows.at[y, mine]

    def owner_copy(b, src, dst, send, receive, act):
        @pl.when(b == t)
        def _():
            act(pltpu.make_async_copy(src, dst, receive.at[t]))

        @pl.when(b != t)
        def _():
            act(remote(src, dst, send.at[b], receive.at[t], (s, b, d)))

    dg1[...] = jnp.zeros_like(dg1)
    dg2[...] = jnp.zeros_like(dg2)
    ds[...] = jnp.zeros_like(ds)

    causal = lax.broadcasted_iota(jnp.int32, (rows, rows), 0) <= lax.broadcasted_iota(
        jnp.int32, (rows, rows), 1
    )
    factor = jnp.concatenate([per_dim(scale[...])] * per, axis=1)
    width_two = heads * head
    row_head = lax.broadcasted_iota(jnp.int32, (heads, width_two), 0)
    start = row_head * head
    place = lax.broadcasted_iota(jnp.int32, (heads, width_two), 1)
    member = jnp.where((place >= start) & (place < start + head), 1.0, 0.0).astype(BF16)

    def save(kind, b, src, dst):
        pltpu.make_async_copy(src, dst, save_sem.at[kind, b]).start()

    def neighbours_sum(b, i):
        lanes = pl.ds(i * (width // 2), width // 2)
        return remote(
            ysend.at[b, :, lanes], yrecv.at[b, :, lanes], ys_sem.at[i, b], yr_sem.at[i, b], core
        )

    def up_part(turn):
        b = last - turn
        at = pl.ds(pl.multiple_of(b * rows, rows), rows)

        @pl.when(s == 1)
        def _():
            incoming(b).wait()

        @pl.when(turn == 0)
        def _():
            pl.semaphore_wait(barrier, 4)

        @pl.when(s == 0)
        def _():
            piece = g.at[b, mine]
            remote(piece, piece, ns_sem.at[b], nr_sem.at[b], core).wait_recv()
            remote(piece, piece, nfs_sem.at[b], nfr_sem.at[b], core).start()
            rest = g.at[b, theirs]
            remote(rest, rest, nfs_sem.at[b], nfr_sem.at[b], core).wait_recv()

        @pl.when(turn == 0)
        def _():
            weight(0).wait()

        load(0, b).wait()
        save(0, b, g.at[b], g_out.at[at])
        grad = g[b]
        grad_act = by_last(grad, wd[...])
        up = u[b]
        sigma = 1.0 / (1.0 + jnp.exp(-up))
        grad_up = (grad_act * sigma * (1.0 + up * (1.0 - sigma))).astype(BF16)
        gu[at] = grad_up

        @pl.when(turn == 0)
        def _():
            weight(1).wait()

        save(1, b, gu.at[at], gu_out.at[at])
        for i in range(2):
            lanes = slice(i * (width // 2), (i + 1) * (width // 2))
            ysend[b, :, lanes] = plain(grad_up, wu[:, lanes]).astype(BF16)
            neighbours_sum(b, i).start()

        @pl.when(turn == 0)
        def _():
            for bb in range(blocks):
                owner_copy(
                    bb, x_in.at[bb], x_rows.at[y, mine], xs_sem, xr_sem, lambda copy: copy.start()
                )

    def one_block(turn, _):
        b = last - turn
        at = pl.ds(pl.multiple_of(b * rows, rows), rows)
        load(1, b).wait()
        for i in range(2):
            neighbours_sum(b, i).wait_recv()
        grad = g[b]
        grad_normed = ysend[b].astype(F32) + yrecv[b].astype(F32)
        middle = m[b]
        inverse = inverse_rms(middle)
        unit = middle * inverse
        grad_unit = grad_normed * gain_two[...]
        dg2[...] += jnp.sum(grad_normed * unit, axis=0, keepdims=True)
        grad_middle = grad.astype(F32) + inverse * (
            grad_unit - unit * jnp.mean(grad_unit * unit, axis=1, keepdims=True)
        )
        gm[...] = grad_middle
        grad_mid = grad_middle.astype(BF16)
        gy[at] = grad_mid
        save(2, b, gy.at[at], gy_out.at[at])

        @pl.when(turn == 0)
        def _():
            weight(2).wait()

        load(2, b).wait()
        grad_mixed = by_last(grad_mid, wo[...]).astype(BF16)
        both = grad_mixed.astype(F32) * o[at].astype(F32)
        high = both.astype(BF16)
        low = (both - high.astype(F32)).astype(BF16)
        delta[...] = by_last(member, high) + by_last(member, low)
        for i in range(heads):
            go_heads[i] = grad_mixed[:, i * head : (i + 1) * head]

        @pl.when(turn == 0)
        def _():
            for bb in range(blocks):
                load(4, bb).wait()
                load(5, bb).wait()

        load(3, b).wait()
        load(6, b).wait()

        @pl.when(turn < last)
        def _():
            for kind in (0, 1, 2, 3, 6, 7):
                load(kind, b - 1).start()

        @pl.when((turn < last) & (s == 1))
        def _():
            incoming(b - 1).start()

        for bb in range(blocks):

            @pl.when(b == bb)
            def _():
                def group(first, _):
                    for j in range(per):
                        i = first * per + j
                        qh = q[i, bb * rows : (bb + 1) * rows]
                        gh = go_heads[i]
                        offset = lse[bb, pl.ds(i, 1)]
                        inner = delta[pl.ds(i, 1)]
                        total = None
                        for lo, hi in ((bb * rows, (bb + 1) * rows), (0, bb * rows)):
                            if lo == hi:
                                continue
                            kj = k[i, lo:hi]
                            weight = jnp.exp(by_last(kj, qh) - offset)
                            if lo == bb * rows and hi > lo and hi == (bb + 1) * rows:
                                weight = jnp.where(causal, weight, 0.0)
                            grad_score = weight * (by_last(v[i, lo:hi], gh) - inner)
                            grad_score = grad_score.astype(BF16)
                            more_v = plain(weight.astype(BF16), gh)
                            more_k = plain(grad_score, qh)
                            if bb == last:
                                dv[i, lo:hi] = more_v
                                dk[i, lo:hi] = more_k
                            else:
                                dv[i, lo:hi] += more_v
                                dk[i, lo:hi] += more_k
                            part = by_first(kj, grad_score)
                            total = part if total is None else total + part
                        gq_heads[i] = jnp.transpose(total)
                    return 0

                lax.fori_loop(0, 2, group, 0)

        for j in range(2):
            mine_heads = range(j * per, (j + 1) * per)
            grad_scaled = jnp.concatenate([gq_heads[i] for i in mine_heads], axis=1)
            queries = jnp.concatenate([q[i, at] for i in mine_heads], axis=1).astype(F32)
            ds[pl.ds(j, 1)] += jnp.sum(grad_scaled * queries, axis=0, keepdims=True)
            grads = [
                (grad_scaled * factor).astype(BF16),
                jnp.concatenate([dk[i, at] for i in mine_heads], axis=1).astype(BF16),
                jnp.concatenate([dv[i, at] for i in mine_heads], axis=1).astype(BF16),
            ]
            gp[j, at] = jnp.concatenate(grads, axis=1)
        save(3, b, gp.at[:, at], gp_out.at[:, at])

        @pl.when(turn == 0)
        def _():
            weight(3).wait()

        n1part[...] = plain(gp[0, at], win[0]) + plain(gp[1, at], win[1])
        copy = remote(n1part.at[theirs], n1recv.at[b], zs_sem.at[b], zr_sem.at[b], core)
        copy.start()

        @pl.when(turn < last)
        def _():
            up_part(turn + 1)

        load(7, b).wait()
        hidden = h[b].astype(F32)
        inverse = inverse_rms(hidden)
        unit = hidden * inverse
        copy.wait_recv()
        grad_normed = n1part[mine] + n1recv[b]
        grad_unit = grad_normed * gain_one[...]
        dg1[...] += jnp.sum(grad_normed * unit, axis=0, keepdims=True)
        xout[b] = (
            gm[mine]
            + inverse * (grad_unit - unit * jnp.mean(grad_unit * unit, axis=1, keepdims=True))
        ).astype(BF16)

        @pl.when(s == 1)
        def _():
            remote(xout.at[b], g.at[b, mine], ns_sem.at[b], nr_sem.at[b], section).start()

        @pl.when(b > 0)
        def _():
            owner_copy(b, xout.at[b], spot, os_sem, or_sem, lambda copy: copy.start())

        @pl.when(b == 0)
        def _():
            save(4, 0, xout.at[0], final)

        copy.wait_send()
        return 0

    up_part(jnp.int32(0))
    lax.fori_loop(0, blocks, one_block, 0)

    for b in range(blocks):
        at = pl.ds(b * rows, rows)
        piece = g.at[b, mine]
        for i in range(2):
            neighbours_sum(b, i).wait_send()
        here = x_rows.at[b // 2, pl.ds((b % 2) * half, half)]
        remote(here, here, xs_sem.at[b], xr_sem.at[b], core).wait_recv()

        @pl.when(b != t)
        def _():
            remote(x_in.at[b], here, xs_sem.at[b], xr_sem.at[b], core).wait_send()

        @pl.when(t > 0)
        def _():
            here = out_rows.at[b // 2, pl.ds((b % 2) * half, half)]
            remote(here, here, os_sem.at[b], or_sem.at[b], core).wait_recv()

        @pl.when((b != t) & (b > 0))
        def _():
            remote(xout.at[b], here, os_sem.at[b], or_sem.at[b], core).wait_send()

        @pl.when(s == 1)
        def _():
            remote(xout.at[b], piece, ns_sem.at[b], nr_sem.at[b], section).wait_send()

        @pl.when(s == 0)
        def _():
            remote(piece, piece, nfs_sem.at[b], nfr_sem.at[b], core).wait_send()

        saved = [
            (g.at[b], g_out.at[at]),
            (gu.at[at], gu_out.at[at]),
            (gy.at[at], gy_out.at[at]),
            (gp.at[:, at], gp_out.at[:, at]),
        ]
        for kind, (src, dst) in enumerate(saved):
            pltpu.make_async_copy(src, dst, save_sem.at[kind, b]).wait()
    pltpu.make_async_copy(xout.at[0], final, save_sem.at[4, 0]).wait()


def backward(saved, gain_one, gain_two, scale):
    g_in, h_in, q_in = saved[:3]
    win_in, wo_in, wu_in, wd_in = saved[9:13]
    blocks, rows, width = g_in.shape
    heads, length, head = q_in.shape
    local = wu_in.shape[0] // 2
    half = rows // 2
    shape = jax.ShapeDtypeStruct
    outs = [
        shape((2, rows, width), BF16),
        shape((2, rows, width), BF16),
        shape((half, width), BF16),
        shape((length, width), BF16),
        shape((length, 2 * local), BF16),
        shape((length, width), BF16),
        shape((2, length, 3 * local), BF16),
        shape((1, width), F32),
        shape((1, width), F32),
        shape((2, local), F32),
    ]
    scratch = [
        pltpu.VMEM((blocks, rows, width), BF16),
        pltpu.VMEM(win_in.shape, BF16),
        pltpu.VMEM(wo_in.shape, BF16),
        pltpu.VMEM(wu_in.shape, BF16),
        pltpu.VMEM(wd_in.shape, BF16),
        pltpu.VMEM((blocks, half, width), BF16),
        pltpu.VMEM((heads, length, head), BF16),
        pltpu.VMEM((heads, length, head), BF16),
        pltpu.VMEM((heads, length, head), BF16),
        pltpu.VMEM((length, 2 * local), BF16),
        pltpu.VMEM((blocks, heads, rows), F32),
        pltpu.VMEM((blocks, rows, width), F32),
        pltpu.VMEM((blocks, rows, 2 * local), F32),
        pltpu.VMEM((length, 2 * local), BF16),
        pltpu.VMEM((length, width), BF16),
        pltpu.VMEM((2, length, 3 * local), BF16),
        pltpu.VMEM((blocks, rows, width), BF16),
        pltpu.VMEM((blocks, rows, width), BF16),
        pltpu.VMEM((rows, width), F32),
        pltpu.VMEM((heads, rows, head), BF16),
        pltpu.VMEM((heads, rows, head), F32),
        pltpu.VMEM((heads, rows), F32),
        pltpu.VMEM((heads, length, head), F32),
        pltpu.VMEM((heads, length, head), F32),
        pltpu.VMEM((rows, width), F32),
        pltpu.VMEM((blocks, half, width), F32),
        pltpu.VMEM((blocks, half, width), BF16),
        DMA((8, blocks)),
        DMA((4,)),
    ]
    scratch += [DMA((blocks,))] * 4 + [DMA((2, blocks))] * 2 + [DMA((blocks,))] * 6 + [DMA((5, blocks))]
    return pl.pallas_call(
        backward_kernel,
        out_shape=outs,
        in_specs=[ANY] * 14 + [VMEM] * 3,
        out_specs=[ANY] * 7 + [VMEM] * 3,
        scratch_shapes=scratch,
        compiler_params=pltpu.CompilerParams(
            collective_id=2, has_side_effects=True, vmem_limit_bytes=62 * MIB
        ),
        name="backward",
    )(*saved, gain_one, gain_two, scale)


def farthest_first(d, k, n):
    found = 0
    for i in range(n):
        above = list(range(n - 1, i, -1))
        below = list(range(i))
        first, second = (above, below) if len(above) >= len(below) else (below, above)
        lead = len(first) - len(second) - 1
        order = first[: max(lead, 0)]
        rest = first[max(lead, 0) :]
        for j in range(max(len(rest), len(second))):
            order += rest[j : j + 1] + second[j : j + 1]
        order.append(i)
        picked = 0
        for j, e in enumerate(order):
            picked = picked + jnp.where(k == j, e, 0)
        found = found + jnp.where(d == i, picked, 0)
    return found


def gradient_kernel(
    n1_in, n2_in, gy_in, g_in, gp_in, gu_in, o_in, a_in, final, rows_in, dg1, dg2, ds, dim_scale,
    q_out, k_out, v_out, u_out, o_out, d_out, rows_out, out_g1, out_g2, out_s,
    out_q, out_k, out_v, out_u, out_o, out_d, x, xt, gp, gu, o, a,
    keep_a, give_a, yrecv_a, flow_a, last_a, keep_b, give_b, yrecv_b, flow_b, last_b,
    line, flow_d, last_d, rest, yd, small, smalls, chain, out_rows_a, out_rows_b,
    x_sem, g_sem, ys_sem, yr_sem, fs_sem, fr_sem, last_sem, ds_sem, dr_sem, last_d_sem,
    yds_sem, ydr_sem, ss_sem, sr_sem, cs_sem, cr_sem, es_sem, er_sem, out_sem, rs_sem, hop_sem, here_sem,
):
    s, t, d = lax.axis_index("section"), lax.axis_index("tensor"), lax.axis_index("dp")
    n, chunk, _ = keep_a.shape
    local = a.shape[1] // 2
    split = yd.shape[1]
    width = dg1.shape[1]
    pieces = ys_sem.shape[2]
    step = chunk // pieces
    core = (s, other(t), d)
    across = (s, lax.rem(t + 2, 4), d)
    diagonal = (s, other(lax.rem(t + 2, 4)), d)
    up = (s, t, lax.rem(d + 1, n))
    down = (s, t, lax.rem(d + n - 1, n))
    c, y = lax.rem(t, 2), t // 2

    sources = [g_in, n1_in, n2_in, gy_in]
    operands = [(a_in, a), (gp_in, gp), (gu_in, gu), (o_in, o)]

    def load(i):
        return pltpu.make_async_copy(sources[i], x.at[i % 2], x_sem.at[i])

    def operand(i):
        return pltpu.make_async_copy(*operands[i], g_sem.at[i])

    section = (1 - s, t, d)
    slanted = (1 - s, 1 - t, d)
    barrier = pltpu.get_barrier_semaphore()
    for device in (core, across, diagonal, up, down):
        pl.semaphore_signal(barrier, inc=1, device_id=device, device_id_type=MESH)

    @pl.when((s == 1) & (t != 1))
    def _():
        pl.semaphore_signal(barrier, inc=1, device_id=section, device_id_type=MESH)

    @pl.when((s == 1) & (t == 1))
    def _():
        pl.semaphore_signal(barrier, inc=1, device_id=slanted, device_id_type=MESH)

    load(0).start()
    operand(0).start()
    load(1).start()
    for i in range(1, 4):
        operand(i).start()

    small[0:1, :width] = dg1[...]
    small[0:1, width : 2 * width] = jnp.where(c == 0, dg2[...], 0.0)
    small[0:1, 2 * width : 2 * width + local] = ds[0:1]
    small[0:1, 2 * width + 384 : 2 * width + 384 + local] = ds[1:2]

    partners = [core, across, diagonal]

    def share(i):
        return remote(small, smalls.at[i], ss_sem.at[i], sr_sem.at[i], partners[i])

    def turn(i):
        load(i).wait()
        turned = jnp.transpose(x[i % 2])
        for e in range(n):
            xt[i, e] = turned[e * chunk : (e + 1) * chunk]
        if i + 2 < 4:
            load(i + 2).start()

    groups = [(keep_a, give_a, yrecv_a, flow_a, last_a), (keep_b, give_b, yrecv_b, flow_b, last_b)]

    def exchange(which, e, i):
        _, give, yrecv, _, _ = groups[which]
        rows = pl.ds(i * step, step)
        return remote(
            give.at[e, rows], yrecv.at[e, rows], ys_sem.at[which, e, i], yr_sem.at[which, e, i], across
        )

    def send_all(which, e):
        for i in range(pieces):
            exchange(which, e, i).start()

    def send_d(e):
        src = line.at[e]

        @pl.when(e > d)
        def _():
            remote(src, flow_d.at[e], ds_sem.at[e], dr_sem.at[e], up).start()

        @pl.when(e < d - 1)
        def _():
            remote(src, flow_d.at[e], ds_sem.at[e], dr_sem.at[e], down).start()

        @pl.when(e == d - 1)
        def _():
            remote(src, last_d, ds_sem.at[e], last_d_sem, down).start()

    def upstream_d(e):
        piece = flow_d.at[e]
        remote(piece, piece, ds_sem.at[e], dr_sem.at[e], up).wait_recv()
        line[e] = (line[e].astype(F32) + flow_d[e].astype(F32)).astype(BF16)

    def down_product(k):
        e = farthest_first(d, k, n)
        both = plain(xt[0, e], a[...]).astype(BF16)
        line[e] = jnp.concatenate([both[:, :split], both[:, local : local + split]], axis=1)
        for j in range(2):
            rest[j, e] = both[:, j * local + split : (j + 1) * local]

    def first_d(k):
        e = farthest_first(d, k, n)

        @pl.when(((d == 0) | (d == n - 1)) & (e != d))
        def _():
            send_d(e)

    def in_product(k, j):
        e = farthest_first(d, k, n)
        (keep_a, give_a)[j][e] = jnp.concatenate(
            [plain(xt[1, e], gp[j]).astype(BF16), rest[j, e]], axis=1
        )

    turn(0)
    operand(0).wait()
    down_product(0)
    turn(1)
    operand(1).wait()
    in_product(0, 1)

    heard = jnp.where(s == 0, jnp.where(t == 0, 2, jnp.where(t == 1, 0, 1)), 0)
    pl.semaphore_wait(barrier, 5 + heard)

    @pl.when((s == 0) & (t == 0))
    def _():
        pl.semaphore_signal(here_sem, inc=1, device_id=section, device_id_type=MESH)
        pl.semaphore_signal(here_sem, inc=1, device_id=slanted, device_id_type=MESH)

    send_all(0, farthest_first(d, 0, n))
    first_d(0)
    for i in range(3):
        share(i).start()

    half = final.shape[0]
    owner = (s, 0, d)
    spot = rows_out.at[y, pl.ds(pl.multiple_of(c * half, half), half)]

    @pl.when(t == 0)
    def _():
        pltpu.make_async_copy(final, spot, er_sem.at[0]).start()

    direct = (t == 1) | ((t > 1) & (s == 1))
    aside = (t > 1) & (s == 0)

    @pl.when(t == 1)
    def _():
        remote(final, spot, es_sem, er_sem.at[t], owner).start()

    @pl.when(aside)
    def _():
        remote(final, out_rows_a, es_sem, rs_sem.at[0], section).start()

    def more_down(k, _):
        down_product(k)
        first_d(k)
        return 0

    lax.fori_loop(1, n, more_down, 0)

    def more_in(k, _):
        in_product(k, 1)

        @pl.when(k < n - 1)
        def _():
            send_all(0, farthest_first(d, k, n))

        in_product(k, 0)
        return 0

    lax.fori_loop(1, n, more_in, 0)
    in_product(0, 0)

    turn(2)
    turn(3)
    operand(2).wait()
    operand(3).wait()

    def other_product(k, _):
        e = farthest_first(d, k, n)
        ups = plain(xt[2, e], gu[...])
        outs = plain(xt[3, e], o[...])
        for j, target in ((1, give_b), (0, keep_b)):
            cut = slice(j * local, (j + 1) * local)
            target[e] = jnp.concatenate([ups[:, cut], outs[:, cut]], axis=1).astype(BF16)
            if j:

                @pl.when(k < n - 1)
                def _():
                    send_all(1, e)

        return 0

    lax.fori_loop(0, n, other_product, 0)
    send_all(0, d)
    send_all(1, d)

    @pl.when((t > 1) & (s == 1))
    def _():
        remote(final, spot, es_sem, er_sem.at[t], owner).start()

    for i in range(3):
        share(i).wait_recv()
    mine = small[...] + smalls[0] + (smalls[1] + smalls[2])

    def link(i, device):
        return remote(chain.at[i], chain.at[2 + i], cs_sem.at[i], cr_sem.at[i], device)

    smalls[0] = mine
    for i, opens, closes, device in ((0, d == 0, d == n - 1, up), (1, d == n - 1, d == 0, down)):
        chain[i] = mine

        @pl.when(jnp.logical_not(opens))
        def _():
            link(i, device).wait_recv()
            chain[i] = mine + chain[2 + i]
            smalls[0] += chain[2 + i]

        @pl.when(jnp.logical_not(closes))
        def _():
            link(i, device).start()

    def middle(k):
        e = farthest_first(d, k, n)

        @pl.when((d > 0) & (d < n - 1) & (e != d))
        def _():
            upstream_d(e)
            send_d(e)

    def flows(which, k):
        e = farthest_first(d, k, n)
        keep, give, yrecv, flow, last = groups[which]
        send, receive = fs_sem.at[which], fr_sem.at[which]
        for i in range(pieces):
            at = pl.ds(i * step, step)
            exchange(which, e, i).wait_recv()
            first = ((e > d) & (d == 0)) | ((e < d) & (d == n - 1))

            @pl.when((e != d) & first)
            def _():
                keep[e, at] = (keep[e, at].astype(F32) + yrecv[e, at].astype(F32)).astype(BF16)

            @pl.when((e != d) & jnp.logical_not(first))
            def _():
                piece = flow.at[e, at]
                remote(piece, piece, send.at[e, i], receive.at[e, i], up).wait_recv()
                total = keep[e, at].astype(F32) + yrecv[e, at].astype(F32)
                keep[e, at] = (total + flow[e, at].astype(F32)).astype(BF16)

            src = keep.at[e, at]

            @pl.when(e > d)
            def _():
                remote(src, flow.at[e, at], send.at[e, i], receive.at[e, i], up).start()

            @pl.when(e < d - 1)
            def _():
                remote(src, flow.at[e, at], send.at[e, i], receive.at[e, i], down).start()

            @pl.when(e == d - 1)
            def _():
                remote(src, last.at[at], send.at[e, i], last_sem.at[which, i], down).start()

    def flows_in(k, _):
        middle(k)
        flows(0, k)
        return 0

    def flows_other(k, _):
        flows(1, k)
        return 0

    lax.fori_loop(0, n - 1, flows_in, 0)

    @pl.when(d > 0)
    def _():
        upstream_d(d)

    @pl.when(d < n - 1)
    def _():
        remote(last_d, last_d, ds_sem.at[0], last_d_sem, down).wait_recv()
        line[d] = (line[d].astype(F32) + last_d[...].astype(F32)).astype(BF16)

    crossing = remote(line.at[d, :, pl.ds(split, split)], yd, yds_sem, ydr_sem, across)
    crossing.start()

    lax.fori_loop(0, n - 1, flows_other, 0)

    second = remote(out_rows_a, out_rows_b, hop_sem.at[0], rs_sem.at[1], across)
    mine_half = pl.ds(pl.multiple_of(c * half, half), half)
    third_dst = rows_out.at[1, mine_half]

    def third(device):
        return remote(out_rows_b, third_dst, hop_sem.at[1], er_sem.at[2 + c], device)

    @pl.when((s == 1) & (t > 1))
    def _():
        remote(out_rows_a, out_rows_a, hop_sem.at[0], rs_sem.at[0], section).wait_recv()
        second.start()

    @pl.when((s == 1) & (t < 2))
    def _():
        second.wait_recv()
        pl.semaphore_wait(here_sem, 1)

    @pl.when((s == 1) & (t == 0))
    def _():
        third(section).start()

    @pl.when((s == 1) & (t == 1))
    def _():
        third(slanted).start()

    def landed(which, i):
        keep, _, yrecv, flow, last = groups[which]
        at = pl.ds(i * step, step)
        exchange(which, d, i).wait_recv()

        @pl.when(d > 0)
        def _():
            piece = flow.at[d, at]
            remote(
                piece, piece, fs_sem.at[which, d, i], fr_sem.at[which, d, i], up
            ).wait_recv()

        @pl.when(d < n - 1)
        def _():
            piece = last.at[at]
            remote(
                piece, piece, fs_sem.at[which, d, i], last_sem.at[which, i], down
            ).wait_recv()

        above = jnp.where(d > 0, flow[d, at].astype(F32), 0.0)
        below = jnp.where(d < n - 1, last[at].astype(F32), 0.0)
        return (keep[d, at].astype(F32) + yrecv[d, at].astype(F32)) + (above + below)

    results = [
        pltpu.make_async_copy(src, dst, out_sem.at[i])
        for i, (src, dst) in enumerate(
            ((out_q, q_out), (out_k, k_out), (out_v, v_out), (out_u, u_out), (out_o, o_out), (out_d, d_out))
        )
    ]
    rests = []
    for i in range(pieces):
        at = pl.ds(i * step, step)
        total = landed(0, i)
        for j, ref in enumerate((out_q, out_k, out_v)):
            ref[at] = total[:, j * local : (j + 1) * local]
        rests.append(total[:, 3 * local :])
    for i in range(3):
        results[i].start()
    found = smalls[0]
    out_g1[...] = found[0:1, :width]
    out_g2[...] = found[0:1, width : 2 * width]
    head = dim_scale.shape[1]
    scale = jnp.zeros((1, head), F32)
    for j in range(2):
        for i in range(local // head):
            start = 2 * width + j * 384 + i * head
            scale = scale + found[0:1, start : start + head]
    raw = dim_scale[...]
    grown = jnp.maximum(raw, 0.0) + jnp.log(1.0 + jnp.exp(-jnp.abs(raw)))
    out_s[...] = scale / grown * (1.0 / (1.0 + jnp.exp(-raw)))
    totals = []
    for i in range(pieces):
        total = landed(1, i)
        out_u[pl.ds(i * step, step)] = total[:, :local]
        totals.append(total[:, local:])
    results[3].start()
    out_o[...] = jnp.transpose(jnp.concatenate(totals, axis=0))
    results[4].start()
    crossing.wait_recv()
    most = line[d, :, :split].astype(F32) + yd[...].astype(F32)
    out_d[...] = jnp.transpose(jnp.concatenate([most, jnp.concatenate(rests, axis=0)], axis=1))
    results[5].start()

    @pl.when(t == 0)
    def _():
        for i in range(4):
            piece = rows_out.at[i // 2, pl.ds(i % 2 * half, half)]
            remote(piece, piece, es_sem, er_sem.at[i], owner).wait_recv()

    @pl.when(direct)
    def _():
        remote(final, spot, es_sem, er_sem.at[t], owner).wait_send()

    @pl.when(aside)
    def _():
        remote(final, out_rows_a, es_sem, rs_sem.at[0], section).wait_send()

    @pl.when((s == 1) & (t > 1))
    def _():
        second.wait_send()

    @pl.when((s == 1) & (t < 2))
    def _():
        third(section).wait_send()

    for copy in results:
        copy.wait()
    crossing.wait_send()
    for i in range(3):
        share(i).wait_send()

    @pl.when(d < n - 1)
    def _():
        link(0, up).wait_send()

    @pl.when(d > 0)
    def _():
        link(1, down).wait_send()

    def drain(e, _):
        for which in range(2):
            for i in range(pieces):
                exchange(which, e, i).wait_send()

        @pl.when(e != d)
        def _():
            for which in range(2):
                for i in range(pieces):
                    piece = groups[which][0].at[e, pl.ds(i * step, step)]
                    remote(
                        piece, piece, fs_sem.at[which, e, i], fr_sem.at[which, e, i], up
                    ).wait_send()
            remote(line.at[e], line.at[e], ds_sem.at[e], dr_sem.at[e], up).wait_send()

        return 0

    lax.fori_loop(0, n, drain, 0)


def gradients(n1, n2, gy, g, gp, gu, o, a, final, rows, dg1, dg2, ds, dim_scale):
    n = lax.axis_size("dp")
    length, width = n1.shape
    local = gp.shape[2] // 3
    chunk = width // n
    pieces = 4 if chunk % 64 == 0 else 1
    small = (1, 2 * width + 768)

    def lines(columns):
        return [pltpu.VMEM((n, chunk, columns), BF16)] * 4 + [pltpu.VMEM((chunk, columns), BF16)]

    split = local // 128 * 128
    line = pltpu.VMEM((n, chunk, 2 * split), BF16)
    return pl.pallas_call(
        gradient_kernel,
        out_shape=[jax.ShapeDtypeStruct((chunk, local), F32)] * 4
        + [jax.ShapeDtypeStruct((local, chunk), F32)] * 2
        + [
            jax.ShapeDtypeStruct(rows.shape, BF16),
            jax.ShapeDtypeStruct(dg1.shape, F32),
            jax.ShapeDtypeStruct(dg2.shape, F32),
            jax.ShapeDtypeStruct(dim_scale.shape, F32),
        ],
        in_specs=[ANY] * 10 + [VMEM] * 4,
        out_specs=[ANY] * 7 + [VMEM] * 3,
        input_output_aliases={9: 6},
        scratch_shapes=[pltpu.VMEM((chunk, local), F32)] * 4
        + [pltpu.VMEM((local, chunk), F32)] * 2
        + [
            pltpu.VMEM((2, length, width), BF16),
            pltpu.VMEM((4, n, chunk, length), BF16),
            pltpu.VMEM(gp.shape, BF16),
            pltpu.VMEM(gu.shape, BF16),
            pltpu.VMEM(o.shape, BF16),
            pltpu.VMEM(a.shape, BF16),
        ]
        + lines(4 * local - split)
        + lines(2 * local)
        + [line] * 2
        + [
            pltpu.VMEM((chunk, 2 * split), BF16),
            pltpu.VMEM((2, n, chunk, local - split), BF16),
            pltpu.VMEM((chunk, split), BF16),
            pltpu.VMEM(small, F32),
            pltpu.VMEM((3,) + small, F32),
            pltpu.VMEM((4,) + small, F32),
            pltpu.VMEM(final.shape, BF16),
            pltpu.VMEM(final.shape, BF16),
            DMA((4,)),
            DMA((4,)),
        ]
        + [DMA((2, n, pieces))] * 4
        + [
            DMA((2, pieces)),
            DMA((n,)),
            DMA((n,)),
            DMA,
            DMA,
            DMA,
            DMA((3,)),
            DMA((3,)),
            DMA((2,)),
            DMA((2,)),
            DMA,
            DMA((4,)),
            DMA((6,)),
            DMA((2,)),
            DMA((2,)),
            pltpu.SemaphoreType.REGULAR,
        ],
        compiler_params=pltpu.CompilerParams(
            collective_id=3, has_side_effects=True, vmem_limit_bytes=62 * MIB
        ),
        name="gradients",
    )(n1, n2, gy, g, gp, gu, o, a, final, rows, dg1, dg2, ds, dim_scale)


def hand_over_kernel(*refs):
    count = (len(refs) - 2) // 3
    sources, results, kept = refs[:count], refs[count : 2 * count], refs[2 * count : 3 * count]
    in_sem, out_sem = refs[3 * count :]
    come = [pltpu.make_async_copy(sources[i], kept[i], in_sem.at[i]) for i in range(count)]
    go = [pltpu.make_async_copy(kept[i], results[i], out_sem.at[i]) for i in range(count)]
    for copy in come:
        copy.start()
    for i in range(count):
        come[i].wait()
        go[i].start()
    for copy in go:
        copy.wait()


def hand_over(arrays):
    count = len(arrays)
    return pl.pallas_call(
        hand_over_kernel,
        out_shape=[jax.ShapeDtypeStruct(x.shape, x.dtype) for x in arrays],
        in_specs=[ANY] * count,
        out_specs=[ANY] * count,
        scratch_shapes=[pltpu.VMEM(x.shape, x.dtype) for x in arrays] + [DMA((count,)), DMA((count,))],
        compiler_params=pltpu.CompilerParams(vmem_limit_bytes=62 * MIB),
        name="hand_over",
    )(*arrays)


def body(
    inputs, cotangent, gain_attn, w_query, w_key, w_value, w_out, dim_scale, gain_mlp, w_up, w_down
):
    head = dim_scale.shape[1]
    shards = (w_query[0].T, w_key[0].T, w_value[0].T, w_out[0], w_up[0].T, w_down[0])
    done = forward(
        inputs, cotangent, shards, gain_attn, gain_mlp, dim_scale, head
    )
    x_halves, h, n1, q, k, v, o, lse, m, n2, u, a, g, win, wo, wu, wd = done
    layer_out, input_grads, final, g_all, gu, gy, gp, dg1, dg2, ds = backward(
        (g, h, q, k, v, o, lse, m, u, win, wo, wu, wd, x_halves),
        gain_attn,
        gain_mlp,
        dim_scale,
    )

    *pieces, input_grads, dg1, dg2, grad_scale = gradients(
        n1, n2, gy, g_all, gp, gu, o, a, final, input_grads, dg1, dg2, ds, dim_scale
    )
    results = hand_over([layer_out, input_grads, dg1, *pieces, grad_scale, dg2])
    layer_out, input_grads, dg1, *pieces, grad_scale, dg2 = results
    return (
        layer_out[None],
        input_grads[None],
        dg1,
        pieces[0][None],
        pieces[1][None],
        pieces[2][None],
        pieces[4][None],
        grad_scale,
        dg2,
        pieces[3][None],
        pieces[5][None],
    )


def solution(mesh):
    in_specs = (
        P("dp", "tensor", None),
        P("dp", "tensor", None),
        P("section", None),
        P("section", None, "tensor"),
        P("section", None, "tensor"),
        P("section", None, "tensor"),
        P("section", "tensor", None),
        P("section", None),
        P("section", None),
        P("section", None, "tensor"),
        P("section", "tensor", None),
    )
    out_specs = (
        P("section", "dp", "tensor", None),
        P("section", "dp", "tensor", None),
        P("section", None),
        P("section", "dp", "tensor"),
        P("section", "dp", "tensor"),
        P("section", "dp", "tensor"),
        P("section", "tensor", "dp"),
        P("section", None),
        P("section", None),
        P("section", "dp", "tensor"),
        P("section", "tensor", "dp"),
    )
    return jax.shard_map(body, mesh=mesh, in_specs=in_specs, out_specs=out_specs, check_vma=False)
```

```python
import functools
import math

import jax
import jax.numpy as jnp
from jax import lax
from jax.experimental import pallas as pl
from jax.experimental.pallas import tpu as pltpu
from jax.sharding import PartitionSpec as P

EPS = 1e-06
LOG2E = 1.442695041
NEGATIVE = -1e30
BF16 = jnp.bfloat16
F32 = jnp.float32
MESH = pl.DeviceIdType.MESH
ANY = pl.BlockSpec(memory_space=pl.ANY)
VMEM = pl.BlockSpec(memory_space=pltpu.VMEM)
DMA = pltpu.SemaphoreType.DMA
MIB = 1 << 20
PIECES = 4


def plain(a, b):
    return jnp.dot(a, b, preferred_element_type=F32)


def by_last(a, b):
    return lax.dot_general(a, b, (((1,), (1,)), ((), ())), preferred_element_type=F32)


def by_first(a, b):
    return lax.dot_general(a, b, (((0,), (0,)), ((), ())), preferred_element_type=F32)


def other(index):
    return index + 1 - 2 * lax.rem(index, 2)


def remote(src, dst, send, receive, device):
    return pltpu.make_async_remote_copy(
        src_ref=src,
        dst_ref=dst,
        send_sem=send,
        recv_sem=receive,
        device_id=device,
        device_id_type=MESH,
    )


def greet(devices):
    barrier = pltpu.get_barrier_semaphore()
    for device in devices:
        pl.semaphore_signal(barrier, inc=1, device_id=device, device_id_type=MESH)
    pl.semaphore_wait(barrier, len(devices))


def per_dim(raw):
    grown = jnp.maximum(raw, 0.0) + jnp.log(1.0 + jnp.exp(-jnp.abs(raw)))
    return (LOG2E / math.sqrt(raw.shape[1])) * grown


def inverse_rms(rows):
    return lax.rsqrt(jnp.mean(rows * rows, axis=1, keepdims=True) + EPS)


def forward_kernel(
    inputs, cotangent, w_q, w_k, w_v, w_o, w_u, w_d, gain_one, gain_two, scale,
    x_out, h_out, n1_out, q_out, k_out, v_out, o_out, lse_out, m_out, n2_out, u_out, a_out,
    g_out, win_out, wo_out, wu_out, wd_out,
    land, win, wo, wu, wd, passing, down_a, down_b, n1, q, k, v, o_heads, o, lse_cols, lse, ysend, yrecv,
    m, n2, u, a, zpart, zrecv, xout,
    own_sem, ps_sem, pr_sem, xs_sem, xp_sem, xr_sem, xfs_sem, wys_sem, wyr_sem, wzs_sem, wzr_sem,
    das_sem, dar_sem, dbs_sem, dbr_sem, dcs_sem, dcr_sem,
    ns_sem, nr_sem, nfs_sem, nfr_sem, ys_sem, yr_sem, zs_sem, zr_sem, save_sem,
):
    s, t, d = lax.axis_index("section"), lax.axis_index("tensor"), lax.axis_index("dp")
    blocks, rows, width = land.shape[1:]
    half = rows // 2
    local = w_o.shape[0]
    heads, _, head = q.shape
    per = heads // 2
    c, y = lax.rem(t, 2), t // 2
    t_core, t_across = other(t), lax.rem(t + 2, 4)
    t_diagonal = other(t_across)
    core = (s, t_core, d)
    across = (s, t_across, d)
    diagonal = (s, t_diagonal, d)
    beside = (s, t, other(d))
    section = (1 - s, t, d)
    greet([core, across, diagonal, beside, section])

    mine = pl.ds(pl.multiple_of(c * half, half), half)
    theirs = pl.ds(pl.multiple_of((1 - c) * half, half), half)

    shards = [w_q, w_k, w_v, w_o, w_u, w_d]

    def place(i, slot, start, size):
        if i < 3:
            return win.at[slot, pl.ds(pl.multiple_of(i * local + start, 16), size)]
        return (wo, wu, wd)[i - 3].at[pl.ds(pl.multiple_of(slot * local + start, 16), size)]

    short = local // 4
    parity = lax.rem(d, 2)

    def own(i):
        return pltpu.make_async_copy(shards[i], place(i, 0, 0, local), own_sem.at[i])

    def strip(i, which):
        return pl.multiple_of(which * 2 * short + i % 2 * short, 16)

    def crossing(i):
        start = strip(i, parity)
        dst = place(i // 2, 1, start, short)
        return remote(
            shards[i // 2].at[pl.ds(start, short)], dst, wys_sem.at[i], wyr_sem.at[i], across
        )

    def beside_copy(i, which):
        piece = place(i // 2, 1, strip(i, which), short)
        return remote(piece, piece, wzs_sem.at[i], wzr_sem.at[i], beside)

    def relay(i):
        crossing(i).wait_recv()
        beside_copy(i, parity).start()

    def arrived(i):
        beside_copy(i, 1 - parity).wait_recv()

    quarter = local // PIECES

    def down_piece(buffer, i):
        return buffer.at[pl.ds(i * quarter, quarter)]

    def down_first(i):
        return remote(
            down_piece(w_d, i), down_piece(down_a, i), das_sem.at[i], dar_sem.at[i], section
        )

    def down_second(i):
        return remote(
            down_piece(down_a, i), down_piece(down_b, i), dbs_sem.at[i], dbr_sem.at[i], across
        )

    def down_third(i):
        return remote(
            down_piece(down_b, i), wd.at[pl.ds(local + i * quarter, quarter)],
            dcs_sem.at[i], dcr_sem.at[i], section,
        )

    step = rows // PIECES

    def passing_copy(i):
        piece = pl.ds(i * step, step)
        return remote(
            inputs.at[1 - y, piece], passing.at[piece], ps_sem.at[i], pr_sem.at[i], across
        )

    def onward(i):
        piece = pl.ds(i * step, step)
        return remote(
            passing.at[piece], land.at[0, t_across, piece], ps_sem.at[PIECES + i], xp_sem.at[i], section
        )

    def over(i):
        piece = pl.ds(i * step, step)
        return remote(
            cotangent.at[1 - y, piece], land.at[0, t, piece], xs_sem.at[i], xp_sem.at[i], across
        )

    def local_rows(source):
        pltpu.make_async_copy(source.at[y], land.at[0, t], xr_sem.at[t]).start()
        remote(source.at[y], land.at[0, t], xs_sem.at[PIECES], xr_sem.at[t], core).start()

    def block_wait(b):
        piece = land.at[0, b]
        remote(piece, piece, xs_sem.at[PIECES], xr_sem.at[b], core).wait_recv()

    def far_rows():
        for i in range(PIECES):
            piece = land.at[0, t_across, pl.ds(i * step, step)]
            remote(piece, piece, xfs_sem, xp_sem.at[i], core).wait_recv()
        piece = land.at[0, t_across]
        remote(piece, piece, xfs_sem, xr_sem.at[t_across], core).start()

    def near_rows():
        block_wait(t)
        block_wait(t_core)

    for i in range(3):
        own(i).start()

    @pl.when(s == 0)
    def _():
        for i in range(10):
            crossing(i).start()
        local_rows(inputs)
        for i in range(PIECES):
            down_first(i).start()

    @pl.when(s == 1)
    def _():
        for i in range(PIECES):
            passing_copy(i).start()
        local_rows(cotangent)

    for i in range(3, 6):
        own(i).start()

    @pl.when(s == 1)
    def _():
        for i in range(PIECES):
            passing_copy(i).wait_recv()
            onward(i).start()
            down_first(i).wait_recv()
            down_second(i).start()
        for i in range(12):
            crossing(i).start()
        for i in range(PIECES):
            over(i).start()
        for i in range(PIECES):
            down_second(i).wait_recv()
            down_third(i).start()
        for i in range(6):
            relay(i)

    for i in range(3):
        own(i).wait()

    def save(kind, b, src, dst):
        pltpu.make_async_copy(src, dst, save_sem.at[kind, b]).start()

    causal = lax.broadcasted_iota(jnp.int32, (rows, rows), 0) >= lax.broadcasted_iota(
        jnp.int32, (rows, rows), 1
    )
    lane = lax.broadcasted_iota(jnp.int32, (rows, 128), 1)

    factor = per_dim(scale[...])

    def attention(turn, _):
        b = jnp.where(s == 0, lax.rem(turn, blocks), turn // 2)
        j = jnp.where(s == 0, turn // blocks, lax.rem(turn, 2))
        at = pl.ds(pl.multiple_of(b * rows, rows), rows)

        @pl.when((s == 0) & (turn == 0))
        def _():
            near_rows()

        @pl.when((s == 0) & (turn == 2 * (1 - y)))
        def _():
            for i in range(4):
                relay(i)
            far_rows()
            block_wait(t_diagonal)

        @pl.when((s == 0) & (turn == blocks))
        def _():
            relay(6)
            relay(7)
            for i in range(6):
                arrived(i)

        @pl.when((s == 1) & (turn == 0))
        def _():
            for i in range(6):
                arrived(i)

        @pl.when((s == 1) & (j == 0))
        def _():
            piece = land.at[1, b, mine]
            remote(piece, piece, ns_sem.at[b], nr_sem.at[b], core).wait_recv()
            remote(piece, piece, nfs_sem.at[b], nfr_sem.at[b], core).start()
            rest = land.at[1, b, theirs]
            remote(rest, rest, nfs_sem.at[b], nfr_sem.at[b], core).wait_recv()

        @pl.when(j == 0)
        def _():
            hidden = land[s, b].astype(F32)
            n1[at] = (hidden * inverse_rms(hidden) * gain_one[...]).astype(BF16)
            lse_cols[b] = jnp.zeros(lse_cols.shape[1:], F32)
            save(0, b, land.at[s, b], h_out.at[b])
            save(1, b, n1.at[at], n1_out.at[at])

        projected = by_last(n1[at], win[j])
        first = j * per
        for i in range(per):
            cut = i * head
            q[first + i, at] = (projected[:, cut : cut + head] * factor).astype(BF16)
            cut += local
            k[first + i, at] = projected[:, cut : cut + head].astype(BF16)
            cut += local
            v[first + i, at] = projected[:, cut : cut + head].astype(BF16)
        for bb in range(blocks):

            @pl.when(b == bb)
            def _():
                for i in range(per):
                    hd = first + i
                    qh = q[hd, bb * rows : (bb + 1) * rows]
                    near = by_last(qh, k[hd, bb * rows : (bb + 1) * rows])
                    near = jnp.where(causal, near, NEGATIVE)
                    top = jnp.max(near, axis=1, keepdims=True)
                    if bb:
                        far = by_last(qh, k[hd, : bb * rows])
                        top = jnp.maximum(top, jnp.max(far, axis=1, keepdims=True))
                    near = jnp.exp(near - top)
                    total = jnp.sum(near, axis=1, keepdims=True)
                    mixed = plain(near.astype(BF16), v[hd, bb * rows : (bb + 1) * rows])
                    if bb:
                        far = jnp.exp(far - top)
                        total = total + jnp.sum(far, axis=1, keepdims=True)
                        mixed = mixed + plain(far.astype(BF16), v[hd, : bb * rows])
                    o_heads[hd, bb * rows : (bb + 1) * rows] = (mixed / total).astype(BF16)
                    lse_cols[bb] = jnp.where(lane == hd, top + jnp.log(total), lse_cols[bb])

        @pl.when(j == 1)
        def _():
            o[at] = jnp.concatenate([o_heads[i, at] for i in range(heads)], axis=1)
            lse[b] = jnp.transpose(lse_cols[b])[:heads]
            save(2, b, q.at[:, at], q_out.at[:, at])
            save(3, b, k.at[:, at], k_out.at[:, at])
            save(4, b, v.at[:, at], v_out.at[:, at])
            save(5, b, o.at[at], o_out.at[at])
            save(6, b, lse.at[b], lse_out.at[b])

        for i, when in ((4, 2), (5, 3), (8, 4), (9, 5)):

            @pl.when((s == 0) & (turn == when))
            def _():
                relay(i)

        for i in range(6):

            @pl.when((s == 1) & (turn == i))
            def _():
                relay(6 + i)

        return 0

    def project(b, _):
        @pl.when(b == 0)
        def _():
            own(3).wait()
            arrived(6)
            arrived(7)

        at = pl.ds(pl.multiple_of(b * rows, rows), rows)
        ysend[b] = plain(o[at], wo[...]).astype(BF16)
        remote(ysend.at[b], yrecv.at[b], ys_sem.at[b], yr_sem.at[b], core).start()
        return 0

    lax.fori_loop(0, 2 * blocks, attention, 0)

    lax.fori_loop(0, blocks, project, 0)

    own(4).wait()
    own(5).wait()
    arrived(8)
    arrived(9)

    @pl.when(s == 0)
    def _():
        for i in range(PIECES):
            down_third(i).wait_recv()

    @pl.when(s == 1)
    def _():
        arrived(10)
        arrived(11)

    weights = [(win, win_out), (wo, wo_out), (wu, wu_out), (wd, wd_out)]
    for i, (src, dst) in enumerate(weights):
        save(11, i, src, dst)

    def feed(b, _):
        at = pl.ds(pl.multiple_of(b * rows, rows), rows)
        remote(ysend.at[b], yrecv.at[b], ys_sem.at[b], yr_sem.at[b], core).wait_recv()
        middle = land[s, b].astype(F32) + (ysend[b].astype(F32) + yrecv[b].astype(F32))
        m[b] = middle
        normed = (middle * inverse_rms(middle) * gain_two[...]).astype(BF16)
        n2[at] = normed
        up = by_last(normed, wu[...])
        u[b] = up
        active = (up / (1.0 + jnp.exp(-up))).astype(BF16)
        a[at] = active
        zpart[b] = plain(active, wd[...])
        copy = remote(zpart.at[b, theirs], zrecv.at[b], zs_sem.at[b], zr_sem.at[b], core)
        copy.start()
        save(7, b, m.at[b], m_out.at[b])
        save(8, b, n2.at[at], n2_out.at[at])
        save(9, b, u.at[b], u_out.at[b])
        save(10, b, a.at[at], a_out.at[at])

        @pl.when(s == 0)
        def _():
            finish(b)

        @pl.when((s == 1) & (b > 0))
        def _():
            finish(b - 1)

        @pl.when((s == 1) & (b == blocks - 2))
        def _():
            near_rows()
            far_rows()

        return 0

    def finish(b):
        copy = remote(zpart.at[b, theirs], zrecv.at[b], zs_sem.at[b], zr_sem.at[b], core)
        copy.wait_recv()
        xout[b] = (m[b, mine] + (zpart[b, mine] + zrecv[b])).astype(BF16)

        @pl.when(s == 0)
        def _():
            remote(xout.at[b], land.at[1, b, mine], ns_sem.at[b], nr_sem.at[b], section).start()

        save(13, b, xout.at[b], x_out.at[b])

    lax.fori_loop(0, blocks, feed, 0)

    @pl.when(s == 1)
    def _():
        finish(blocks - 1)


    @pl.when(s == 1)
    def _():
        block_wait(t_diagonal)

    for b in range(blocks):
        pltpu.make_async_copy(land.at[0, b], g_out.at[b], save_sem.at[12, b]).start()

    block = land.at[0, t]
    remote(block, block, xs_sem.at[PIECES], xr_sem.at[t], core).wait_send()
    remote(block, block, xfs_sem, xr_sem.at[t], core).wait_send()

    @pl.when(s == 1)
    def _():
        for i in range(PIECES):
            passing_copy(i).wait_send()
            onward(i).wait_send()
            over(i).wait_send()
            down_second(i).wait_send()
            down_third(i).wait_send()
        for i in range(10, 12):
            crossing(i).wait_send()
            beside_copy(i, parity).wait_send()

    @pl.when(s == 0)
    def _():
        for i in range(PIECES):
            down_first(i).wait_send()

    for b in range(blocks):
        piece = land.at[0, b, mine]
        remote(ysend.at[b], yrecv.at[b], ys_sem.at[b], yr_sem.at[b], core).wait_send()
        remote(zpart.at[b, theirs], zrecv.at[b], zs_sem.at[b], zr_sem.at[b], core).wait_send()

        @pl.when(s == 0)
        def _():
            remote(xout.at[b], piece, ns_sem.at[b], nr_sem.at[b], section).wait_send()

        @pl.when(s == 1)
        def _():
            remote(piece, piece, nfs_sem.at[b], nfr_sem.at[b], core).wait_send()

    for i in range(10):
        crossing(i).wait_send()
        beside_copy(i, parity).wait_send()
    for i, (src, dst) in enumerate(weights):
        pltpu.make_async_copy(src, dst, save_sem.at[11, i]).wait()
    for b in range(blocks):
        at = pl.ds(b * rows, rows)
        saved = [
            (land.at[s, b], h_out.at[b]),
            (n1.at[at], n1_out.at[at]),
            (q.at[:, at], q_out.at[:, at]),
            (k.at[:, at], k_out.at[:, at]),
            (v.at[:, at], v_out.at[:, at]),
            (o.at[at], o_out.at[at]),
            (lse.at[b], lse_out.at[b]),
            (m.at[b], m_out.at[b]),
            (n2.at[at], n2_out.at[at]),
            (u.at[b], u_out.at[b]),
            (a.at[at], a_out.at[at]),
        ]
        for kind, (src, dst) in enumerate(saved):
            pltpu.make_async_copy(src, dst, save_sem.at[kind, b]).wait()
        pltpu.make_async_copy(land.at[0, b], g_out.at[b], save_sem.at[12, b]).wait()
        pltpu.make_async_copy(xout.at[b], x_out.at[b], save_sem.at[13, b]).wait()


def forward(inputs, cotangent, shards, gain_one, gain_two, scale, head):
    _, rows, width = inputs.shape
    local = shards[0].shape[0]
    heads = 2 * local // head
    blocks = lax.axis_size("tensor")
    length = blocks * rows
    half = rows // 2
    shape = jax.ShapeDtypeStruct
    weights = [(2, 3 * local, width), (2 * local, width), (2 * local, width), (2 * local, width)]
    outs = [
        shape((blocks, half, width), BF16),
        shape((blocks, rows, width), BF16),
        shape((length, width), BF16),
        shape((heads, length, head), BF16),
        shape((heads, length, head), BF16),
        shape((heads, length, head), BF16),
        shape((length, 2 * local), BF16),
        shape((blocks, heads, rows), F32),
        shape((blocks, rows, width), F32),
        shape((length, width), BF16),
        shape((blocks, rows, 2 * local), F32),
        shape((length, 2 * local), BF16),
        shape((blocks, rows, width), BF16),
    ] + [shape(w, BF16) for w in weights]
    scratch = [pltpu.VMEM((2, blocks, rows, width), BF16)]
    scratch += [pltpu.VMEM(w, BF16) for w in weights]
    scratch += [
        pltpu.VMEM((rows, width), BF16),
        pltpu.VMEM((local, width), BF16),
        pltpu.VMEM((local, width), BF16),
        pltpu.VMEM((length, width), BF16),
        pltpu.VMEM((heads, length, head), BF16),
        pltpu.VMEM((heads, length, head), BF16),
        pltpu.VMEM((heads, length, head), BF16),
        pltpu.VMEM((heads, length, head), BF16),
        pltpu.VMEM((length, 2 * local), BF16),
        pltpu.VMEM((blocks, rows, 128), F32),
        pltpu.VMEM((blocks, heads, rows), F32),
        pltpu.VMEM((blocks, rows, width), BF16),
        pltpu.VMEM((blocks, rows, width), BF16),
        pltpu.VMEM((blocks, rows, width), F32),
        pltpu.VMEM((length, width), BF16),
        pltpu.VMEM((blocks, rows, 2 * local), F32),
        pltpu.VMEM((length, 2 * local), BF16),
        pltpu.VMEM((blocks, rows, width), F32),
        pltpu.VMEM((blocks, half, width), F32),
        pltpu.VMEM((blocks, half, width), BF16),
        DMA((6,)),
        DMA((2 * PIECES,)),
        DMA((PIECES,)),
        DMA((PIECES + 1,)),
        DMA((PIECES,)),
        DMA((blocks,)),
        DMA,
    ]
    scratch += [DMA((12,))] * 4 + [DMA((PIECES,))] * 6 + [DMA((blocks,))] * 8 + [DMA((14, blocks))]
    return pl.pallas_call(
        forward_kernel,
        out_shape=outs,
        in_specs=[ANY] * 8 + [VMEM] * 3,
        out_specs=[ANY] * len(outs),
        scratch_shapes=scratch,
        compiler_params=pltpu.CompilerParams(
            collective_id=1, has_side_effects=True, vmem_limit_bytes=62 * MIB
        ),
        name="forward",
    )(inputs, cotangent, *shards, gain_one, gain_two, scale)


def backward_kernel(
    g_in, h_in, q_in, k_in, v_in, o_in, lse_in, m_in, u_in, win_in, wo_in, wu_in, wd_in, x_in,
    gain_one, gain_two, scale,
    x_rows, out_rows, final, g_out, gu_out, gy_out, gp_out, dg1, dg2, ds,
    g, win, wo, wu, wd, h, q, k, v, o, lse, m, u, gu, gy, gp, ysend, yrecv, gm, go_heads, gq_heads,
    delta, dk, dv, n1part, n1recv, xout,
    load_sem, w_sem, ns_sem, nr_sem, nfs_sem, nfr_sem, ys_sem, yr_sem, zs_sem, zr_sem, os_sem, or_sem,
    xs_sem, xr_sem, save_sem,
):
    s, t, d = lax.axis_index("section"), lax.axis_index("tensor"), lax.axis_index("dp")
    blocks, rows, width = g.shape
    half = rows // 2
    local = wu.shape[0] // 2
    heads, _, head = q.shape
    per = heads // 2
    c, y = lax.rem(t, 2), t // 2
    core = (s, other(t), d)
    across = (s, lax.rem(t + 2, 4), d)
    diagonal = (s, other(lax.rem(t + 2, 4)), d)
    section = (1 - s, t, d)
    mine = pl.ds(pl.multiple_of(c * half, half), half)
    theirs = pl.ds(pl.multiple_of((1 - c) * half, half), half)

    weights = [(wd_in, wd), (wu_in, wu), (wo_in, wo), (win_in, win)]

    def weight(i):
        return pltpu.make_async_copy(*weights[i], w_sem.at[i])

    def load(kind, b):
        at = pl.ds(pl.multiple_of(b * rows, rows), rows)
        src, dst = [
            (u_in.at[b], u.at[b]),
            (m_in.at[b], m.at[b]),
            (o_in.at[at], o.at[at]),
            (q_in.at[:, at], q.at[:, at]),
            (k_in.at[:, at], k.at[:, at]),
            (v_in.at[:, at], v.at[:, at]),
            (lse_in.at[b], lse.at[b]),
            (h_in.at[b, mine], h.at[b]),
        ][kind]
        return pltpu.make_async_copy(src, dst, load_sem.at[kind, b])

    def incoming(b):
        return pltpu.make_async_copy(g_in.at[b], g.at[b], nr_sem.at[b])

    last = blocks - 1

    @pl.when(s == 1)
    def _():
        incoming(last).start()

    weight(0).start()
    load(0, last).start()
    weight(1).start()
    load(1, last).start()

    barrier = pltpu.get_barrier_semaphore()
    for device in (core, across, diagonal, section):
        pl.semaphore_signal(barrier, inc=1, device_id=device, device_id_type=MESH)

    weight(2).start()
    for kind in (2, 3, 6):
        load(kind, last).start()
    for bb in reversed(range(blocks)):
        load(4, bb).start()
        load(5, bb).start()
    weight(3).start()
    load(7, last).start()

    spot = out_rows.at[y, mine]

    def owner_copy(b, src, dst, send, receive, act):
        @pl.when(b == t)
        def _():
            act(pltpu.make_async_copy(src, dst, receive.at[t]))

        @pl.when(b != t)
        def _():
            act(remote(src, dst, send.at[b], receive.at[t], (s, b, d)))

    dg1[...] = jnp.zeros_like(dg1)
    dg2[...] = jnp.zeros_like(dg2)
    ds[...] = jnp.zeros_like(ds)

    causal = lax.broadcasted_iota(jnp.int32, (rows, rows), 0) <= lax.broadcasted_iota(
        jnp.int32, (rows, rows), 1
    )
    factor = jnp.concatenate([per_dim(scale[...])] * per, axis=1)
    width_two = heads * head
    row_head = lax.broadcasted_iota(jnp.int32, (heads, width_two), 0)
    start = row_head * head
    place = lax.broadcasted_iota(jnp.int32, (heads, width_two), 1)
    member = jnp.where((place >= start) & (place < start + head), 1.0, 0.0).astype(BF16)

    def save(kind, b, src, dst):
        pltpu.make_async_copy(src, dst, save_sem.at[kind, b]).start()

    def neighbours_sum(b, i):
        lanes = pl.ds(i * (width // 2), width // 2)
        return remote(
            ysend.at[b, :, lanes], yrecv.at[b, :, lanes], ys_sem.at[i, b], yr_sem.at[i, b], core
        )

    def up_part(turn):
        b = last - turn
        at = pl.ds(pl.multiple_of(b * rows, rows), rows)

        @pl.when(s == 1)
        def _():
            incoming(b).wait()

        @pl.when(turn == 0)
        def _():
            pl.semaphore_wait(barrier, 4)

        @pl.when(s == 0)
        def _():
            piece = g.at[b, mine]
            remote(piece, piece, ns_sem.at[b], nr_sem.at[b], core).wait_recv()
            remote(piece, piece, nfs_sem.at[b], nfr_sem.at[b], core).start()
            rest = g.at[b, theirs]
            remote(rest, rest, nfs_sem.at[b], nfr_sem.at[b], core).wait_recv()

        @pl.when(turn == 0)
        def _():
            weight(0).wait()

        load(0, b).wait()
        save(0, b, g.at[b], g_out.at[at])
        grad = g[b]
        grad_act = by_last(grad, wd[...])
        up = u[b]
        sigma = 1.0 / (1.0 + jnp.exp(-up))
        grad_up = (grad_act * sigma * (1.0 + up * (1.0 - sigma))).astype(BF16)
        gu[at] = grad_up

        @pl.when(turn == 0)
        def _():
            weight(1).wait()

        save(1, b, gu.at[at], gu_out.at[at])
        for i in range(2):
            lanes = slice(i * (width // 2), (i + 1) * (width // 2))
            ysend[b, :, lanes] = plain(grad_up, wu[:, lanes]).astype(BF16)
            neighbours_sum(b, i).start()

        @pl.when(turn == 0)
        def _():
            for bb in range(blocks):
                owner_copy(
                    bb, x_in.at[bb], x_rows.at[y, mine], xs_sem, xr_sem, lambda copy: copy.start()
                )

    def one_block(turn, _):
        b = last - turn
        at = pl.ds(pl.multiple_of(b * rows, rows), rows)
        load(1, b).wait()
        for i in range(2):
            neighbours_sum(b, i).wait_recv()
        grad = g[b]
        grad_normed = ysend[b].astype(F32) + yrecv[b].astype(F32)
        middle = m[b]
        inverse = inverse_rms(middle)
        unit = middle * inverse
        grad_unit = grad_normed * gain_two[...]
        dg2[...] += jnp.sum(grad_normed * unit, axis=0, keepdims=True)
        grad_middle = grad.astype(F32) + inverse * (
            grad_unit - unit * jnp.mean(grad_unit * unit, axis=1, keepdims=True)
        )
        gm[...] = grad_middle
        grad_mid = grad_middle.astype(BF16)
        gy[at] = grad_mid
        save(2, b, gy.at[at], gy_out.at[at])

        @pl.when(turn == 0)
        def _():
            weight(2).wait()

        load(2, b).wait()
        grad_mixed = by_last(grad_mid, wo[...]).astype(BF16)
        both = grad_mixed.astype(F32) * o[at].astype(F32)
        high = both.astype(BF16)
        low = (both - high.astype(F32)).astype(BF16)
        delta[...] = by_last(member, high) + by_last(member, low)
        for i in range(heads):
            go_heads[i] = grad_mixed[:, i * head : (i + 1) * head]

        @pl.when(turn == 0)
        def _():
            for bb in range(blocks):
                load(4, bb).wait()
                load(5, bb).wait()

        load(3, b).wait()
        load(6, b).wait()

        @pl.when(turn < last)
        def _():
            for kind in (0, 1, 2, 3, 6, 7):
                load(kind, b - 1).start()

        @pl.when((turn < last) & (s == 1))
        def _():
            incoming(b - 1).start()

        for bb in range(blocks):

            @pl.when(b == bb)
            def _():
                def group(first, _):
                    for j in range(per):
                        i = first * per + j
                        qh = q[i, bb * rows : (bb + 1) * rows]
                        gh = go_heads[i]
                        offset = lse[bb, pl.ds(i, 1)]
                        inner = delta[pl.ds(i, 1)]
                        total = None
                        for lo, hi in ((bb * rows, (bb + 1) * rows), (0, bb * rows)):
                            if lo == hi:
                                continue
                            kj = k[i, lo:hi]
                            weight = jnp.exp(by_last(kj, qh) - offset)
                            if lo == bb * rows and hi > lo and hi == (bb + 1) * rows:
                                weight = jnp.where(causal, weight, 0.0)
                            grad_score = weight * (by_last(v[i, lo:hi], gh) - inner)
                            grad_score = grad_score.astype(BF16)
                            more_v = plain(weight.astype(BF16), gh)
                            more_k = plain(grad_score, qh)
                            if bb == last:
                                dv[i, lo:hi] = more_v
                                dk[i, lo:hi] = more_k
                            else:
                                dv[i, lo:hi] += more_v
                                dk[i, lo:hi] += more_k
                            part = by_first(kj, grad_score)
                            total = part if total is None else total + part
                        gq_heads[i] = jnp.transpose(total)
                    return 0

                lax.fori_loop(0, 2, group, 0)

        for j in range(2):
            mine_heads = range(j * per, (j + 1) * per)
            grad_scaled = jnp.concatenate([gq_heads[i] for i in mine_heads], axis=1)
            queries = jnp.concatenate([q[i, at] for i in mine_heads], axis=1).astype(F32)
            ds[pl.ds(j, 1)] += jnp.sum(grad_scaled * queries, axis=0, keepdims=True)
            grads = [
                (grad_scaled * factor).astype(BF16),
                jnp.concatenate([dk[i, at] for i in mine_heads], axis=1).astype(BF16),
                jnp.concatenate([dv[i, at] for i in mine_heads], axis=1).astype(BF16),
            ]
            gp[j, at] = jnp.concatenate(grads, axis=1)
        save(3, b, gp.at[:, at], gp_out.at[:, at])

        @pl.when(turn == 0)
        def _():
            weight(3).wait()


        def by_half(place, which):
            rows_at = pl.ds(pl.multiple_of(b * rows + which * half, half), half)
            n1part[place] = plain(gp[0, rows_at], win[0]) + plain(gp[1, rows_at], win[1])

        @pl.when(turn < last)
        def _():
            n1part[...] = plain(gp[0, at], win[0]) + plain(gp[1, at], win[1])

        @pl.when(turn == last)
        def _():
            by_half(theirs, 1 - c)

        copy = remote(n1part.at[theirs], n1recv.at[b], zs_sem.at[b], zr_sem.at[b], core)
        copy.start()

        @pl.when(turn == last)
        def _():
            by_half(mine, c)


        @pl.when(turn < last)
        def _():
            up_part(turn + 1)

        load(7, b).wait()
        hidden = h[b].astype(F32)
        inverse = inverse_rms(hidden)
        unit = hidden * inverse
        copy.wait_recv()
        grad_normed = n1part[mine] + n1recv[b]
        grad_unit = grad_normed * gain_one[...]
        dg1[...] += jnp.sum(grad_normed * unit, axis=0, keepdims=True)
        xout[b] = (
            gm[mine]
            + inverse * (grad_unit - unit * jnp.mean(grad_unit * unit, axis=1, keepdims=True))
        ).astype(BF16)

        @pl.when(s == 1)
        def _():
            remote(xout.at[b], g.at[b, mine], ns_sem.at[b], nr_sem.at[b], section).start()

        @pl.when(b > 0)
        def _():
            owner_copy(b, xout.at[b], spot, os_sem, or_sem, lambda copy: copy.start())

        @pl.when(b == 0)
        def _():
            save(4, 0, xout.at[0], final)

        copy.wait_send()
        return 0

    up_part(jnp.int32(0))
    lax.fori_loop(0, blocks, one_block, 0)

    for b in range(blocks):
        at = pl.ds(b * rows, rows)
        piece = g.at[b, mine]
        for i in range(2):
            neighbours_sum(b, i).wait_send()
        here = x_rows.at[b // 2, pl.ds((b % 2) * half, half)]
        remote(here, here, xs_sem.at[b], xr_sem.at[b], core).wait_recv()

        @pl.when(b != t)
        def _():
            remote(x_in.at[b], here, xs_sem.at[b], xr_sem.at[b], core).wait_send()

        @pl.when(t > 0)
        def _():
            here = out_rows.at[b // 2, pl.ds((b % 2) * half, half)]
            remote(here, here, os_sem.at[b], or_sem.at[b], core).wait_recv()

        @pl.when((b != t) & (b > 0))
        def _():
            remote(xout.at[b], here, os_sem.at[b], or_sem.at[b], core).wait_send()

        @pl.when(s == 1)
        def _():
            remote(xout.at[b], piece, ns_sem.at[b], nr_sem.at[b], section).wait_send()

        @pl.when(s == 0)
        def _():
            remote(piece, piece, nfs_sem.at[b], nfr_sem.at[b], core).wait_send()

        saved = [
            (g.at[b], g_out.at[at]),
            (gu.at[at], gu_out.at[at]),
            (gy.at[at], gy_out.at[at]),
            (gp.at[:, at], gp_out.at[:, at]),
        ]
        for kind, (src, dst) in enumerate(saved):
            pltpu.make_async_copy(src, dst, save_sem.at[kind, b]).wait()
    pltpu.make_async_copy(xout.at[0], final, save_sem.at[4, 0]).wait()


def backward(saved, gain_one, gain_two, scale):
    g_in, h_in, q_in = saved[:3]
    win_in, wo_in, wu_in, wd_in = saved[9:13]
    blocks, rows, width = g_in.shape
    heads, length, head = q_in.shape
    local = wu_in.shape[0] // 2
    half = rows // 2
    shape = jax.ShapeDtypeStruct
    outs = [
        shape((2, rows, width), BF16),
        shape((2, rows, width), BF16),
        shape((half, width), BF16),
        shape((length, width), BF16),
        shape((length, 2 * local), BF16),
        shape((length, width), BF16),
        shape((2, length, 3 * local), BF16),
        shape((1, width), F32),
        shape((1, width), F32),
        shape((2, local), F32),
    ]
    scratch = [
        pltpu.VMEM((blocks, rows, width), BF16),
        pltpu.VMEM(win_in.shape, BF16),
        pltpu.VMEM(wo_in.shape, BF16),
        pltpu.VMEM(wu_in.shape, BF16),
        pltpu.VMEM(wd_in.shape, BF16),
        pltpu.VMEM((blocks, half, width), BF16),
        pltpu.VMEM((heads, length, head), BF16),
        pltpu.VMEM((heads, length, head), BF16),
        pltpu.VMEM((heads, length, head), BF16),
        pltpu.VMEM((length, 2 * local), BF16),
        pltpu.VMEM((blocks, heads, rows), F32),
        pltpu.VMEM((blocks, rows, width), F32),
        pltpu.VMEM((blocks, rows, 2 * local), F32),
        pltpu.VMEM((length, 2 * local), BF16),
        pltpu.VMEM((length, width), BF16),
        pltpu.VMEM((2, length, 3 * local), BF16),
        pltpu.VMEM((blocks, rows, width), BF16),
        pltpu.VMEM((blocks, rows, width), BF16),
        pltpu.VMEM((rows, width), F32),
        pltpu.VMEM((heads, rows, head), BF16),
        pltpu.VMEM((heads, rows, head), F32),
        pltpu.VMEM((heads, rows), F32),
        pltpu.VMEM((heads, length, head), F32),
        pltpu.VMEM((heads, length, head), F32),
        pltpu.VMEM((rows, width), F32),
        pltpu.VMEM((blocks, half, width), F32),
        pltpu.VMEM((blocks, half, width), BF16),
        DMA((8, blocks)),
        DMA((4,)),
    ]
    scratch += [DMA((blocks,))] * 4 + [DMA((2, blocks))] * 2 + [DMA((blocks,))] * 6 + [DMA((5, blocks))]
    return pl.pallas_call(
        backward_kernel,
        out_shape=outs,
        in_specs=[ANY] * 14 + [VMEM] * 3,
        out_specs=[ANY] * 7 + [VMEM] * 3,
        scratch_shapes=scratch,
        compiler_params=pltpu.CompilerParams(
            collective_id=2, has_side_effects=True, vmem_limit_bytes=62 * MIB
        ),
        name="backward",
    )(*saved, gain_one, gain_two, scale)


def farthest_first(d, k, n):
    found = 0
    for i in range(n):
        above = list(range(n - 1, i, -1))
        below = list(range(i))
        first, second = (above, below) if len(above) >= len(below) else (below, above)
        lead = len(first) - len(second) - 1
        order = first[: max(lead, 0)]
        rest = first[max(lead, 0) :]
        for j in range(max(len(rest), len(second))):
            order += rest[j : j + 1] + second[j : j + 1]
        order.append(i)
        picked = 0
        for j, e in enumerate(order):
            picked = picked + jnp.where(k == j, e, 0)
        found = found + jnp.where(d == i, picked, 0)
    return found


def gradient_kernel(
    n1_in, n2_in, gy_in, g_in, gp_in, gu_in, o_in, a_in, final, rows_in, dg1, dg2, ds, dim_scale,
    q_out, k_out, v_out, u_out, o_out, d_out, rows_out, out_g1, out_g2, out_s,
    out_q, out_k, out_v, out_u, out_o, out_d, x, xt, gp, gu, o, a,
    keep_a, give_a, yrecv_a, flow_a, last_a, keep_b, give_b, yrecv_b, flow_b, last_b,
    line, flow_d, last_d, rest, yd, small, smalls, chain, out_rows_a, out_rows_b,
    x_sem, g_sem, ys_sem, yr_sem, fs_sem, fr_sem, last_sem, ds_sem, dr_sem, last_d_sem,
    yds_sem, ydr_sem, ss_sem, sr_sem, cs_sem, cr_sem, es_sem, er_sem, out_sem, rs_sem, hop_sem, here_sem,
):
    s, t, d = lax.axis_index("section"), lax.axis_index("tensor"), lax.axis_index("dp")
    n, chunk, _ = keep_a.shape
    local = a.shape[1] // 2
    split = yd.shape[1]
    width = dg1.shape[1]
    pieces = ys_sem.shape[2]
    step = chunk // pieces
    core = (s, other(t), d)
    across = (s, lax.rem(t + 2, 4), d)
    diagonal = (s, other(lax.rem(t + 2, 4)), d)
    up = (s, t, lax.rem(d + 1, n))
    down = (s, t, lax.rem(d + n - 1, n))
    c, y = lax.rem(t, 2), t // 2

    sources = [g_in, n1_in, n2_in, gy_in]
    operands = [(a_in, a), (gp_in, gp), (gu_in, gu), (o_in, o)]

    def load(i):
        return pltpu.make_async_copy(sources[i], x.at[i % 2], x_sem.at[i])

    def operand(i):
        return pltpu.make_async_copy(*operands[i], g_sem.at[i])

    section = (1 - s, t, d)
    slanted = (1 - s, 1 - t, d)
    barrier = pltpu.get_barrier_semaphore()
    for device in (core, across, diagonal, up, down):
        pl.semaphore_signal(barrier, inc=1, device_id=device, device_id_type=MESH)

    @pl.when((s == 1) & (t != 1))
    def _():
        pl.semaphore_signal(barrier, inc=1, device_id=section, device_id_type=MESH)

    @pl.when((s == 1) & (t == 1))
    def _():
        pl.semaphore_signal(barrier, inc=1, device_id=slanted, device_id_type=MESH)

    load(0).start()
    operand(0).start()
    load(1).start()
    for i in range(1, 4):
        operand(i).start()

    small[0:1, :width] = dg1[...]
    small[0:1, width : 2 * width] = jnp.where(c == 0, dg2[...], 0.0)
    small[0:1, 2 * width : 2 * width + local] = ds[0:1]
    small[0:1, 2 * width + 384 : 2 * width + 384 + local] = ds[1:2]

    partners = [core, across, diagonal]

    def share(i):
        return remote(small, smalls.at[i], ss_sem.at[i], sr_sem.at[i], partners[i])

    def turn(i):
        load(i).wait()
        turned = jnp.transpose(x[i % 2])
        for e in range(n):
            xt[i, e] = turned[e * chunk : (e + 1) * chunk]
        if i + 2 < 4:
            load(i + 2).start()

    groups = [(keep_a, give_a, yrecv_a, flow_a, last_a), (keep_b, give_b, yrecv_b, flow_b, last_b)]

    def exchange(which, e, i):
        _, give, yrecv, _, _ = groups[which]
        rows = pl.ds(i * step, step)
        return remote(
            give.at[e, rows], yrecv.at[e, rows], ys_sem.at[which, e, i], yr_sem.at[which, e, i], across
        )

    def send_all(which, e):
        for i in range(pieces):
            exchange(which, e, i).start()

    def send_d(e):
        src = line.at[e]

        @pl.when(e > d)
        def _():
            remote(src, flow_d.at[e], ds_sem.at[e], dr_sem.at[e], up).start()

        @pl.when(e < d - 1)
        def _():
            remote(src, flow_d.at[e], ds_sem.at[e], dr_sem.at[e], down).start()

        @pl.when(e == d - 1)
        def _():
            remote(src, last_d, ds_sem.at[e], last_d_sem, down).start()

    def upstream_d(e):
        piece = flow_d.at[e]
        remote(piece, piece, ds_sem.at[e], dr_sem.at[e], up).wait_recv()
        line[e] = (line[e].astype(F32) + flow_d[e].astype(F32)).astype(BF16)

    def down_product(k):
        e = farthest_first(d, k, n)
        both = plain(xt[0, e], a[...]).astype(BF16)
        line[e] = jnp.concatenate([both[:, :split], both[:, local : local + split]], axis=1)
        for j in range(2):
            rest[j, e] = both[:, j * local + split : (j + 1) * local]

    def first_d(k):
        e = farthest_first(d, k, n)

        @pl.when(((d == 0) | (d == n - 1)) & (e != d))
        def _():
            send_d(e)

    def in_product(k, j):
        e = farthest_first(d, k, n)
        (keep_a, give_a)[j][e] = jnp.concatenate(
            [plain(xt[1, e], gp[j]).astype(BF16), rest[j, e]], axis=1
        )

    turn(0)
    operand(0).wait()
    down_product(0)
    turn(1)
    operand(1).wait()
    in_product(0, 1)

    heard = jnp.where(s == 0, jnp.where(t == 0, 2, jnp.where(t == 1, 0, 1)), 0)
    pl.semaphore_wait(barrier, 5 + heard)

    @pl.when((s == 0) & (t == 0))
    def _():
        pl.semaphore_signal(here_sem, inc=1, device_id=section, device_id_type=MESH)
        pl.semaphore_signal(here_sem, inc=1, device_id=slanted, device_id_type=MESH)

    send_all(0, farthest_first(d, 0, n))
    first_d(0)
    for i in range(3):
        share(i).start()

    half = final.shape[0]
    owner = (s, 0, d)
    spot = rows_out.at[y, pl.ds(pl.multiple_of(c * half, half), half)]

    @pl.when(t == 0)
    def _():
        pltpu.make_async_copy(final, spot, er_sem.at[0]).start()

    direct = (t == 1) | ((t > 1) & (s == 1))
    aside = (t > 1) & (s == 0)

    @pl.when(t == 1)
    def _():
        remote(final, spot, es_sem, er_sem.at[t], owner).start()

    @pl.when(aside)
    def _():
        remote(final, out_rows_a, es_sem, rs_sem.at[0], section).start()

    def more_down(k, _):
        down_product(k)
        first_d(k)
        return 0

    lax.fori_loop(1, n, more_down, 0)

    def more_in(k, _):
        in_product(k, 1)

        @pl.when(k < n - 1)
        def _():
            send_all(0, farthest_first(d, k, n))

        in_product(k, 0)
        return 0

    lax.fori_loop(1, n, more_in, 0)
    in_product(0, 0)

    turn(2)
    turn(3)
    operand(2).wait()
    operand(3).wait()

    def other_product(k, _):
        e = farthest_first(d, k, n)
        ups = plain(xt[2, e], gu[...])
        outs = plain(xt[3, e], o[...])
        for j, target in ((1, give_b), (0, keep_b)):
            cut = slice(j * local, (j + 1) * local)
            target[e] = jnp.concatenate([ups[:, cut], outs[:, cut]], axis=1).astype(BF16)
            if j:

                @pl.when(k < n - 1)
                def _():
                    send_all(1, e)

        return 0

    lax.fori_loop(0, n, other_product, 0)
    send_all(0, d)
    send_all(1, d)

    @pl.when((t > 1) & (s == 1))
    def _():
        remote(final, spot, es_sem, er_sem.at[t], owner).start()

    for i in range(3):
        share(i).wait_recv()
    mine = small[...] + smalls[0] + (smalls[1] + smalls[2])

    def link(i, device):
        return remote(chain.at[i], chain.at[2 + i], cs_sem.at[i], cr_sem.at[i], device)

    smalls[0] = mine
    for i, opens, closes, device in ((0, d == 0, d == n - 1, up), (1, d == n - 1, d == 0, down)):
        chain[i] = mine

        @pl.when(jnp.logical_not(opens))
        def _():
            link(i, device).wait_recv()
            chain[i] = mine + chain[2 + i]
            smalls[0] += chain[2 + i]

        @pl.when(jnp.logical_not(closes))
        def _():
            link(i, device).start()

    def middle(k):
        e = farthest_first(d, k, n)

        @pl.when((d > 0) & (d < n - 1) & (e != d))
        def _():
            upstream_d(e)
            send_d(e)

    def flows(which, k):
        e = farthest_first(d, k, n)
        keep, give, yrecv, flow, last = groups[which]
        send, receive = fs_sem.at[which], fr_sem.at[which]
        for i in range(pieces):
            at = pl.ds(i * step, step)
            exchange(which, e, i).wait_recv()
            first = ((e > d) & (d == 0)) | ((e < d) & (d == n - 1))

            @pl.when((e != d) & first)
            def _():
                keep[e, at] = (keep[e, at].astype(F32) + yrecv[e, at].astype(F32)).astype(BF16)

            @pl.when((e != d) & jnp.logical_not(first))
            def _():
                piece = flow.at[e, at]
                remote(piece, piece, send.at[e, i], receive.at[e, i], up).wait_recv()
                total = keep[e, at].astype(F32) + yrecv[e, at].astype(F32)
                keep[e, at] = (total + flow[e, at].astype(F32)).astype(BF16)

            src = keep.at[e, at]

            @pl.when(e > d)
            def _():
                remote(src, flow.at[e, at], send.at[e, i], receive.at[e, i], up).start()

            @pl.when(e < d - 1)
            def _():
                remote(src, flow.at[e, at], send.at[e, i], receive.at[e, i], down).start()

            @pl.when(e == d - 1)
            def _():
                remote(src, last.at[at], send.at[e, i], last_sem.at[which, i], down).start()

    def flows_in(k, _):
        middle(k)
        flows(0, k)
        return 0

    def flows_other(k, _):
        flows(1, k)
        return 0

    lax.fori_loop(0, n - 1, flows_in, 0)

    @pl.when(d > 0)
    def _():
        upstream_d(d)

    @pl.when(d < n - 1)
    def _():
        remote(last_d, last_d, ds_sem.at[0], last_d_sem, down).wait_recv()
        line[d] = (line[d].astype(F32) + last_d[...].astype(F32)).astype(BF16)

    crossing = remote(line.at[d, :, pl.ds(split, split)], yd, yds_sem, ydr_sem, across)
    crossing.start()

    lax.fori_loop(0, n - 1, flows_other, 0)

    second = remote(out_rows_a, out_rows_b, hop_sem.at[0], rs_sem.at[1], across)
    mine_half = pl.ds(pl.multiple_of(c * half, half), half)
    third_dst = rows_out.at[1, mine_half]

    def third(device):
        return remote(out_rows_b, third_dst, hop_sem.at[1], er_sem.at[2 + c], device)

    @pl.when((s == 1) & (t > 1))
    def _():
        remote(out_rows_a, out_rows_a, hop_sem.at[0], rs_sem.at[0], section).wait_recv()
        second.start()

    @pl.when((s == 1) & (t < 2))
    def _():
        second.wait_recv()
        pl.semaphore_wait(here_sem, 1)

    @pl.when((s == 1) & (t == 0))
    def _():
        third(section).start()

    @pl.when((s == 1) & (t == 1))
    def _():
        third(slanted).start()

    def landed(which, i):
        keep, _, yrecv, flow, last = groups[which]
        at = pl.ds(i * step, step)
        exchange(which, d, i).wait_recv()

        @pl.when(d > 0)
        def _():
            piece = flow.at[d, at]
            remote(
                piece, piece, fs_sem.at[which, d, i], fr_sem.at[which, d, i], up
            ).wait_recv()

        @pl.when(d < n - 1)
        def _():
            piece = last.at[at]
            remote(
                piece, piece, fs_sem.at[which, d, i], last_sem.at[which, i], down
            ).wait_recv()

        above = jnp.where(d > 0, flow[d, at].astype(F32), 0.0)
        below = jnp.where(d < n - 1, last[at].astype(F32), 0.0)
        return (keep[d, at].astype(F32) + yrecv[d, at].astype(F32)) + (above + below)

    results = [
        pltpu.make_async_copy(src, dst, out_sem.at[i])
        for i, (src, dst) in enumerate(
            ((out_q, q_out), (out_k, k_out), (out_v, v_out), (out_u, u_out), (out_o, o_out), (out_d, d_out))
        )
    ]
    rests = []
    for i in range(pieces):
        at = pl.ds(i * step, step)
        total = landed(0, i)
        for j, ref in enumerate((out_q, out_k, out_v)):
            ref[at] = total[:, j * local : (j + 1) * local]
        rests.append(total[:, 3 * local :])
    for i in range(3):
        results[i].start()
    found = smalls[0]
    out_g1[...] = found[0:1, :width]
    out_g2[...] = found[0:1, width : 2 * width]
    head = dim_scale.shape[1]
    scale = jnp.zeros((1, head), F32)
    for j in range(2):
        for i in range(local // head):
            start = 2 * width + j * 384 + i * head
            scale = scale + found[0:1, start : start + head]
    raw = dim_scale[...]
    grown = jnp.maximum(raw, 0.0) + jnp.log(1.0 + jnp.exp(-jnp.abs(raw)))
    out_s[...] = scale / grown * (1.0 / (1.0 + jnp.exp(-raw)))
    totals = []
    for i in range(pieces):
        total = landed(1, i)
        out_u[pl.ds(i * step, step)] = total[:, :local]
        totals.append(total[:, local:])
    results[3].start()
    out_o[...] = jnp.transpose(jnp.concatenate(totals, axis=0))
    results[4].start()
    crossing.wait_recv()
    most = line[d, :, :split].astype(F32) + yd[...].astype(F32)
    out_d[...] = jnp.transpose(jnp.concatenate([most, jnp.concatenate(rests, axis=0)], axis=1))
    results[5].start()

    @pl.when(t == 0)
    def _():
        for i in range(4):
            piece = rows_out.at[i // 2, pl.ds(i % 2 * half, half)]
            remote(piece, piece, es_sem, er_sem.at[i], owner).wait_recv()

    @pl.when(direct)
    def _():
        remote(final, spot, es_sem, er_sem.at[t], owner).wait_send()

    @pl.when(aside)
    def _():
        remote(final, out_rows_a, es_sem, rs_sem.at[0], section).wait_send()

    @pl.when((s == 1) & (t > 1))
    def _():
        second.wait_send()

    @pl.when((s == 1) & (t < 2))
    def _():
        third(section).wait_send()

    for copy in results:
        copy.wait()
    crossing.wait_send()
    for i in range(3):
        share(i).wait_send()

    @pl.when(d < n - 1)
    def _():
        link(0, up).wait_send()

    @pl.when(d > 0)
    def _():
        link(1, down).wait_send()

    def drain(e, _):
        for which in range(2):
            for i in range(pieces):
                exchange(which, e, i).wait_send()

        @pl.when(e != d)
        def _():
            for which in range(2):
                for i in range(pieces):
                    piece = groups[which][0].at[e, pl.ds(i * step, step)]
                    remote(
                        piece, piece, fs_sem.at[which, e, i], fr_sem.at[which, e, i], up
                    ).wait_send()
            remote(line.at[e], line.at[e], ds_sem.at[e], dr_sem.at[e], up).wait_send()

        return 0

    lax.fori_loop(0, n, drain, 0)


def gradients(n1, n2, gy, g, gp, gu, o, a, final, rows, dg1, dg2, ds, dim_scale):
    n = lax.axis_size("dp")
    length, width = n1.shape
    local = gp.shape[2] // 3
    chunk = width // n
    pieces = 4 if chunk % 64 == 0 else 1
    small = (1, 2 * width + 768)

    def lines(columns):
        return [pltpu.VMEM((n, chunk, columns), BF16)] * 4 + [pltpu.VMEM((chunk, columns), BF16)]

    split = local // 128 * 128
    line = pltpu.VMEM((n, chunk, 2 * split), BF16)
    return pl.pallas_call(
        gradient_kernel,
        out_shape=[jax.ShapeDtypeStruct((chunk, local), F32)] * 4
        + [jax.ShapeDtypeStruct((local, chunk), F32)] * 2
        + [
            jax.ShapeDtypeStruct(rows.shape, BF16),
            jax.ShapeDtypeStruct(dg1.shape, F32),
            jax.ShapeDtypeStruct(dg2.shape, F32),
            jax.ShapeDtypeStruct(dim_scale.shape, F32),
        ],
        in_specs=[ANY] * 10 + [VMEM] * 4,
        out_specs=[ANY] * 7 + [VMEM] * 3,
        input_output_aliases={9: 6},
        scratch_shapes=[pltpu.VMEM((chunk, local), F32)] * 4
        + [pltpu.VMEM((local, chunk), F32)] * 2
        + [
            pltpu.VMEM((2, length, width), BF16),
            pltpu.VMEM((4, n, chunk, length), BF16),
            pltpu.VMEM(gp.shape, BF16),
            pltpu.VMEM(gu.shape, BF16),
            pltpu.VMEM(o.shape, BF16),
            pltpu.VMEM(a.shape, BF16),
        ]
        + lines(4 * local - split)
        + lines(2 * local)
        + [line] * 2
        + [
            pltpu.VMEM((chunk, 2 * split), BF16),
            pltpu.VMEM((2, n, chunk, local - split), BF16),
            pltpu.VMEM((chunk, split), BF16),
            pltpu.VMEM(small, F32),
            pltpu.VMEM((3,) + small, F32),
            pltpu.VMEM((4,) + small, F32),
            pltpu.VMEM(final.shape, BF16),
            pltpu.VMEM(final.shape, BF16),
            DMA((4,)),
            DMA((4,)),
        ]
        + [DMA((2, n, pieces))] * 4
        + [
            DMA((2, pieces)),
            DMA((n,)),
            DMA((n,)),
            DMA,
            DMA,
            DMA,
            DMA((3,)),
            DMA((3,)),
            DMA((2,)),
            DMA((2,)),
            DMA,
            DMA((4,)),
            DMA((6,)),
            DMA((2,)),
            DMA((2,)),
            pltpu.SemaphoreType.REGULAR,
        ],
        compiler_params=pltpu.CompilerParams(
            collective_id=3, has_side_effects=True, vmem_limit_bytes=62 * MIB
        ),
        name="gradients",
    )(n1, n2, gy, g, gp, gu, o, a, final, rows, dg1, dg2, ds, dim_scale)


def hand_over_kernel(*refs):
    count = (len(refs) - 2) // 3
    sources, results, kept = refs[:count], refs[count : 2 * count], refs[2 * count : 3 * count]
    in_sem, out_sem = refs[3 * count :]
    come = [pltpu.make_async_copy(sources[i], kept[i], in_sem.at[i]) for i in range(count)]
    go = [pltpu.make_async_copy(kept[i], results[i], out_sem.at[i]) for i in range(count)]
    for copy in come:
        copy.start()
    for i in range(count):
        come[i].wait()
        go[i].start()
    for copy in go:
        copy.wait()


def hand_over(arrays):
    count = len(arrays)
    return pl.pallas_call(
        hand_over_kernel,
        out_shape=[jax.ShapeDtypeStruct(x.shape, x.dtype) for x in arrays],
        in_specs=[ANY] * count,
        out_specs=[ANY] * count,
        scratch_shapes=[pltpu.VMEM(x.shape, x.dtype) for x in arrays] + [DMA((count,)), DMA((count,))],
        compiler_params=pltpu.CompilerParams(vmem_limit_bytes=62 * MIB),
        name="hand_over",
    )(*arrays)


def body(
    inputs, cotangent, gain_attn, w_query, w_key, w_value, w_out, dim_scale, gain_mlp, w_up, w_down
):
    head = dim_scale.shape[1]
    shards = (w_query[0].T, w_key[0].T, w_value[0].T, w_out[0], w_up[0].T, w_down[0])
    done = forward(
        inputs, cotangent, shards, gain_attn, gain_mlp, dim_scale, head
    )
    x_halves, h, n1, q, k, v, o, lse, m, n2, u, a, g, win, wo, wu, wd = done
    layer_out, input_grads, final, g_all, gu, gy, gp, dg1, dg2, ds = backward(
        (g, h, q, k, v, o, lse, m, u, win, wo, wu, wd, x_halves),
        gain_attn,
        gain_mlp,
        dim_scale,
    )

    *pieces, input_grads, dg1, dg2, grad_scale = gradients(
        n1, n2, gy, g_all, gp, gu, o, a, final, input_grads, dg1, dg2, ds, dim_scale
    )
    results = hand_over([layer_out, input_grads, dg1, *pieces, grad_scale, dg2])
    layer_out, input_grads, dg1, *pieces, grad_scale, dg2 = results
    return (
        layer_out[None],
        input_grads[None],
        dg1,
        pieces[0][None],
        pieces[1][None],
        pieces[2][None],
        pieces[4][None],
        grad_scale,
        dg2,
        pieces[3][None],
        pieces[5][None],
    )


def solution(mesh):
    in_specs = (
        P("dp", "tensor", None),
        P("dp", "tensor", None),
        P("section", None),
        P("section", None, "tensor"),
        P("section", None, "tensor"),
        P("section", None, "tensor"),
        P("section", "tensor", None),
        P("section", None),
        P("section", None),
        P("section", None, "tensor"),
        P("section", "tensor", None),
    )
    out_specs = (
        P("section", "dp", "tensor", None),
        P("section", "dp", "tensor", None),
        P("section", None),
        P("section", "dp", "tensor"),
        P("section", "dp", "tensor"),
        P("section", "dp", "tensor"),
        P("section", "tensor", "dp"),
        P("section", None),
        P("section", None),
        P("section", "dp", "tensor"),
        P("section", "tensor", "dp"),
    )
    return jax.shard_map(body, mesh=mesh, in_specs=in_specs, out_specs=out_specs, check_vma=False)
```
